32 devices in a mesh: shard: 8 (over z, y), replica: 4 (over x, core).
Axes of the slice: x: 2, y: 2, z: 4, core: 2. Of those that a mesh axis runs over, the one named last changes fastest.
Arguments:
- tokens: bfloat16 [4096, 2304], P(('shard', 'replica')), may hold values from -6 to 6
- attn_gain: bfloat16 [2304], P('shard'), may hold values from 0.5 to 1.5
- w_query: bfloat16 [2304, 2304], P('shard'), may hold values from -0.125 to 0.125
- w_key: bfloat16 [2304, 2304], P('shard'), may hold values from -0.125 to 0.125
- w_value: bfloat16 [2304, 2304], P('shard'), may hold values from -0.125 to 0.125
- w_out: bfloat16 [2304, 2304], P('shard'), may hold values from -3 to 3
- ffn_gain: bfloat16 [2304], P('shard'), may hold values from 0.5 to 1.5
- w_gate: bfloat16 [2304, 5760], P('shard'), may hold values from -0.125 to 0.125
- w_up: bfloat16 [2304, 5760], P('shard'), may hold values from -0.125 to 0.125
- w_down: bfloat16 [5760, 2304], P('shard'), may hold values from -0.3125 to 0.3125
- seq_ids: int32 [4096], P('shard'), may hold values from 0 to 15, as said below
- block_ids: int32 [4096], P('shard'), may hold values from 0 to 4095, as said below
- cotangent: bfloat16 [4096, 2304], P(('shard', 'replica')), may hold values from -6 to 6
Outputs:
- result: bfloat16 [4096, 2304], P(('shard', 'replica'))
- grad_tokens: bfloat16 [4096, 2304], P(('shard', 'replica'))
- grad_attn_gain: float32 [2304], P('shard')
- grad_query: float32 [2304, 2304], P('shard')
- grad_key: float32 [2304, 2304], P('shard')
- grad_value: float32 [2304, 2304], P('shard')
- grad_out: float32 [2304, 2304], P('shard')
- grad_ffn_gain: float32 [2304], P('shard')
- grad_gate: float32 [2304, 5760], P('shard')
- grad_up: float32 [2304, 5760], P('shard')
- grad_down: float32 [5760, 2304], P('shard')
The draws below stay inside these ranges and needn't reach their ends.
Inputs may be any that keep to these rules, and one draw needn't show every extreme that they name: `seq_ids`: within each aligned block of 512 tokens held by one index of shard lie two whole documents with ids rising by one: the first begins at the run's first token and ends inside the run's last 128 tokens, the second fills the rest; no id is shared by two runs. `block_ids`: block ids never fall along the tokens and are equal exactly within one block; a block lies in one document, a new block begins at every document's first token, and no block holds more than 256 tokens.
All inputs are finite; a program needn't handle non-finite values.
Results may differ from the reference program's by a relative error of at most 0.022.
Values may be sent and summed in bfloat16 or wider, within the bound.
A program may use at most 512 MiB of HBM per device.

```python
import math
import jax
import jax.numpy as jnp
from jax import lax

D = 2304
H = 36
FF = 5760
HD = 64
TOK_DEV = 128
BLOCK = 256
GROUP = 512
TOKENS = 4096


def document_layout(key):
    groups = TOKENS // GROUP
    key_end, key_shift = jax.random.split(key, 2)
    end_at = jax.random.randint(key_end, (groups, 1), GROUP - TOK_DEV + 1, GROUP)
    places = jnp.arange(GROUP, dtype=jnp.int32)[None, :]
    local_doc = (places >= end_at).astype(jnp.int32)
    seq_values = local_doc + 2 * jnp.arange(groups, dtype=jnp.int32)[:, None]
    doc_begin = jnp.where(local_doc == 0, 0, end_at)
    shifts = jax.random.randint(key_shift, (groups, 2), 0, BLOCK)
    shift_here = jnp.where(local_doc == 0, shifts[:, 0:1], shifts[:, 1:2])
    new_block = (((places - doc_begin + shift_here) % BLOCK == 0) | (places == doc_begin)).reshape(-1)
    positions = jnp.arange(TOKENS, dtype=jnp.int32)
    first_index = lax.cummax(jnp.where(new_block, positions, 0).astype(jnp.int32), axis=0)
    block_values = jnp.where(first_index == first_index[TOKENS - 1], TOKENS - 1, first_index)
    return (seq_values.reshape(-1).astype(jnp.int32), block_values.astype(jnp.int32))


def draw_seq_ids(key, part):
    return document_layout(key)[0]


def draw_block_ids(key, part):
    return document_layout(key)[1]


def strengthened(values, key, source, target, parts, factor):
    def block_of(dim):
        return (jnp.arange(values.shape[dim]) // (values.shape[dim] // parts)).reshape((-1,) + (1,) * (values.ndim - 1 - dim))

    one_side = jax.random.permutation(key, parts)[block_of(target)]
    second = (block_of(target) + parts // 2) % parts
    return jnp.where((block_of(source) == one_side) | (block_of(source) == second), factor * values, values)


def block_scale(own_key, extent, cuts, low, high):
    factor_of = 1.0
    for axis_at, parts in cuts:
        heights = jax.random.uniform(jax.random.fold_in(jax.random.fold_in(own_key, 6), axis_at), (parts,), jnp.float32, low / len(cuts), high / len(cuts))
        factor_of = factor_of * jnp.repeat(jnp.exp(heights), extent[axis_at] // parts).reshape((-1,) + (1,) * (len(extent) - 1 - axis_at))
    return factor_of


def bell_draw(own_key, dims, scale, reach, cuts=(), kind=jnp.bfloat16):
    level = block_scale(own_key, dims, cuts, -0.22, 0.18) if cuts else 1.0
    values = jax.random.normal(own_key, dims, jnp.float32) * scale * level
    return jnp.minimum(jnp.maximum(values, -reach), reach).astype(kind)


def gaussian_with(own_key, extent, spread, bound, shards, heavy, kind=jnp.bfloat16):
    entries = spread * jax.random.normal(own_key, extent, jnp.float32)
    if shards:
        entries = entries * block_scale(own_key, extent, shards, -0.22, 0.18)
    return jnp.clip(strengthened(entries, jax.random.fold_in(own_key, 3), *heavy), -bound, bound).astype(kind)


def setup_inputs(seed: int = 0) -> dict:
    keys = jax.random.split(jax.random.key(seed), 14)
    return {
        "tokens": bell_draw(keys[0], (TOKENS, D), 1.0, 6.0, ((0, 32),)),
        "attn_gain": jnp.clip(1.0 + 0.1 * jax.random.normal(keys[1], (D,), jnp.float32), 0.5, 1.5).astype(jnp.bfloat16),
        "w_query": bell_draw(keys[2], (D, D), D ** -0.5, 0.125, ((0, 8),)),
        "w_key": bell_draw(keys[3], (D, D), D ** -0.5, 0.125, ((0, 8),)),
        "w_value": bell_draw(keys[4], (D, D), D ** -0.5, 0.125, ((0, 8),)),
        "w_out": bell_draw(keys[5], (D, D), (max(1, D // GROUP)) ** -0.5, 3.0, ((0, 8),)),
        "ffn_gain": jnp.clip(1.0 + 0.1 * jax.random.normal(keys[6], (D,), jnp.float32), 0.5, 1.5).astype(jnp.bfloat16),
        "w_gate": bell_draw(keys[7], (D, FF), D ** -0.5, 0.125, ((0, 8),)),
        "w_up": bell_draw(keys[8], (D, FF), D ** -0.5, 0.125, ((0, 8),)),
        "w_down": bell_draw(keys[9], (FF, D), (FF // 16) ** -0.5, 0.3125, ((0, 8),)),
        "seq_ids": draw_seq_ids(jax.random.fold_in(keys[13], 71), 0),
        "block_ids": draw_block_ids(jax.random.fold_in(keys[13], 71), 0),
        "cotangent": gaussian_with(keys[12], (TOKENS, D), 1.0, 6.0, ((0, 32),), (0, 1, 32, 2.75)),
    }


@jax.custom_vjp
def low(v):
    return lax.optimization_barrier(v.astype(jnp.bfloat16)).astype(jnp.float32)

@jax.custom_vjp
def low_back(v):
    return v

def low_keep(v):
    return (low(v), None)

def low_pass(kept, grad):
    return (grad,)

def back_keep(v):
    return (v, None)

def back_low(kept, grad):
    return (low(grad),)
low.defvjp(low_keep, low_pass)
low_back.defvjp(back_keep, back_low)
highest = lax.Precision.HIGHEST
branch_scale = 1.4 / math.sqrt(40.0)
norm_eps = 1e-05
rope_base = 10000.0
masked_score = -1e+30

def matmul(left_side, right_side):
    return jnp.dot(left_side, right_side, precision=highest, preferred_element_type=jnp.float32)

def rms_scale(values, gain_vec):
    factor = lax.rsqrt(lax.optimization_barrier(jnp.mean(values * values, axis=-1, keepdims=True)) + norm_eps)
    return values * factor * gain_vec

def angle_tables(places, head_dim):
    halves = head_dim // 2
    frequency = jnp.exp(jnp.arange(halves).astype(jnp.float32) * (-2.0 * math.log(rope_base) / head_dim))
    angles = places.astype(jnp.float32)[:, None] * frequency[None, :]
    return (jnp.cos(angles)[:, None, :], jnp.sin(angles)[:, None, :])

def rotate(values, cosine, sine_table):
    halves = values.shape[-1] // 2
    former = values[..., :halves]
    latter = values[..., halves:]
    return jnp.concatenate([former * cosine - latter * sine_table, latter * cosine + former * sine_table], axis=-1)

def group_attention(pieces):
    queries, key_block, value_block, seq_group, block_group = pieces
    score_scale = 1.0 / math.sqrt(HD)
    scores = low_back(jnp.einsum('qhd,khd->hqk', queries, key_block, precision=highest) * score_scale)
    allowed = (seq_group[None, :] == seq_group[:, None]) & (block_group[None, :] <= block_group[:, None])
    scores = jnp.where(allowed[None], scores, masked_score)
    softmax_probs = low(jax.nn.softmax(scores, axis=-1))
    attn_mixed = jnp.einsum('hqk,khd->qhd', softmax_probs, value_block, precision=highest)
    return attn_mixed.reshape(attn_mixed.shape[0], -1)

def reference(tokens, attn_gain, w_query, w_key, w_value, w_out, ffn_gain, w_gate, w_up, w_down, seq_ids, block_ids, cotangent):
    groups = tokens.shape[0] // GROUP
    seq_group = seq_ids.reshape(groups, GROUP)
    block_group = block_ids.reshape(groups, GROUP)
    earlier = lax.optimization_barrier(jnp.sum((seq_group[:, None, :] < seq_group[:, :, None]).astype(jnp.int32), axis=2))
    places = (jnp.arange(GROUP, dtype=jnp.int32)[None, :] - earlier).reshape(-1)
    cosine, sine_table = angle_tables(places, HD)

    def reshape_groups(stacked):
        return stacked.reshape((groups, GROUP) + stacked.shape[1:])

    def layer_forward(inputs, gain_one, query_w, key_w, value_w, out_w, gain_two, gate_w, up_w, down_w):
        row_count = inputs.shape[0]
        normed = low(rms_scale(inputs, gain_one))
        query_raw = low_back(matmul(normed, query_w))
        key_raw = low_back(matmul(normed, key_w))
        value_raw = low(low_back(matmul(normed, value_w)))
        queries = low(rotate(query_raw.reshape(row_count, H, HD), cosine, sine_table))
        key_local = low(rotate(key_raw.reshape(row_count, H, HD), cosine, sine_table))
        value_local = value_raw.reshape(row_count, H, HD)
        attn_mixed = lax.map(jax.checkpoint(group_attention), (reshape_groups(queries), reshape_groups(key_local), reshape_groups(value_local), seq_group, block_group))
        attn_mixed = low(low_back(attn_mixed.reshape(row_count, D)))
        after_attn = inputs + branch_scale * low_back(matmul(attn_mixed, out_w))
        normed_two = low(rms_scale(after_attn, gain_two))
        gate_pre = low_back(matmul(normed_two, gate_w))
        up_proj = low_back(matmul(normed_two, up_w))
        hidden = low(jax.nn.silu(gate_pre) * up_proj)
        return after_attn + branch_scale * low_back(matmul(hidden, down_w))
    primals = (tokens.astype(jnp.float32), attn_gain.astype(jnp.float32), w_query.astype(jnp.float32), w_key.astype(jnp.float32), w_value.astype(jnp.float32), w_out.astype(jnp.float32), ffn_gain.astype(jnp.float32), w_gate.astype(jnp.float32), w_up.astype(jnp.float32), w_down.astype(jnp.float32))
    result, pullback = jax.vjp(layer_forward, *primals)
    grads = pullback(cotangent.astype(jnp.float32))
    return (result.astype(jnp.bfloat16), grads[0].astype(jnp.bfloat16), grads[1], grads[2], grads[3], grads[4], grads[5], grads[6], grads[7], grads[8], grads[9])
```

```python
import math

import jax
import jax.numpy as jnp
from jax import lax
from jax.sharding import PartitionSpec as P

H = 36
A = 4

branch_scale = 1.4 / math.sqrt(40.0)
norm_eps = 1e-05
rope_base = 10000.0
masked_score = -1e30


def product(left_side, right_side):
    return jnp.dot(left_side, right_side, preferred_element_type=jnp.float32)


def against(left_side, right_side):
    return lax.dot_general(
        left_side, right_side, (((1,), (1,)), ((), ())), preferred_element_type=jnp.float32
    )


def across(left_side, right_side):
    return lax.dot_general(
        left_side, right_side, (((0,), (0,)), ((), ())), preferred_element_type=jnp.float32
    )


def rms_norm(values, gain_vec):
    factor = lax.rsqrt(jnp.mean(values * values, axis=-1, keepdims=True) + norm_eps)
    return (factor, (values * factor * gain_vec).astype(jnp.bfloat16))


def norm_back(values, factor, gain_vec, upstream):
    scaled = upstream * gain_vec
    inner_mean = jnp.mean(scaled * values, axis=-1, keepdims=True)
    return (
        factor * scaled - values * (factor * factor * factor) * inner_mean,
        jnp.sum(upstream * values * factor, axis=0),
    )


def angle_tables(places, head_dim):
    halves = head_dim // 2
    frequency = jnp.exp(
        jnp.arange(halves).astype(jnp.float32) * (-2.0 * math.log(rope_base) / head_dim)
    )
    angles = places.astype(jnp.float32)[:, None] * frequency[None, :]
    return (jnp.cos(angles)[:, None, :], jnp.sin(angles)[:, None, :])


def rotate(values, cosine, sine_table):
    halves = values.shape[-1] // 2
    former = values[..., :halves]
    latter = values[..., halves:]
    return jnp.concatenate(
        [former * cosine - latter * sine_table, latter * cosine + former * sine_table], axis=-1
    )


def body(
    tokens,
    attn_gain,
    w_query,
    w_key,
    w_value,
    w_out,
    ffn_gain,
    w_gate,
    w_up,
    w_down,
    seq_ids,
    block_ids,
    cotangent,
):
    S = lax.axis_size("shard")
    R = lax.axis_size("replica")
    B = S // A
    rows, width = tokens.shape
    group = rows * R
    head_dim = width // H
    heads = H // R
    wcols = width // R
    ff = w_gate.shape[1]
    fcols = ff // (A * R)
    wrows = width // S
    shard_at = lax.axis_index("shard")
    r = lax.axis_index("replica")
    a, b = shard_at // B, shard_at % B
    a_groups = [[i * B + j for i in range(A)] for j in range(B)]
    b_groups = [[i * B + j for j in range(B)] for i in range(A)]
    bf = jnp.bfloat16
    score_scale = 1.0 / math.sqrt(head_dim)

    earlier = jnp.sum((seq_ids[None, :] < seq_ids[:, None]).astype(jnp.int32), axis=1)
    places = jnp.arange(group, dtype=jnp.int32) - earlier
    cosine, sine_table = angle_tables(places, head_dim)
    allowed = (seq_ids[None, :] == seq_ids[:, None]) & (block_ids[None, :] <= block_ids[:, None])

    gains = lax.all_gather(jnp.stack([attn_gain, ffn_gain]), "shard", axis=1, tiled=True)
    gain_one, gain_two = gains[0].astype(jnp.float32), gains[1].astype(jnp.float32)
    own_cols = lambda w: lax.dynamic_slice_in_dim(w, r * wcols, wcols, 1)
    w4 = jnp.concatenate([own_cols(w) for w in (w_query, w_key, w_value, w_out)], axis=1)
    w4 = lax.all_gather(w4, "shard", axis=0, tiled=True)
    wqkv, wo = w4[:, : 3 * wcols], w4[:, 3 * wcols :]
    tokens_group = lax.all_gather(tokens, "replica", axis=0, tiled=True)

    def spread(w):
        w = w.reshape(wrows, A, R, fcols)
        w = lax.dynamic_index_in_dim(w, r, 2, keepdims=False).transpose(1, 0, 2)
        w = lax.all_to_all(w, "shard", 0, 0, axis_index_groups=a_groups, tiled=True)
        w = lax.all_gather(w, "shard", axis=1, axis_index_groups=b_groups, tiled=True)
        return w.reshape(width, fcols)

    gate_w, up_w = spread(w_gate), spread(w_up)
    down_a = lax.all_gather(w_down, "shard", axis=0, axis_index_groups=b_groups, tiled=True)
    down_w = lax.dynamic_slice_in_dim(down_a, r * fcols, fcols, 0)

    def widen(v):
        v = lax.all_gather(v, "shard", axis=0, axis_index_groups=a_groups, tiled=True)
        return lax.all_gather(v, "replica", axis=0, tiled=True)

    def shrink(v):
        v = lax.psum_scatter(v, "replica", scatter_dimension=0, tiled=True)
        return lax.psum_scatter(
            v, "shard", scatter_dimension=0, axis_index_groups=a_groups, tiled=True
        )

    upstream = cotangent.astype(jnp.float32)
    d_down = widen((branch_scale * upstream).astype(bf))

    inputs = tokens.astype(jnp.float32)
    _, normed = rms_norm(tokens_group.astype(jnp.float32), gain_one)
    qkv = product(normed, wqkv)
    heads_of = lambda v: v.reshape(group, heads, head_dim)
    queries = rotate(heads_of(qkv[:, :wcols]), cosine, sine_table).astype(bf)
    keys = rotate(heads_of(qkv[:, wcols : 2 * wcols]), cosine, sine_table).astype(bf)
    values = heads_of(qkv[:, 2 * wcols :].astype(bf))
    scores = (
        jnp.einsum("thd,khd->htk", queries, keys, preferred_element_type=jnp.float32)
        * score_scale
    )
    scores = jnp.where(allowed[None], scores, masked_score)
    probs = jax.nn.softmax(scores, axis=-1)
    probs_low = probs.astype(bf)
    mixed = (
        jnp.einsum("htk,khd->thd", probs_low, values, preferred_element_type=jnp.float32)
        .reshape(group, wcols)
        .astype(bf)
    )
    mixed_all = lax.all_gather(mixed, "replica", axis=1, tiled=True)
    proj = product(mixed_all, wo).astype(bf)
    proj = lax.all_to_all(proj, "replica", 0, 1, tiled=True)
    after_attn = inputs + branch_scale * proj.astype(jnp.float32)
    factor_two, normed_two = rms_norm(after_attn, gain_two)

    n2 = widen(normed_two)
    gate_pre = product(n2, gate_w)
    up_proj = product(n2, up_w)
    sig = jax.nn.sigmoid(gate_pre)
    hidden = (gate_pre * sig * up_proj).astype(bf)
    d_hidden = against(d_down, down_w)
    d_gate = (d_hidden * up_proj * sig * (1.0 + gate_pre * (1.0 - sig))).astype(bf)
    d_up = (d_hidden * gate_pre * sig).astype(bf)
    d_n2 = shrink((against(d_gate, gate_w) + against(d_up, up_w)).astype(bf))
    ffn_out = shrink(product(hidden, down_w).astype(bf))
    result = after_attn + branch_scale * ffn_out.astype(jnp.float32)

    d_norm_two, gain_two_part = norm_back(
        after_attn, factor_two, gain_two, d_n2.astype(jnp.float32)
    )
    d_after = upstream + d_norm_two
    d_proj = (branch_scale * d_after).astype(bf)
    d_proj = lax.all_to_all(d_proj, "replica", 1, 0, tiled=True)
    d_mixed = lax.psum_scatter(
        against(d_proj, wo).astype(bf), "replica", scatter_dimension=1, tiled=True
    )
    d_mixed = heads_of(d_mixed)

    d_probs = jnp.einsum("thd,khd->htk", d_mixed, values, preferred_element_type=jnp.float32)
    d_scores = (
        probs * (d_probs - jnp.sum(d_probs * probs, axis=-1, keepdims=True))
    ).astype(bf)
    d_queries = (
        jnp.einsum("htk,khd->thd", d_scores, keys, preferred_element_type=jnp.float32)
        * score_scale
    )
    d_keys = (
        jnp.einsum("htk,thd->khd", d_scores, queries, preferred_element_type=jnp.float32)
        * score_scale
    )
    d_values = jnp.einsum("htk,thd->khd", probs_low, d_mixed, preferred_element_type=jnp.float32)
    d_qkv = jnp.concatenate(
        [
            rotate(d_queries, cosine, -sine_table).reshape(group, wcols).astype(bf),
            rotate(d_keys, cosine, -sine_table).reshape(group, wcols).astype(bf),
            d_values.reshape(group, wcols).astype(bf),
        ],
        axis=1,
    )
    d_normed = lax.psum_scatter(
        against(d_qkv, wqkv).astype(bf), "replica", scatter_dimension=0, tiled=True
    )
    factor_one, _ = rms_norm(inputs, gain_one)
    d_norm_one, gain_one_part = norm_back(
        inputs, factor_one, gain_one, d_normed.astype(jnp.float32)
    )
    grad_tokens = (d_after + d_norm_one).astype(bf)

    g4 = jnp.concatenate([across(normed, d_qkv), across(mixed_all, d_proj)], axis=1).astype(bf)
    g4 = lax.psum_scatter(g4, "shard", scatter_dimension=0, tiled=True)
    g4 = lax.all_gather(g4.reshape(wrows, 4, wcols), "replica", axis=2, tiled=True)
    g4 = g4.astype(jnp.float32)

    def collect(g):
        g = g.reshape(A, B, wrows, fcols)
        g = lax.psum_scatter(
            g, "shard", scatter_dimension=1, axis_index_groups=b_groups, tiled=True
        ).reshape(A, wrows, fcols)
        g = lax.all_to_all(g, "shard", 0, 0, axis_index_groups=a_groups, tiled=True)
        g = lax.all_gather(g, "replica", axis=0)
        return g.transpose(2, 1, 0, 3).reshape(wrows, ff).astype(jnp.float32)

    grad_gate = collect(across(n2, d_gate).astype(bf))
    grad_up = collect(across(n2, d_up).astype(bf))
    g_down = lax.all_gather(across(hidden, d_down).astype(bf), "replica", axis=0, tiled=True)
    grad_down = lax.psum_scatter(
        g_down, "shard", scatter_dimension=0, axis_index_groups=b_groups, tiled=True
    ).astype(jnp.float32)

    gain_grads = lax.psum(jnp.stack([gain_one_part, gain_two_part]), ("shard", "replica"))
    gain_grads = lax.dynamic_slice_in_dim(gain_grads, shard_at * wrows, wrows, 1)
    return (
        result.astype(bf),
        grad_tokens,
        gain_grads[0],
        g4[:, 0],
        g4[:, 1],
        g4[:, 2],
        g4[:, 3],
        gain_grads[1],
        grad_gate,
        grad_up,
        grad_down,
    )


def solution(mesh):
    split = P(("shard", "replica"), None)
    vec, mat = P("shard"), P("shard", None)
    in_specs = (split, vec, mat, mat, mat, mat, vec, mat, mat, mat, vec, vec, split)
    out_specs = (split, split, vec, mat, mat, mat, mat, vec, mat, mat, mat)
    return jax.shard_map(body, mesh=mesh, in_specs=in_specs, out_specs=out_specs, check_vma=False)
```

```python
import functools
import math

import jax
import jax.numpy as jnp
from jax import lax
from jax.experimental import pallas as pl
from jax.experimental.pallas import tpu as pltpu
from jax.sharding import PartitionSpec as P

H = 36
A = 4
X = 2

branch_scale = 1.4 / math.sqrt(40.0)
norm_eps = 1e-05
rope_base = 10000.0
masked_score = -1e30
MESH = pl.DeviceIdType.MESH
bf = jnp.bfloat16
f32 = jnp.float32
DMA = pltpu.SemaphoreType.DMA


class Place:
    def __init__(self, B):
        self.B = B
        s, r = lax.axis_index("shard"), lax.axis_index("replica")
        self.s, self.r = s, r
        self.a, self.b = s // B, s % B
        self.x, self.c = r // X, r % X
        self.rx = (1 - self.x) * X + self.c
        self.rc = self.x * X + 1 - self.c

    def line(self, a):
        return (a * self.B + self.b, self.r)

    def side(self, b):
        return (self.a * self.B + b, self.r)

    @property
    def over_x(self):
        return (self.s, self.rx)

    @property
    def over_core(self):
        return (self.s, self.rc)


def greet(place, a_peers=True, b_peers=False, r_peers=True, everyone=None):
    barrier = pltpu.get_barrier_semaphore()

    def signal(device):
        pl.semaphore_signal(barrier, inc=1, device_id=device, device_id_type=MESH)

    if everyone is not None:
        S, R = everyone

        def one(k, carry):
            signal((lax.rem(place.s + k // R, S), lax.rem(place.r + k % R, R)))
            return carry

        lax.fori_loop(1, S * R, one, 0)
        pl.semaphore_wait(barrier, S * R - 1)
        return
    count = 0
    if a_peers:
        for k in range(1, A):
            signal(place.line((place.a + k) % A))
            count += 1
    if b_peers:
        for k in range(1, place.B):
            signal(place.side((place.b + k) % place.B))
            count += 1
    if r_peers:
        signal(place.over_x)
        signal(place.over_core)
        count += 2
    pl.semaphore_wait(barrier, count)


def remote(src, dst, send, recv, device):
    return pltpu.make_async_remote_copy(
        src_ref=src, dst_ref=dst, send_sem=send, recv_sem=recv, device_id=device,
        device_id_type=MESH,
    )


def add_into(dst, first, second, tile=32):
    rows = dst.shape[0]
    tile = math.gcd(rows, tile) if math.gcd(rows, tile) >= 16 else rows

    def step(i, carry):
        at = pl.ds(pl.multiple_of(i * tile, tile), tile)
        dst[at, :] = (first[at, :].astype(f32) + second[at, :].astype(f32)).astype(dst.dtype)
        return carry

    lax.fori_loop(0, rows // tile, step, 0)


def run_flows(flows):
    flows = list(flows)
    while flows:
        for flow in list(flows):
            try:
                next(flow)
            except StopIteration:
                flows.remove(flow)


def widen_sems():
    return [DMA((A,)), DMA((X,)), DMA((A, 2)), DMA((A, 2)), DMA((X, A, 2)), DMA((1,))]


def widen_flow(place, own, out, sems):
    line_recv, _, line_send, over_x, over_core, local = sems
    a, r = place.a, place.r
    keep = pltpu.make_async_copy(own, out.at[r, a], local.at[0])
    keep.start()

    def to_line(src, block, way):
        at = 0 if way > 0 else 1
        return remote(
            src, out.at[r, block], line_send.at[block, at], line_recv.at[block],
            place.line(a + way),
        )

    def to_x(src, block):
        return remote(
            src, out.at[r, block], over_x.at[block, 0], over_x.at[block, 1], place.over_x
        )

    def to_core(src, x, block):
        return remote(
            src, out.at[x * X + place.c, block], over_core.at[x, block, 0],
            over_core.at[x, block, 1], place.over_core,
        )

    @pl.when(a < A - 1)
    def _():
        to_line(own, a, 1).start()

    @pl.when(a > 0)
    def _():
        to_line(own, a, -1).start()

    to_x(own, a).start()
    to_core(own, place.x, a).start()

    def pass_x(k):
        for ok, block in ((a - k >= 0, a - k), (a + k < A, a + k)) if k else ((None, a),):
            def go():
                src = out.at[place.rx, block]
                to_x(src, block).wait_recv()
                to_core(src, 1 - place.x, block).start()

            go() if ok is None else pl.when(ok)(go)

    for k in range(1, A):
        yield
        for way in (1, -1):
            block = a - way * k

            @pl.when((block >= 0) & (block < A))
            def _():
                src = out.at[r, block]
                to_line(src, block, way).wait_recv()

                @pl.when((a + way >= 0) & (a + way < A))
                def _():
                    to_line(src, block, way).start()

                to_x(src, block).start()
                to_core(src, place.x, block).start()

        yield
        pass_x(k - 1)
    yield
    pass_x(A - 1)
    yield
    keep.wait()
    for block in range(A):
        src = out.at[r, block]

        @pl.when((a < A - 1) & (block <= a))
        def _():
            to_line(src, block, 1).wait_send()

        @pl.when((a > 0) & (block >= a))
        def _():
            to_line(src, block, -1).wait_send()

        to_x(src, block).wait_send()
        for x in range(X):
            to_core(src, x, block).wait()


def shrink_scratch(rows, width):
    block = (rows, width)
    return [
        pltpu.VMEM((X, A) + block, bf),
        pltpu.VMEM((X, A) + block, bf),
        pltpu.VMEM((A,) + block, bf),
        pltpu.VMEM((2, A) + block, bf),
        DMA((X, A)), DMA((X, A, 2)), DMA((A, 2)), DMA((2, A, 2)),
    ]


shrink_order = (3, 0, 2, 1)


def line_reduce(place, sums, landed, sems, ready, final):
    a = place.a

    def hop(d, way):
        at = 0 if way > 0 else 1
        return remote(
            sums.at[d], landed.at[at, d], sems.at[at, d, 0], sems.at[at, d, 1],
            place.line(a + way),
        )

    for d in shrink_order:
        yield
        ready(d)
        for way in (1, -1):
            @pl.when((d - a) * way > 0)
            def _():
                @pl.when((a - way >= 0) & (a - way < A))
                def _():
                    hop(d, way).wait_recv()
                    add_into(sums.at[d], sums.at[d], landed.at[0 if way > 0 else 1, d])

                hop(d, way).start()

    yield
    for d in range(A):
        @pl.when(d == a)
        def _():
            for way in (1, -1):
                @pl.when((a - way >= 0) & (a - way < A))
                def _():
                    hop(d, way).wait_recv()
                    add_into(sums.at[d], sums.at[d], landed.at[0 if way > 0 else 1, d])

            final(sums.at[d])

        for way in (1, -1):
            @pl.when((d - a) * way > 0)
            def _():
                hop(d, way).wait_send()


def shrink_flow(place, part, out, scratch):
    half, from_core, from_x, landed, load_sem, core_sem, x_sem, line_sem = scratch
    x, c = place.x, place.c

    def load(i, d):
        return pltpu.make_async_copy(part.at[i * X + c, d], half.at[i, d], load_sem.at[i, d])

    def to_core(i, d):
        return remote(
            part.at[i * X + 1 - c, d], from_core.at[i, d], core_sem.at[i, d, 0],
            core_sem.at[i, d, 1], place.over_core,
        )

    def to_x(d):
        return remote(
            half.at[1 - x, d], from_x.at[d], x_sem.at[d, 0], x_sem.at[d, 1], place.over_x
        )

    for j in range(X):
        for d in shrink_order:
            i = 1 - x if j == 0 else x
            load(i, d).start()
            to_core(i, d).start()
    for d in shrink_order:
        yield
        load(1 - x, d).wait()
        to_core(1 - x, d).wait_recv()
        add_into(half.at[1 - x, d], half.at[1 - x, d], from_core.at[1 - x, d])
        to_x(d).start()

    def ready(d):
        load(x, d).wait()
        to_core(x, d).wait_recv()
        add_into(half.at[x, d], half.at[x, d], from_core.at[x, d])
        to_x(d).wait_recv()
        add_into(half.at[x, d], half.at[x, d], from_x.at[d])

    def final(ref):
        out[...] = ref[...]

    yield from line_reduce(place, half.at[x], landed, line_sem, ready, final)
    for d in range(A):
        to_x(d).wait_send()
        for i in range(X):
            to_core(i, d).wait_send()


def fold_scratch(rows, width):
    block = (rows, width)
    return [
        pltpu.VMEM((X,) + block, bf), pltpu.VMEM((X,) + block, bf), pltpu.VMEM(block, bf),
        DMA((X,)), DMA((X, 2)), DMA((2,)),
    ]


def fold_flow(place, part, out, scratch):
    half, from_core, from_x, load_sem, core_sem, x_sem = scratch
    x, c = place.x, place.c

    def load(i):
        return pltpu.make_async_copy(part.at[i * X + c], half.at[i], load_sem.at[i])

    def to_core(i):
        return remote(
            part.at[i * X + 1 - c], from_core.at[i], core_sem.at[i, 0], core_sem.at[i, 1],
            place.over_core,
        )

    to_x = remote(half.at[1 - x], from_x, x_sem.at[0], x_sem.at[1], place.over_x)
    for i in (1 - x, x):
        load(i).start()
        to_core(i).start()
    yield
    for i in (1 - x, x):
        load(i).wait()
        to_core(i).wait_recv()
        add_into(half.at[i], half.at[i], from_core.at[i])
        if i is not x:
            to_x.start()
    yield
    to_x.wait_recv()
    add_into(out, half.at[x], from_x)
    yield
    to_x.wait_send()
    for i in range(X):
        to_core(i).wait_send()


def share_sems():
    return [DMA((2,)), DMA((X, 2)), DMA((1,))]


def share_flow(place, own, out, sems, ready=None):
    x_sem, core_sem, local = sems
    r, x, c = place.r, place.x, place.c
    if ready is not None:
        yield
        ready()
    keep = pltpu.make_async_copy(own, out.at[r], local.at[0])
    to_x = remote(own, out.at[r], x_sem.at[0], x_sem.at[1], place.over_x)
    near = remote(own, out.at[r], core_sem.at[x, 0], core_sem.at[x, 1], place.over_core)
    far = remote(
        out.at[place.rx], out.at[place.rx], core_sem.at[1 - x, 0], core_sem.at[1 - x, 1],
        place.over_core,
    )
    to_x.start()
    near.start()
    keep.start()
    yield
    to_x.wait_recv()
    far.start()
    yield
    keep.wait()
    to_x.wait_send()
    near.wait()
    far.wait()


def exchange_sems():
    return [DMA((4, 2)), DMA((1,))]


def exchange_flow(place, part, out, sems):
    sem, local = sems
    r = place.r
    keep = pltpu.make_async_copy(part.at[r], out.at[r], local.at[0])
    keep.start()
    copies = []
    for k in (2, 3, 1):
        to = (r + k) % 4
        copies.append(
            remote(part.at[to], out.at[r], sem.at[k, 0], sem.at[k, 1], (place.s, to))
        )
        copies[-1].start()
    yield
    keep.wait()
    for copy in copies:
        copy.wait()


def greet_replicas(place):
    barrier = pltpu.get_barrier_semaphore()
    for k in range(1, 4):
        pl.semaphore_signal(
            barrier, inc=1, device_id=(place.s, (place.r + k) % 4), device_id_type=MESH
        )
    pl.semaphore_wait(barrier, 3)


def spread_sems(B):
    return [DMA((A,)), DMA((A, 2)), DMA((B, A, 2)), DMA((1,))]


def spread_flow(place, own, out, sems):
    line_recv, line_send, side, local = sems
    a, b, B = place.a, place.b, place.B
    keep = pltpu.make_async_copy(own, out.at[a, b], local.at[0])
    keep.start()

    def to_line(src, block, way):
        return remote(
            src, out.at[block, b], line_send.at[block, 0 if way > 0 else 1],
            line_recv.at[block], place.line(a + way),
        )

    def to_side(src, block, k):
        return remote(
            src, out.at[block, b], side.at[k, block, 0], side.at[k, block, 1],
            place.side((b + k) % B),
        )

    @pl.when(a < A - 1)
    def _():
        to_line(own, a, 1).start()

    @pl.when(a > 0)
    def _():
        to_line(own, a, -1).start()

    for k in range(1, B):
        to_side(own, a, k).start()
    for step in range(1, A):
        yield
        for way in (1, -1):
            block = a - way * step

            @pl.when((block >= 0) & (block < A))
            def _():
                src = out.at[block, b]
                to_line(src, block, way).wait_recv()

                @pl.when((a + way >= 0) & (a + way < A))
                def _():
                    to_line(src, block, way).start()

                for k in range(1, B):
                    to_side(src, block, k).start()

    yield
    keep.wait()
    for block in range(A):
        src = out.at[block, b]

        @pl.when((a < A - 1) & (block <= a))
        def _():
            to_line(src, block, 1).wait_send()

        @pl.when((a > 0) & (block >= a))
        def _():
            to_line(src, block, -1).wait_send()

        for k in range(1, B):
            to_side(src, block, k).wait()


def columns_sems(B):
    return [DMA((A, 2)), DMA((B, A, 2)), DMA((1,))]


def columns_flow(place, own, out, sems):
    line, side, local = sems
    a, b, B = place.a, place.b, place.B
    keep = pltpu.make_async_copy(own.at[a], out.at[a, b], local.at[0])
    keep.start()

    def to_line(k):
        to = (a + k) % A
        return remote(own.at[to], out.at[a, b], line.at[k, 0], line.at[k, 1], place.line(to))

    def to_side(src, block, k):
        return remote(
            src, out.at[block, b], side.at[k, block, 0], side.at[k, block, 1],
            place.side((b + k) % B),
        )

    for k in range(1, A):
        to_line(k).start()
    for k in range(1, B):
        to_side(own.at[a], a, k).start()
    for k in (1, 3, 2):
        yield
        to_line(k).wait_recv()
        block = (a + A - k) % A
        for j in range(1, B):
            to_side(out.at[block, b], block, j).start()
    yield
    keep.wait()
    for k in range(1, A):
        to_line(k).wait_send()
    for block in range(A):
        for k in range(1, B):
            to_side(out.at[block, b], block, k).wait()


def sides_sems(B):
    return [DMA((B, 2)), DMA((1,))]


def sides_flow(place, own, out, sems):
    side, local = sems
    b, B = place.b, place.B
    keep = pltpu.make_async_copy(own, out.at[b], local.at[0])
    keep.start()
    copies = [
        remote(own, out.at[b], side.at[k, 0], side.at[k, 1], place.side((b + k) % B))
        for k in range(1, B)
    ]
    for copy in copies:
        copy.start()
    yield
    keep.wait()
    for copy in copies:
        copy.wait()


def gather_scratch(B, rows, width):
    block = (rows, width)
    return [
        pltpu.VMEM((A,) + block, bf),
        pltpu.VMEM((B - 1, A) + block, bf),
        pltpu.VMEM((2, A) + block, bf),
        DMA((A,)), DMA((B, A, 2)), DMA((2, A, 2)),
    ]


def gather_flow(place, part, keep_at, scratch):
    sums, from_side, landed, load_sem, side_sem, line_sem = scratch
    b, B = place.b, place.B

    def load(d):
        return pltpu.make_async_copy(part.at[d, b], sums.at[d], load_sem.at[d])

    def to_side(k, d):
        to = (b + k) % B
        return remote(
            part.at[d, to], from_side.at[k - 1, d], side_sem.at[k, d, 0], side_sem.at[k, d, 1],
            place.side(to),
        )

    for d in shrink_order:
        load(d).start()
        for k in range(1, B):
            to_side(k, d).start()

    def ready(d):
        load(d).wait()
        for k in range(1, B):
            to_side(k, d).wait_recv()
            add_into(sums.at[d], sums.at[d], from_side.at[k - 1, d])

    yield from line_reduce(place, sums, landed, line_sem, ready, keep_at)
    for d in range(A):
        for k in range(1, B):
            to_side(k, d).wait_send()


def owners_scratch(B, rows, width):
    block = (rows, width)
    return [
        pltpu.VMEM((A,) + block, bf), pltpu.VMEM((B - 1, A) + block, bf),
        DMA((A,)), DMA((B, A, 2)), DMA((A, 2)), DMA((1,)),
    ]


def owners_flow(place, part, out, scratch):
    sums, from_side, load_sem, side_sem, line_sem, local = scratch
    a, b, B = place.a, place.b, place.B

    def load(d):
        return pltpu.make_async_copy(part.at[d, b], sums.at[d], load_sem.at[d])

    def to_side(k, d):
        to = (b + k) % B
        return remote(
            part.at[d, to], from_side.at[k - 1, d], side_sem.at[k, d, 0], side_sem.at[k, d, 1],
            place.side(to),
        )

    def to_line(k):
        to = (a + k) % A
        return remote(sums.at[to], out.at[a], line_sem.at[k, 0], line_sem.at[k, 1], place.line(to))

    for k in (1, 3, 2, 0):
        d = (a + k) % A
        load(d).start()
        for j in range(1, B):
            to_side(j, d).start()
    for k in (1, 3, 2, 0):
        yield
        d = (a + k) % A
        load(d).wait()
        for j in range(1, B):
            to_side(j, d).wait_recv()
            add_into(sums.at[d], sums.at[d], from_side.at[j - 1, d])
        if k:
            to_line(k).start()
    keep = pltpu.make_async_copy(sums.at[a], out.at[a], local.at[0])
    keep.start()
    yield
    keep.wait()
    for k in range(1, A):
        to_line(k).wait()
    for d in range(A):
        for j in range(1, B):
            to_side(j, d).wait_send()


ANY = pl.BlockSpec(memory_space=pl.ANY)
VMEM = pl.BlockSpec(memory_space=pltpu.VMEM)


def call(kernel, name, collective_id, outs, out_specs, scratch, args, in_specs):
    return pl.pallas_call(
        kernel,
        out_shape=outs,
        in_specs=in_specs,
        out_specs=out_specs,
        scratch_shapes=scratch,
        name=name,
        compiler_params=pltpu.CompilerParams(
            collective_id=collective_id, has_side_effects=True, vmem_limit_bytes=60 * 2**20
        ),
    )(*args)


def shape(*dims, dtype=bf):
    return jax.ShapeDtypeStruct(dims, dtype)


def split_refs(refs, *sizes):
    found, at = [], 0
    for size in sizes:
        found.append(refs[at : at + size])
        at += size
    return found


def first_gather(B, w4, tokens, d_down):
    def kernel(w4_in, tok_in, d_in, w4_out, tok_out, d_out, *refs):
        place = Place(B)
        s1, s2, s3 = split_refs(refs, 4, 3, 6)
        greet(place, True, True, True)
        run_flows(
            [
                share_flow(place, tok_in, tok_out, s2),
                spread_flow(place, w4_in, w4_out, s1),
                widen_flow(place, d_in, d_out, s3),
            ]
        )

    return call(
        kernel, "first_gather", 1,
        [
            shape(A, B, *w4.shape), shape(4, *tokens.shape), shape(4, A, *d_down.shape),
        ],
        [ANY] * 3,
        spread_sems(B) + share_sems() + widen_sems(),
        [w4, tokens, d_down],
        [ANY] * 3,
    )


def ffn_gather(B, normed_two, gate_up, down):
    def kernel(n_in, g_in, w_in, n_out, g_out, w_out, *refs):
        place = Place(B)
        s1, s2, s3 = split_refs(refs, 6, 3, 2)
        greet(place, True, True, True)
        run_flows(
            [
                widen_flow(place, n_in, n_out, s1),
                columns_flow(place, g_in, g_out, s2),
                sides_flow(place, w_in, w_out, s3),
            ]
        )

    return call(
        kernel, "ffn_gather", 2,
        [
            shape(4, A, *normed_two.shape), shape(A, B, *gate_up.shape[1:]),
            shape(B, *down.shape),
        ],
        [ANY] * 3,
        widen_sems() + columns_sems(B) + sides_sems(B),
        [normed_two, gate_up, down],
        [ANY] * 3,
    )


def share(name, collective_id, own):
    def kernel(own_in, out, *sems):
        place = Place(1)
        place.s = lax.axis_index("shard")
        greet(place, False, False, True)
        run_flows([share_flow(place, own_in, out, sems)])

    return call(
        kernel, name, collective_id, shape(4, *own.shape), ANY, share_sems(), [own], [ANY]
    )


def exchange(name, collective_id, part):
    def kernel(part_in, out, *sems):
        place = Place(1)
        greet_replicas(place)
        run_flows([exchange_flow(place, part_in, out, sems)])

    return call(
        kernel, name, collective_id, shape(*part.shape), ANY, exchange_sems(), [part], [ANY]
    )


def fold(name, collective_id, part):
    def kernel(part_in, out, *refs):
        place = Place(1)
        greet(place, False, False, True)
        run_flows([fold_flow(place, part_in, out, refs)])

    return call(
        kernel, name, collective_id, shape(*part.shape[1:]), VMEM,
        fold_scratch(*part.shape[1:]), [part], [ANY],
    )


def ffn_reduce(B, d_n2, g_gate_up, g_down):
    rows, width = d_n2.shape[2:]
    gu_rows, gu_cols = g_gate_up.shape[2:]
    d_rows = g_down.shape[1]

    def kernel(d_in, gu_in, gd_in, d_out, gu_out, gd_out, *refs):
        place = Place(B)
        s1, s2, s3 = split_refs(refs, 8, 6, 6)
        greet(place, True, True, True)
        run_flows(
            [
                shrink_flow(place, d_in, d_out, s1),
                owners_flow(place, gu_in, gu_out, s2),
                side_sum_flow(place, gd_in, gd_out, s3),
            ]
        )

    return call(
        kernel, "ffn_reduce", 3,
        [shape(rows, width), shape(A, gu_rows, gu_cols), shape(4, d_rows, width)],
        [VMEM, ANY, ANY],
        shrink_scratch(rows, width) + owners_scratch(B, gu_rows, gu_cols)
        + side_sum_scratch(B, d_rows, width),
        [d_n2, g_gate_up, g_down],
        [ANY] * 3,
    )


def side_sum_scratch(B, rows, width):
    return [
        pltpu.VMEM((rows, width), bf), pltpu.VMEM((B - 1, rows, width), bf),
        DMA((1,)), DMA((B, 2)), share_sems_pack(), DMA((1,)),
    ]


def share_sems_pack():
    return DMA((X + 1, 2))


def side_sum_flow(place, part, out, scratch):
    sums, from_side, load_sem, side_sem, share_sem, local = scratch
    b, B = place.b, place.B
    load = pltpu.make_async_copy(part.at[b], sums, load_sem.at[0])
    load.start()

    def to_side(k):
        to = (b + k) % B
        return remote(
            part.at[to], from_side.at[k - 1], side_sem.at[k, 0], side_sem.at[k, 1], place.side(to)
        )

    for k in range(1, B):
        to_side(k).start()
    yield
    yield
    load.wait()
    for k in range(1, B):
        to_side(k).wait_recv()
        add_into(sums, sums, from_side.at[k - 1])
    yield from share_flow(
        place, sums, out, [share_sem.at[X], share_sem, local]
    )
    for k in range(1, B):
        to_side(k).wait_send()


def last_reduce(B, S, g4, d_normed, ffn_out, g_gate_up, gains):
    g_rows, width = g4.shape[2:]
    rows = d_normed.shape[1]

    def kernel(g4_in, dn_in, f_in, gu_in, gain_in, g4_out, dn_out, f_out, gu_out, gain_out, *refs):
        place = Place(B)
        s1, s2, s3, s4, s5, s6 = split_refs(refs, 6, 6, 8, 3, 3, 2)
        own = s1[0]
        greet(place, everyone=(S, 4))

        def total():
            yield from gather_flow(place, g4_in, lambda ref: None, s1)
            yield from share_flow(place, own.at[place.a], g4_out, s4)

        run_flows(
            [
                total(),
                gains_flow(place, S, gain_in, gain_out, s6),
                fold_flow(place, dn_in, dn_out, s2),
                share_flow(place, gu_in, gu_out, s5),
                shrink_flow(place, f_in, f_out, s3),
            ]
        )

    return call(
        kernel, "last_reduce", 4,
        [
            shape(4, g_rows, width), shape(rows, width), shape(rows, width),
            shape(4, *g_gate_up.shape), shape(4 * S, *gains.shape[1:], dtype=f32),
        ],
        [ANY, VMEM, VMEM, ANY, ANY],
        gather_scratch(B, g_rows, width) + fold_scratch(rows, width)
        + shrink_scratch(rows, width) + share_sems() + share_sems() + gains_sems(S),
        [g4, d_normed, ffn_out, g_gate_up, gains],
        [ANY] * 5,
    )


def gains_sems(S):
    return [DMA((4 * S, 2)), DMA((1,))]


def gains_flow(place, S, part, out, sems):
    sem, local = sems
    keep = pltpu.make_async_copy(part.at[place.s], out.at[0], local.at[0])
    keep.start()

    def copy(k):
        to = lax.rem(place.s + k // 4, S)
        return remote(
            part.at[to], out.at[k], sem.at[k, 0], sem.at[k, 1], (to, lax.rem(place.r + k % 4, 4))
        )

    def begin(k, carry):
        copy(k).start()
        return carry

    def end(k, carry):
        copy(k).wait()
        return carry

    lax.fori_loop(1, 4 * S, begin, 0)
    yield
    yield
    yield
    yield
    keep.wait()
    lax.fori_loop(1, 4 * S, end, 0)


def product(left_side, right_side):
    return jnp.dot(left_side, right_side, preferred_element_type=f32)


def against(left_side, right_side):
    return lax.dot_general(
        left_side, right_side, (((1,), (1,)), ((), ())), preferred_element_type=f32
    )


def across(left_side, right_side):
    return lax.dot_general(
        left_side, right_side, (((0,), (0,)), ((), ())), preferred_element_type=f32
    )


def rms_norm(values, gain_vec):
    factor = lax.rsqrt(jnp.mean(values * values, axis=-1, keepdims=True) + norm_eps)
    return (factor, (values * factor * gain_vec).astype(bf))


def norm_back(values, factor, gain_vec, upstream):
    scaled = upstream * gain_vec
    inner_mean = jnp.mean(scaled * values, axis=-1, keepdims=True)
    return factor * scaled - values * (factor * factor * factor) * inner_mean


def angle_tables(places, head_dim):
    halves = head_dim // 2
    frequency = jnp.exp(
        jnp.arange(halves).astype(f32) * (-2.0 * math.log(rope_base) / head_dim)
    )
    angles = frequency[:, None] * places.astype(f32)[None, :]
    return (jnp.cos(angles)[None], jnp.sin(angles)[None])


def rotate(values, cosine, sine_table):
    halves = values.shape[1] // 2
    former = values[:, :halves]
    latter = values[:, halves:]
    return jnp.concatenate(
        [former * cosine - latter * sine_table, latter * cosine + former * sine_table], axis=1
    )


def body(
    tokens,
    attn_gain,
    w_query,
    w_key,
    w_value,
    w_out,
    ffn_gain,
    w_gate,
    w_up,
    w_down,
    seq_ids,
    block_ids,
    cotangent,
):
    S = lax.axis_size("shard")
    R = lax.axis_size("replica")
    B = S // A
    rows, width = tokens.shape
    group = rows * R
    head_dim = width // H
    heads = H // R
    wcols = width // R
    ff = w_gate.shape[1]
    sub = ff // (S * R)
    pad = -(-sub // 16) * 16
    fcols = B * pad
    wrows = width // S
    r = lax.axis_index("replica")
    score_scale = 1.0 / math.sqrt(head_dim)

    earlier = jnp.sum((seq_ids[None, :] < seq_ids[:, None]).astype(jnp.int32), axis=1)
    places = jnp.arange(group, dtype=jnp.int32) - earlier
    cosine, sine_table = angle_tables(places, head_dim)
    allowed = (seq_ids[None, :] == seq_ids[:, None]) & (block_ids[None, :] <= block_ids[:, None])

    gains = lax.all_gather(jnp.stack([attn_gain, ffn_gain]), "shard", axis=1, tiled=True)
    gain_one, gain_two = gains[0].astype(f32), gains[1].astype(f32)
    own_cols = lambda w: lax.dynamic_slice_in_dim(w, r * wcols, wcols, 1)
    w4 = jnp.concatenate([own_cols(w) for w in (w_query, w_key, w_value, w_out)], axis=1)
    upstream = cotangent.astype(f32)
    w4, tokens_group, d_down = first_gather(
        B, w4, tokens, (branch_scale * upstream).astype(bf)
    )
    w4 = w4.reshape(width, 4 * wcols)
    wqkv, wo = w4[:, : 3 * wcols], w4[:, 3 * wcols :]
    tokens_group = tokens_group.reshape(group, width).astype(f32)
    d_down = d_down.reshape(R * A * rows, width)

    def own_hidden(w):
        w = w.reshape(wrows, A, B, R, sub)
        w = lax.dynamic_index_in_dim(w, r, 3, keepdims=False)
        w = jnp.pad(w, ((0, 0), (0, 0), (0, 0), (0, pad - sub)))
        return w.transpose(1, 0, 2, 3).reshape(A, wrows, fcols)

    gate_up = jnp.concatenate([own_hidden(w_gate), own_hidden(w_up)], axis=1)
    down = lax.dynamic_index_in_dim(w_down.reshape(R, sub, width), r, 0, keepdims=False)
    down = jnp.pad(down, ((0, pad - sub), (0, 0)))

    inputs = tokens.astype(f32)
    factor_group, normed = rms_norm(tokens_group, gain_one)
    qkv = lax.dot_general(wqkv, normed, (((0,), (1,)), ((), ())), preferred_element_type=f32)
    heads_of = lambda v: v.reshape(heads, head_dim, group)
    queries = rotate(heads_of(qkv[:wcols]), cosine, sine_table).astype(bf)
    keys = rotate(heads_of(qkv[wcols : 2 * wcols]), cosine, sine_table).astype(bf)
    values = heads_of(qkv[2 * wcols :].astype(bf))
    scores = (
        jnp.einsum("hdt,hdk->htk", queries, keys, preferred_element_type=f32) * score_scale
    )
    scores = jnp.where(allowed[None], scores, masked_score)
    probs = jax.nn.softmax(scores, axis=-1)
    probs_low = probs.astype(bf)
    mixed = (
        jnp.einsum("htk,hdk->hdt", probs_low, values, preferred_element_type=f32)
        .reshape(wcols, group)
        .astype(bf)
    )
    mixed_all = share("mixed_share", 5, mixed).reshape(width, group)
    proj = across(mixed_all, wo).astype(bf)
    proj = exchange("proj_exchange", 6, proj.reshape(R, rows, wcols))
    proj = proj.transpose(1, 0, 2).reshape(rows, width)
    after_attn = inputs + branch_scale * proj.astype(f32)
    factor_two, normed_two = rms_norm(after_attn, gain_two)

    n2, gate_up, down_w = ffn_gather(B, normed_two, gate_up, down)
    n2 = n2.reshape(R * A * rows, width)
    gate_up = gate_up.reshape(S, 2, wrows, fcols)
    gate_w = gate_up[:, 0].reshape(width, fcols)
    up_w = gate_up[:, 1].reshape(width, fcols)
    down_w = down_w.reshape(fcols, width)
    gate_pre = product(n2, gate_w)
    up_proj = product(n2, up_w)
    sig = jax.nn.sigmoid(gate_pre)
    hidden = (gate_pre * sig * up_proj).astype(bf)
    d_hidden = against(d_down, down_w)
    d_gate = (d_hidden * up_proj * sig * (1.0 + gate_pre * (1.0 - sig))).astype(bf)
    d_up = (d_hidden * gate_pre * sig).astype(bf)
    d_n2 = (against(d_gate, gate_w) + against(d_up, up_w)).astype(bf)
    g_gate = across(n2, d_gate).astype(bf).reshape(A, B, wrows, fcols)
    g_up = across(n2, d_up).astype(bf).reshape(A, B, wrows, fcols)
    g_down = across(hidden, d_down).astype(bf).reshape(B, pad, width)
    d_n2, g_gate_up, g_down = ffn_reduce(
        B, d_n2.reshape(R, A, rows, width), jnp.concatenate([g_gate, g_up], axis=2), g_down
    )
    grad_down = g_down[:, :sub].astype(f32).reshape(R * sub, width)
    ffn_out = product(hidden, down_w).astype(bf).reshape(R, A, rows, width)

    d_n2 = d_n2.astype(f32)
    gain_two_part = jnp.sum(d_n2 * after_attn * factor_two, axis=0)
    d_after = upstream + norm_back(after_attn, factor_two, gain_two, d_n2)
    d_proj = (branch_scale * d_after).astype(bf)
    d_proj = exchange(
        "d_proj_exchange", 7, d_proj.reshape(rows, R, wcols).transpose(1, 0, 2)
    ).reshape(group, wcols)
    d_mixed = against(wo, d_proj).astype(bf).reshape(R, wcols, group)
    d_mixed = heads_of(fold("d_mixed_fold", 8, d_mixed))

    d_probs = jnp.einsum("hdt,hdk->htk", d_mixed, values, preferred_element_type=f32)
    d_scores = (
        probs * (d_probs - jnp.sum(d_probs * probs, axis=-1, keepdims=True))
    ).astype(bf)
    d_queries = (
        jnp.einsum("htk,hdk->hdt", d_scores, keys, preferred_element_type=f32) * score_scale
    )
    d_keys = (
        jnp.einsum("htk,hdt->hdk", d_scores, queries, preferred_element_type=f32) * score_scale
    )
    d_values = jnp.einsum("htk,hdt->hdk", probs_low, d_mixed, preferred_element_type=f32)
    d_qkv = jnp.concatenate(
        [
            rotate(d_queries, cosine, -sine_table).reshape(wcols, group).astype(bf),
            rotate(d_keys, cosine, -sine_table).reshape(wcols, group).astype(bf),
            d_values.reshape(wcols, group).astype(bf),
        ],
        axis=0,
    )
    d_normed = lax.dot_general(
        d_qkv, wqkv, (((0,), (1,)), ((), ())), preferred_element_type=f32
    )
    gain_one_part = jnp.sum(d_normed * tokens_group * factor_group, axis=0)
    g_qkv = lax.dot_general(
        normed, d_qkv, (((0,), (1,)), ((), ())), preferred_element_type=f32
    )
    g4 = jnp.concatenate([g_qkv, product(mixed_all, d_proj)], axis=1).astype(bf)
    gain_parts = jnp.stack(
        [gain_one_part.reshape(S, wrows), gain_two_part.reshape(S, wrows)], axis=1
    )
    g4, d_normed, ffn_out, g_gate_up, gain_sums = last_reduce(
        B, S, g4.reshape(A, B, wrows, 4 * wcols), d_normed.astype(bf).reshape(R, rows, width),
        ffn_out, g_gate_up, gain_parts,
    )
    result = after_attn + branch_scale * ffn_out.astype(f32)
    factor_one, _ = rms_norm(inputs, gain_one)
    grad_tokens = d_after + norm_back(inputs, factor_one, gain_one, d_normed.astype(f32))
    g4 = g4.reshape(R, wrows, 4, wcols).transpose(2, 1, 0, 3).reshape(4, wrows, width)
    g4 = g4.astype(f32)
    g_gate_up = g_gate_up.reshape(R, A, 2, wrows, B, pad)[..., :sub]
    g_gate_up = g_gate_up.transpose(2, 3, 1, 4, 0, 5).reshape(2, wrows, ff).astype(f32)
    gain_sums = jnp.sum(gain_sums, axis=0)
    return (
        result.astype(bf),
        grad_tokens.astype(bf),
        gain_sums[0],
        g4[0],
        g4[1],
        g4[2],
        g4[3],
        gain_sums[1],
        g_gate_up[0],
        g_gate_up[1],
        grad_down,
    )


def solution(mesh):
    split = P(("shard", "replica"), None)
    vec, mat = P("shard"), P("shard", None)
    in_specs = (split, vec, mat, mat, mat, mat, vec, mat, mat, mat, vec, vec, split)
    out_specs = (split, split, vec, mat, mat, mat, mat, vec, mat, mat, mat)
    return jax.shard_map(body, mesh=mesh, in_specs=in_specs, out_specs=out_specs, check_vma=False)
```

```python
import functools
import math

import jax
import jax.numpy as jnp
from jax import lax
from jax.experimental import pallas as pl
from jax.experimental.pallas import tpu as pltpu
from jax.sharding import PartitionSpec as P

H = 36
A = 4
X = 2

branch_scale = 1.4 / math.sqrt(40.0)
norm_eps = 1e-05
rope_base = 10000.0
masked_score = -1e30
MESH = pl.DeviceIdType.MESH
bf = jnp.bfloat16
f32 = jnp.float32
DMA = pltpu.SemaphoreType.DMA


class Place:
    def __init__(self, B):
        self.B = B
        s, r = lax.axis_index("shard"), lax.axis_index("replica")
        self.s, self.r = s, r
        self.a, self.b = s // B, s % B
        self.x, self.c = r // X, r % X
        self.rx = (1 - self.x) * X + self.c
        self.rc = self.x * X + 1 - self.c

    def line(self, a):
        return (a * self.B + self.b, self.r)

    def side(self, b):
        return (self.a * self.B + b, self.r)

    @property
    def over_x(self):
        return (self.s, self.rx)

    @property
    def over_core(self):
        return (self.s, self.rc)


def greet(place, a_peers=True, b_peers=False, r_peers=True, everyone=None):
    barrier = pltpu.get_barrier_semaphore()

    def signal(device):
        pl.semaphore_signal(barrier, inc=1, device_id=device, device_id_type=MESH)

    if everyone is not None:
        S, R = everyone

        def one(k, carry):
            signal((lax.rem(place.s + k // R, S), lax.rem(place.r + k % R, R)))
            return carry

        lax.fori_loop(1, S * R, one, 0)
        pl.semaphore_wait(barrier, S * R - 1)
        return
    count = 0
    if a_peers:
        for k in range(1, A):
            signal(place.line((place.a + k) % A))
            count += 1
    if b_peers:
        for k in range(1, place.B):
            signal(place.side((place.b + k) % place.B))
            count += 1
    if r_peers:
        signal(place.over_x)
        signal(place.over_core)
        count += 2
    pl.semaphore_wait(barrier, count)


def remote(src, dst, send, recv, device):
    return pltpu.make_async_remote_copy(
        src_ref=src, dst_ref=dst, send_sem=send, recv_sem=recv, device_id=device,
        device_id_type=MESH,
    )


def add_into(dst, first, second, tile=32):
    rows = dst.shape[0]
    tile = math.gcd(rows, tile) if math.gcd(rows, tile) >= 16 else rows

    def step(i, carry):
        at = pl.ds(pl.multiple_of(i * tile, tile), tile)
        dst[at, :] = (first[at, :].astype(f32) + second[at, :].astype(f32)).astype(dst.dtype)
        return carry

    lax.fori_loop(0, rows // tile, step, 0)


def run_flows(flows, turns=()):
    ended = set()

    def step(at):
        if at not in ended:
            try:
                next(flows[at])
            except StopIteration:
                ended.add(at)

    for at in turns:
        step(at)
    while len(ended) < len(flows):
        for at in range(len(flows)):
            step(at)


def halves(rows):
    return 2 if rows % 32 == 0 else 1


def piece(ref, at, h, parts):
    if parts == 1:
        return ref.at[at]
    rows = ref.shape[-2] // parts
    index = at if isinstance(at, tuple) else (at,)
    return ref.at[index + (pl.ds(h * rows, rows),)]


def widen_sems():
    return [DMA((A,)), DMA((X,)), DMA((A, 2)), DMA((A, 2)), DMA((X, A, 2)), DMA((1,))]


def widen_flow(place, own, out, sems):
    line_recv, _, line_send, over_x, over_core, local = sems
    a, r = place.a, place.r
    keep = pltpu.make_async_copy(own, out.at[r, a], local.at[0])
    keep.start()

    def to_line(src, block, way):
        at = 0 if way > 0 else 1
        return remote(
            src, out.at[r, block], line_send.at[block, at], line_recv.at[block],
            place.line(a + way),
        )

    def to_x(src, block):
        return remote(
            src, out.at[r, block], over_x.at[block, 0], over_x.at[block, 1], place.over_x
        )

    def to_core(src, x, block):
        return remote(
            src, out.at[x * X + place.c, block], over_core.at[x, block, 0],
            over_core.at[x, block, 1], place.over_core,
        )

    @pl.when(a < A - 1)
    def _():
        to_line(own, a, 1).start()

    @pl.when(a > 0)
    def _():
        to_line(own, a, -1).start()

    to_x(own, a).start()
    to_core(own, place.x, a).start()

    def pass_x(k):
        for ok, block in ((a - k >= 0, a - k), (a + k < A, a + k)) if k else ((None, a),):
            def go():
                src = out.at[place.rx, block]
                to_x(src, block).wait_recv()
                to_core(src, 1 - place.x, block).start()

            go() if ok is None else pl.when(ok)(go)

    for k in range(1, A):
        yield
        for way in (1, -1):
            block = a - way * k

            @pl.when((block >= 0) & (block < A))
            def _():
                src = out.at[r, block]
                to_line(src, block, way).wait_recv()

                @pl.when((a + way >= 0) & (a + way < A))
                def _():
                    to_line(src, block, way).start()

                to_x(src, block).start()
                to_core(src, place.x, block).start()

        yield
        pass_x(k - 1)
    yield
    pass_x(A - 1)
    yield
    keep.wait()
    for block in range(A):
        src = out.at[r, block]

        @pl.when((a < A - 1) & (block <= a))
        def _():
            to_line(src, block, 1).wait_send()

        @pl.when((a > 0) & (block >= a))
        def _():
            to_line(src, block, -1).wait_send()

        to_x(src, block).wait_send()
        for x in range(X):
            to_core(src, x, block).wait()


def shrink_scratch(rows, width):
    block = (rows, width)
    P_ = halves(rows)
    return [
        pltpu.VMEM((X, A) + block, bf),
        pltpu.VMEM((X, A) + block, bf),
        pltpu.VMEM((A,) + block, bf),
        pltpu.VMEM((A + 1,) + block, bf),
        DMA((X, A, P_)), DMA((X, A, P_, 2)), DMA((A, P_, 2)), DMA((2, A, P_, 2)),
    ]


shrink_order = (3, 0, 2, 1)


def line_reduce(place, sums, landed, sems, parts, ready, final):
    a = place.a

    def hop(d, h, way):
        at = 0 if way > 0 else 1
        return remote(
            piece(sums, d, h, parts), piece(landed, d + 1 - at, h, parts), sems.at[at, d, h, 0],
            sems.at[at, d, h, 1], place.line(a + way),
        )

    def take(d, h, way):
        @pl.when((a - way >= 0) & (a - way < A))
        def _():
            hop(d, h, way).wait_recv()
            here = piece(sums, d, h, parts)
            add_into(here, here, piece(landed, d + (way > 0), h, parts))

    def finish(d):
        @pl.when(d == a)
        def _():
            for h in range(parts):
                take(d, h, 1)
                take(d, h, -1)
                final(d, h)

    for i, d in enumerate(shrink_order):
        for h in range(parts):
            yield
            ready(d, h)
            for way in (1, -1):
                @pl.when((d - a) * way > 0)
                def _():
                    take(d, h, way)
                    hop(d, h, way).start()

        if i:
            yield
            finish(shrink_order[i - 1])
    yield
    finish(shrink_order[-1])
    yield
    for d in range(A):
        for h in range(parts):
            for way in (1, -1):
                @pl.when((d - a) * way > 0)
                def _():
                    hop(d, h, way).wait_send()


def shrink_flow(place, part, out, scratch):
    half, from_core, from_x, landed, load_sem, core_sem, x_sem, line_sem = scratch
    x, c = place.x, place.c
    parts = halves(out.shape[0])

    def load(i, d, h):
        return pltpu.make_async_copy(
            piece(part, (i * X + c, d), h, parts), piece(half, (i, d), h, parts),
            load_sem.at[i, d, h],
        )

    def to_core(i, d, h):
        return remote(
            piece(part, (i * X + 1 - c, d), h, parts), piece(from_core, (i, d), h, parts),
            core_sem.at[i, d, h, 0], core_sem.at[i, d, h, 1], place.over_core,
        )

    def to_x(d, h):
        return remote(
            piece(half, (1 - x, d), h, parts), piece(from_x, d, h, parts), x_sem.at[d, h, 0],
            x_sem.at[d, h, 1], place.over_x,
        )

    def merge(i, d, h):
        load(i, d, h).wait()
        to_core(i, d, h).wait_recv()
        here = piece(half, (i, d), h, parts)
        add_into(here, here, piece(from_core, (i, d), h, parts))

    every = [(d, h) for d in shrink_order for h in range(parts)]
    for i in (1 - x, x):
        for d, h in every:
            load(i, d, h).start()
            to_core(i, d, h).start()
    for d, h in every:
        yield
        merge(1 - x, d, h)
        to_x(d, h).start()

    def ready(d, h):
        merge(x, d, h)
        to_x(d, h).wait_recv()
        here = piece(half, (x, d), h, parts)
        add_into(here, here, piece(from_x, d, h, parts))

    rows = out.shape[0] // parts

    def final(d, h):
        at = pl.ds(h * rows, rows)
        out[at, :] = half[x, d, at, :]

    yield from line_reduce(place, half.at[x], landed, line_sem, parts, ready, final)
    for d, h in every:
        to_x(d, h).wait_send()
        for i in range(X):
            to_core(i, d, h).wait_send()


def fold_scratch(rows, width):
    block = (rows, width)
    return [
        pltpu.VMEM((X,) + block, bf), pltpu.VMEM((X,) + block, bf), pltpu.VMEM(block, bf),
        DMA((X,)), DMA((X, 2)), DMA((2,)),
    ]


def fold_flow(place, part, out, scratch):
    half, from_core, from_x, load_sem, core_sem, x_sem = scratch
    x, c = place.x, place.c

    def load(i):
        return pltpu.make_async_copy(part.at[i * X + c], half.at[i], load_sem.at[i])

    def to_core(i):
        return remote(
            part.at[i * X + 1 - c], from_core.at[i], core_sem.at[i, 0], core_sem.at[i, 1],
            place.over_core,
        )

    to_x = remote(half.at[1 - x], from_x, x_sem.at[0], x_sem.at[1], place.over_x)
    for i in (1 - x, x):
        load(i).start()
        to_core(i).start()
    yield
    for i in (1 - x, x):
        load(i).wait()
        to_core(i).wait_recv()
        add_into(half.at[i], half.at[i], from_core.at[i])
        if i is not x:
            to_x.start()
    yield
    to_x.wait_recv()
    add_into(out, half.at[x], from_x)
    yield
    to_x.wait_send()
    for i in range(X):
        to_core(i).wait_send()


def share_sems():
    return [DMA((2,)), DMA((X, 2)), DMA((1,))]


def share_flow(place, own, out, sems, ready=None):
    x_sem, core_sem, local = sems
    r, x, c = place.r, place.x, place.c
    if ready is not None:
        yield
        ready()
    keep = pltpu.make_async_copy(own, out.at[r], local.at[0])
    to_x = remote(own, out.at[r], x_sem.at[0], x_sem.at[1], place.over_x)
    near = remote(own, out.at[r], core_sem.at[x, 0], core_sem.at[x, 1], place.over_core)
    far = remote(
        out.at[place.rx], out.at[place.rx], core_sem.at[1 - x, 0], core_sem.at[1 - x, 1],
        place.over_core,
    )
    to_x.start()
    near.start()
    keep.start()
    yield
    to_x.wait_recv()
    far.start()
    yield
    keep.wait()
    to_x.wait_send()
    near.wait()
    far.wait()


def exchange_sems():
    return [DMA((4, 2)), DMA((1,))]


def exchange_flow(place, part, out, sems):
    sem, local = sems
    r = place.r
    keep = pltpu.make_async_copy(part.at[r], out.at[r], local.at[0])
    keep.start()
    copies = []
    for k in (2, 3, 1):
        to = (r + k) % 4
        copies.append(
            remote(part.at[to], out.at[r], sem.at[k, 0], sem.at[k, 1], (place.s, to))
        )
        copies[-1].start()
    yield
    keep.wait()
    for copy in copies:
        copy.wait()


def greet_replicas(place):
    barrier = pltpu.get_barrier_semaphore()
    for k in range(1, 4):
        pl.semaphore_signal(
            barrier, inc=1, device_id=(place.s, (place.r + k) % 4), device_id_type=MESH
        )
    pl.semaphore_wait(barrier, 3)


def spread_sems(B):
    return [DMA((A,)), DMA((A, 2)), DMA((B, A, 2)), DMA((1,))]


def spread_flow(place, own, out, sems):
    line_recv, line_send, side, local = sems
    a, b, B = place.a, place.b, place.B
    keep = pltpu.make_async_copy(own, out.at[a, b], local.at[0])
    keep.start()

    def to_line(src, block, way):
        return remote(
            src, out.at[block, b], line_send.at[block, 0 if way > 0 else 1],
            line_recv.at[block], place.line(a + way),
        )

    def to_side(src, block, k):
        return remote(
            src, out.at[block, b], side.at[k, block, 0], side.at[k, block, 1],
            place.side((b + k) % B),
        )

    @pl.when(a < A - 1)
    def _():
        to_line(own, a, 1).start()

    @pl.when(a > 0)
    def _():
        to_line(own, a, -1).start()

    for k in range(1, B):
        to_side(own, a, k).start()
    for step in range(1, A):
        yield
        for way in (1, -1):
            block = a - way * step

            @pl.when((block >= 0) & (block < A))
            def _():
                src = out.at[block, b]
                to_line(src, block, way).wait_recv()

                @pl.when((a + way >= 0) & (a + way < A))
                def _():
                    to_line(src, block, way).start()

                for k in range(1, B):
                    to_side(src, block, k).start()

    yield
    keep.wait()
    for block in range(A):
        src = out.at[block, b]

        @pl.when((a < A - 1) & (block <= a))
        def _():
            to_line(src, block, 1).wait_send()

        @pl.when((a > 0) & (block >= a))
        def _():
            to_line(src, block, -1).wait_send()

        for k in range(1, B):
            to_side(src, block, k).wait()


def columns_sems(B):
    return [DMA((A, 2)), DMA((B, A, 2)), DMA((1,))]


def columns_flow(place, own, out, sems):
    line, side, local = sems
    a, b, B = place.a, place.b, place.B
    keep = pltpu.make_async_copy(own.at[a], out.at[a, b], local.at[0])
    keep.start()

    def to_line(k):
        to = (a + k) % A
        return remote(own.at[to], out.at[a, b], line.at[k, 0], line.at[k, 1], place.line(to))

    def to_side(src, block, k):
        return remote(
            src, out.at[block, b], side.at[k, block, 0], side.at[k, block, 1],
            place.side((b + k) % B),
        )

    for k in range(1, A):
        to_line(k).start()
    for k in range(1, B):
        to_side(own.at[a], a, k).start()
    for k in (1, 3, 2):
        yield
        to_line(k).wait_recv()
        block = (a + A - k) % A
        for j in range(1, B):
            to_side(out.at[block, b], block, j).start()
    yield
    keep.wait()
    for k in range(1, A):
        to_line(k).wait_send()
    for block in range(A):
        for k in range(1, B):
            to_side(out.at[block, b], block, k).wait()


def sides_sems(B):
    return [DMA((B, 2)), DMA((1,))]


def sides_flow(place, own, out, sems):
    side, local = sems
    b, B = place.b, place.B
    keep = pltpu.make_async_copy(own, out.at[b], local.at[0])
    keep.start()
    copies = [
        remote(own, out.at[b], side.at[k, 0], side.at[k, 1], place.side((b + k) % B))
        for k in range(1, B)
    ]
    for copy in copies:
        copy.start()
    yield
    keep.wait()
    for copy in copies:
        copy.wait()


def gather_scratch(B, rows, width):
    block = (rows, width)
    P_ = halves(rows)
    return [
        pltpu.VMEM((A,) + block, bf),
        pltpu.VMEM((B - 1, A) + block, bf),
        pltpu.VMEM((A + 1,) + block, bf),
        DMA((A, P_)), DMA((B, A, P_, 2)), DMA((2, A, P_, 2)),
        DMA((P_, 2)), DMA((X, P_, 2)), DMA((P_,)),
    ]


def gather_flow(place, part, out, scratch):
    sums, from_side, landed, load_sem, side_sem, line_sem, x_sem, core_sem, local = scratch
    b, B, r, x = place.b, place.B, place.r, place.x
    parts = halves(out.shape[1])

    def load(d, h):
        return pltpu.make_async_copy(
            piece(part, (d, b), h, parts), piece(sums, d, h, parts), load_sem.at[d, h]
        )

    def to_side(k, d, h):
        to = (b + k) % B
        return remote(
            piece(part, (d, to), h, parts), piece(from_side, (k - 1, d), h, parts),
            side_sem.at[k, d, h, 0], side_sem.at[k, d, h, 1], place.side(to),
        )

    for d in shrink_order:
        for h in range(parts):
            load(d, h).start()
            for k in range(1, B):
                to_side(k, d, h).start()

    def ready(d, h):
        load(d, h).wait()
        for k in range(1, B):
            to_side(k, d, h).wait_recv()
            here = piece(sums, d, h, parts)
            add_into(here, here, piece(from_side, (k - 1, d), h, parts))

    def keep(src, h):
        return pltpu.make_async_copy(src, piece(out, r, h, parts), local.at[h])

    def to_x(src, h):
        return remote(src, piece(out, r, h, parts), x_sem.at[h, 0], x_sem.at[h, 1], place.over_x)

    def near(src, h):
        return remote(
            src, piece(out, r, h, parts), core_sem.at[x, h, 0], core_sem.at[x, h, 1],
            place.over_core,
        )

    def far(h):
        src = piece(out, place.rx, h, parts)
        return remote(
            src, src, core_sem.at[1 - x, h, 0], core_sem.at[1 - x, h, 1], place.over_core
        )

    def final(d, h):
        src = piece(sums, d, h, parts)
        to_x(src, h).start()
        near(src, h).start()
        keep(src, h).start()

    yield from line_reduce(place, sums, landed, line_sem, parts, ready, final)
    yield
    for h in range(parts):
        src = piece(out, r, h, parts)
        to_x(src, h).wait_recv()
        far(h).start()
    yield
    for h in range(parts):
        src = piece(out, r, h, parts)
        keep(src, h).wait()
        to_x(src, h).wait_send()
        near(src, h).wait()
    for d in shrink_order:
        for h in range(parts):
            for k in range(1, B):
                to_side(k, d, h).wait_send()
    for h in range(parts):
        far(h).wait()


def owners_scratch(B, rows, width):
    block = (rows, width)
    return [
        pltpu.VMEM((A,) + block, bf), pltpu.VMEM((B - 1, A) + block, bf),
        DMA((A,)), DMA((B, A, 2)), DMA((A, 2)), DMA((1,)),
    ]


def owners_flow(place, part, out, scratch):
    sums, from_side, load_sem, side_sem, line_sem, local = scratch
    a, b, B = place.a, place.b, place.B

    def load(d):
        return pltpu.make_async_copy(part.at[d, b], sums.at[d], load_sem.at[d])

    def to_side(k, d):
        to = (b + k) % B
        return remote(
            part.at[d, to], from_side.at[k - 1, d], side_sem.at[k, d, 0], side_sem.at[k, d, 1],
            place.side(to),
        )

    def to_line(k):
        to = (a + k) % A
        return remote(sums.at[to], out.at[a], line_sem.at[k, 0], line_sem.at[k, 1], place.line(to))

    for k in (1, 3, 2, 0):
        d = (a + k) % A
        load(d).start()
        for j in range(1, B):
            to_side(j, d).start()
    for k in (1, 3, 2, 0):
        yield
        d = (a + k) % A
        load(d).wait()
        for j in range(1, B):
            to_side(j, d).wait_recv()
            add_into(sums.at[d], sums.at[d], from_side.at[j - 1, d])
        if k:
            to_line(k).start()
    keep = pltpu.make_async_copy(sums.at[a], out.at[a], local.at[0])
    keep.start()
    yield
    keep.wait()
    for k in range(1, A):
        to_line(k).wait()
    for d in range(A):
        for j in range(1, B):
            to_side(j, d).wait_send()


ANY = pl.BlockSpec(memory_space=pl.ANY)
VMEM = pl.BlockSpec(memory_space=pltpu.VMEM)


def call(kernel, name, collective_id, outs, out_specs, scratch, args, in_specs):
    return pl.pallas_call(
        kernel,
        out_shape=outs,
        in_specs=in_specs,
        out_specs=out_specs,
        scratch_shapes=scratch,
        name=name,
        compiler_params=pltpu.CompilerParams(
            collective_id=collective_id, has_side_effects=True, vmem_limit_bytes=60 * 2**20
        ),
    )(*args)


def shape(*dims, dtype=bf):
    return jax.ShapeDtypeStruct(dims, dtype)


def split_refs(refs, *sizes):
    found, at = [], 0
    for size in sizes:
        found.append(refs[at : at + size])
        at += size
    return found


def select(rows, cols, shift, at, width):
    row = lax.broadcasted_iota(jnp.int32, (rows, cols), 0)
    col = lax.broadcasted_iota(jnp.int32, (rows, cols), 1)
    j = col - at
    return jnp.where((row - shift == j) & (j >= 0) & (j < width), 1.0, 0.0).astype(bf)


def first_gather(B, weights, gates, w_down, gains, tokens, d_down):
    wrows, width = weights[0].shape
    ff = gates[0].shape[1]
    wcols = width // 4
    sub = ff // (A * B * 4)
    pad = -(-sub // 16) * 16
    fcols = B * pad
    wide = 384
    span = -(-wcols // 128) * 128
    pair = 2 * wcols

    def kernel(*refs):
        w_in, g_in, (wd_in, gain_in, tok_in, d_in), outs, scratch, refs = split_refs(
            refs, 4, 2, 4, 6, 7, 100
        )
        w4_out, gain_out, tok_out, d_out, gu_out, dn_out = outs
        w_all, g_all, wd_all, own4, gu_own, dn_own, load = scratch
        s1, s2, s3, s4 = split_refs(refs, 4, 4, 3, 6)
        place = Place(B)
        r = place.r
        loads = [pltpu.make_async_copy(w, w_all.at[i], load.at[i]) for i, w in enumerate(w_in)]
        loads += [
            pltpu.make_async_copy(w, g_all.at[i], load.at[4 + i]) for i, w in enumerate(g_in)
        ]
        loads.append(pltpu.make_async_copy(wd_in, wd_all, load.at[6]))
        for copy in loads:
            copy.start()
        start = pl.multiple_of(r * wcols // 128 * 128, 128)
        shift = r * wcols - start
        for i in range(2):
            total = jnp.zeros((wrows, pair), f32)
            for j in range(2):
                loads[2 * i + j].wait()
                total += jnp.dot(
                    w_all[2 * i + j, :, pl.ds(start, span)],
                    select(span, pair, shift, j * wcols, wcols), preferred_element_type=f32,
                )
            own4[:, i * pair : (i + 1) * pair] = total.astype(bf)
        greet(place, True, True, True)

        def pack():
            for i in range(2):
                loads[4 + i].wait()
            loads[6].wait()
            yield

            def one(n, carry):
                i, block = n // A, n % A
                total = jnp.zeros((wrows, fcols), f32)
                for j in range(B):
                    first = ((block * B + j) * 4 + r) * sub
                    at = pl.multiple_of(jnp.minimum(first // 128 * 128, ff - wide), 128)
                    total += jnp.dot(
                        g_all[i, :, pl.ds(at, wide)],
                        select(wide, fcols, first - at, j * pad, sub),
                        preferred_element_type=f32,
                    )
                gu_own[block, i] = total.astype(bf)
                return carry

            lax.fori_loop(0, 2 * A, one, 0)
            row = lax.broadcasted_iota(jnp.int32, (pad, ff // (A * B)), 0)
            col = lax.broadcasted_iota(jnp.int32, (pad, ff // (A * B)), 1)
            pick = jnp.where((col - r * sub == row) & (row < sub), 1.0, 0.0).astype(bf)
            tile = 768

            def down(n, carry):
                at = pl.ds(pl.multiple_of(n * tile, tile), tile)
                dn_own[:, at] = jnp.dot(
                    pick, wd_all[:, at], preferred_element_type=f32
                ).astype(bf)
                return carry

            lax.fori_loop(0, width // tile, down, 0)
            out = [
                pltpu.make_async_copy(gu_own, gu_out, load.at[0]),
                pltpu.make_async_copy(dn_own, dn_out, load.at[1]),
            ]
            for copy in out:
                copy.start()
            yield
            for copy in out:
                copy.wait()

        run_flows(
            [
                spread_flow(place, own4, w4_out, s1),
                share_flow(place, tok_in, tok_out, s3),
                spread_flow(place, gain_in, gain_out, s2),
                widen_flow(place, d_in, d_out, s4),
                pack(),
            ],
            (0, 1, 2, 3, 4, 1, 4),
        )

    return call(
        kernel, "first_gather", 1,
        [
            shape(A, B, wrows, 4 * wcols), shape(A, B, *gains.shape, dtype=f32),
            shape(4, *tokens.shape), shape(4, A, *d_down.shape),
            shape(A, 2, wrows, fcols), shape(pad, width),
        ],
        [ANY] * 6,
        [
            pltpu.VMEM((4, wrows, width), bf), pltpu.VMEM((2, wrows, ff), bf),
            pltpu.VMEM(w_down.shape, bf), pltpu.VMEM((wrows, 4 * wcols), bf),
            pltpu.VMEM((A, 2, wrows, fcols), bf), pltpu.VMEM((pad, width), bf), DMA((7,)),
        ]
        + spread_sems(B) + spread_sems(B) + share_sems() + widen_sems(),
        [*weights, *gates, w_down, gains, tokens, d_down],
        [ANY] * 10,
    )


def ffn_gather(B, normed_two, gate_up, down):
    def kernel(n_in, g_in, w_in, n_out, g_out, w_out, *refs):
        place = Place(B)
        s1, s2, s3 = split_refs(refs, 6, 3, 2)
        greet(place, True, True, True)
        run_flows(
            [
                widen_flow(place, n_in, n_out, s1),
                columns_flow(place, g_in, g_out, s2),
                sides_flow(place, w_in, w_out, s3),
            ]
        )

    return call(
        kernel, "ffn_gather", 2,
        [
            shape(4, A, *normed_two.shape), shape(A, B, *gate_up.shape[1:]),
            shape(B, *down.shape),
        ],
        [ANY] * 3,
        widen_sems() + columns_sems(B) + sides_sems(B),
        [normed_two, gate_up, down],
        [ANY] * 3,
    )


def share(name, collective_id, own):
    def kernel(own_in, out, *sems):
        place = Place(1)
        place.s = lax.axis_index("shard")
        greet(place, False, False, True)
        run_flows([share_flow(place, own_in, out, sems)])

    return call(
        kernel, name, collective_id, shape(4, *own.shape), ANY, share_sems(), [own], [ANY]
    )


def exchange(name, collective_id, part):
    def kernel(part_in, out, *sems):
        place = Place(1)
        greet_replicas(place)
        run_flows([exchange_flow(place, part_in, out, sems)])

    return call(
        kernel, name, collective_id, shape(*part.shape), ANY, exchange_sems(), [part], [ANY]
    )


def fold(name, collective_id, part):
    def kernel(part_in, out, *refs):
        place = Place(1)
        greet(place, False, False, True)
        run_flows([fold_flow(place, part_in, out, refs)])

    return call(
        kernel, name, collective_id, shape(*part.shape[1:]), VMEM,
        fold_scratch(*part.shape[1:]), [part], [ANY],
    )


def ffn_reduce(B, d_n2, g_gate_up, g_down):
    rows, width = d_n2.shape[2:]
    gu_rows, gu_cols = g_gate_up.shape[2:]
    d_rows = g_down.shape[1]

    def kernel(d_in, gu_in, gd_in, d_out, gu_out, gd_out, *refs):
        place = Place(B)
        s1, s2, s3 = split_refs(refs, 8, 6, 6)
        greet(place, True, True, True)
        run_flows(
            [
                shrink_flow(place, d_in, d_out, s1),
                owners_flow(place, gu_in, gu_out, s2),
                side_sum_flow(place, gd_in, gd_out, s3),
            ],
            (0, 1, 2) + (0,) * 8 + (0, 0, 1, 0, 0, 0, 1, 0, 0, 0, 1, 0, 0, 0, 1, 2, 2, 0, 1, 2),
        )

    return call(
        kernel, "ffn_reduce", 3,
        [shape(rows, width), shape(A, gu_rows, gu_cols), shape(4, d_rows, width)],
        [VMEM, ANY, ANY],
        shrink_scratch(rows, width) + owners_scratch(B, gu_rows, gu_cols)
        + side_sum_scratch(B, d_rows, width),
        [d_n2, g_gate_up, g_down],
        [ANY] * 3,
    )


def side_sum_scratch(B, rows, width):
    return [
        pltpu.VMEM((rows, width), bf), pltpu.VMEM((B - 1, rows, width), bf),
        DMA((1,)), DMA((B, 2)), share_sems_pack(), DMA((1,)),
    ]


def share_sems_pack():
    return DMA((X + 1, 2))


def side_sum_flow(place, part, out, scratch):
    sums, from_side, load_sem, side_sem, share_sem, local = scratch
    b, B = place.b, place.B
    load = pltpu.make_async_copy(part.at[b], sums, load_sem.at[0])
    load.start()

    def to_side(k):
        to = (b + k) % B
        return remote(
            part.at[to], from_side.at[k - 1], side_sem.at[k, 0], side_sem.at[k, 1], place.side(to)
        )

    for k in range(1, B):
        to_side(k).start()
    yield
    yield
    load.wait()
    for k in range(1, B):
        to_side(k).wait_recv()
        add_into(sums, sums, from_side.at[k - 1])
    yield from share_flow(
        place, sums, out, [share_sem.at[X], share_sem, local]
    )
    for k in range(1, B):
        to_side(k).wait_send()


def last_reduce(B, S, g4, d_normed, g_gate_up, g_down, gains, ff):
    wrows, width = g4.shape[2], g4.shape[3]
    rows = d_normed.shape[1]
    wcols = width // 4
    sub = ff // (S * 4)
    pad = -(-sub // 16) * 16
    fcols = B * pad
    wide = 384
    span = -(-wcols // 128) * 128
    pair = 2 * wcols
    drows = ff // S

    def kernel(*refs):
        ins, outs, own, refs = split_refs(refs, 5, 9, 6, 100)
        g4_in, dn_in, gu_in, gd_in, gain_in = ins
        dn_out, gain_out = outs[:2]
        g4_outs, gu_outs, gd_out = outs[2:6], outs[6:8], outs[8]
        g4_all, gu_all, gd_all, stage, stage_down, sem = own
        s1, s2, s3, s4 = split_refs(refs, 9, 6, 3, 2)
        place = Place(B)
        greet(place, everyone=(S, 4))

        def lay_down():
            load = pltpu.make_async_copy(gd_in, gd_all, sem.at[0])
            load.start()
            yield
            load.wait()
            row = lax.broadcasted_iota(jnp.int32, (drows, 4 * pad), 0)
            col = lax.broadcasted_iota(jnp.int32, (drows, 4 * pad), 1)
            pick = (col % pad < sub) & (col // pad * sub + col % pad == row)
            pick = jnp.where(pick, 1.0, 0.0).astype(bf)

            def copy(n):
                at = pl.ds(pl.multiple_of(n * wide, 128), wide)
                return pltpu.make_async_copy(
                    stage_down.at[n % 2], gd_out.at[:, at], sem.at[1 + n % 2]
                )

            def one(n, carry):
                @pl.when(n >= 2)
                def _():
                    copy(n - 2).wait()

                at = pl.ds(pl.multiple_of(n * wide, 128), wide)
                stage_down[n % 2] = jnp.dot(pick, gd_all[:, at], preferred_element_type=f32)
                copy(n).start()
                return carry

            count = width // wide
            lax.fori_loop(0, count, one, 0)
            yield
            for n in range(count - 2, count):
                copy(n).wait()

        def lay_gate_up():
            def one(n, carry):
                i, block = n % 2, n // 2
                total = jnp.zeros((wrows, wide), f32)
                for t in range(-(-wide // sub) + 1):
                    m = block * wide // sub + t
                    inside = jnp.where(m < 4 * S, sub, 0)
                    m = jnp.minimum(m, 4 * S - 1)
                    s = m // 4
                    total += jnp.dot(
                        gu_all[m % 4, s // B, i],
                        select(fcols, wide, s % B * pad, m * sub - block * wide, inside),
                        preferred_element_type=f32,
                    )
                stage[i, :, pl.ds(pl.multiple_of(block * wide, 128), wide)] = total
                return carry

            count = 2 * (ff // wide)
            cuts = [count * k // 5 for k in range(6)]
            for k in range(5):
                lax.fori_loop(cuts[k], cuts[k + 1], one, 0)
                yield
            copies = [
                pltpu.make_async_copy(stage.at[i], gu_outs[i], sem.at[3 + i]) for i in range(2)
            ]
            for copy in copies:
                copy.start()
            yield
            for copy in copies:
                copy.wait()

        run_flows(
            [
                gather_flow(place, g4_in, g4_all, s1),
                gains_flow(place, S, gain_in, gain_out, s4),
                fold_flow(place, dn_in, dn_out, s2),
                share_flow(place, gu_in, gu_all, s3),
                lay_down(),
                lay_gate_up(),
            ],
            (0, 1, 2, 3, 4, 2, 4, 0, 2, 0, 0, 0, 0, 3, 3, 3, 5, 0, 5, 0, 5, 0, 5, 0, 5, 0, 5, 0)
            + (0,) * 10,
        )

        def lay(n, carry):
            i, side = n % 4, n // 4
            at = pl.multiple_of(i * wcols // 128 * 128, 128)
            total = jnp.zeros((wrows, pair), f32)
            for c in range(2):
                total += jnp.dot(
                    g4_all[side * 2 + c, :, pl.ds(at, span)],
                    select(span, pair, i * wcols - at, c * wcols, wcols),
                    preferred_element_type=f32,
                )
            to = pl.multiple_of(i % 2 * width + side * pair, 128)
            stage[i // 2, :, pl.ds(to, pair)] = total
            return carry

        lax.fori_loop(0, 8, lay, 0)
        copies = [
            pltpu.make_async_copy(
                stage.at[i // 2, :, pl.ds(i % 2 * width, width)], g4_outs[i], sem.at[3 + i]
            )
            for i in range(4)
        ]
        for copy in copies:
            copy.start()
        for copy in copies:
            copy.wait()

    return call(
        kernel, "last_reduce", 4,
        [shape(rows, width), shape(4 * S, *gains.shape[1:], dtype=f32)]
        + [shape(wrows, width, dtype=f32)] * 4 + [shape(wrows, ff, dtype=f32)] * 2
        + [shape(drows, width, dtype=f32)],
        [VMEM] + [ANY] * 8,
        [
            pltpu.VMEM((4, wrows, width), bf), pltpu.VMEM((4, A, 2, wrows, fcols), bf),
            pltpu.VMEM((4 * pad, width), bf), pltpu.VMEM((2, wrows, ff), f32),
            pltpu.VMEM((2, drows, wide), f32), DMA((7,)),
        ]
        + gather_scratch(B, wrows, width) + fold_scratch(rows, width) + share_sems()
        + gains_sems(S),
        [g4, d_normed, g_gate_up, g_down, gains],
        [ANY] * 5,
    )


def gains_sems(S):
    return [DMA((4 * S, 2)), DMA((1,))]


def gains_flow(place, S, part, out, sems):
    sem, local = sems
    keep = pltpu.make_async_copy(part.at[place.s], out.at[0], local.at[0])
    keep.start()

    def copy(k):
        to = lax.rem(place.s + k // 4, S)
        return remote(
            part.at[to], out.at[k], sem.at[k, 0], sem.at[k, 1], (to, lax.rem(place.r + k % 4, 4))
        )

    def begin(k, carry):
        copy(k).start()
        return carry

    def end(k, carry):
        copy(k).wait()
        return carry

    lax.fori_loop(1, 4 * S, begin, 0)
    yield
    yield
    yield
    yield
    keep.wait()
    lax.fori_loop(1, 4 * S, end, 0)


def product(left_side, right_side):
    return jnp.dot(left_side, right_side, preferred_element_type=f32)


def against(left_side, right_side):
    return lax.dot_general(
        left_side, right_side, (((1,), (1,)), ((), ())), preferred_element_type=f32
    )


def across(left_side, right_side):
    return lax.dot_general(
        left_side, right_side, (((0,), (0,)), ((), ())), preferred_element_type=f32
    )


def rms_norm(values, gain_vec):
    factor = lax.rsqrt(jnp.mean(values * values, axis=-1, keepdims=True) + norm_eps)
    return (factor, (values * factor * gain_vec).astype(bf))


def norm_back(values, factor, gain_vec, upstream):
    scaled = upstream * gain_vec
    inner_mean = jnp.mean(scaled * values, axis=-1, keepdims=True)
    return factor * scaled - values * (factor * factor * factor) * inner_mean


def angle_tables(places, head_dim):
    halves = head_dim // 2
    frequency = jnp.exp(
        jnp.arange(halves).astype(f32) * (-2.0 * math.log(rope_base) / head_dim)
    )
    angles = frequency[:, None] * places.astype(f32)[None, :]
    return (jnp.cos(angles)[None], jnp.sin(angles)[None])


def rotate(values, cosine, sine_table):
    halves = values.shape[1] // 2
    former = values[:, :halves]
    latter = values[:, halves:]
    return jnp.concatenate(
        [former * cosine - latter * sine_table, latter * cosine + former * sine_table], axis=1
    )


def body(
    tokens,
    attn_gain,
    w_query,
    w_key,
    w_value,
    w_out,
    ffn_gain,
    w_gate,
    w_up,
    w_down,
    seq_ids,
    block_ids,
    cotangent,
):
    S = lax.axis_size("shard")
    R = lax.axis_size("replica")
    B = S // A
    rows, width = tokens.shape
    group = rows * R
    head_dim = width // H
    heads = H // R
    wcols = width // R
    ff = w_gate.shape[1]
    sub = ff // (S * R)
    pad = -(-sub // 16) * 16
    fcols = B * pad
    wrows = width // S
    r = lax.axis_index("replica")
    score_scale = 1.0 / math.sqrt(head_dim)

    earlier = jnp.sum((seq_ids[None, :] < seq_ids[:, None]).astype(jnp.int32), axis=1)
    places = jnp.arange(group, dtype=jnp.int32) - earlier
    cosine, sine_table = angle_tables(places, head_dim)
    allowed = (seq_ids[None, :] == seq_ids[:, None]) & (block_ids[None, :] <= block_ids[:, None])

    upstream = cotangent.astype(f32)
    w4, gains, tokens_group, d_down, gate_up, down = first_gather(
        B, [w_query, w_key, w_value, w_out], [w_gate, w_up], w_down,
        jnp.stack([attn_gain, ffn_gain]).astype(f32), tokens, (branch_scale * upstream).astype(bf),
    )
    gains = gains.reshape(S, 2, wrows)
    gain_one, gain_two = gains[:, 0].reshape(width), gains[:, 1].reshape(width)
    w4 = w4.reshape(width, 4 * wcols)
    wqkv, wo = w4[:, : 3 * wcols], w4[:, 3 * wcols :]
    tokens_group = tokens_group.reshape(group, width).astype(f32)
    d_down = d_down.reshape(R * A * rows, width)
    gate_up = gate_up.reshape(A, 2 * wrows, fcols)

    inputs = tokens.astype(f32)
    factor_group, normed = rms_norm(tokens_group, gain_one)
    qkv = lax.dot_general(wqkv, normed, (((0,), (1,)), ((), ())), preferred_element_type=f32)
    heads_of = lambda v: v.reshape(heads, head_dim, group)
    queries = rotate(heads_of(qkv[:wcols]), cosine, sine_table).astype(bf)
    keys = rotate(heads_of(qkv[wcols : 2 * wcols]), cosine, sine_table).astype(bf)
    values = heads_of(qkv[2 * wcols :].astype(bf))
    scores = (
        jnp.einsum("hdt,hdk->htk", queries, keys, preferred_element_type=f32) * score_scale
    )
    scores = jnp.where(allowed[None], scores, masked_score)
    probs = jax.nn.softmax(scores, axis=-1)
    probs_low = probs.astype(bf)
    mixed = (
        jnp.einsum("htk,hdk->hdt", probs_low, values, preferred_element_type=f32)
        .reshape(wcols, group)
        .astype(bf)
    )
    mixed_all = share("mixed_share", 5, mixed).reshape(width, group)
    proj = across(mixed_all, wo).astype(bf)
    proj = exchange("proj_exchange", 6, proj.reshape(R, rows, wcols))
    proj = proj.transpose(1, 0, 2).reshape(rows, width)
    after_attn = inputs + branch_scale * proj.astype(f32)
    factor_two, normed_two = rms_norm(after_attn, gain_two)

    n2, gate_up, down_w = ffn_gather(B, normed_two, gate_up, down)
    n2 = n2.reshape(R * A * rows, width)
    gate_up = gate_up.reshape(S, 2, wrows, fcols)
    gate_w = gate_up[:, 0].reshape(width, fcols)
    up_w = gate_up[:, 1].reshape(width, fcols)
    down_w = down_w.reshape(fcols, width)
    gate_pre = product(n2, gate_w)
    up_proj = product(n2, up_w)
    sig = jax.nn.sigmoid(gate_pre)
    hidden = (gate_pre * sig * up_proj).astype(bf)
    d_hidden = against(d_down, down_w)
    d_gate = (d_hidden * up_proj * sig * (1.0 + gate_pre * (1.0 - sig))).astype(bf)
    d_up = (d_hidden * gate_pre * sig).astype(bf)
    d_n2 = (against(d_gate, gate_w) + against(d_up, up_w)).astype(bf)
    g_gate = across(n2, d_gate).astype(bf).reshape(A, B, wrows, fcols)
    g_up = across(n2, d_up).astype(bf).reshape(A, B, wrows, fcols)
    g_down = across(hidden, d_down).astype(bf).reshape(B, pad, width)
    d_n2, g_gate_up, g_down = ffn_reduce(
        B, d_n2.reshape(R, A, rows, width), jnp.concatenate([g_gate, g_up], axis=2), g_down
    )
    ffn_out = product(hidden, down_w).astype(bf)
    ffn_out = lax.psum_scatter(ffn_out, "replica", scatter_dimension=0, tiled=True)
    ffn_out = lax.psum_scatter(
        ffn_out, "shard", scatter_dimension=0, tiled=True,
        axis_index_groups=[[i * B + j for i in range(A)] for j in range(B)],
    )

    d_n2 = d_n2.astype(f32)
    gain_two_part = jnp.sum(d_n2 * after_attn * factor_two, axis=0)
    d_after = upstream + norm_back(after_attn, factor_two, gain_two, d_n2)
    d_proj = (branch_scale * d_after).astype(bf)
    d_proj = exchange(
        "d_proj_exchange", 7, d_proj.reshape(rows, R, wcols).transpose(1, 0, 2)
    ).reshape(group, wcols)
    d_mixed = against(wo, d_proj).astype(bf).reshape(R, wcols, group)
    d_mixed = heads_of(fold("d_mixed_fold", 8, d_mixed))

    d_probs = jnp.einsum("hdt,hdk->htk", d_mixed, values, preferred_element_type=f32)
    d_scores = (
        probs * (d_probs - jnp.sum(d_probs * probs, axis=-1, keepdims=True))
    ).astype(bf)
    d_queries = (
        jnp.einsum("htk,hdk->hdt", d_scores, keys, preferred_element_type=f32) * score_scale
    )
    d_keys = (
        jnp.einsum("htk,hdt->hdk", d_scores, queries, preferred_element_type=f32) * score_scale
    )
    d_values = jnp.einsum("htk,hdt->hdk", probs_low, d_mixed, preferred_element_type=f32)
    d_qkv = jnp.concatenate(
        [
            rotate(d_queries, cosine, -sine_table).reshape(wcols, group).astype(bf),
            rotate(d_keys, cosine, -sine_table).reshape(wcols, group).astype(bf),
            d_values.reshape(wcols, group).astype(bf),
        ],
        axis=0,
    )
    d_normed = lax.dot_general(
        d_qkv, wqkv, (((0,), (1,)), ((), ())), preferred_element_type=f32
    )
    gain_one_part = jnp.sum(d_normed * tokens_group * factor_group, axis=0)
    g_qkv = lax.dot_general(
        normed, d_qkv, (((0,), (1,)), ((), ())), preferred_element_type=f32
    )
    g4 = jnp.concatenate([g_qkv, product(mixed_all, d_proj)], axis=1).astype(bf)
    gain_parts = jnp.stack(
        [gain_one_part.reshape(S, wrows), gain_two_part.reshape(S, wrows)], axis=1
    )
    d_normed, gain_sums, *g_attn, grad_gate, grad_up, grad_down = last_reduce(
        B, S, g4.reshape(A, B, wrows, 4 * wcols), d_normed.astype(bf).reshape(R, rows, width),
        g_gate_up.reshape(A, 2, wrows, fcols), g_down.reshape(R * pad, width), gain_parts, ff,
    )
    result = after_attn + branch_scale * ffn_out.astype(f32)
    factor_one, _ = rms_norm(inputs, gain_one)
    grad_tokens = d_after + norm_back(inputs, factor_one, gain_one, d_normed.astype(f32))
    gain_sums = jnp.sum(gain_sums, axis=0)
    return (
        result.astype(bf),
        grad_tokens.astype(bf),
        gain_sums[0],
        *g_attn,
        gain_sums[1],
        grad_gate,
        grad_up,
        grad_down,
    )


def solution(mesh):
    split = P(("shard", "replica"), None)
    vec, mat = P("shard"), P("shard", None)
    in_specs = (split, vec, mat, mat, mat, mat, vec, mat, mat, mat, vec, vec, split)
    out_specs = (split, split, vec, mat, mat, mat, mat, vec, mat, mat, mat)
    return jax.shard_map(body, mesh=mesh, in_specs=in_specs, out_specs=out_specs, check_vma=False)
```

```python
import functools
import math

import jax
import jax.numpy as jnp
from jax import lax
from jax.experimental import pallas as pl
from jax.experimental.pallas import tpu as pltpu
from jax.sharding import PartitionSpec as P

H = 36
A = 4
X = 2

branch_scale = 1.4 / math.sqrt(40.0)
norm_eps = 1e-05
rope_base = 10000.0
masked_score = -1e30
MESH = pl.DeviceIdType.MESH
bf = jnp.bfloat16
f32 = jnp.float32
DMA = pltpu.SemaphoreType.DMA


class Place:
    def __init__(self, B):
        self.B = B
        s, r = lax.axis_index("shard"), lax.axis_index("replica")
        self.s, self.r = s, r
        self.a, self.b = s // B, s % B
        self.x, self.c = r // X, r % X
        self.rx = (1 - self.x) * X + self.c
        self.rc = self.x * X + 1 - self.c

    def line(self, a):
        return (a * self.B + self.b, self.r)

    def side(self, b):
        return (self.a * self.B + b, self.r)

    @property
    def over_x(self):
        return (self.s, self.rx)

    @property
    def over_core(self):
        return (self.s, self.rc)


def greet(place, a_peers=True, b_peers=False, r_peers=True, everyone=None):
    barrier = pltpu.get_barrier_semaphore()

    def signal(device):
        pl.semaphore_signal(barrier, inc=1, device_id=device, device_id_type=MESH)

    if everyone is not None:
        S, R = everyone

        def one(k, carry):
            signal((lax.rem(place.s + k // R, S), lax.rem(place.r + k % R, R)))
            return carry

        lax.fori_loop(1, S * R, one, 0)
        pl.semaphore_wait(barrier, S * R - 1)
        return
    count = 0
    if a_peers:
        for k in range(1, A):
            signal(place.line((place.a + k) % A))
            count += 1
    if b_peers:
        for k in range(1, place.B):
            signal(place.side((place.b + k) % place.B))
            count += 1
    if r_peers:
        for k in range(1, 4):
            signal((place.s, (place.r + k) % 4))
            count += 1
    pl.semaphore_wait(barrier, count)


def remote(src, dst, send, recv, device):
    return pltpu.make_async_remote_copy(
        src_ref=src, dst_ref=dst, send_sem=send, recv_sem=recv, device_id=device,
        device_id_type=MESH,
    )


def add_into(dst, first, second, tile=32):
    rows = dst.shape[0]
    tile = math.gcd(rows, tile) if math.gcd(rows, tile) >= 16 else rows

    def step(i, carry):
        at = pl.ds(pl.multiple_of(i * tile, tile), tile)
        dst[at, :] = (first[at, :].astype(f32) + second[at, :].astype(f32)).astype(dst.dtype)
        return carry

    lax.fori_loop(0, rows // tile, step, 0)


def run_flows(flows, turns=()):
    ended = set()

    def step(at):
        if at not in ended:
            try:
                next(flows[at])
            except StopIteration:
                ended.add(at)

    for at in turns:
        step(at)
    while len(ended) < len(flows):
        for at in range(len(flows)):
            step(at)


def halves(rows):
    return 2 if rows % 32 == 0 else 1


def piece(ref, at, h, parts):
    if parts == 1:
        return ref.at[at]
    rows = ref.shape[-2] // parts
    index = at if isinstance(at, tuple) else (at,)
    return ref.at[index + (pl.ds(h * rows, rows),)]


def widen_sems():
    return [DMA((A,)), DMA((X,)), DMA((A, 2)), DMA((A, 2)), DMA((X, A, 2)), DMA((1,))]


def widen_flow(place, own, out, sems):
    line_recv, _, line_send, over_x, over_core, local = sems
    a, x, c = place.a, place.x, place.c
    keep = pltpu.make_async_copy(own, out.at[x, a, c], local.at[0])
    keep.start()

    def to_line(src, block, way):
        at = 0 if way > 0 else 1
        return remote(
            src, out.at[x, block, c], line_send.at[block, at], line_recv.at[block],
            place.line(a + way),
        )

    def to_x(src, block):
        return remote(
            src, out.at[x, block, c], over_x.at[block, 0], over_x.at[block, 1], place.over_x
        )

    def to_core(src, side, block):
        return remote(
            src, out.at[side, block, c], over_core.at[side, block, 0],
            over_core.at[side, block, 1], place.over_core,
        )

    @pl.when(a < A - 1)
    def _():
        to_line(own, a, 1).start()

    @pl.when(a > 0)
    def _():
        to_line(own, a, -1).start()

    to_x(own, a).start()
    to_core(own, x, a).start()

    def pass_x(k):
        for ok, block in ((a - k >= 0, a - k), (a + k < A, a + k)) if k else ((None, a),):
            def go():
                src = out.at[1 - x, block, c]
                to_x(src, block).wait_recv()
                to_core(src, 1 - x, block).start()

            go() if ok is None else pl.when(ok)(go)

    for k in range(1, A):
        yield
        for way in (1, -1):
            block = a - way * k

            @pl.when((block >= 0) & (block < A))
            def _():
                src = out.at[x, block, c]
                to_line(src, block, way).wait_recv()

                @pl.when((a + way >= 0) & (a + way < A))
                def _():
                    to_line(src, block, way).start()

                to_x(src, block).start()
                to_core(src, x, block).start()

        yield
        pass_x(k - 1)
    yield
    pass_x(A - 1)
    yield
    keep.wait()
    for block in range(A):
        src = out.at[x, block, c]

        @pl.when((a < A - 1) & (block <= a))
        def _():
            to_line(src, block, 1).wait_send()

        @pl.when((a > 0) & (block >= a))
        def _():
            to_line(src, block, -1).wait_send()

        to_x(src, block).wait_send()
        for side in range(X):
            to_core(src, side, block).wait()


def shrink_scratch(rows, width):
    block = (rows, width)
    P_ = halves(rows)
    return [
        pltpu.VMEM((X, A) + block, bf),
        pltpu.VMEM((X, A) + block, bf),
        pltpu.VMEM((A,) + block, bf),
        pltpu.VMEM((A + 1,) + block, bf),
        DMA((X, A, P_)), DMA((X, A, P_, 2)), DMA((A, P_, 2)), DMA((2, A, P_, 2)),
    ]


def far_first(a, i):
    inner = (3, 0, 2, 1)[i]
    return jnp.where(a == 0, 3 - i, jnp.where(a == 1, inner, jnp.where(a == 2, 3 - inner, i)))


def line_slots(place, sums, landing, sems, parts, ready, final, near=False):
    a = place.a
    last = 2 * A - 3 if near else A - 1

    def part(ref, h):
        if parts == 1:
            return ref
        rows = ref.shape[0] // parts
        return ref.at[pl.ds(h * rows, rows)]

    def hop(d, h, way):
        at = 0 if way > 0 else 1
        return remote(
            part(sums(d), h), part(landing(d, way), h), sems.at[at, d, h, 0],
            sems.at[at, d, h, 1], place.line(a + way),
        )

    def take(d, h, way):
        @pl.when((a - way >= 0) & (a - way < A))
        def _():
            hop(d, h, way).wait_recv()
            here = part(sums(d), h)
            add_into(here, here, part(landing(d, way), h))

    for t in range(last + 1):
        for way in (1, -1):
            at = a if way > 0 else A - 1 - a
            to = t - at + 1 if near else A - 1 - t + at
            d = to if way > 0 else A - 1 - to

            @pl.when((to > at) & (to < A))
            def _():
                for h in range(parts):
                    ready(d, h)
                    take(d, h, way)
                    hop(d, h, way).start()

        if t == last:
            for h in range(parts):
                ready(a, h)
                take(a, h, 1)
                take(a, h, -1)
                final(h)
        yield
    for d in range(A):
        for h in range(parts):
            for way in (1, -1):
                @pl.when((d - a) * way > 0)
                def _():
                    hop(d, h, way).wait_send()


def share_sems():
    return [DMA((2,)), DMA((X, 2)), DMA((1,))]


def share_flow(place, own, out, sems, ready=None):
    x_sem, core_sem, local = sems
    r, x, c = place.r, place.x, place.c
    if ready is not None:
        yield
        ready()
    keep = pltpu.make_async_copy(own, out.at[r], local.at[0])
    to_x = remote(own, out.at[r], x_sem.at[0], x_sem.at[1], place.over_x)
    near = remote(own, out.at[r], core_sem.at[x, 0], core_sem.at[x, 1], place.over_core)
    far = remote(
        out.at[place.rx], out.at[place.rx], core_sem.at[1 - x, 0], core_sem.at[1 - x, 1],
        place.over_core,
    )
    to_x.start()
    near.start()
    keep.start()
    yield
    to_x.wait_recv()
    far.start()
    yield
    keep.wait()
    to_x.wait_send()
    near.wait()
    far.wait()


def spread_sems(B, parts=1):
    return [DMA((A, parts)), DMA((A, 2, parts)), DMA((B, A, parts, 2)), DMA((1,))]


def spread_flow(place, own, out, sems, parts=1):
    line_recv, line_send, side, local = sems
    a, b, B = place.a, place.b, place.B
    keep = pltpu.make_async_copy(own, out.at[a, b], local.at[0])
    keep.start()

    def half(h):
        return own if parts == 1 else own.at[pl.ds(h * own.shape[0] // parts, own.shape[0] // parts)]

    def to_line(src, block, h, way):
        return remote(
            src, piece(out, (block, b), h, parts), line_send.at[block, 0 if way > 0 else 1, h],
            line_recv.at[block, h], place.line(a + way),
        )

    def to_side(src, block, h, k):
        return remote(
            src, piece(out, (block, b), h, parts), side.at[k, block, h, 0],
            side.at[k, block, h, 1], place.side((b + k) % B),
        )

    for h in range(parts):
        @pl.when(a < A - 1)
        def _():
            to_line(half(h), a, h, 1).start()

        @pl.when(a > 0)
        def _():
            to_line(half(h), a, h, -1).start()

        for k in range(1, B):
            to_side(half(h), a, h, k).start()
    for step in range(1, A):
        for h in range(parts):
            yield
            for way in (1, -1):
                block = a - way * step

                @pl.when((block >= 0) & (block < A))
                def _():
                    src = piece(out, (block, b), h, parts)
                    to_line(src, block, h, way).wait_recv()

                    @pl.when((a + way >= 0) & (a + way < A))
                    def _():
                        to_line(src, block, h, way).start()

                    for k in range(1, B):
                        to_side(src, block, h, k).start()

    yield
    keep.wait()
    for block in range(A):
        for h in range(parts):
            src = piece(out, (block, b), h, parts)

            @pl.when((a < A - 1) & (block <= a))
            def _():
                to_line(src, block, h, 1).wait_send()

            @pl.when((a > 0) & (block >= a))
            def _():
                to_line(src, block, h, -1).wait_send()

            for k in range(1, B):
                to_side(src, block, h, k).wait()


def columns_sems(B):
    return [DMA((A, 2)), DMA((B, A, 2)), DMA((1,))]


def columns_flow(place, own, out, sems):
    line, side, local = sems
    a, b, B = place.a, place.b, place.B
    keep = pltpu.make_async_copy(own.at[a], out.at[a, b], local.at[0])
    keep.start()

    def to_line(k):
        to = (a + k) % A
        return remote(own.at[to], out.at[a, b], line.at[k, 0], line.at[k, 1], place.line(to))

    def to_side(src, block, k):
        return remote(
            src, out.at[block, b], side.at[k, block, 0], side.at[k, block, 1],
            place.side((b + k) % B),
        )

    for k in range(1, A):
        to_line(k).start()
    for k in range(1, B):
        to_side(own.at[a], a, k).start()
    for k in (1, 3, 2):
        yield
        to_line(k).wait_recv()
        block = (a + A - k) % A
        for j in range(1, B):
            to_side(out.at[block, b], block, j).start()
    yield
    keep.wait()
    for k in range(1, A):
        to_line(k).wait_send()
    for block in range(A):
        for k in range(1, B):
            to_side(out.at[block, b], block, k).wait()


def sides_sems(B):
    return [DMA((B, 2)), DMA((1,))]


def sides_flow(place, own, out, sems):
    side, local = sems
    b, B = place.b, place.B
    keep = pltpu.make_async_copy(own, out.at[b], local.at[0])
    keep.start()
    copies = [
        remote(own, out.at[b], side.at[k, 0], side.at[k, 1], place.side((b + k) % B))
        for k in range(1, B)
    ]
    for copy in copies:
        copy.start()
    yield
    keep.wait()
    for copy in copies:
        copy.wait()


ANY = pl.BlockSpec(memory_space=pl.ANY)
VMEM = pl.BlockSpec(memory_space=pltpu.VMEM)


def call(kernel, name, collective_id, outs, out_specs, scratch, args, in_specs):
    return pl.pallas_call(
        kernel,
        out_shape=outs,
        in_specs=in_specs,
        out_specs=out_specs,
        scratch_shapes=scratch,
        name=name,
        compiler_params=pltpu.CompilerParams(
            collective_id=collective_id, has_side_effects=True, vmem_limit_bytes=63 * 2**20
        ),
    )(*args)


def shape(*dims, dtype=bf):
    return jax.ShapeDtypeStruct(dims, dtype)


def split_refs(refs, *sizes):
    found, at = [], 0
    for size in sizes:
        found.append(refs[at : at + size])
        at += size
    return found


def select(rows, cols, shift, at, width):
    j = lax.broadcasted_iota(jnp.int32, (1, cols), 1) - at
    wanted = jnp.where((j >= 0) & (j < width), j + shift, -1)
    row = lax.broadcasted_iota(jnp.int32, (rows, cols), 0)
    return jnp.where(row == wanted, 1.0, 0.0).astype(bf)


def rope(ref, at, cosine, sine, out, to, head_dim):
    half = head_dim // 2
    former, latter = ref[pl.ds(at, half), :], ref[pl.ds(at + half, half), :]
    out[pl.ds(to, half), :] = (former * cosine - latter * sine).astype(out.dtype)
    out[pl.ds(to + half, half), :] = (latter * cosine + former * sine).astype(out.dtype)


def attention_forward(B, weights, gates, w_down, gains, tokens, cotangent, ids):
    wrows, width = weights[0].shape
    rows = tokens.shape[0]
    group = 4 * rows
    ff = gates[0].shape[1]
    wcols = width // 4
    head_dim = width // H
    heads = H // 4
    sub = ff // (A * B * 4)
    pad = -(-sub // 16) * 16
    fcols = B * pad
    wide = 384
    span = -(-wcols // 128) * 128
    pair = 2 * wcols
    parts = halves(wrows)
    trio = 3
    score_scale = 1.0 / math.sqrt(head_dim)

    def kernel(*refs):
        w_in, g_in, ins, outs, scratch, refs = split_refs(refs, 4, 2, 8, 12, 18, 100)
        wd_in, gain_in, tok_in, cot_in, seq_row, seq_col, blk_row, blk_col = ins
        (w4_out, gain_out, tok_out, d_out, gu_out, dn_out, qkv_out, mixed_out, after_out,
         n2_out, table_out, normed_t) = outs
        (w_all, g_all, wd_all, own4, gu_own, dn_own, own_gain, gain_all, tok_all, d_own, w4_all,
         normed, raw, bias, mixed, proj, proj_all, load) = scratch
        s1, s2, s3, s4, s5, s6, s7 = split_refs(refs, 4, 4, 3, 6, 3, 2, 100)
        qkv, mix_x, mix_core, ex_sem, save = s7
        place = Place(B)
        r, x, c = place.r, place.x, place.c
        loads = [pltpu.make_async_copy(w, w_all.at[i], load.at[i]) for i, w in enumerate(w_in)]
        loads += [
            pltpu.make_async_copy(w, g_all.at[i], load.at[4 + i]) for i, w in enumerate(g_in)
        ]
        loads.append(pltpu.make_async_copy(wd_in, wd_all, load.at[6]))
        for copy in loads:
            copy.start()
        start = pl.multiple_of(r * wcols // 128 * 128, 128)
        shift = r * wcols - start
        for i in range(2):
            total = jnp.zeros((wrows, pair), f32)
            for j in range(2):
                loads[2 * i + j].wait()
                total += jnp.dot(
                    w_all[2 * i + j, :, pl.ds(start, span)],
                    select(span, pair, shift, j * wcols, wcols), preferred_element_type=f32,
                )
            own4[:, i * pair : (i + 1) * pair] = total.astype(bf)
        for k in range(width // wide):
            own_gain[:, k * wide : (k + 1) * wide] = jnp.dot(
                gain_in[...], select(wrows, wide, 0, place.s * wrows - k * wide, wrows),
                preferred_element_type=f32,
            )
        greet(place, True, True, True)

        def prepare():
            for i in range(2):
                loads[4 + i].wait()
            loads[6].wait()

            def one(n, carry):
                i, block = n // A, n % A
                total = jnp.zeros((wrows, fcols), f32)
                for j in range(B):
                    first = ((block * B + j) * 4 + r) * sub
                    at = pl.multiple_of(jnp.minimum(first // 128 * 128, ff - wide), 128)
                    total += jnp.dot(
                        g_all[i, :, pl.ds(at, wide)],
                        select(wide, fcols, first - at, j * pad, sub),
                        preferred_element_type=f32,
                    )
                at = pl.multiple_of(i * fcols, 128)
                gu_own[block, :, pl.ds(at, fcols)] = total.astype(bf)
                return carry

            lax.fori_loop(0, 2 * A, one, 0)
            row = lax.broadcasted_iota(jnp.int32, (pad, ff // (A * B)), 0)
            col = lax.broadcasted_iota(jnp.int32, (pad, ff // (A * B)), 1)
            pick = jnp.where((col - r * sub == row) & (row < sub), 1.0, 0.0).astype(bf)
            tile = 768

            def down(n, carry):
                at = pl.ds(pl.multiple_of(n * tile, tile), tile)
                dn_own[:, at] = jnp.dot(
                    pick, wd_all[:, at], preferred_element_type=f32
                ).astype(bf)
                return carry

            lax.fori_loop(0, width // tile, down, 0)
            d_own[...] = (branch_scale * cot_in[...].astype(f32)).astype(bf)
            less = jnp.where(seq_col[...] < seq_row[...], 1.0, 0.0)
            earlier = jnp.sum(less, axis=0, keepdims=True)
            at = lax.broadcasted_iota(jnp.int32, (1, group), 1).astype(f32) - earlier
            half = head_dim // 2
            index = lax.broadcasted_iota(jnp.int32, (half, group), 0).astype(f32)
            angle = at * jnp.exp(index * (-2.0 * math.log(rope_base) / head_dim))
            table_out[0] = jnp.cos(angle)
            table_out[1] = jnp.sin(angle)
            allowed = (seq_col[...] == seq_row[...]) & (blk_col[...] <= blk_row[...])
            bias[...] = jnp.where(allowed, 0.0, masked_score)
            yield
            total = jnp.zeros((8, width), f32)
            for block in range(A):
                for side in range(B):
                    total += gain_all[block, side]
            gain_out[...] = total
            for i in range(4):
                value = tok_all[i].astype(f32)
                factor = lax.rsqrt(jnp.mean(value * value, axis=1, keepdims=True) + norm_eps)
                value = value * factor * total[0:1]
                at = slice(i * rows, (i + 1) * rows)
                normed[at, :] = value.astype(bf)
                normed_t[:, at] = value.T.astype(bf)

        def share_piece(k):
            at = pl.ds(k * trio * head_dim, trio * head_dim)
            own = mixed.at[r, at]
            far = mixed.at[place.rx, at]
            return (
                remote(own, own, mix_x.at[k, 0], mix_x.at[k, 1], place.over_x),
                remote(own, own, mix_core.at[x, k, 0], mix_core.at[x, k, 1], place.over_core),
                remote(
                    far, far, mix_core.at[1 - x, k, 0], mix_core.at[1 - x, k, 1],
                    place.over_core,
                ),
            )

        pieces = heads // trio

        def attend():
            step = 256

            def project(n, carry):
                cols = pl.ds(pl.multiple_of(span - 128 + n * step, 128), step)
                w = w4_all[:, :, :, cols].reshape(width, step)
                at = pl.ds(pl.multiple_of(n * step, step), step)
                raw[at, :] = product(normed[...], w).T
                return carry

            lax.fori_loop(0, (width - span + 128) // step, project, 0)
            skip = wcols - (span - 128)
            cosine, sine = table_out[0], table_out[1]

            def turn(n, carry):
                at = pl.multiple_of(wcols + n * head_dim, 32)
                rope(raw, pl.multiple_of(skip + at, 32), cosine, sine, qkv, at, head_dim)
                return carry

            lax.fori_loop(0, 2 * heads, turn, 0)
            qkv[:wcols, :] = raw[pl.ds(skip, wcols), :].astype(bf)
            pltpu.make_async_copy(qkv, qkv_out, save.at[0]).start()
            yield

            def head(n, carry):
                at = lambda part: pl.ds(pl.multiple_of(part * wcols + n * head_dim, 64), head_dim)
                scores = across(qkv[at(2), :], qkv[at(1), :]) * score_scale + bias[...]
                top = jnp.max(scores, axis=0, keepdims=True)
                powers = jnp.exp(scores - top)
                probs = powers * (1.0 / jnp.sum(powers, axis=0, keepdims=True))
                mixed[r, at(0), :] = product(qkv[at(0), :], probs.astype(bf)).astype(bf)
                return carry

            for k in range(pieces):
                lax.fori_loop(k * trio, (k + 1) * trio, head, 0)
                to_x, near, far = share_piece(k)
                to_x.start()
                near.start()
                if k:
                    to_x, near, far = share_piece(k - 1)
                    to_x.wait_recv()
                    far.start()
                yield
            to_x, near, far = share_piece(pieces - 1)
            to_x.wait_recv()
            far.start()
            for k in range(pieces):
                to_x, near, far = share_piece(k)
                near.wait_recv()
                far.wait_recv()
            everyone = mixed[...].reshape(width, group)
            value = across(everyone, w4_all[:, :, :, :span].reshape(width, span))
            proj[...] = value.astype(bf).reshape(4, rows, span)
            proj_all[r] = proj[r]
            copies = []
            for k in (2, 3, 1):
                to = (r + k) % 4
                copies.append(
                    remote(
                        proj.at[to], proj_all.at[r], ex_sem.at[k, 0], ex_sem.at[k, 1],
                        (place.s, to),
                    )
                )
                copies[-1].start()
            saved = pltpu.make_async_copy(mixed, mixed_out, save.at[1])
            saved.start()
            yield
            for copy in copies:
                copy.wait()
            own = tok_all[r].astype(f32)
            halves_ = []
            for side in range(2):
                total = jnp.zeros((rows, pair), f32)
                for core in range(2):
                    total += jnp.dot(
                        proj_all[side * 2 + core],
                        select(span, pair, 0, core * wcols, wcols), preferred_element_type=f32,
                    )
                at = slice(side * pair, (side + 1) * pair)
                halves_.append(own[:, at] + branch_scale * total)
                after_out[:, at] = halves_[-1]
            mean = sum(jnp.sum(v * v, axis=1, keepdims=True) for v in halves_) / width
            factor = lax.rsqrt(mean + norm_eps)
            for side in range(2):
                at = slice(side * pair, (side + 1) * pair)
                n2_out[:, at] = (halves_[side] * factor * gain_out[1:2, at]).astype(bf)
            yield
            saved.wait()
            pltpu.make_async_copy(qkv, qkv_out, save.at[0]).wait()
            for k in range(pieces):
                to_x, near, far = share_piece(k)
                to_x.wait_send()
                near.wait_send()
                far.wait_send()

        def weights_flow():
            yield from spread_flow(place, own4, w4_all, s1, parts)
            pltpu.make_async_copy(w4_all, w4_out, save.at[2]).start()

        run_flows(
            [
                weights_flow(),
                share_flow(place, tok_in, tok_all, s3),
                spread_flow(place, own_gain, gain_all, s2),
                prepare(),
                widen_flow(place, d_own, d_out, s4),
                columns_flow(place, gu_own, gu_out, s5),
                sides_flow(place, dn_own, dn_out, s6),
                attend(),
            ],
            (0, 1, 2, 3, 1, 1, 1, 2, 2, 2, 2, 2, 3, 3) + (0,) * (3 * parts) + (4, 5, 6, 0, 0)
            + (4, 7, 4, 5, 7, 4, 5, 7, 4, 5, 7, 4, 4, 5, 7, 4),
        )
        saved = pltpu.make_async_copy(tok_all, tok_out, save.at[1])
        saved.start()
        saved.wait()
        pltpu.make_async_copy(w4_all, w4_out, save.at[2]).wait()

    block = (rows, width)
    return call(
        kernel, "attention_forward", 1,
        [
            shape(A, B, wrows, 4 * wcols), shape(8, width, dtype=f32), shape(4, *block),
            shape(X, A, X, *block), shape(A, B, wrows, 2 * fcols), shape(B, pad, width),
            shape(3 * wcols, group), shape(4, wcols, group), shape(*block, dtype=f32),
            shape(*block), shape(2, head_dim // 2, group, dtype=f32), shape(width, group),
        ],
        [ANY, VMEM, ANY, ANY, ANY, ANY, ANY, ANY, VMEM, VMEM, VMEM, VMEM],
        [
            pltpu.VMEM((4, wrows, width), bf), pltpu.VMEM((2, wrows, ff), bf),
            pltpu.VMEM(w_down.shape, bf), pltpu.VMEM((wrows, 4 * wcols), bf),
            pltpu.VMEM((A, wrows, 2 * fcols), bf), pltpu.VMEM((pad, width), bf),
            pltpu.VMEM((8, width), f32), pltpu.VMEM((A, B, 8, width), f32),
            pltpu.VMEM((4,) + block, bf), pltpu.VMEM(block, bf),
            pltpu.VMEM((A, B, wrows, 4 * wcols), bf), pltpu.VMEM((group, width), bf),
            pltpu.VMEM((width - span + 128, group), f32), pltpu.VMEM((group, group), f32),
            pltpu.VMEM((4, wcols, group), bf), pltpu.VMEM((4, rows, span), bf),
            pltpu.VMEM((4, rows, span), bf), DMA((7,)),
        ]
        + spread_sems(B, parts) + spread_sems(B) + share_sems() + widen_sems() + columns_sems(B)
        + sides_sems(B)
        + [
            pltpu.VMEM((3 * wcols, group), bf), DMA((3, 2)), DMA((X, 3, 2)), DMA((4, 2)),
            DMA((3,)),
        ],
        [*weights, *gates, w_down, gains, tokens, cotangent, *ids],
        [ANY] * 7 + [VMEM, ANY] + [VMEM] * 5,
    )


def feed_forward(B, normed_two, d_down, gate_up, down):
    rows, width = normed_two.shape
    fcols = down.shape[0]
    every = X * A * X * rows
    pair = X * rows
    parts = halves(rows)
    wide = 768
    tile = 384

    wrows = gate_up.shape[0] // (A * B)
    pad = fcols // B
    many = 1152

    def kernel(n_in, d_in, gu_in, dn_in, out, f_out, ggu_out, gd_out, *refs):
        bufs, (line_recv, line_send, over_x, over_core), sems = split_refs(refs, 11, 4, 100)
        n_all, d_all, gu, dn, part, hid, d_gu, from_core, from_x, landed, g_all = bufs
        (g_down, load, core_sem, x_sem, line_sem, gu_side, gd_side, gu_sem, gd_sem, f_core, f_x,
         free, f_line) = sems
        place = Place(B)
        a, x, c = place.a, place.x, place.c
        loads = [
            pltpu.make_async_copy(n_in, n_all.at[x, a, c], load.at[0]),
            pltpu.make_async_copy(gu_in, gu, load.at[1]),
            pltpu.make_async_copy(dn_in, dn, load.at[2]),
            pltpu.make_async_copy(d_in, d_all, load.at[3]),
        ]
        for copy in loads:
            copy.start()
        greet(place, True, True, True)

        def to_line(block, way):
            src = n_all.at[x, block, c]
            return remote(
                src, src, line_send.at[block, (1 - way) // 2], line_recv.at[block],
                place.line(a + way),
            )

        def to_x(block):
            src = n_all.at[x, block, c]
            return remote(src, src, over_x.at[block, 0], over_x.at[block, 1], place.over_x)

        def to_core(side, block):
            src = n_all.at[side, block, c]
            return remote(
                src, src, over_core.at[side, block, 0], over_core.at[side, block, 1],
                place.over_core,
            )

        def sum_core(side, d, h):
            return remote(
                piece(part, (side, d, 1 - c), h, parts), piece(from_core, (side, d), h, parts),
                core_sem.at[side, d, h, 0], core_sem.at[side, d, h, 1], place.over_core,
            )

        def sum_x(d, h):
            return remote(
                piece(part, (1 - x, d, c), h, parts), piece(from_x, d, h, parts),
                x_sem.at[d, h, 0], x_sem.at[d, h, 1], place.over_x,
            )

        def merge(side, d, h):
            sum_core(side, d, h).wait_recv()
            here = piece(part, (side, d, c), h, parts)
            add_into(here, here, piece(from_core, (side, d), h, parts))

        def send_sum(d):
            for h in range(parts):
                merge(1 - x, d, h)
                sum_x(d, h).start()

        loads[0].wait()

        @pl.when(a < A - 1)
        def _():
            to_line(a, 1).start()

        @pl.when(a > 0)
        def _():
            to_line(a, -1).start()

        to_x(a).start()
        to_core(x, a).start()
        for copy in loads[1:]:
            copy.wait()

        def nearest(i):
            left = jnp.where(a == 1, jnp.where(i == 1, 0, i), jnp.where(i == 0, 0, i))
            left = jnp.where((a == 1) & (i == 0), 1, left)
            right = jnp.where(a == 2, jnp.where(i == 0, 2, jnp.where(i == 1, 1, 3)), A - 1 - i)
            right = jnp.where((a == 2) & (i == A - 1), 0, right)
            return jnp.where(a < 2, left, right)

        def item(j):
            near = (j == 0) | ((j % 2 == 1) & (j < 2 * A - 1))
            i = jnp.where(near, (j + 1) // 2, jnp.where(j == 2 * A - 1, A - 1, j // 2 - 1))
            return near, nearest(i)

        def compute(side, block):
            n = n_all[side, block].reshape(pair, width)
            d = d_all[side, block].reshape(pair, width)
            both = product(n, gu[...])
            gate, up = both[:, :fcols], both[:, fcols:]
            d_hidden = against(d, dn[...])
            sig = jax.nn.sigmoid(gate)
            at = pl.ds(pl.multiple_of((side * A + block) * pair, pair), pair)
            hid[at, :] = (gate * sig * up).astype(bf)
            d_gate = (d_hidden * up * sig * (1.0 + gate * (1.0 - sig))).astype(bf)
            d_up = (d_hidden * gate * sig).astype(bf)
            both = jnp.concatenate([d_gate, d_up], axis=1)
            d_gu[at, :] = both
            for k in range(width // wide):
                cols = pl.ds(k * wide, wide)
                value = against(both, gu[cols, :]).astype(bf)
                part[side, block, :, :, cols] = value.reshape(X, rows, wide)

        def arrive(j, carry):
            near, block = item(j)
            side = jnp.where(near, x, 1 - x)

            @pl.when(near & (j > 0))
            def _():
                way = jnp.where(block < a, 1, -1)
                to_line(block, way).wait_recv()

                @pl.when((a + way >= 0) & (a + way < A))
                def _():
                    to_line(block, way).start()

                to_x(block).start()
                to_core(x, block).start()

            @pl.when(jnp.logical_not(near))
            def _():
                to_x(block).wait_recv()
                to_core(1 - x, block).start()

            to_core(side, block).wait_recv()
            compute(side, block)
            for h in range(parts):
                sum_core(side, block, h).start()

            before, last = item(jnp.maximum(j - 1, 0))

            @pl.when((j > 3) & jnp.logical_not(before))
            def _():
                send_sum(last)

            return carry

        lax.fori_loop(0, 2 * A, arrive, 0)
        send_sum(nearest(A - 1))
        send_sum(a)

        def ready(d, h):
            merge(x, d, h)
            sum_x(d, h).wait_recv()
            here = piece(part, (x, d, c), h, parts)
            add_into(here, here, piece(from_x, d, h, parts))

        piece_rows = rows // parts

        def final(h):
            at = pl.ds(h * piece_rows, piece_rows)
            out[at, :] = part[x, a, c, at, :]

        chain = line_slots(
            place, lambda d: part.at[x, d, c], lambda d, way: landed.at[d + (way > 0)], line_sem,
            parts, ready, final, near=True,
        )

        def grad_down(k, carry):
            at = pl.ds(pl.multiple_of(k * tile, tile), tile)
            d = d_all[:, :, :, :, at].reshape(every, tile)
            g_down[:, at] = across(hid[...], d).astype(bf)
            return carry

        def grad_gate_up(k, carry):
            at = pl.ds(pl.multiple_of(k * many, many), many)
            n = n_all[:, :, :, :, at].reshape(every, many)
            count = many // wrows
            for i in range(2):
                cols = pl.ds(i * fcols, fcols)
                value = across(n, d_gu[:, cols]).astype(bf)
                g_all[pl.ds(k * count, count), :, cols] = value.reshape(count, wrows, fcols)
            return carry

        def aside(d, k):
            to = (place.b + k) % B
            return remote(
                g_all.at[d * B + to], gu_side.at[k - 1, d], gu_sem.at[k, d, 0],
                gu_sem.at[k, d, 1], place.side(to),
            )

        def aside_down(k):
            to = (place.b + k) % B
            at = pl.ds(pl.multiple_of(to * pad, 16), pad)
            return remote(
                g_down.at[at], gd_side.at[k - 1], gd_sem.at[k, 0], gd_sem.at[k, 1], place.side(to)
            )

        def forward(k, carry):
            side, block = k // A, k % A
            at = pl.ds(pl.multiple_of(k * pair, pair), pair)
            for i in range(width // wide):
                cols = pl.ds(i * wide, wide)
                value = product(hid[at, :], dn[:, cols]).astype(bf)
                d_all[side, block, :, :, cols] = value.reshape(X, rows, wide)
            return carry

        mine = pl.ds(pl.multiple_of(place.b * pad, 16), pad)
        outs = [pltpu.make_async_copy(g_down.at[mine], gd_out, load.at[0])] + [
            pltpu.make_async_copy(g_all.at[d * B + place.b], ggu_out.at[d], load.at[1 + d])
            for d in range(A)
        ]

        def out_core(side, d):
            return remote(
                d_all.at[side, d, 1 - c], n_all.at[side, d, 0], f_core.at[side, d, 0],
                f_core.at[side, d, 1], place.over_core,
            )

        def out_x(d):
            return remote(
                d_all.at[1 - x, d, c], n_all.at[0, d, 1], f_x.at[d, 0], f_x.at[d, 1],
                place.over_x,
            )

        def out_merge(side, d):
            out_core(side, d).wait_recv()
            here = d_all.at[side, d, c]
            add_into(here, here, n_all.at[side, d, 0])
        def out_ready(d, h):
            out_merge(x, d)
            out_x(d).wait_recv()
            here = d_all.at[x, d, c]
            add_into(here, here, n_all.at[0, d, 1])

        def out_final(h):
            pltpu.make_async_copy(d_all.at[x, a, c], f_out, load.at[1 + A]).start()

        def out_landing(d, way):
            return part.at[0, d, 1 - c] if way > 0 else n_all.at[1, d, 1]

        out_chain = line_slots(
            place, lambda d: d_all.at[x, d, c], out_landing, f_line, 1, out_ready, out_final
        )

        lax.fori_loop(0, width // tile, grad_down, 0)
        for k in range(1, B):
            aside_down(k).start()
        next(chain)
        for k in range(width // many):
            grad_gate_up(k, 0)
            for d in range(k * many // (wrows * B), (k + 1) * many // (wrows * B)):
                for j in range(1, B):
                    aside(d, j).start()
            next(chain)
        for d in range(A):
            to_x(d).wait_send()
            for side in range(X):
                to_core(side, d).wait_send()
                for h in range(parts):
                    sum_core(side, d, h).wait_send()

            @pl.when((a < A - 1) & (d <= a))
            def _():
                to_line(d, 1).wait_send()

            @pl.when((a > 0) & (d >= a))
            def _():
                to_line(d, -1).wait_send()

        def tell(device):
            pl.semaphore_signal(free, inc=1, device_id=device, device_id_type=MESH)

        tell(place.over_core)
        tell(place.over_x)

        for k in range(1, A):
            tell(place.line((a + k) % A))

        lax.fori_loop(0, X * A, forward, 0)
        pl.semaphore_wait(free, A + 1)
        for side in (1 - x, x):
            for i in range(A):
                out_core(side, far_first(a, i)).start()
        next(chain)
        for i in range(A):
            d = far_first(a, i)
            out_merge(1 - x, d)
            out_x(d).start()
        for _ in chain:
            pass
        for k in range(1, B):
            aside_down(k).wait_recv()
            add_into(g_down.at[mine], g_down.at[mine], gd_side.at[k - 1])
        outs[0].start()
        next(out_chain)
        for d in range(A):
            for k in range(1, B):
                aside(d, k).wait_recv()
                here = g_all.at[d * B + place.b]
                add_into(here, here, gu_side.at[k - 1, d])
            outs[1 + d].start()
        for _ in out_chain:
            pass
        pltpu.make_async_copy(d_all.at[x, a, c], f_out, load.at[1 + A]).wait()
        for copy in outs:
            copy.wait()
        for k in range(1, B):
            aside_down(k).wait_send()
            for d in range(A):
                aside(d, k).wait_send()
        for d in range(A):
            out_x(d).wait_send()
            for side in range(X):
                out_core(side, d).wait_send()
            for h in range(parts):
                sum_x(d, h).wait_send()

    block = (rows, width)
    return call(
        kernel, "feed_forward", 2,
        [
            shape(*block), shape(*block), shape(A, wrows, 2 * fcols),
            shape(pad, width),
        ],
        [VMEM, ANY, ANY, ANY],
        [
            pltpu.VMEM((X, A, X) + block, bf), pltpu.VMEM((X, A, X) + block, bf),
            pltpu.VMEM(gate_up.shape, bf), pltpu.VMEM(down.shape, bf),
            pltpu.VMEM((X, A, X) + block, bf), pltpu.VMEM((every, fcols), bf),
            pltpu.VMEM((every, 2 * fcols), bf), pltpu.VMEM((X, A) + block, bf),
            pltpu.VMEM((A,) + block, bf), pltpu.VMEM((A + 1,) + block, bf),
            pltpu.VMEM((A * B, wrows, 2 * fcols), bf),
            DMA((A,)), DMA((A, 2)), DMA((A, 2)), DMA((X, A, 2)),
            pltpu.VMEM((fcols, width), bf), DMA((2 + A,)), DMA((X, A, parts, 2)),
            DMA((A, parts, 2)), DMA((2, A, parts, 2)),
            pltpu.VMEM((B - 1, A, wrows, 2 * fcols), bf), pltpu.VMEM((B - 1, pad, width), bf),
            DMA((B, A, 2)), DMA((B, 2)), DMA((X, A, 2)), DMA((A, 2)), pltpu.SemaphoreType.REGULAR,
            DMA((2, A, 1, 2)),
        ],
        [normed_two, d_down, gate_up, down],
        [ANY] * 4,
    )


def fold_scratch(rows, width):
    block = (rows, width)
    return [
        pltpu.VMEM((X * X,) + block, bf), pltpu.VMEM((X,) + block, bf), pltpu.VMEM(block, bf),
        DMA((X, 2)), DMA((2,)),
    ]


def fold_flow(place, scratch):
    part, from_core, from_x, core_sem, x_sem = scratch
    x, c = place.x, place.c

    def to_core(i):
        return remote(
            part.at[i * X + 1 - c], from_core.at[i], core_sem.at[i, 0], core_sem.at[i, 1],
            place.over_core,
        )

    def merge(i):
        to_core(i).wait_recv()
        here = part.at[i * X + c]
        add_into(here, here, from_core.at[i])

    to_x = remote(part.at[place.rx], from_x, x_sem.at[0], x_sem.at[1], place.over_x)
    to_core(1 - x).start()
    to_core(x).start()
    yield
    merge(1 - x)
    to_x.start()
    merge(x)
    yield
    to_x.wait_recv()
    here = part.at[place.r]
    add_into(here, here, from_x)
    yield
    to_x.wait_send()
    for i in range(X):
        to_core(i).wait_send()


def grad_scratch(B, rows, width):
    block = (rows, width)
    P_ = halves(rows)
    return [
        pltpu.VMEM((A,) + block, bf),
        pltpu.VMEM((B - 1, A) + block, bf),
        pltpu.VMEM((A + 1,) + block, bf),
        DMA((1,)), DMA((B, A, P_, 2)), DMA((2, A, P_, 2)),
        DMA((P_, 2)), DMA((X, P_, 2)), DMA((P_,)),
    ]


def grad_flow(place, produce, tile, sent, out, scratch):
    sums, from_side, landed, stage_sem, side_sem, line_sem, x_sem, core_sem, local = scratch
    b, B, r, x = place.b, place.B, place.r, place.x
    parts = halves(out.shape[1])
    wide = out.shape[2]

    def to_side(k, d, h):
        return remote(
            piece(sent, (k - 1, d), h, parts), piece(from_side, (k - 1, d), h, parts),
            side_sem.at[k, d, h, 0], side_sem.at[k, d, h, 1], place.side((b + k) % B),
        )

    for i in range(A):
        d = far_first(place.a, i)
        for k in range(1, B):
            tile[:, :wide] = produce(d * B + (b + k) % B)
            copy = pltpu.make_async_copy(
                tile.at[:, pl.ds(0, wide)], sent.at[k - 1, d], stage_sem.at[0]
            )
            copy.start()
            if k == 1:
                sums[d] = produce(d * B + b)
            copy.wait()
            for h in range(parts):
                to_side(k, d, h).start()
        yield

    def ready(d, h):
        for k in range(1, B):
            to_side(k, d, h).wait_recv()
            here = piece(sums, d, h, parts)
            add_into(here, here, piece(from_side, (k - 1, d), h, parts))

    def keep(src, h):
        return pltpu.make_async_copy(src, piece(out, r, h, parts), local.at[h])

    def to_x(src, h):
        return remote(src, piece(out, r, h, parts), x_sem.at[h, 0], x_sem.at[h, 1], place.over_x)

    def near(src, h):
        return remote(
            src, piece(out, r, h, parts), core_sem.at[x, h, 0], core_sem.at[x, h, 1],
            place.over_core,
        )

    def far(h):
        src = piece(out, place.rx, h, parts)
        return remote(
            src, src, core_sem.at[1 - x, h, 0], core_sem.at[1 - x, h, 1], place.over_core
        )

    def final(h):
        src = piece(sums, place.a, h, parts)
        to_x(src, h).start()
        near(src, h).start()
        keep(src, h).start()

    yield from line_slots(
        place, lambda d: sums.at[d], lambda d, way: landed.at[d + (way > 0)], line_sem, parts,
        ready, final,
    )
    for h in range(parts):
        src = piece(out, r, h, parts)
        keep(src, h).wait()
        near(src, h).wait()
    yield
    for h in range(parts):
        src = piece(out, r, h, parts)
        to_x(src, h).wait_recv()
        far(h).start()
    yield
    for h in range(parts):
        to_x(piece(out, r, h, parts), h).wait_send()
    for d in range(A):
        for h in range(parts):
            for k in range(1, B):
                to_side(k, d, h).wait_send()
    for h in range(parts):
        far(h).wait()


def owners_flow(place, own, out, sems):
    line, local = sems
    a = place.a
    keep = pltpu.make_async_copy(own.at[a], out.at[a], local.at[0])
    keep.start()
    copies = []
    for k in (1, 3, 2):
        to = (a + k) % A
        copies.append(
            remote(own.at[to], out.at[a], line.at[k, 0], line.at[k, 1], place.line(to))
        )
        copies[-1].start()
    yield
    keep.wait()
    for copy in copies:
        copy.wait()


def attention_backward(
    B, S, d_n2, after_attn, cotangent, gains, w4, qkv, mixed, tokens, normed_t, tables, ids,
    g_gate_up, g_down,
):
    rows, width = d_n2.shape
    group = 4 * rows
    wrows, wcols = width // S, width // 4
    head_dim = width // H
    heads = H // 4
    wide = 384
    span = -(-wcols // 128) * 128
    skip = wcols - (span - 128)
    tail = width - span + 128
    pair = 2 * wcols
    score_scale = 1.0 / math.sqrt(head_dim)
    widths = (span, span, pair)
    parts = halves(wrows)

    def window(s):
        return pl.multiple_of(jnp.minimum(s * wrows // 128 * 128, width - wide), 128)

    def kernel(*refs):
        ins, ids_in, outs, mids, own, refs = split_refs(refs, 12, 4, 2, 9, 15, 100)
        (dn2_in, after_in, cot_in, gain_in, w4_in, qkv_in, mixed_in, tok_in, nt_in, table_in,
         gu_in, gd_in) = ins
        seq_row, seq_col, blk_row, blk_col = ids_in
        gt_out, gain_out = outs
        all_o, all_v, all_qk, sent_o, sent_v, sent_qk, gu_cols, gu_all, gd_all = mids
        (w4, qkv_, mix, tok, n_t, bias, factors, d_nat, ex_send, ex_all, d_after, tile,
         own_gain, gain_all, load) = own
        f1, f2, g1, g2, g3, u1, u2, u3, (ex_sem, gain_sem) = split_refs(
            refs, 5, 5, 9, 9, 9, 2, 3, 3, 2
        )
        place = Place(B)
        r, x, c = place.r, place.x, place.c
        loads = [
            pltpu.make_async_copy(src, dst, load.at[i])
            for i, (src, dst) in enumerate(
                [(w4_in, w4), (mixed_in, mix), (qkv_in, qkv_), (nt_in, n_t), (tok_in, tok)]
            )
        ]
        for copy in loads:
            copy.start()
        part1, part2 = f1[0], f2[0]
        d_t = mix
        gain_one, gain_two = gain_in[0:1], gain_in[1:2]
        own_gain[...] = jnp.zeros_like(own_gain)
        step = 32

        def back_two(i, carry):
            at = pl.ds(pl.multiple_of(i * step, step), step)
            after = after_in[at, :]
            d = dn2_in[at, :].astype(f32)
            factor = lax.rsqrt(jnp.mean(after * after, axis=1, keepdims=True) + norm_eps)
            own_gain[1:2, :] += jnp.sum(d * after * factor, axis=0, keepdims=True)
            u = d * gain_two
            mean = jnp.mean(u * after, axis=1, keepdims=True)
            d_after[at, :] = (
                cot_in[at, :].astype(f32) + factor * u - after * (factor * factor * factor) * mean
            )
            return carry

        lax.fori_loop(0, rows // step, back_two, 0)
        d_proj = (branch_scale * d_after[...]).astype(bf)
        for k in range(4):
            at = k * wcols // 128 * 128
            ex_send[k] = product(
                d_proj[:, at : at + span], select(span, span, k * wcols - at, 0, wcols)
            ).astype(bf)
        ex_all[r] = ex_send[r]
        greet(place, everyone=(S, 4))
        exchange = []
        for k in (2, 3, 1):
            to = (r + k) % 4
            exchange.append(
                remote(
                    ex_send.at[to], ex_all.at[r], ex_sem.at[k, 0], ex_sem.at[k, 1],
                    (place.s, to),
                )
            )
            exchange[-1].start()

        def at_head(part, n):
            return pl.ds(pl.multiple_of(part * wcols + n * head_dim, 64), head_dim)

        def probs_of(n):
            scores = across(qkv_[at_head(2, n), :], qkv_[at_head(1, n), :]) * score_scale
            scores = scores + bias[...].astype(f32)
            powers = jnp.exp(scores - jnp.max(scores, axis=0, keepdims=True))
            return powers * (1.0 / jnp.sum(powers, axis=0, keepdims=True))

        def compute():
            allowed = (seq_col[...] == seq_row[...]) & (blk_col[...] <= blk_row[...])
            bias[...] = jnp.where(allowed, 0.0, masked_score).astype(bf)
            for i in range(4):
                loads[4].wait() if i == 0 else None
                value = tok[i].astype(f32)
                factors[i * rows : (i + 1) * rows, :] = lax.rsqrt(
                    jnp.mean(value * value, axis=1, keepdims=True) + norm_eps
                )
            for copy in loads[:4]:
                copy.wait()
            for copy in exchange:
                copy.wait()
            d_proj = ex_all[...].reshape(group, span)
            for i in (1 - c, c):
                for side in range(X):
                    k = side * X + i
                    at = pl.ds(pl.multiple_of(k * wcols, 64), wcols)
                    part1[k] = against(w4[at, :span], d_proj).astype(bf)
            yield

            def values_back(n, carry):
                d_m = part1[r, pl.ds(pl.multiple_of(n * head_dim, 64), head_dim), :]
                value = against(d_m, probs_of(n).astype(bf))
                at = pl.ds(pl.multiple_of(skip + n * head_dim, 64), head_dim)
                d_t[at, :] = value.astype(bf)
                return carry

            def flip(n, carry):
                at = pl.ds(pl.multiple_of(n * 128, 128), 128)
                d_nat[:, at] = d_t[at, :].astype(f32).T.astype(bf)
                return carry

            d_t[:skip, :] = jnp.zeros((skip, group), bf)
            lax.fori_loop(0, heads, values_back, 0)
            lax.fori_loop(0, span // 128, flip, 0)
            yield
            cosine, sine = table_in[0], table_in[1]
            half = head_dim // 2

            def turn_back(value, at):
                former, latter = value[:half], value[half:]
                d_t[pl.ds(at, half), :] = (former * cosine + latter * sine).astype(bf)
                d_t[pl.ds(at + half, half), :] = (latter * cosine - former * sine).astype(bf)

            def scores_back(n, carry):
                d_m = part1[r, pl.ds(pl.multiple_of(n * head_dim, 64), head_dim), :]
                probs = probs_of(n)
                d_probs = across(qkv_[at_head(0, n), :], d_m)
                d_s = probs * (d_probs - jnp.sum(d_probs * probs, axis=0, keepdims=True))
                d_s = d_s.astype(bf)
                at = pl.multiple_of(span + n * head_dim, 64)
                turn_back(product(qkv_[at_head(2, n), :], d_s) * score_scale, at)
                turn_back(
                    against(qkv_[at_head(1, n), :], d_s) * score_scale,
                    pl.multiple_of(at + wcols, 64),
                )
                return carry

            for k in range(3):
                lax.fori_loop(heads * k // 3, heads * (k + 1) // 3, scores_back, 0)
                if k < 2:
                    yield
            lax.fori_loop(span // 128, tail // 128, flip, 0)
            yield

            def inputs_back(n, carry):
                at = pl.ds(pl.multiple_of(n * wide, 128), wide)
                value = against(d_nat[...], w4[at, pl.ds(span - 128, tail)])
                x_f = tok[:, :, at].reshape(group, wide).astype(f32) * factors[...]
                own_gain[0:1, at] = jnp.sum(value * x_f, axis=0, keepdims=True)
                part2[:, :, at] = value.astype(bf).reshape(4, rows, wide)
                return carry

            lax.fori_loop(0, width // wide, inputs_back, 0)

        def row_block(ref, k):
            if wrows % 16 == 0:
                return ref[pl.ds(pl.multiple_of(k * wrows, 16), wrows), :]
            return product(select(wrows, width, 0, k * wrows, wrows), ref[...]).astype(bf)

        def make_o(k):
            return product(row_block(mix, k), ex_all[...].reshape(group, span)).astype(bf)

        def make_v(k):
            return product(row_block(n_t, k), d_nat[:, :span]).astype(bf)

        def make_qk(k):
            return product(row_block(n_t, k), d_nat[:, span:]).astype(bf)

        def gains_flow():
            def copy(k):
                to = lax.rem(place.s + k // 4, S)
                return remote(
                    own_gain.at[:, pl.ds(window(to), wide)], gain_all.at[k], gain_sem.at[k, 0],
                    gain_sem.at[k, 1], (to, lax.rem(r + k % 4, 4)),
                )

            def begin(k, carry):
                copy(k).start()
                return carry

            def end(k, total):
                copy(k).wait()
                return total + gain_all[k]

            start = window(place.s)
            lax.fori_loop(1, 4 * S, begin, 0)
            yield
            total = lax.fori_loop(1, 4 * S, end, own_gain[:, pl.ds(start, wide)])
            pick = select(wide, wide, place.s * wrows - start, 0, wrows)
            value = jnp.zeros_like(total)
            for _ in range(3):
                low = total.astype(bf)
                value += product(low, pick)
                total = total - low.astype(f32)
            gain_out[...] = value

        def input_end():
            def back_one(i, carry):
                at = pl.ds(pl.multiple_of(i * step, step), step)
                value = tok[r, at, :].astype(f32)
                d = part2[r, at, :].astype(f32)
                factor = lax.rsqrt(jnp.mean(value * value, axis=1, keepdims=True) + norm_eps)
                u = d * gain_one
                mean = jnp.mean(u * value, axis=1, keepdims=True)
                gt_out[at, :] = (
                    d_after[at, :] + factor * u - value * (factor * factor * factor) * mean
                ).astype(bf)
                return carry

            lax.fori_loop(0, rows // step, back_one, 0)
            yield

        M, O, V, Q, F1, F2, GU, SU, SD, G, T = range(11)
        flows = [
            compute(),
            grad_flow(place, make_o, tile, sent_o, all_o, g1),
            grad_flow(place, make_v, tile, sent_v, all_v, g2),
            grad_flow(place, make_qk, tile, sent_qk, all_qk, g3),
            fold_flow(place, f1),
            fold_flow(place, f2),
            owners_flow(place, gu_in, gu_cols, u1),
            share_flow(place, gu_cols, gu_all, u2),
            share_flow(place, gd_in, gd_all, u3),
            gains_flow(),
            input_end(),
        ]
        turns = [
            GU, M, F1, O, O, O, O, F1, F1, F1, SD, M, GU, SU, V, V, V, V, M, O, M, O, M, Q, Q, Q,
            Q, O, O, M, F2, G, V, F2, V, SD, SD, O, V, V, V, F2, F2, T, SU, SU, O, V, Q, V, G, Q,
        ]
        run_flows(flows, turns)

    block = (rows, width)
    o_block, q_block = (wrows, span), (wrows, pair)
    blocks = [(wrows, w) for w in widths]
    return call(
        kernel, "attention_backward", 3,
        [
            shape(*block), shape(8, wide, dtype=f32),
        ]
        + [shape(4, *v) for v in blocks] + [shape(B - 1, A, *v) for v in blocks]
        + [shape(*g_gate_up.shape), shape(4, *g_gate_up.shape), shape(4, *g_down.shape)],
        [VMEM, VMEM] + [ANY] * 9,
        [
            pltpu.VMEM((width, width), bf), pltpu.VMEM((3 * wcols, group), bf),
            pltpu.VMEM((width, group), bf), pltpu.VMEM((4,) + block, bf),
            pltpu.VMEM((width, group), bf), pltpu.VMEM((group, group), bf),
            pltpu.VMEM((group, 1), f32),
            pltpu.VMEM((group, tail), bf), pltpu.VMEM((4, rows, span), bf),
            pltpu.VMEM((4, rows, span), bf), pltpu.VMEM(block, f32), pltpu.VMEM((wrows, pair), bf),
            pltpu.VMEM((8, width), f32), pltpu.VMEM((4 * S, 8, wide), f32), DMA((5,)),
        ]
        + fold_scratch(wcols, group) + fold_scratch(*block)
        + grad_scratch(B, wrows, span) + grad_scratch(B, wrows, span)
        + grad_scratch(B, wrows, pair)
        + [DMA((A, 2)), DMA((1,))] + share_sems() + share_sems()
        + [DMA((4, 2)), DMA((4 * S, 2))],
        [
            d_n2, after_attn, cotangent, gains, w4, qkv, mixed, tokens, normed_t, tables,
            g_gate_up, g_down, *ids,
        ],
        [VMEM] * 4 + [ANY] * 5 + [VMEM] + [ANY] * 2 + [VMEM] * 4,
    )


def lay_out(S, ff, out, value, query_key, gate_up, down):
    wrows, span = out.shape[1:]
    pair = query_key.shape[2]
    wcols = pair // 2
    width = 4 * wcols
    skip = wcols - (span - 128)
    sub = ff // (S * 4)
    pad = down.shape[1]
    fcols = gate_up.shape[3] // 2
    B = fcols // pad
    drows = ff // S
    steps = 9 if wrows % 144 == 0 else 1
    rows, cols = wrows // steps, width // steps

    def kernel(o_in, v_in, qk_in, gu_in, d_in, o_out, q_out, k_out, v_out, g_out, u_out, d_out):
        def beside(ref, at, to):
            for side in range(2):
                parts = [
                    ref[side * 2 + core].astype(f32)[:, at : at + wcols] for core in range(2)
                ]
                to[:, side * pair : (side + 1) * pair] = jnp.concatenate(parts, axis=1)

        beside(o_in, 0, o_out)
        beside(v_in, skip, v_out)
        beside(qk_in, 0, q_out)
        beside(qk_in, wcols, k_out)
        for i, to in enumerate((g_out, u_out)):
            parts = []
            for m in range(4 * S):
                s = m // 4
                at = i * fcols + s % B * pad
                parts.append(gu_in[m % 4, s // B].astype(f32)[:, at : at + sub])
            to[...] = jnp.concatenate(parts, axis=1)
        d_out[...] = jnp.concatenate([d_in[k].astype(f32)[:sub] for k in range(4)], axis=0)

    def by_rows(ref):
        lead = len(ref.shape) - 2
        return pl.BlockSpec(
            ref.shape[:lead] + (rows, ref.shape[-1]), lambda i: (0,) * lead + (i, 0)
        )

    outs = [shape(wrows, width, dtype=f32)] * 4 + [shape(wrows, ff, dtype=f32)] * 2
    return pl.pallas_call(
        kernel,
        grid=(steps,),
        out_shape=outs + [shape(drows, width, dtype=f32)],
        in_specs=[by_rows(v) for v in (out, value, query_key, gate_up)]
        + [pl.BlockSpec((4, pad, cols), lambda i: (0, 0, i))],
        out_specs=[by_rows(v) for v in outs] + [pl.BlockSpec((drows, cols), lambda i: (0, i))],
        name="lay_out",
        compiler_params=pltpu.CompilerParams(vmem_limit_bytes=60 * 2**20),
    )(out, value, query_key, gate_up, down)


def product(left_side, right_side):
    return jnp.dot(left_side, right_side, preferred_element_type=f32)


def against(left_side, right_side):
    return lax.dot_general(
        left_side, right_side, (((1,), (1,)), ((), ())), preferred_element_type=f32
    )


def across(left_side, right_side):
    return lax.dot_general(
        left_side, right_side, (((0,), (0,)), ((), ())), preferred_element_type=f32
    )


def body(
    tokens,
    attn_gain,
    w_query,
    w_key,
    w_value,
    w_out,
    ffn_gain,
    w_gate,
    w_up,
    w_down,
    seq_ids,
    block_ids,
    cotangent,
):
    S = lax.axis_size("shard")
    R = lax.axis_size("replica")
    B = S // A
    rows, width = tokens.shape
    ff = w_gate.shape[1]
    wrows = width // S
    ids = (seq_ids[None, :], seq_ids[:, None], block_ids[None, :], block_ids[:, None])
    gains = jnp.pad(jnp.stack([attn_gain, ffn_gain]), ((0, 6), (0, 0)))
    (
        w4, gains, tokens_group, d_down, gate_up, down_w, qkv, mixed_all, after_attn, normed_two,
        tables, normed_t,
    ) = attention_forward(
        B, [w_out, w_value, w_query, w_key], [w_gate, w_up], w_down, gains, tokens, cotangent, ids
    )
    d_n2, ffn_out, g_gate_up, g_down = feed_forward(
        B, normed_two, d_down, gate_up.reshape(width, -1), down_w.reshape(-1, width)
    )
    grad_tokens, gain_sums, *parts = attention_backward(
        B, S, d_n2, after_attn, cotangent, gains, w4.reshape(width, width), qkv,
        mixed_all.reshape(width, -1), tokens_group, normed_t, tables, ids, g_gate_up, g_down,
    )
    g_out, g_query, g_key, g_value, g_gate, g_up, g_down = lay_out(
        S, ff, *parts[:3], *parts[7:]
    )
    result = after_attn + branch_scale * ffn_out.astype(f32)
    return (
        result.astype(bf), grad_tokens, gain_sums[0, :wrows], g_query, g_key, g_value, g_out,
        gain_sums[1, :wrows], g_gate, g_up, g_down,
    )


def solution(mesh):
    split = P(("shard", "replica"), None)
    vec, mat = P("shard"), P("shard", None)
    in_specs = (split, vec, mat, mat, mat, mat, vec, mat, mat, mat, vec, vec, split)
    out_specs = (split, split, vec, mat, mat, mat, mat, vec, mat, mat, mat)
    return jax.shard_map(body, mesh=mesh, in_specs=in_specs, out_specs=out_specs, check_vma=False)
```

```python
import functools
import math

import jax
import jax.numpy as jnp
from jax import lax
from jax.experimental import pallas as pl
from jax.experimental.pallas import tpu as pltpu
from jax.sharding import PartitionSpec as P

H = 36
A = 4
X = 2

branch_scale = 1.4 / math.sqrt(40.0)
norm_eps = 1e-05
rope_base = 10000.0
masked_score = -1e30
MESH = pl.DeviceIdType.MESH
bf = jnp.bfloat16
f32 = jnp.float32
DMA = pltpu.SemaphoreType.DMA


class Place:
    def __init__(self, B):
        self.B = B
        s, r = lax.axis_index("shard"), lax.axis_index("replica")
        self.s, self.r = s, r
        self.a, self.b = s // B, s % B
        self.x, self.c = r // X, r % X
        self.rx = (1 - self.x) * X + self.c
        self.rc = self.x * X + 1 - self.c

    def line(self, a):
        return (a * self.B + self.b, self.r)

    def side(self, b):
        return (self.a * self.B + b, self.r)

    @property
    def over_x(self):
        return (self.s, self.rx)

    @property
    def over_core(self):
        return (self.s, self.rc)


def greet(place, a_peers=True, b_peers=False, r_peers=True, everyone=None):
    barrier = pltpu.get_barrier_semaphore()

    def signal(device):
        pl.semaphore_signal(barrier, inc=1, device_id=device, device_id_type=MESH)

    if everyone is not None:
        S, R = everyone

        def one(k, carry):
            signal((lax.rem(place.s + k // R, S), lax.rem(place.r + k % R, R)))
            return carry

        lax.fori_loop(1, S * R, one, 0)
        pl.semaphore_wait(barrier, S * R - 1)
        return
    count = 0
    if a_peers:
        for k in range(1, A):
            signal(place.line((place.a + k) % A))
            count += 1
    if b_peers:
        for k in range(1, place.B):
            signal(place.side((place.b + k) % place.B))
            count += 1
    if r_peers:
        for k in range(1, 4):
            signal((place.s, (place.r + k) % 4))
            count += 1
    pl.semaphore_wait(barrier, count)


def remote(src, dst, send, recv, device):
    return pltpu.make_async_remote_copy(
        src_ref=src, dst_ref=dst, send_sem=send, recv_sem=recv, device_id=device,
        device_id_type=MESH,
    )


def add_into(dst, first, second, tile=32):
    rows = dst.shape[0]
    tile = math.gcd(rows, tile) if math.gcd(rows, tile) >= 16 else rows

    def step(i, carry):
        at = pl.ds(pl.multiple_of(i * tile, tile), tile)
        dst[at, :] = (first[at, :].astype(f32) + second[at, :].astype(f32)).astype(dst.dtype)
        return carry

    lax.fori_loop(0, rows // tile, step, 0)


def run_flows(flows, turns=()):
    ended = set()

    def step(at):
        if at not in ended:
            try:
                next(flows[at])
            except StopIteration:
                ended.add(at)

    for at in turns:
        step(at)
    while len(ended) < len(flows):
        for at in range(len(flows)):
            step(at)


def halves(rows):
    return 2 if rows % 32 == 0 else 1


def piece(ref, at, h, parts):
    if parts == 1:
        return ref.at[at]
    rows = ref.shape[-2] // parts
    index = at if isinstance(at, tuple) else (at,)
    return ref.at[index + (pl.ds(h * rows, rows),)]


def widen_sems():
    return [DMA((A,)), DMA((X,)), DMA((A, 2)), DMA((A, 2)), DMA((X, A, 2)), DMA((1,))]


def widen_flow(place, own, out, sems):
    line_recv, _, line_send, over_x, over_core, local = sems
    a, x, c = place.a, place.x, place.c
    keep = pltpu.make_async_copy(own, out.at[x, a, c], local.at[0])
    keep.start()

    def to_line(src, block, way):
        at = 0 if way > 0 else 1
        return remote(
            src, out.at[x, block, c], line_send.at[block, at], line_recv.at[block],
            place.line(a + way),
        )

    def to_x(src, block):
        return remote(
            src, out.at[x, block, c], over_x.at[block, 0], over_x.at[block, 1], place.over_x
        )

    def to_core(src, side, block):
        return remote(
            src, out.at[side, block, c], over_core.at[side, block, 0],
            over_core.at[side, block, 1], place.over_core,
        )

    @pl.when(a < A - 1)
    def _():
        to_line(own, a, 1).start()

    @pl.when(a > 0)
    def _():
        to_line(own, a, -1).start()

    to_x(own, a).start()
    to_core(own, x, a).start()

    def pass_x(k):
        for ok, block in ((a - k >= 0, a - k), (a + k < A, a + k)) if k else ((None, a),):
            def go():
                src = out.at[1 - x, block, c]
                to_x(src, block).wait_recv()
                to_core(src, 1 - x, block).start()

            go() if ok is None else pl.when(ok)(go)

    for k in range(1, A):
        yield
        for way in (1, -1):
            block = a - way * k

            @pl.when((block >= 0) & (block < A))
            def _():
                src = out.at[x, block, c]
                to_line(src, block, way).wait_recv()

                @pl.when((a + way >= 0) & (a + way < A))
                def _():
                    to_line(src, block, way).start()

                to_x(src, block).start()
                to_core(src, x, block).start()

        yield
        pass_x(k - 1)
    yield
    pass_x(A - 1)
    yield
    keep.wait()
    for block in range(A):
        src = out.at[x, block, c]

        @pl.when((a < A - 1) & (block <= a))
        def _():
            to_line(src, block, 1).wait_send()

        @pl.when((a > 0) & (block >= a))
        def _():
            to_line(src, block, -1).wait_send()

        to_x(src, block).wait_send()
        for side in range(X):
            to_core(src, side, block).wait()


def shrink_scratch(rows, width):
    block = (rows, width)
    P_ = halves(rows)
    return [
        pltpu.VMEM((X, A) + block, bf),
        pltpu.VMEM((X, A) + block, bf),
        pltpu.VMEM((A,) + block, bf),
        pltpu.VMEM((A + 1,) + block, bf),
        DMA((X, A, P_)), DMA((X, A, P_, 2)), DMA((A, P_, 2)), DMA((2, A, P_, 2)),
    ]


def far_first(a, i):
    inner = (3, 0, 2, 1)[i]
    return jnp.where(a == 0, 3 - i, jnp.where(a == 1, inner, jnp.where(a == 2, 3 - inner, i)))


def line_slots(place, sums, landing, sems, parts, ready, final, near=False):
    a = place.a
    last = 2 * A - 3 if near else A - 1

    def part(ref, h):
        if parts == 1:
            return ref
        rows = ref.shape[0] // parts
        return ref.at[pl.ds(h * rows, rows)]

    def hop(d, h, way):
        at = 0 if way > 0 else 1
        return remote(
            part(sums(d), h), part(landing(d, way), h), sems.at[at, d, h, 0],
            sems.at[at, d, h, 1], place.line(a + way),
        )

    def take(d, h, way):
        @pl.when((a - way >= 0) & (a - way < A))
        def _():
            hop(d, h, way).wait_recv()
            here = part(sums(d), h)
            add_into(here, here, part(landing(d, way), h))

    for t in range(last + 1):
        for way in (1, -1):
            at = a if way > 0 else A - 1 - a
            to = t - at + 1 if near else A - 1 - t + at
            d = to if way > 0 else A - 1 - to

            @pl.when((to > at) & (to < A))
            def _():
                for h in range(parts):
                    ready(d, h)
                    take(d, h, way)
                    hop(d, h, way).start()

        if t == last:
            for h in range(parts):
                ready(a, h)
                take(a, h, 1)
                take(a, h, -1)
                final(h)
        yield
    for d in range(A):
        for h in range(parts):
            for way in (1, -1):
                @pl.when((d - a) * way > 0)
                def _():
                    hop(d, h, way).wait_send()


def share_sems():
    return [DMA((2,)), DMA((X, 2)), DMA((1,))]


def share_flow(place, own, out, sems, ready=None):
    x_sem, core_sem, local = sems
    r, x, c = place.r, place.x, place.c
    if ready is not None:
        yield
        ready()
    keep = pltpu.make_async_copy(own, out.at[r], local.at[0])
    to_x = remote(own, out.at[r], x_sem.at[0], x_sem.at[1], place.over_x)
    near = remote(own, out.at[r], core_sem.at[x, 0], core_sem.at[x, 1], place.over_core)
    far = remote(
        out.at[place.rx], out.at[place.rx], core_sem.at[1 - x, 0], core_sem.at[1 - x, 1],
        place.over_core,
    )
    to_x.start()
    near.start()
    keep.start()
    yield
    to_x.wait_recv()
    far.start()
    yield
    keep.wait()
    to_x.wait_send()
    near.wait()
    far.wait()


def spread_sems(B, parts=1):
    return [DMA((A, parts)), DMA((A, 2, parts)), DMA((B, A, parts, 2)), DMA((1,))]


def spread_flow(place, own, out, sems, parts=1):
    line_recv, line_send, side, local = sems
    a, b, B = place.a, place.b, place.B
    keep = pltpu.make_async_copy(own, out.at[a, b], local.at[0])
    keep.start()

    def half(h):
        return own if parts == 1 else own.at[pl.ds(h * own.shape[0] // parts, own.shape[0] // parts)]

    def to_line(src, block, h, way):
        return remote(
            src, piece(out, (block, b), h, parts), line_send.at[block, 0 if way > 0 else 1, h],
            line_recv.at[block, h], place.line(a + way),
        )

    def to_side(src, block, h, k):
        return remote(
            src, piece(out, (block, b), h, parts), side.at[k, block, h, 0],
            side.at[k, block, h, 1], place.side((b + k) % B),
        )

    for h in range(parts):
        @pl.when(a < A - 1)
        def _():
            to_line(half(h), a, h, 1).start()

        @pl.when(a > 0)
        def _():
            to_line(half(h), a, h, -1).start()

        for k in range(1, B):
            to_side(half(h), a, h, k).start()
    for step in range(1, A):
        for h in range(parts):
            yield
            for way in (1, -1):
                block = a - way * step

                @pl.when((block >= 0) & (block < A))
                def _():
                    src = piece(out, (block, b), h, parts)
                    to_line(src, block, h, way).wait_recv()

                    @pl.when((a + way >= 0) & (a + way < A))
                    def _():
                        to_line(src, block, h, way).start()

                    for k in range(1, B):
                        to_side(src, block, h, k).start()

    yield
    keep.wait()
    for block in range(A):
        for h in range(parts):
            src = piece(out, (block, b), h, parts)

            @pl.when((a < A - 1) & (block <= a))
            def _():
                to_line(src, block, h, 1).wait_send()

            @pl.when((a > 0) & (block >= a))
            def _():
                to_line(src, block, h, -1).wait_send()

            for k in range(1, B):
                to_side(src, block, h, k).wait()


def columns_sems(B):
    return [DMA((A, 2)), DMA((B, A, 2)), DMA((1,))]


def columns_flow(place, own, out, sems):
    line, side, local = sems
    a, b, B = place.a, place.b, place.B
    keep = pltpu.make_async_copy(own.at[a], out.at[a, b], local.at[0])
    keep.start()

    def to_line(k):
        to = (a + k) % A
        return remote(own.at[to], out.at[a, b], line.at[k, 0], line.at[k, 1], place.line(to))

    def to_side(src, block, k):
        return remote(
            src, out.at[block, b], side.at[k, block, 0], side.at[k, block, 1],
            place.side((b + k) % B),
        )

    for k in range(1, A):
        to_line(k).start()
    for k in range(1, B):
        to_side(own.at[a], a, k).start()
    for k in (1, 3, 2):
        yield
        to_line(k).wait_recv()
        block = (a + A - k) % A
        for j in range(1, B):
            to_side(out.at[block, b], block, j).start()
    yield
    keep.wait()
    for k in range(1, A):
        to_line(k).wait_send()
    for block in range(A):
        for k in range(1, B):
            to_side(out.at[block, b], block, k).wait()


def sides_sems(B):
    return [DMA((B, 2)), DMA((1,))]


def sides_flow(place, own, out, sems):
    side, local = sems
    b, B = place.b, place.B
    keep = pltpu.make_async_copy(own, out.at[b], local.at[0])
    keep.start()
    copies = [
        remote(own, out.at[b], side.at[k, 0], side.at[k, 1], place.side((b + k) % B))
        for k in range(1, B)
    ]
    for copy in copies:
        copy.start()
    yield
    keep.wait()
    for copy in copies:
        copy.wait()


ANY = pl.BlockSpec(memory_space=pl.ANY)
VMEM = pl.BlockSpec(memory_space=pltpu.VMEM)


def call(kernel, name, collective_id, outs, out_specs, scratch, args, in_specs):
    return pl.pallas_call(
        kernel,
        out_shape=outs,
        in_specs=in_specs,
        out_specs=out_specs,
        scratch_shapes=scratch,
        name=name,
        compiler_params=pltpu.CompilerParams(
            collective_id=collective_id, has_side_effects=True, vmem_limit_bytes=63 * 2**20
        ),
    )(*args)


def shape(*dims, dtype=bf):
    return jax.ShapeDtypeStruct(dims, dtype)


def split_refs(refs, *sizes):
    found, at = [], 0
    for size in sizes:
        found.append(refs[at : at + size])
        at += size
    return found


def select(rows, cols, shift, at, width):
    j = lax.broadcasted_iota(jnp.int32, (1, cols), 1) - at
    wanted = jnp.where((j >= 0) & (j < width), j + shift, -1)
    row = lax.broadcasted_iota(jnp.int32, (rows, cols), 0)
    return jnp.where(row == wanted, 1.0, 0.0).astype(bf)


def select_mixed(rows, cols, shift, j, part):
    col = lax.broadcasted_iota(jnp.int32, (1, cols), 1)
    wanted = jnp.where(
        col // part % 2 == j, shift + col // (2 * part) * part + col % part, -1
    )
    row = lax.broadcasted_iota(jnp.int32, (rows, cols), 0)
    return jnp.where(row == wanted, 1.0, 0.0).astype(bf)


def rope(ref, at, cosine, sine, out, to, head_dim):
    half = head_dim // 2
    former, latter = ref[pl.ds(at, half), :], ref[pl.ds(at + half, half), :]
    out[pl.ds(to, half), :] = (former * cosine - latter * sine).astype(out.dtype)
    out[pl.ds(to + half, half), :] = (latter * cosine + former * sine).astype(out.dtype)


def attention_forward(B, weights, gates, w_down, gains, tokens, cotangent, ids):
    wrows, width = weights[0].shape
    rows = tokens.shape[0]
    group = 4 * rows
    ff = gates[0].shape[1]
    wcols = width // 4
    head_dim = width // H
    heads = H // 4
    sub = ff // (A * B * 4)
    pad = -(-sub // 16) * 16
    fcols = B * pad
    wide = 384
    span = -(-wcols // 128) * 128
    pair = 2 * wcols
    parts = halves(wrows)
    trio = 3
    score_scale = 1.0 / math.sqrt(head_dim)

    def kernel(*refs):
        w_in, g_in, ins, outs, scratch, refs = split_refs(refs, 4, 2, 8, 12, 18, 100)
        wd_in, gain_in, tok_in, cot_in, seq_row, seq_col, blk_row, blk_col = ins
        (w4_out, gain_out, tok_out, d_out, gu_out, dn_out, qkv_out, mixed_out, after_out,
         n2_out, table_out, normed_t) = outs
        (w_all, g_all, wd_all, own4, gu_own, dn_own, own_gain, gain_all, tok_all, d_own, w4_all,
         normed, raw, bias, mixed, proj, proj_all, load) = scratch
        s1, s2, s3, s4, s5, s6, s7 = split_refs(refs, 4, 4, 3, 6, 3, 2, 100)
        qkv, mix_x, mix_core, ex_sem, save = s7
        place = Place(B)
        r, x, c = place.r, place.x, place.c
        loads = [pltpu.make_async_copy(w, w_all.at[i], load.at[i]) for i, w in enumerate(w_in)]
        loads += [
            pltpu.make_async_copy(w, g_all.at[i], load.at[4 + i]) for i, w in enumerate(g_in)
        ]
        loads.append(pltpu.make_async_copy(wd_in, wd_all, load.at[6]))
        for copy in loads:
            copy.start()
        start = pl.multiple_of(r * wcols // 128 * 128, 128)
        shift = r * wcols - start
        for i in range(2):
            total = jnp.zeros((wrows, pair), f32)
            for j in range(2):
                loads[2 * i + j].wait()
                pick = select(span, pair, shift, j * wcols, wcols)
                if i:
                    pick = select_mixed(span, pair, shift, j, trio * head_dim)
                total += product(w_all[2 * i + j, :, pl.ds(start, span)], pick)
            own4[:, i * pair : (i + 1) * pair] = total.astype(bf)
        for k in range(width // wide):
            own_gain[:, k * wide : (k + 1) * wide] = jnp.dot(
                gain_in[...], select(wrows, wide, 0, place.s * wrows - k * wide, wrows),
                preferred_element_type=f32,
            )
        greet(place, True, True, True)

        def prepare():
            for i in range(2):
                loads[4 + i].wait()
            loads[6].wait()

            def one(n, carry):
                i, block = n // A, n % A
                total = jnp.zeros((wrows, fcols), f32)
                for j in range(B):
                    first = ((block * B + j) * 4 + r) * sub
                    at = pl.multiple_of(jnp.minimum(first // 128 * 128, ff - wide), 128)
                    total += jnp.dot(
                        g_all[i, :, pl.ds(at, wide)],
                        select(wide, fcols, first - at, j * pad, sub),
                        preferred_element_type=f32,
                    )
                at = pl.multiple_of(i * fcols, 128)
                gu_own[block, :, pl.ds(at, fcols)] = total.astype(bf)
                return carry

            lax.fori_loop(0, 2 * A, one, 0)
            row = lax.broadcasted_iota(jnp.int32, (pad, ff // (A * B)), 0)
            col = lax.broadcasted_iota(jnp.int32, (pad, ff // (A * B)), 1)
            pick = jnp.where((col - r * sub == row) & (row < sub), 1.0, 0.0).astype(bf)
            tile = 768

            def down(n, carry):
                at = pl.ds(pl.multiple_of(n * tile, tile), tile)
                dn_own[:, at] = jnp.dot(
                    pick, wd_all[:, at], preferred_element_type=f32
                ).astype(bf)
                return carry

            lax.fori_loop(0, width // tile, down, 0)
            d_own[...] = (branch_scale * cot_in[...].astype(f32)).astype(bf)
            less = jnp.where(seq_col[...] < seq_row[...], 1.0, 0.0)
            earlier = jnp.sum(less, axis=0, keepdims=True)
            at = lax.broadcasted_iota(jnp.int32, (1, group), 1).astype(f32) - earlier
            half = head_dim // 2
            index = lax.broadcasted_iota(jnp.int32, (half, group), 0).astype(f32)
            angle = at * jnp.exp(index * (-2.0 * math.log(rope_base) / head_dim))
            table_out[0] = jnp.cos(angle)
            table_out[1] = jnp.sin(angle)
            allowed = (seq_col[...] == seq_row[...]) & (blk_col[...] <= blk_row[...])
            bias[...] = jnp.where(allowed, 0.0, masked_score)
            yield
            total = jnp.zeros((8, width), f32)
            for block in range(A):
                for side in range(B):
                    total += gain_all[block, side]
            gain_out[...] = total
            for i in range(4):
                value = tok_all[i].astype(f32)
                factor = lax.rsqrt(jnp.mean(value * value, axis=1, keepdims=True) + norm_eps)
                value = value * factor * total[0:1]
                at = slice(i * rows, (i + 1) * rows)
                normed[at, :] = value.astype(bf)
                normed_t[:, at] = value.T.astype(bf)

        def share_piece(k):
            at = pl.ds(k * trio * head_dim, trio * head_dim)
            own = mixed.at[r, at]
            far = mixed.at[place.rx, at]
            return (
                remote(own, own, mix_x.at[k, 0], mix_x.at[k, 1], place.over_x),
                remote(own, own, mix_core.at[x, k, 0], mix_core.at[x, k, 1], place.over_core),
                remote(
                    far, far, mix_core.at[1 - x, k, 0], mix_core.at[1 - x, k, 1],
                    place.over_core,
                ),
            )

        pieces = heads // trio

        def attend():
            step = 256

            def project(n, carry):
                cols = pl.ds(pl.multiple_of(span - 128 + n * step, 128), step)
                w = w4_all[:, :, :, cols].reshape(width, step)
                at = pl.ds(pl.multiple_of(n * step, step), step)
                raw[at, :] = product(normed[...], w).T
                return carry

            lax.fori_loop(0, (width - span + 128) // step, project, 0)
            skip = wcols - (span - 128)
            cosine, sine = table_out[0], table_out[1]

            def turn(n, carry):
                at = pl.multiple_of(wcols + n * head_dim, 32)
                i, h = n // heads, n % heads
                first = skip + wcols + (h // trio * 2 + i) * trio * head_dim + h % trio * head_dim
                rope(raw, pl.multiple_of(first, 32), cosine, sine, qkv, at, head_dim)
                return carry

            lax.fori_loop(0, 2 * heads, turn, 0)
            qkv[:wcols, :] = raw[pl.ds(skip, wcols), :].astype(bf)
            pltpu.make_async_copy(qkv, qkv_out, save.at[0]).start()
            yield

            def head(n, carry):
                at = lambda part: pl.ds(pl.multiple_of(part * wcols + n * head_dim, 64), head_dim)
                scores = across(qkv[at(2), :], qkv[at(1), :]) * score_scale + bias[...]
                top = jnp.max(scores, axis=0, keepdims=True)
                powers = jnp.exp(scores - top)
                probs = powers * (1.0 / jnp.sum(powers, axis=0, keepdims=True))
                mixed[r, at(0), :] = product(qkv[at(0), :], probs.astype(bf)).astype(bf)
                return carry

            for k in range(pieces):
                lax.fori_loop(k * trio, (k + 1) * trio, head, 0)
                to_x, near, far = share_piece(k)
                to_x.start()
                near.start()
                if k:
                    to_x, near, far = share_piece(k - 1)
                    to_x.wait_recv()
                    far.start()
                yield
            to_x, near, far = share_piece(pieces - 1)
            to_x.wait_recv()
            far.start()
            for k in range(pieces):
                to_x, near, far = share_piece(k)
                near.wait_recv()
                far.wait_recv()
            everyone = mixed[...].reshape(width, group)
            value = across(everyone, w4_all[:, :, :, :span].reshape(width, span))
            proj[...] = value.astype(bf).reshape(4, rows, span)
            proj_all[r] = proj[r]
            copies = []
            for k in (2, 3, 1):
                to = (r + k) % 4
                copies.append(
                    remote(
                        proj.at[to], proj_all.at[r], ex_sem.at[k, 0], ex_sem.at[k, 1],
                        (place.s, to),
                    )
                )
                copies[-1].start()
            saved = pltpu.make_async_copy(mixed, mixed_out, save.at[1])
            saved.start()
            yield
            for copy in copies:
                copy.wait()
            own = tok_all[r].astype(f32)
            halves_ = []
            for side in range(2):
                total = jnp.zeros((rows, pair), f32)
                for core in range(2):
                    total += jnp.dot(
                        proj_all[side * 2 + core],
                        select(span, pair, 0, core * wcols, wcols), preferred_element_type=f32,
                    )
                at = slice(side * pair, (side + 1) * pair)
                halves_.append(own[:, at] + branch_scale * total)
                after_out[:, at] = halves_[-1]
            mean = sum(jnp.sum(v * v, axis=1, keepdims=True) for v in halves_) / width
            factor = lax.rsqrt(mean + norm_eps)
            for side in range(2):
                at = slice(side * pair, (side + 1) * pair)
                n2_out[:, at] = (halves_[side] * factor * gain_out[1:2, at]).astype(bf)
            yield
            saved.wait()
            pltpu.make_async_copy(qkv, qkv_out, save.at[0]).wait()
            for k in range(pieces):
                to_x, near, far = share_piece(k)
                to_x.wait_send()
                near.wait_send()
                far.wait_send()

        def weights_flow():
            yield from spread_flow(place, own4, w4_all, s1, parts)
            pltpu.make_async_copy(w4_all, w4_out, save.at[2]).start()

        run_flows(
            [
                weights_flow(),
                share_flow(place, tok_in, tok_all, s3),
                spread_flow(place, own_gain, gain_all, s2),
                prepare(),
                widen_flow(place, d_own, d_out, s4),
                columns_flow(place, gu_own, gu_out, s5),
                sides_flow(place, dn_own, dn_out, s6),
                attend(),
            ],
            (0, 1, 2, 3, 1, 1, 1, 2, 2, 2, 2, 2, 3, 3) + (0,) * (3 * parts)
            + (4, 4, 4, 0, 6, 5, 7, 4, 7, 7, 7, 5, 4, 7, 4, 5, 7, 5, 4, 4, 7, 6, 5, 4),
        )
        saved = pltpu.make_async_copy(tok_all, tok_out, save.at[1])
        saved.start()
        saved.wait()
        pltpu.make_async_copy(w4_all, w4_out, save.at[2]).wait()

    block = (rows, width)
    return call(
        kernel, "attention_forward", 1,
        [
            shape(A, B, wrows, 4 * wcols), shape(8, width, dtype=f32), shape(4, *block),
            shape(X, A, X, *block), shape(A, B, wrows, 2 * fcols), shape(B, pad, width),
            shape(3 * wcols, group), shape(4, wcols, group), shape(*block, dtype=f32),
            shape(*block), shape(2, head_dim // 2, group, dtype=f32), shape(width, group),
        ],
        [ANY, VMEM, ANY, ANY, ANY, ANY, ANY, ANY, VMEM, VMEM, VMEM, VMEM],
        [
            pltpu.VMEM((4, wrows, width), bf), pltpu.VMEM((2, wrows, ff), bf),
            pltpu.VMEM(w_down.shape, bf), pltpu.VMEM((wrows, 4 * wcols), bf),
            pltpu.VMEM((A, wrows, 2 * fcols), bf), pltpu.VMEM((pad, width), bf),
            pltpu.VMEM((8, width), f32), pltpu.VMEM((A, B, 8, width), f32),
            pltpu.VMEM((4,) + block, bf), pltpu.VMEM(block, bf),
            pltpu.VMEM((A, B, wrows, 4 * wcols), bf), pltpu.VMEM((group, width), bf),
            pltpu.VMEM((width - span + 128, group), f32), pltpu.VMEM((group, group), f32),
            pltpu.VMEM((4, wcols, group), bf), pltpu.VMEM((4, rows, span), bf),
            pltpu.VMEM((4, rows, span), bf), DMA((7,)),
        ]
        + spread_sems(B, parts) + spread_sems(B) + share_sems() + widen_sems() + columns_sems(B)
        + sides_sems(B)
        + [
            pltpu.VMEM((3 * wcols, group), bf), DMA((3, 2)), DMA((X, 3, 2)), DMA((4, 2)),
            DMA((3,)),
        ],
        [*weights, *gates, w_down, gains, tokens, cotangent, *ids],
        [ANY] * 7 + [VMEM, ANY] + [VMEM] * 5,
    )


def feed_forward(B, normed_two, d_down, gate_up, down, lefts):
    rows, width = normed_two.shape
    fcols = down.shape[0]
    every = X * A * X * rows
    pair = X * rows
    parts = halves(rows)
    wide = 768
    tile = 384

    wrows = gate_up.shape[0] // (A * B)
    pad = fcols // B
    many = 1152

    def kernel(n_in, d_in, gu_in, dn_in, *refs):
        lefts_in, (out, f_out, ggu_out, gd_out), lefts_out, refs = split_refs(refs, 2, 4, 2, 100)
        bufs, (line_recv, line_send, over_x, over_core), sems = split_refs(refs, 11, 4, 100)
        n_all, d_all, gu, dn, part, hid, d_gu, from_core, from_x, landed, g_all = bufs
        (g_down, load, core_sem, x_sem, line_sem, gu_side, gd_side, gu_sem, gd_sem, f_core, f_x,
         free, core_free, f_line, left_sem) = sems
        place = Place(B)
        a, x, c = place.a, place.x, place.c
        loads = [
            pltpu.make_async_copy(n_in, n_all.at[x, a, c], load.at[0]),
            pltpu.make_async_copy(gu_in, gu, load.at[1]),
            pltpu.make_async_copy(dn_in, dn, load.at[2]),
            pltpu.make_async_copy(d_in, d_all, load.at[3]),
        ]
        for copy in loads:
            copy.start()
        greet(place, True, True, True)

        def to_line(block, way):
            src = n_all.at[x, block, c]
            return remote(
                src, src, line_send.at[block, (1 - way) // 2], line_recv.at[block],
                place.line(a + way),
            )

        def to_x(block):
            src = n_all.at[x, block, c]
            return remote(src, src, over_x.at[block, 0], over_x.at[block, 1], place.over_x)

        def to_core(side, block):
            src = n_all.at[side, block, c]
            return remote(
                src, src, over_core.at[side, block, 0], over_core.at[side, block, 1],
                place.over_core,
            )

        def sum_core(side, d, h):
            return remote(
                piece(part, (side, d, 1 - c), h, parts), piece(from_core, (side, d), h, parts),
                core_sem.at[side, d, h, 0], core_sem.at[side, d, h, 1], place.over_core,
            )

        def sum_x(d, h):
            return remote(
                piece(part, (1 - x, d, c), h, parts), piece(from_x, d, h, parts),
                x_sem.at[d, h, 0], x_sem.at[d, h, 1], place.over_x,
            )

        def merge(side, d, h):
            sum_core(side, d, h).wait_recv()
            here = piece(part, (side, d, c), h, parts)
            add_into(here, here, piece(from_core, (side, d), h, parts))

        def send_sum(d):
            for h in range(parts):
                merge(1 - x, d, h)
                sum_x(d, h).start()

        loads[0].wait()

        @pl.when(a < A - 1)
        def _():
            to_line(a, 1).start()

        @pl.when(a > 0)
        def _():
            to_line(a, -1).start()

        to_x(a).start()
        to_core(x, a).start()

        def left_aside(i, d, k):
            to = (place.b + k) % B
            return remote(
                lefts_in[i].at[d, to], lefts_out[i].at[k - 1, d], left_sem.at[i, k, d, 0],
                left_sem.at[i, k, d, 1], place.side(to),
            )

        left_copies = [(i, d, k) for i in range(2) for d in range(A) for k in range(1, B)]
        for at in left_copies:
            left_aside(*at).start()
        for copy in loads[1:]:
            copy.wait()

        def nearest(i):
            left = jnp.where(a == 1, jnp.where(i == 1, 0, i), jnp.where(i == 0, 0, i))
            left = jnp.where((a == 1) & (i == 0), 1, left)
            right = jnp.where(a == 2, jnp.where(i == 0, 2, jnp.where(i == 1, 1, 3)), A - 1 - i)
            right = jnp.where((a == 2) & (i == A - 1), 0, right)
            return jnp.where(a < 2, left, right)

        def item(j):
            near = (j == 0) | ((j % 2 == 1) & (j < 2 * A - 1))
            i = jnp.where(near, (j + 1) // 2, jnp.where(j == 2 * A - 1, A - 1, j // 2 - 1))
            return near, nearest(i)

        def compute(side, block):
            n = n_all[side, block].reshape(pair, width)
            d = d_all[side, block].reshape(pair, width)
            both = product(n, gu[...])
            gate, up = both[:, :fcols], both[:, fcols:]
            d_hidden = against(d, dn[...])
            sig = jax.nn.sigmoid(gate)
            at = pl.ds(pl.multiple_of((side * A + block) * pair, pair), pair)
            hid[at, :] = (gate * sig * up).astype(bf)
            d_gate = (d_hidden * up * sig * (1.0 + gate * (1.0 - sig))).astype(bf)
            d_up = (d_hidden * gate * sig).astype(bf)
            both = jnp.concatenate([d_gate, d_up], axis=1)
            d_gu[at, :] = both
            for k in range(width // wide):
                cols = pl.ds(k * wide, wide)
                value = against(both, gu[cols, :]).astype(bf)
                part[side, block, :, :, cols] = value.reshape(X, rows, wide)

        def arrive(j, carry):
            near, block = item(j)
            side = jnp.where(near, x, 1 - x)

            @pl.when(near & (j > 0))
            def _():
                way = jnp.where(block < a, 1, -1)
                to_line(block, way).wait_recv()

                @pl.when((a + way >= 0) & (a + way < A))
                def _():
                    to_line(block, way).start()

                to_x(block).start()
                to_core(x, block).start()

            @pl.when(jnp.logical_not(near))
            def _():
                to_x(block).wait_recv()
                to_core(1 - x, block).start()

            to_core(side, block).wait_recv()
            compute(side, block)
            for h in range(parts):
                sum_core(side, block, h).start()

            before, last = item(jnp.maximum(j - 1, 0))

            @pl.when((j > 3) & jnp.logical_not(before))
            def _():
                send_sum(last)

            return carry

        lax.fori_loop(0, 2 * A, arrive, 0)
        send_sum(nearest(A - 1))
        send_sum(a)
        for d in range(A):
            for h in range(parts):
                merge(x, d, h)
        pl.semaphore_signal(
            core_free, inc=1, device_id=place.over_core, device_id_type=MESH
        )

        def ready(d, h):
            sum_x(d, h).wait_recv()
            here = piece(part, (x, d, c), h, parts)
            add_into(here, here, piece(from_x, d, h, parts))

        piece_rows = rows // parts

        def final(h):
            at = pl.ds(h * piece_rows, piece_rows)
            out[at, :] = part[x, a, c, at, :]

        chain = line_slots(
            place, lambda d: part.at[x, d, c], lambda d, way: landed.at[d + (way > 0)], line_sem,
            parts, ready, final, near=True,
        )

        def grad_down(k, carry):
            at = pl.ds(pl.multiple_of(k * tile, tile), tile)
            d = d_all[:, :, :, :, at].reshape(every, tile)
            g_down[:, at] = across(hid[...], d).astype(bf)
            return carry

        def grad_gate_up(k, carry):
            at = pl.ds(pl.multiple_of(k * many, many), many)
            n = n_all[:, :, :, :, at].reshape(every, many)
            count = many // wrows
            for i in range(2):
                cols = pl.ds(i * fcols, fcols)
                value = across(n, d_gu[:, cols]).astype(bf)
                g_all[pl.ds(k * count, count), :, cols] = value.reshape(count, wrows, fcols)
            return carry

        def aside(d, k):
            to = (place.b + k) % B
            return remote(
                g_all.at[d * B + to], gu_side.at[k - 1, d], gu_sem.at[k, d, 0],
                gu_sem.at[k, d, 1], place.side(to),
            )

        def aside_down(k):
            to = (place.b + k) % B
            at = pl.ds(pl.multiple_of(to * pad, 16), pad)
            return remote(
                g_down.at[at], gd_side.at[k - 1], gd_sem.at[k, 0], gd_sem.at[k, 1], place.side(to)
            )

        def forward(k, carry):
            side, block = k // A, k % A
            at = pl.ds(pl.multiple_of(k * pair, pair), pair)
            for i in range(width // wide):
                cols = pl.ds(i * wide, wide)
                value = product(hid[at, :], dn[:, cols]).astype(bf)
                d_all[side, block, :, :, cols] = value.reshape(X, rows, wide)
            return carry

        mine = pl.ds(pl.multiple_of(place.b * pad, 16), pad)
        outs = [pltpu.make_async_copy(g_down.at[mine], gd_out, load.at[0])] + [
            pltpu.make_async_copy(g_all.at[d * B + place.b], ggu_out.at[d], load.at[1 + d])
            for d in range(A)
        ]

        def out_core(side, d):
            return remote(
                d_all.at[side, d, 1 - c], from_core.at[side, d], f_core.at[side, d, 0],
                f_core.at[side, d, 1], place.over_core,
            )

        def out_x(d):
            return remote(
                d_all.at[1 - x, d, c], n_all.at[0, d, 1], f_x.at[d, 0], f_x.at[d, 1],
                place.over_x,
            )

        def out_merge(side, d):
            out_core(side, d).wait_recv()
            here = d_all.at[side, d, c]
            add_into(here, here, from_core.at[side, d])

        def out_ready(d, h):
            out_merge(x, d)
            out_x(d).wait_recv()
            here = d_all.at[x, d, c]
            add_into(here, here, n_all.at[0, d, 1])

        def out_final(h):
            pltpu.make_async_copy(d_all.at[x, a, c], f_out, load.at[1 + A]).start()

        def out_landing(d, way):
            return part.at[0, d, 1 - c] if way > 0 else n_all.at[1, d, 1]

        out_chain = line_slots(
            place, lambda d: d_all.at[x, d, c], out_landing, f_line, 1, out_ready, out_final
        )

        lax.fori_loop(0, width // tile, grad_down, 0)
        for k in range(1, B):
            aside_down(k).start()
        next(chain)
        lax.fori_loop(0, X * A, forward, 0)
        pl.semaphore_wait(core_free, 1)
        for side in (1 - x, x):
            for i in range(A):
                out_core(side, far_first(a, i)).start()
        next(chain)
        for k in range(width // many):
            grad_gate_up(k, 0)
            for d in range(k * many // (wrows * B), (k + 1) * many // (wrows * B)):
                for j in range(1, B):
                    aside(d, j).start()
            next(chain)
        for d in range(A):
            to_x(d).wait_send()
            for side in range(X):
                to_core(side, d).wait_send()
                for h in range(parts):
                    sum_core(side, d, h).wait_send()

            @pl.when((a < A - 1) & (d <= a))
            def _():
                to_line(d, 1).wait_send()

            @pl.when((a > 0) & (d >= a))
            def _():
                to_line(d, -1).wait_send()

        for device in [place.over_x] + [place.line((a + k) % A) for k in range(1, A)]:
            pl.semaphore_signal(free, inc=1, device_id=device, device_id_type=MESH)
        for i in range(A):
            out_merge(1 - x, far_first(a, i))
        pl.semaphore_wait(free, A)
        for i in range(A):
            out_x(far_first(a, i)).start()
        next(chain)
        for k in range(1, B):
            aside_down(k).wait_recv()
            add_into(g_down.at[mine], g_down.at[mine], gd_side.at[k - 1])
        outs[0].start()
        for _ in chain:
            pass
        next(out_chain)
        for d in range(A):
            for k in range(1, B):
                aside(d, k).wait_recv()
                here = g_all.at[d * B + place.b]
                add_into(here, here, gu_side.at[k - 1, d])
            outs[1 + d].start()
        for _ in out_chain:
            pass
        pltpu.make_async_copy(d_all.at[x, a, c], f_out, load.at[1 + A]).wait()
        for at in left_copies:
            left_aside(*at).wait()
        for copy in outs:
            copy.wait()
        for k in range(1, B):
            aside_down(k).wait_send()
            for d in range(A):
                aside(d, k).wait_send()
        for d in range(A):
            out_x(d).wait_send()
            for side in range(X):
                out_core(side, d).wait_send()
            for h in range(parts):
                sum_x(d, h).wait_send()

    block = (rows, width)
    return call(
        kernel, "feed_forward", 2,
        [
            shape(*block), shape(*block), shape(A, wrows, 2 * fcols),
            shape(pad, width),
        ]
        + [shape(B - 1, A, *v.shape[2:]) for v in lefts],
        [VMEM] + [ANY] * 5,
        [
            pltpu.VMEM((X, A, X) + block, bf), pltpu.VMEM((X, A, X) + block, bf),
            pltpu.VMEM(gate_up.shape, bf), pltpu.VMEM(down.shape, bf),
            pltpu.VMEM((X, A, X) + block, bf), pltpu.VMEM((every, fcols), bf),
            pltpu.VMEM((every, 2 * fcols), bf), pltpu.VMEM((X, A) + block, bf),
            pltpu.VMEM((A,) + block, bf), pltpu.VMEM((A + 1,) + block, bf),
            pltpu.VMEM((A * B, wrows, 2 * fcols), bf),
            DMA((A,)), DMA((A, 2)), DMA((A, 2)), DMA((X, A, 2)),
            pltpu.VMEM((fcols, width), bf), DMA((2 + A,)), DMA((X, A, parts, 2)),
            DMA((A, parts, 2)), DMA((2, A, parts, 2)),
            pltpu.VMEM((B - 1, A, wrows, 2 * fcols), bf), pltpu.VMEM((B - 1, pad, width), bf),
            DMA((B, A, 2)), DMA((B, 2)), DMA((X, A, 2)), DMA((A, 2)), pltpu.SemaphoreType.REGULAR,
            pltpu.SemaphoreType.REGULAR,
            DMA((2, A, 1, 2)), DMA((2, B, A, 2)),
        ],
        [normed_two, d_down, gate_up, down, *lefts],
        [ANY] * 6,
    )


def fold_scratch(rows, width):
    block = (rows, width)
    return [
        pltpu.VMEM((X * X,) + block, bf), pltpu.VMEM((X,) + block, bf), pltpu.VMEM(block, bf),
        DMA((X, 2)), DMA((2,)),
    ]


def fold_flow(place, scratch):
    part, from_core, from_x, core_sem, x_sem = scratch
    x, c = place.x, place.c

    def to_core(i):
        return remote(
            part.at[i * X + 1 - c], from_core.at[i], core_sem.at[i, 0], core_sem.at[i, 1],
            place.over_core,
        )

    def merge(i):
        to_core(i).wait_recv()
        here = part.at[i * X + c]
        add_into(here, here, from_core.at[i])

    to_x = remote(part.at[place.rx], from_x, x_sem.at[0], x_sem.at[1], place.over_x)
    to_core(1 - x).start()
    to_core(x).start()
    yield
    merge(1 - x)
    to_x.start()
    merge(x)
    yield
    to_x.wait_recv()
    here = part.at[place.r]
    add_into(here, here, from_x)
    yield
    to_x.wait_send()
    for i in range(X):
        to_core(i).wait_send()


def owners_flow(place, own, out, sems):
    line, local = sems
    a = place.a
    keep = pltpu.make_async_copy(own.at[a], out.at[a], local.at[0])
    keep.start()
    copies = []
    for k in (1, 3, 2):
        to = (a + k) % A
        copies.append(
            remote(own.at[to], out.at[a], line.at[k, 0], line.at[k, 1], place.line(to))
        )
        copies[-1].start()
    yield
    keep.wait()
    for copy in copies:
        copy.wait()


def grad_scratch(rows, width):
    block = (rows, width)
    P_ = halves(rows)
    return [
        pltpu.VMEM((A,) + block, bf), pltpu.VMEM((A + 1,) + block, bf), DMA((2, A, P_, 2)),
        DMA((P_, 2)), DMA((X, P_, 2)), DMA((P_,)),
    ]


def grad_flow(place, produce, out, scratch):
    sums, landed, line_sem, x_sem, core_sem, local = scratch
    r, x = place.r, place.x
    parts = halves(out.shape[1])
    for i in range(A):
        d = far_first(place.a, i)
        sums[d] = produce(d)
    yield

    def keep(src, h):
        return pltpu.make_async_copy(src, piece(out, r, h, parts), local.at[h])

    def to_x(src, h):
        return remote(src, piece(out, r, h, parts), x_sem.at[h, 0], x_sem.at[h, 1], place.over_x)

    def near(src, h):
        return remote(
            src, piece(out, r, h, parts), core_sem.at[x, h, 0], core_sem.at[x, h, 1],
            place.over_core,
        )

    def far(h):
        src = piece(out, place.rx, h, parts)
        return remote(
            src, src, core_sem.at[1 - x, h, 0], core_sem.at[1 - x, h, 1], place.over_core
        )

    def final(h):
        src = piece(sums, place.a, h, parts)
        to_x(src, h).start()
        near(src, h).start()
        keep(src, h).start()

    yield from line_slots(
        place, lambda d: sums.at[d], lambda d, way: landed.at[d + (way > 0)], line_sem, parts,
        lambda d, h: None, final,
    )
    for h in range(parts):
        src = piece(out, r, h, parts)
        keep(src, h).wait()
        near(src, h).wait()
    yield
    for h in range(parts):
        src = piece(out, r, h, parts)
        to_x(src, h).wait_recv()
        far(h).start()
    yield
    for h in range(parts):
        to_x(piece(out, r, h, parts), h).wait_send()
        far(h).wait()


def attention_backward(
    B, S, d_n2, after_attn, cotangent, gains, w4, qkv, tokens, lefts, tables, ids, g_gate_up,
    g_down,
):
    rows, width = d_n2.shape
    group = 4 * rows
    wrows, wcols = width // S, width // 4
    head_dim = width // H
    heads = H // 4
    wide = 384
    span = -(-wcols // 128) * 128
    skip = wcols - (span - 128)
    tail = width - span + 128
    trio = 3
    third = 2 * trio * head_dim
    thirds = heads // trio
    score_scale = 1.0 / math.sqrt(head_dim)
    widths = (span, span) + (third,) * thirds
    count = len(widths)
    wrows_wide = -(-wrows // 128) * 128

    def kernel(*refs):
        ins, lefts_in, ids_in, outs, mids, own, refs = split_refs(
            refs, 10, 4, 4, 2, count + 3, 20, 100
        )
        (dn2_in, after_in, cot_in, gain_in, w4_in, qkv_in, tok_in, table_in, gu_in, gd_in) = ins
        seq_row, seq_col, blk_row, blk_col = ids_in
        gt_out, gain_out = outs
        shared, (gu_cols, gu_all, gd_all) = mids[:count], mids[count:]
        (w4, qkv_, mix, mix_far, n_t, n_far, tok, bias, factors, d_t, d_nat, d_far, ex_send,
         ex_all, ex_far, d_after, own_gain, gain_all, load, side_sem) = own
        f1, f2, u1, u2, u3, (ex_sem, gain_sem), *grads = split_refs(
            refs, 5, 5, 2, 3, 3, 2, *(6,) * count
        )
        place = Place(B)
        r, x, c = place.r, place.x, place.c
        loads = [
            pltpu.make_async_copy(src, dst, load.at[i])
            for i, (src, dst) in enumerate(
                [
                    (tok_in, tok), (w4_in, w4), (lefts_in[0].at[:, place.b], mix),
                    (lefts_in[1], mix_far), (qkv_in, qkv_), (lefts_in[2].at[:, place.b], n_t),
                    (lefts_in[3], n_far),
                ]
            )
        ]
        for copy in loads:
            copy.start()
        part1, part2 = f1[0], f2[0]
        gain_one, gain_two = gain_in[0:1], gain_in[1:2]
        own_gain[...] = jnp.zeros_like(own_gain)
        step = 32

        def back_two(i, carry):
            at = pl.ds(pl.multiple_of(i * step, step), step)
            after = after_in[at, :]
            d = dn2_in[at, :].astype(f32)
            factor = lax.rsqrt(jnp.mean(after * after, axis=1, keepdims=True) + norm_eps)
            own_gain[1:2, :] += jnp.sum(d * after * factor, axis=0, keepdims=True)
            u = d * gain_two
            mean = jnp.mean(u * after, axis=1, keepdims=True)
            d_after[at, :] = (
                cot_in[at, :].astype(f32) + factor * u - after * (factor * factor * factor) * mean
            )
            return carry

        lax.fori_loop(0, rows // step, back_two, 0)
        d_proj = (branch_scale * d_after[...]).astype(bf)
        for k in range(4):
            at = k * wcols // 128 * 128
            ex_send[k] = product(
                d_proj[:, at : at + span], select(span, span, k * wcols - at, 0, wcols)
            ).astype(bf)
        ex_all[r] = ex_send[r]
        greet(place, True, True, True)
        exchange = []
        for k in (2, 3, 1):
            to = (r + k) % 4
            exchange.append(
                remote(
                    ex_send.at[to], ex_all.at[r], ex_sem.at[k, 0], ex_sem.at[k, 1],
                    (place.s, to),
                )
            )
            exchange[-1].start()

        def at_head(part, n):
            return pl.ds(pl.multiple_of(part * wcols + n * head_dim, 64), head_dim)

        def probs_of(n):
            scores = across(qkv_[at_head(2, n), :], qkv_[at_head(1, n), :]) * score_scale
            scores = scores + bias[...].astype(f32)
            powers = jnp.exp(scores - jnp.max(scores, axis=0, keepdims=True))
            return powers * (1.0 / jnp.sum(powers, axis=0, keepdims=True))

        def aside(src, dst, i):
            return [
                remote(
                    src, dst(k - 1), side_sem.at[i, k, 0], side_sem.at[i, k, 1],
                    place.side((place.b + k) % B),
                )
                for k in range(1, B)
            ]

        def lanes(i):
            return pl.ds(0, span) if i == 1 else pl.ds(span + (i - 2) * third, third)

        def aside_of(i):
            if i == 0:
                return aside(ex_all, lambda k: ex_far.at[k], 0)
            return aside(d_nat.at[:, lanes(i)], lambda k: d_far.at[k, :, lanes(i)], i)

        def compute():
            allowed = (seq_col[...] == seq_row[...]) & (blk_col[...] <= blk_row[...])
            bias[...] = jnp.where(allowed, 0.0, masked_score).astype(bf)
            for i in range(4):
                loads[0].wait() if i == 0 else None
                value = tok[i].astype(f32)
                factors[i * rows : (i + 1) * rows, :] = lax.rsqrt(
                    jnp.mean(value * value, axis=1, keepdims=True) + norm_eps
                )
            for copy in exchange:
                copy.wait()
            for copy in aside_of(0):
                copy.start()
            for copy in loads[1:]:
                copy.wait()
            d_proj = ex_all[...].reshape(group, span)
            for i in (1 - c, c):
                for side in range(X):
                    k = side * X + i
                    at = pl.ds(pl.multiple_of(k * wcols, 64), wcols)
                    part1[k] = against(w4[at, :span], d_proj).astype(bf)
            yield

            def values_back(n, carry):
                d_m = part1[r, pl.ds(pl.multiple_of(n * head_dim, 64), head_dim), :]
                value = against(d_m, probs_of(n).astype(bf))
                at = pl.ds(pl.multiple_of(skip + n * head_dim, 64), head_dim)
                d_t[at, :] = value.astype(bf)
                return carry

            def flip(n, carry):
                at = pl.ds(pl.multiple_of(n * 128, 128), 128)
                d_nat[:, at] = d_t[at, :].astype(f32).T.astype(bf)
                return carry

            d_t[:skip, :] = jnp.zeros((skip, group), bf)
            lax.fori_loop(0, heads, values_back, 0)
            lax.fori_loop(0, span // 128, flip, 0)
            for copy in aside_of(1):
                copy.start()
            yield
            cosine, sine = table_in[0], table_in[1]
            half = head_dim // 2

            def turn_back(value, at):
                former, latter = value[:half], value[half:]
                d_t[pl.ds(at, half), :] = (former * cosine + latter * sine).astype(bf)
                d_t[pl.ds(at + half, half), :] = (latter * cosine - former * sine).astype(bf)

            def scores_back(n, carry):
                d_m = part1[r, pl.ds(pl.multiple_of(n * head_dim, 64), head_dim), :]
                probs = probs_of(n)
                d_probs = across(qkv_[at_head(0, n), :], d_m)
                d_s = probs * (d_probs - jnp.sum(d_probs * probs, axis=0, keepdims=True))
                d_s = d_s.astype(bf)
                at = span + n // trio * third + n % trio * head_dim
                turn_back(
                    product(qkv_[at_head(2, n), :], d_s) * score_scale, pl.multiple_of(at, 64)
                )
                turn_back(
                    against(qkv_[at_head(1, n), :], d_s) * score_scale,
                    pl.multiple_of(at + third // 2, 64),
                )
                return carry

            for k in range(thirds):
                lax.fori_loop(trio * k, trio * (k + 1), scores_back, 0)
                first = (span + third * k) // 128
                lax.fori_loop(first, first + third // 128, flip, 0)
                for copy in aside_of(2 + k):
                    copy.start()
                yield

            def inputs_back(n, carry):
                at = pl.ds(pl.multiple_of(n * wide, 128), wide)
                value = against(d_nat[...], w4[at, pl.ds(span - 128, tail)])
                x_f = tok[:, :, at].reshape(group, wide).astype(f32) * factors[...]
                own_gain[0:1, at] = jnp.sum(value * x_f, axis=0, keepdims=True)
                part2[:, :, at] = value.astype(bf).reshape(4, rows, wide)
                return carry

            lax.fori_loop(0, width // wide, inputs_back, 0)

        def make(i):
            def produce(d):
                if i == 0:
                    own, far, right = mix, mix_far, ex_all[...].reshape(group, span)
                else:
                    own, far, right = n_t, n_far, d_nat[:, lanes(i)]
                total = product(own[d], right)
                for k in range(B - 1):
                    if i == 0:
                        right = ex_far[k].reshape(group, span)
                    else:
                        right = d_far[k, :, lanes(i)]
                    total += product(far[k, d], right)
                return total.astype(bf)

            return produce

        def grad(i):
            for copy in aside_of(i):
                copy.wait_recv()
            yield from grad_flow(place, make(i), shared[i], grads[i])
            for copy in aside_of(i):
                copy.wait_send()

        def gains_flow():
            def send(i, device):
                return remote(
                    own_gain, gain_all.at[i], gain_sem.at[i, 0], gain_sem.at[i, 1], device
                )

            stages = [
                [place.over_core], [place.over_x],
                [place.side((place.b + k) % B) for k in range(1, B)],
                [place.line((place.a + k) % A) for k in range(1, A)],
            ]
            at = 0
            for stage in stages:
                copies = [send(at + i, device) for i, device in enumerate(stage)]
                for copy in copies:
                    copy.start()
                yield
                for copy in copies:
                    copy.wait()
                for i in range(len(stage)):
                    own_gain[...] += gain_all[at + i]
                at += len(stage)
            for n in range(width // wide):
                own = slice(n * wide, (n + 1) * wide)
                total = own_gain[:, own]
                pick = select(wide, wrows_wide, place.s * wrows - n * wide, 0, wrows)
                value = jnp.zeros((8, wrows_wide), f32)
                for _ in range(3):
                    low = total.astype(bf)
                    value += product(low, pick)
                    total = total - low.astype(f32)
                gain_out[...] = value if n == 0 else gain_out[...] + value

        def input_end():
            def back_one(i, carry):
                at = pl.ds(pl.multiple_of(i * step, step), step)
                value = tok[r, at, :].astype(f32)
                d = part2[r, at, :].astype(f32)
                factor = lax.rsqrt(jnp.mean(value * value, axis=1, keepdims=True) + norm_eps)
                u = d * gain_one
                mean = jnp.mean(u * value, axis=1, keepdims=True)
                gt_out[at, :] = (
                    d_after[at, :] + factor * u - value * (factor * factor * factor) * mean
                ).astype(bf)
                return carry

            lax.fori_loop(0, rows // step, back_one, 0)
            yield

        M, F1, F2, GU, SU, SD, G, T, O, V, P, Q, R = range(13)
        flows = [
            compute(),
            fold_flow(place, f1),
            fold_flow(place, f2),
            owners_flow(place, gu_in, gu_cols, u1),
            share_flow(place, gu_cols, gu_all, u2),
            share_flow(place, gd_in, gd_all, u3),
            gains_flow(),
            input_end(),
        ] + [grad(i) for i in range(count)]
        turns = [
            GU, M, F1, F1, F1, F1, O, M, O, GU, SU, SD, M, O, V, M, O, V, M, O, V, P, M, F2, G, V,
            P, Q, F2, G, V, P, Q, R, O, P, G, Q, R, F2, F2, T, G, P, Q, R, O, V, SD, G, Q, R, SD,
            SU, SU, V, R, O, P, V,
        ]
        run_flows(flows, turns)

    block = (rows, width)
    left = (wrows, group)
    return call(
        kernel, "attention_backward", 3,
        [shape(*block), shape(8, wrows_wide, dtype=f32)]
        + [shape(4, wrows, w) for w in widths]
        + [shape(*g_gate_up.shape), shape(4, *g_gate_up.shape), shape(4, *g_down.shape)],
        [VMEM, VMEM] + [ANY] * (count + 3),
        [
            pltpu.VMEM((width, width), bf), pltpu.VMEM((3 * wcols, group), bf),
            pltpu.VMEM((A,) + left, bf), pltpu.VMEM((B - 1, A) + left, bf),
            pltpu.VMEM((A,) + left, bf), pltpu.VMEM((B - 1, A) + left, bf),
            pltpu.VMEM((4,) + block, bf), pltpu.VMEM((group, group), bf),
            pltpu.VMEM((group, 1), f32), pltpu.VMEM((tail, group), bf),
            pltpu.VMEM((group, tail), bf), pltpu.VMEM((B - 1, group, tail), bf),
            pltpu.VMEM((4, rows, span), bf), pltpu.VMEM((4, rows, span), bf),
            pltpu.VMEM((B - 1, 4, rows, span), bf), pltpu.VMEM(block, f32),
            pltpu.VMEM((8, width), f32), pltpu.VMEM((A + B, 8, width), f32), DMA((7,)),
            DMA((count, B, 2)),
        ]
        + fold_scratch(wcols, group) + fold_scratch(*block)
        + [DMA((A, 2)), DMA((1,))] + share_sems() + share_sems()
        + [DMA((4, 2)), DMA((A + B, 2))]
        + [v for w in widths for v in grad_scratch(wrows, w)],
        [
            d_n2, after_attn, cotangent, gains, w4, qkv, tokens, tables, g_gate_up, g_down,
            *lefts, *ids,
        ],
        [VMEM] * 4 + [ANY] * 3 + [VMEM] + [ANY] * 6 + [VMEM] * 4,
    )


def lay_out(S, ff, width, out, value, groups, gate_up, down):
    wrows, span = out.shape[1:]
    wcols = width // 4
    pair = 2 * wcols
    skip = wcols - (span - 128)
    sub = ff // (S * 4)
    pad = down.shape[1]
    fcols = gate_up.shape[3] // 2
    B = fcols // pad
    drows = ff // S
    steps = 9 if wrows % 144 == 0 else 1
    rows, cols = wrows // steps, width // steps

    def kernel(o_in, v_in, *refs):
        g_in, (gu_in, d_in, o_out, q_out, k_out, v_out, g_out, u_out, d_out) = split_refs(
            refs, len(groups), 9
        )

        def beside(pieces, to):
            for side in range(2):
                parts = [
                    ref[side * 2 + core].astype(f32)[:, at : at + size]
                    for core in range(2) for ref, at, size in pieces
                ]
                to[:, side * pair : (side + 1) * pair] = jnp.concatenate(parts, axis=1)

        half = groups[0].shape[2] // 2
        beside([(o_in, 0, wcols)], o_out)
        beside([(v_in, skip, wcols)], v_out)
        beside([(ref, 0, half) for ref in g_in], q_out)
        beside([(ref, half, half) for ref in g_in], k_out)
        for i, to in enumerate((g_out, u_out)):
            parts = []
            for m in range(4 * S):
                s = m // 4
                at = i * fcols + s % B * pad
                parts.append(gu_in[m % 4, s // B].astype(f32)[:, at : at + sub])
            to[...] = jnp.concatenate(parts, axis=1)
        d_out[...] = jnp.concatenate([d_in[k].astype(f32)[:sub] for k in range(4)], axis=0)

    def by_rows(ref):
        lead = len(ref.shape) - 2
        return pl.BlockSpec(
            ref.shape[:lead] + (rows, ref.shape[-1]), lambda i: (0,) * lead + (i, 0)
        )

    outs = [shape(wrows, width, dtype=f32)] * 4 + [shape(wrows, ff, dtype=f32)] * 2
    return pl.pallas_call(
        kernel,
        grid=(steps,),
        out_shape=outs + [shape(drows, width, dtype=f32)],
        in_specs=[by_rows(v) for v in (out, value, *groups, gate_up)]
        + [pl.BlockSpec((4, pad, cols), lambda i: (0, 0, i))],
        out_specs=[by_rows(v) for v in outs] + [pl.BlockSpec((drows, cols), lambda i: (0, i))],
        name="lay_out",
        compiler_params=pltpu.CompilerParams(vmem_limit_bytes=60 * 2**20),
    )(out, value, *groups, gate_up, down)


def product(left_side, right_side):
    return jnp.dot(left_side, right_side, preferred_element_type=f32)


def against(left_side, right_side):
    return lax.dot_general(
        left_side, right_side, (((1,), (1,)), ((), ())), preferred_element_type=f32
    )


def across(left_side, right_side):
    return lax.dot_general(
        left_side, right_side, (((0,), (0,)), ((), ())), preferred_element_type=f32
    )


def body(
    tokens,
    attn_gain,
    w_query,
    w_key,
    w_value,
    w_out,
    ffn_gain,
    w_gate,
    w_up,
    w_down,
    seq_ids,
    block_ids,
    cotangent,
):
    S = lax.axis_size("shard")
    R = lax.axis_size("replica")
    B = S // A
    rows, width = tokens.shape
    ff = w_gate.shape[1]
    wrows = width // S
    ids = (seq_ids[None, :], seq_ids[:, None], block_ids[None, :], block_ids[:, None])
    gains = jnp.pad(jnp.stack([attn_gain, ffn_gain]), ((0, 6), (0, 0)))
    (
        w4, gains, tokens_group, d_down, gate_up, down_w, qkv, mixed_all, after_attn, normed_two,
        tables, normed_t,
    ) = attention_forward(
        B, [w_out, w_value, w_query, w_key], [w_gate, w_up], w_down, gains, tokens, cotangent, ids
    )
    lefts = [v.reshape(A, B, wrows, -1) for v in (mixed_all, normed_t)]
    d_n2, ffn_out, g_gate_up, g_down, mixed_far, normed_far = feed_forward(
        B, normed_two, d_down, gate_up.reshape(width, -1), down_w.reshape(-1, width), lefts
    )
    grad_tokens, gain_sums, g_out, g_value, *parts = attention_backward(
        B, S, d_n2, after_attn, cotangent, gains, w4.reshape(width, width), qkv, tokens_group,
        [lefts[0], mixed_far, lefts[1], normed_far], tables, ids, g_gate_up, g_down,
    )
    g_out, g_query, g_key, g_value, g_gate, g_up, g_down = lay_out(
        S, ff, width, g_out, g_value, parts[:-3], *parts[-2:]
    )
    result = after_attn + branch_scale * ffn_out.astype(f32)
    return (
        result.astype(bf), grad_tokens, gain_sums[0, :wrows], g_query, g_key, g_value, g_out,
        gain_sums[1, :wrows], g_gate, g_up, g_down,
    )


def solution(mesh):
    split = P(("shard", "replica"), None)
    vec, mat = P("shard"), P("shard", None)
    in_specs = (split, vec, mat, mat, mat, mat, vec, mat, mat, mat, vec, vec, split)
    out_specs = (split, split, vec, mat, mat, mat, mat, vec, mat, mat, mat)
    return jax.shard_map(body, mesh=mesh, in_specs=in_specs, out_specs=out_specs, check_vma=False)
```

```python
import functools
import math

import jax
import jax.numpy as jnp
from jax import lax
from jax.experimental import pallas as pl
from jax.experimental.pallas import tpu as pltpu
from jax.sharding import PartitionSpec as P

H = 36
A = 4
X = 2

branch_scale = 1.4 / math.sqrt(40.0)
norm_eps = 1e-05
rope_base = 10000.0
masked_score = -1e30
MESH = pl.DeviceIdType.MESH
bf = jnp.bfloat16
f32 = jnp.float32
DMA = pltpu.SemaphoreType.DMA


class Place:
    def __init__(self, B):
        self.B = B
        s, r = lax.axis_index("shard"), lax.axis_index("replica")
        self.s, self.r = s, r
        self.a, self.b = s // B, s % B
        self.x, self.c = r // X, r % X
        self.rx = (1 - self.x) * X + self.c
        self.rc = self.x * X + 1 - self.c

    def line(self, a):
        return (a * self.B + self.b, self.r)

    def side(self, b):
        return (self.a * self.B + b, self.r)

    @property
    def over_x(self):
        return (self.s, self.rx)

    @property
    def over_core(self):
        return (self.s, self.rc)


def greet(place, a_peers=True, b_peers=False, r_peers=True, everyone=None):
    barrier = pltpu.get_barrier_semaphore()

    def signal(device):
        pl.semaphore_signal(barrier, inc=1, device_id=device, device_id_type=MESH)

    if everyone is not None:
        S, R = everyone

        def one(k, carry):
            signal((lax.rem(place.s + k // R, S), lax.rem(place.r + k % R, R)))
            return carry

        lax.fori_loop(1, S * R, one, 0)
        pl.semaphore_wait(barrier, S * R - 1)
        return
    count = 0
    if a_peers:
        for k in range(1, A):
            signal(place.line((place.a + k) % A))
            count += 1
    if b_peers:
        for k in range(1, place.B):
            signal(place.side((place.b + k) % place.B))
            count += 1
    if r_peers:
        for k in range(1, 4):
            signal((place.s, (place.r + k) % 4))
            count += 1
    pl.semaphore_wait(barrier, count)


def remote(src, dst, send, recv, device):
    return pltpu.make_async_remote_copy(
        src_ref=src, dst_ref=dst, send_sem=send, recv_sem=recv, device_id=device,
        device_id_type=MESH,
    )


def add_into(dst, first, second, tile=32):
    rows = dst.shape[0]
    tile = math.gcd(rows, tile) if math.gcd(rows, tile) >= 16 else rows

    def step(i, carry):
        at = pl.ds(pl.multiple_of(i * tile, tile), tile)
        dst[at, :] = (first[at, :].astype(f32) + second[at, :].astype(f32)).astype(dst.dtype)
        return carry

    lax.fori_loop(0, rows // tile, step, 0)


def run_flows(flows, turns=()):
    ended = set()

    def step(at):
        if at not in ended:
            try:
                next(flows[at])
            except StopIteration:
                ended.add(at)

    for at in turns:
        step(at)
    while len(ended) < len(flows):
        for at in range(len(flows)):
            step(at)


def halves(rows):
    return 2 if rows % 32 == 0 else 1


def piece(ref, at, h, parts):
    if parts == 1:
        return ref.at[at]
    rows = ref.shape[-2] // parts
    index = at if isinstance(at, tuple) else (at,)
    return ref.at[index + (pl.ds(h * rows, rows),)]


def widen_sems():
    return [DMA((A,)), DMA((X,)), DMA((A, 2)), DMA((A, 2)), DMA((X, A, 2)), DMA((1,))]


def widen_flow(place, own, out, sems):
    line_recv, _, line_send, over_x, over_core, local = sems
    a, x, c = place.a, place.x, place.c
    keep = pltpu.make_async_copy(own, out.at[x, a, c], local.at[0])
    keep.start()

    def to_line(src, block, way):
        at = 0 if way > 0 else 1
        return remote(
            src, out.at[x, block, c], line_send.at[block, at], line_recv.at[block],
            place.line(a + way),
        )

    def to_x(src, block):
        return remote(
            src, out.at[x, block, c], over_x.at[block, 0], over_x.at[block, 1], place.over_x
        )

    def to_core(src, side, block):
        return remote(
            src, out.at[side, block, c], over_core.at[side, block, 0],
            over_core.at[side, block, 1], place.over_core,
        )

    @pl.when(a < A - 1)
    def _():
        to_line(own, a, 1).start()

    @pl.when(a > 0)
    def _():
        to_line(own, a, -1).start()

    to_x(own, a).start()
    to_core(own, x, a).start()

    def pass_x(k):
        for ok, block in ((a - k >= 0, a - k), (a + k < A, a + k)) if k else ((None, a),):
            def go():
                src = out.at[1 - x, block, c]
                to_x(src, block).wait_recv()
                to_core(src, 1 - x, block).start()

            go() if ok is None else pl.when(ok)(go)

    for k in range(1, A):
        yield
        for way in (1, -1):
            block = a - way * k

            @pl.when((block >= 0) & (block < A))
            def _():
                src = out.at[x, block, c]
                to_line(src, block, way).wait_recv()

                @pl.when((a + way >= 0) & (a + way < A))
                def _():
                    to_line(src, block, way).start()

                to_x(src, block).start()
                to_core(src, x, block).start()

        yield
        pass_x(k - 1)
    yield
    pass_x(A - 1)
    yield
    keep.wait()
    for block in range(A):
        src = out.at[x, block, c]

        @pl.when((a < A - 1) & (block <= a))
        def _():
            to_line(src, block, 1).wait_send()

        @pl.when((a > 0) & (block >= a))
        def _():
            to_line(src, block, -1).wait_send()

        to_x(src, block).wait_send()
        for side in range(X):
            to_core(src, side, block).wait()


def shrink_scratch(rows, width):
    block = (rows, width)
    P_ = halves(rows)
    return [
        pltpu.VMEM((X, A) + block, bf),
        pltpu.VMEM((X, A) + block, bf),
        pltpu.VMEM((A,) + block, bf),
        pltpu.VMEM((A + 1,) + block, bf),
        DMA((X, A, P_)), DMA((X, A, P_, 2)), DMA((A, P_, 2)), DMA((2, A, P_, 2)),
    ]


def far_first(a, i):
    inner = (3, 0, 2, 1)[i]
    return jnp.where(a == 0, 3 - i, jnp.where(a == 1, inner, jnp.where(a == 2, 3 - inner, i)))


def line_slots(place, sums, landing, sems, parts, ready, final, near=False):
    a = place.a
    last = 2 * A - 3 if near else A - 1

    def part(ref, h):
        if parts == 1:
            return ref
        rows = ref.shape[0] // parts
        return ref.at[pl.ds(h * rows, rows)]

    def hop(d, h, way):
        at = 0 if way > 0 else 1
        return remote(
            part(sums(d), h), part(landing(d, way), h), sems.at[at, d, h, 0],
            sems.at[at, d, h, 1], place.line(a + way),
        )

    def take(d, h, way):
        @pl.when((a - way >= 0) & (a - way < A))
        def _():
            hop(d, h, way).wait_recv()
            here = part(sums(d), h)
            add_into(here, here, part(landing(d, way), h))

    for t in range(last + 1):
        for way in (1, -1):
            at = a if way > 0 else A - 1 - a
            to = t - at + 1 if near else A - 1 - t + at
            d = to if way > 0 else A - 1 - to

            @pl.when((to > at) & (to < A))
            def _():
                for h in range(parts):
                    ready(d, h)
                    take(d, h, way)
                    hop(d, h, way).start()

        if t == last:
            for h in range(parts):
                ready(a, h)
                take(a, h, 1)
                take(a, h, -1)
                final(h)
        yield
    for d in range(A):
        for h in range(parts):
            for way in (1, -1):
                @pl.when((d - a) * way > 0)
                def _():
                    hop(d, h, way).wait_send()


def share_sems():
    return [DMA((2,)), DMA((X, 2)), DMA((1,))]


def share_flow(place, own, out, sems, ready=None):
    x_sem, core_sem, local = sems
    r, x, c = place.r, place.x, place.c
    if ready is not None:
        yield
        ready()
    keep = pltpu.make_async_copy(own, out.at[r], local.at[0])
    to_x = remote(own, out.at[r], x_sem.at[0], x_sem.at[1], place.over_x)
    near = remote(own, out.at[r], core_sem.at[x, 0], core_sem.at[x, 1], place.over_core)
    far = remote(
        out.at[place.rx], out.at[place.rx], core_sem.at[1 - x, 0], core_sem.at[1 - x, 1],
        place.over_core,
    )
    to_x.start()
    near.start()
    keep.start()
    yield
    to_x.wait_recv()
    far.start()
    yield
    keep.wait()
    to_x.wait_send()
    near.wait()
    far.wait()


def spread_sems(B, parts=1):
    return [DMA((A, parts)), DMA((A, 2, parts)), DMA((B, A, parts, 2)), DMA((1,))]


def spread_flow(place, own, out, sems, parts=1):
    line_recv, line_send, side, local = sems
    a, b, B = place.a, place.b, place.B
    keep = pltpu.make_async_copy(own, out.at[a, b], local.at[0])
    keep.start()

    def half(h):
        return own if parts == 1 else own.at[pl.ds(h * own.shape[0] // parts, own.shape[0] // parts)]

    def to_line(src, block, h, way):
        return remote(
            src, piece(out, (block, b), h, parts), line_send.at[block, 0 if way > 0 else 1, h],
            line_recv.at[block, h], place.line(a + way),
        )

    def to_side(src, block, h, k):
        return remote(
            src, piece(out, (block, b), h, parts), side.at[k, block, h, 0],
            side.at[k, block, h, 1], place.side((b + k) % B),
        )

    for h in range(parts):
        @pl.when(a < A - 1)
        def _():
            to_line(half(h), a, h, 1).start()

        @pl.when(a > 0)
        def _():
            to_line(half(h), a, h, -1).start()

        for k in range(1, B):
            to_side(half(h), a, h, k).start()
    for step in range(1, A):
        for h in range(parts):
            yield
            for way in (1, -1):
                block = a - way * step

                @pl.when((block >= 0) & (block < A))
                def _():
                    src = piece(out, (block, b), h, parts)
                    to_line(src, block, h, way).wait_recv()

                    @pl.when((a + way >= 0) & (a + way < A))
                    def _():
                        to_line(src, block, h, way).start()

                    for k in range(1, B):
                        to_side(src, block, h, k).start()

    yield
    keep.wait()
    for block in range(A):
        for h in range(parts):
            src = piece(out, (block, b), h, parts)

            @pl.when((a < A - 1) & (block <= a))
            def _():
                to_line(src, block, h, 1).wait_send()

            @pl.when((a > 0) & (block >= a))
            def _():
                to_line(src, block, h, -1).wait_send()

            for k in range(1, B):
                to_side(src, block, h, k).wait()


def columns_sems(B):
    return [DMA((A, 2)), DMA((B, A, 2)), DMA((1,))]


def columns_flow(place, own, out, sems):
    line, side, local = sems
    a, b, B = place.a, place.b, place.B
    keep = pltpu.make_async_copy(own.at[a], out.at[a, b], local.at[0])
    keep.start()

    def to_line(k):
        to = (a + k) % A
        return remote(own.at[to], out.at[a, b], line.at[k, 0], line.at[k, 1], place.line(to))

    def to_side(src, block, k):
        return remote(
            src, out.at[block, b], side.at[k, block, 0], side.at[k, block, 1],
            place.side((b + k) % B),
        )

    for k in range(1, A):
        to_line(k).start()
    for k in range(1, B):
        to_side(own.at[a], a, k).start()
    for k in (1, 3, 2):
        yield
        to_line(k).wait_recv()
        block = (a + A - k) % A
        for j in range(1, B):
            to_side(out.at[block, b], block, j).start()
    yield
    keep.wait()
    for k in range(1, A):
        to_line(k).wait_send()
    for block in range(A):
        for k in range(1, B):
            to_side(out.at[block, b], block, k).wait()


def sides_sems(B):
    return [DMA((B, 2)), DMA((1,))]


def sides_flow(place, own, out, sems):
    side, local = sems
    b, B = place.b, place.B
    keep = pltpu.make_async_copy(own, out.at[b], local.at[0])
    keep.start()
    copies = [
        remote(own, out.at[b], side.at[k, 0], side.at[k, 1], place.side((b + k) % B))
        for k in range(1, B)
    ]
    for copy in copies:
        copy.start()
    yield
    keep.wait()
    for copy in copies:
        copy.wait()


ANY = pl.BlockSpec(memory_space=pl.ANY)
VMEM = pl.BlockSpec(memory_space=pltpu.VMEM)


def call(kernel, name, collective_id, outs, out_specs, scratch, args, in_specs):
    return pl.pallas_call(
        kernel,
        out_shape=outs,
        in_specs=in_specs,
        out_specs=out_specs,
        scratch_shapes=scratch,
        name=name,
        compiler_params=pltpu.CompilerParams(
            collective_id=collective_id, has_side_effects=True, vmem_limit_bytes=63 * 2**20
        ),
    )(*args)


def shape(*dims, dtype=bf):
    return jax.ShapeDtypeStruct(dims, dtype)


def split_refs(refs, *sizes):
    found, at = [], 0
    for size in sizes:
        found.append(refs[at : at + size])
        at += size
    return found


def select(rows, cols, shift, at, width):
    j = lax.broadcasted_iota(jnp.int32, (1, cols), 1) - at
    wanted = jnp.where((j >= 0) & (j < width), j + shift, -1)
    row = lax.broadcasted_iota(jnp.int32, (rows, cols), 0)
    return jnp.where(row == wanted, 1.0, 0.0).astype(bf)


def select_mixed(rows, cols, shift, j, part):
    col = lax.broadcasted_iota(jnp.int32, (1, cols), 1)
    wanted = jnp.where(
        col // part % 2 == j, shift + col // (2 * part) * part + col % part, -1
    )
    row = lax.broadcasted_iota(jnp.int32, (rows, cols), 0)
    return jnp.where(row == wanted, 1.0, 0.0).astype(bf)


def masks(seq_row, blk_row):
    def columns(ref):
        row = ref[...].astype(f32)
        return row, jnp.broadcast_to(row, (8, row.shape[1])).T[:, :1]

    seq, seq_t = columns(seq_row)
    blk, blk_t = columns(blk_row)
    return seq_t < seq, (seq_t == seq) & (blk_t <= blk)


def rope(ref, at, cosine, sine, out, to, head_dim):
    half = head_dim // 2
    former, latter = ref[pl.ds(at, half), :], ref[pl.ds(at + half, half), :]
    out[pl.ds(to, half), :] = (former * cosine - latter * sine).astype(out.dtype)
    out[pl.ds(to + half, half), :] = (latter * cosine + former * sine).astype(out.dtype)


def attention_forward(B, weights, gates, w_down, gains, tokens, cotangent, ids):
    wrows, width = weights[0].shape
    rows = tokens.shape[0]
    group = 4 * rows
    ff = gates[0].shape[1]
    wcols = width // 4
    head_dim = width // H
    heads = H // 4
    sub = ff // (A * B * 4)
    pad = -(-sub // 16) * 16
    fcols = B * pad
    wide = 384
    span = -(-wcols // 128) * 128
    pair = 2 * wcols
    parts = halves(wrows)
    trio = 3
    score_scale = 1.0 / math.sqrt(head_dim)

    def kernel(*refs):
        w_in, g_in, ins, outs, scratch, refs = split_refs(refs, 4, 2, 6, 12, 18, 100)
        wd_in, gain_in, tok_in, cot_in, seq_row, blk_row = ins
        (w4_out, gain_out, tok_out, d_out, gu_out, dn_out, qkv_out, mixed_out, after_out,
         n2_out, table_out, normed_t) = outs
        (w_all, g_all, wd_all, own4, gu_own, dn_own, own_gain, gain_all, tok_all, d_own, w4_all,
         normed, raw, bias, mixed, proj, proj_all, load) = scratch
        s1, s2, s3, s4, s5, s6, s7 = split_refs(refs, 4, 4, 3, 6, 3, 2, 100)
        qkv, mix_x, mix_core, ex_sem, save = s7
        place = Place(B)
        r, x, c = place.r, place.x, place.c
        loads = [pltpu.make_async_copy(w, w_all.at[i], load.at[i]) for i, w in enumerate(w_in)]
        loads += [
            pltpu.make_async_copy(w, g_all.at[i], load.at[4 + i]) for i, w in enumerate(g_in)
        ]
        loads.append(pltpu.make_async_copy(wd_in, wd_all, load.at[6]))
        for copy in loads:
            copy.start()
        start = pl.multiple_of(r * wcols // 128 * 128, 128)
        shift = r * wcols - start
        for i in range(2):
            total = jnp.zeros((wrows, pair), f32)
            for j in range(2):
                loads[2 * i + j].wait()
                pick = select(span, pair, shift, j * wcols, wcols)
                if i:
                    pick = select_mixed(span, pair, shift, j, trio * head_dim)
                total += product(w_all[2 * i + j, :, pl.ds(start, span)], pick)
            own4[:, i * pair : (i + 1) * pair] = total.astype(bf)
        for k in range(width // wide):
            own_gain[:, k * wide : (k + 1) * wide] = jnp.dot(
                gain_in[...], select(wrows, wide, 0, place.s * wrows - k * wide, wrows),
                preferred_element_type=f32,
            )
        greet(place, True, True, True)

        def prepare():
            for i in range(2):
                loads[4 + i].wait()
            loads[6].wait()

            def one(n, carry):
                i, block = n // A, n % A
                total = jnp.zeros((wrows, fcols), f32)
                for j in range(B):
                    first = ((block * B + j) * 4 + r) * sub
                    at = pl.multiple_of(jnp.minimum(first // 128 * 128, ff - wide), 128)
                    total += jnp.dot(
                        g_all[i, :, pl.ds(at, wide)],
                        select(wide, fcols, first - at, j * pad, sub),
                        preferred_element_type=f32,
                    )
                at = pl.multiple_of(i * fcols, 128)
                gu_own[block, :, pl.ds(at, fcols)] = total.astype(bf)
                return carry

            lax.fori_loop(0, 2 * A, one, 0)
            row = lax.broadcasted_iota(jnp.int32, (pad, ff // (A * B)), 0)
            col = lax.broadcasted_iota(jnp.int32, (pad, ff // (A * B)), 1)
            pick = jnp.where((col - r * sub == row) & (row < sub), 1.0, 0.0).astype(bf)
            tile = 768

            def down(n, carry):
                at = pl.ds(pl.multiple_of(n * tile, tile), tile)
                dn_own[:, at] = jnp.dot(
                    pick, wd_all[:, at], preferred_element_type=f32
                ).astype(bf)
                return carry

            lax.fori_loop(0, width // tile, down, 0)
            d_own[...] = (branch_scale * cot_in[...].astype(f32)).astype(bf)
            less, allowed = masks(seq_row, blk_row)
            earlier = jnp.sum(jnp.where(less, 1.0, 0.0), axis=0, keepdims=True)
            at = lax.broadcasted_iota(jnp.int32, (1, group), 1).astype(f32) - earlier
            half = head_dim // 2
            index = lax.broadcasted_iota(jnp.int32, (half, group), 0).astype(f32)
            angle = at * jnp.exp(index * (-2.0 * math.log(rope_base) / head_dim))
            table_out[0] = jnp.cos(angle)
            table_out[1] = jnp.sin(angle)
            bias[...] = jnp.where(allowed, 0.0, masked_score)
            yield
            total = jnp.zeros((8, width), f32)
            for block in range(A):
                for side in range(B):
                    total += gain_all[block, side]
            gain_out[...] = total
            for i in range(4):
                value = tok_all[i].astype(f32)
                factor = lax.rsqrt(jnp.mean(value * value, axis=1, keepdims=True) + norm_eps)
                value = value * factor * total[0:1]
                at = slice(i * rows, (i + 1) * rows)
                normed[at, :] = value.astype(bf)
                normed_t[:, at] = value.T.astype(bf)

        def share_piece(k):
            at = pl.ds(k * trio * head_dim, trio * head_dim)
            own = mixed.at[r, at]
            far = mixed.at[place.rx, at]
            return (
                remote(own, own, mix_x.at[k, 0], mix_x.at[k, 1], place.over_x),
                remote(own, own, mix_core.at[x, k, 0], mix_core.at[x, k, 1], place.over_core),
                remote(
                    far, far, mix_core.at[1 - x, k, 0], mix_core.at[1 - x, k, 1],
                    place.over_core,
                ),
            )

        pieces = heads // trio

        def attend():
            step = 256

            def project(n, carry):
                cols = pl.ds(pl.multiple_of(span - 128 + n * step, 128), step)
                w = w4_all[:, :, :, cols].reshape(width, step)
                at = pl.ds(pl.multiple_of(n * step, step), step)
                raw[at, :] = product(normed[...], w).T
                return carry

            lax.fori_loop(0, (width - span + 128) // step, project, 0)
            skip = wcols - (span - 128)
            cosine, sine = table_out[0], table_out[1]

            def turn(n, carry):
                at = pl.multiple_of(wcols + n * head_dim, 32)
                i, h = n // heads, n % heads
                first = skip + wcols + (h // trio * 2 + i) * trio * head_dim + h % trio * head_dim
                rope(raw, pl.multiple_of(first, 32), cosine, sine, qkv, at, head_dim)
                return carry

            lax.fori_loop(0, 2 * heads, turn, 0)
            qkv[:wcols, :] = raw[pl.ds(skip, wcols), :].astype(bf)
            pltpu.make_async_copy(qkv, qkv_out, save.at[0]).start()
            yield

            def head(n, carry):
                at = lambda part: pl.ds(pl.multiple_of(part * wcols + n * head_dim, 64), head_dim)
                scores = across(qkv[at(2), :], qkv[at(1), :]) * score_scale + bias[...]
                top = jnp.max(scores, axis=0, keepdims=True)
                powers = jnp.exp(scores - top)
                probs = powers * (1.0 / jnp.sum(powers, axis=0, keepdims=True))
                mixed[r, at(0), :] = product(qkv[at(0), :], probs.astype(bf)).astype(bf)
                return carry

            for k in range(pieces):
                lax.fori_loop(k * trio, (k + 1) * trio, head, 0)
                to_x, near, far = share_piece(k)
                to_x.start()
                near.start()
                if k:
                    to_x, near, far = share_piece(k - 1)
                    to_x.wait_recv()
                    far.start()
                yield
            to_x, near, far = share_piece(pieces - 1)
            to_x.wait_recv()
            far.start()
            for k in range(pieces):
                to_x, near, far = share_piece(k)
                near.wait_recv()
                far.wait_recv()
            everyone = mixed[...].reshape(width, group)
            value = across(everyone, w4_all[:, :, :, :span].reshape(width, span))
            proj[...] = value.astype(bf).reshape(4, rows, span)
            proj_all[r] = proj[r]
            copies = []
            for k in (2, 3, 1):
                to = (r + k) % 4
                copies.append(
                    remote(
                        proj.at[to], proj_all.at[r], ex_sem.at[k, 0], ex_sem.at[k, 1],
                        (place.s, to),
                    )
                )
                copies[-1].start()
            saved = pltpu.make_async_copy(mixed, mixed_out, save.at[1])
            saved.start()
            yield
            for copy in copies:
                copy.wait()
            own = tok_all[r].astype(f32)
            halves_ = []
            for side in range(2):
                total = jnp.zeros((rows, pair), f32)
                for core in range(2):
                    total += jnp.dot(
                        proj_all[side * 2 + core],
                        select(span, pair, 0, core * wcols, wcols), preferred_element_type=f32,
                    )
                at = slice(side * pair, (side + 1) * pair)
                halves_.append(own[:, at] + branch_scale * total)
                after_out[:, at] = halves_[-1]
            mean = sum(jnp.sum(v * v, axis=1, keepdims=True) for v in halves_) / width
            factor = lax.rsqrt(mean + norm_eps)
            for side in range(2):
                at = slice(side * pair, (side + 1) * pair)
                n2_out[:, at] = (halves_[side] * factor * gain_out[1:2, at]).astype(bf)
            yield
            saved.wait()
            pltpu.make_async_copy(qkv, qkv_out, save.at[0]).wait()
            for k in range(pieces):
                to_x, near, far = share_piece(k)
                to_x.wait_send()
                near.wait_send()
                far.wait_send()

        def weights_flow():
            yield from spread_flow(place, own4, w4_all, s1, parts)
            pltpu.make_async_copy(w4_all, w4_out, save.at[2]).start()

        run_flows(
            [
                weights_flow(),
                share_flow(place, tok_in, tok_all, s3),
                spread_flow(place, own_gain, gain_all, s2),
                prepare(),
                widen_flow(place, d_own, d_out, s4),
                columns_flow(place, gu_own, gu_out, s5),
                sides_flow(place, dn_own, dn_out, s6),
                attend(),
            ],
            (0, 1, 2, 3, 1, 1, 1, 2, 2, 2, 2, 2, 3, 3) + (0,) * (2 * parts) + (4,)
            + (0,) * parts + (4, 4, 0, 6, 5, 7, 4, 7, 7, 7, 5, 4, 7, 4, 5, 7, 5, 4, 4, 7, 6, 5, 4),
        )
        saved = pltpu.make_async_copy(tok_all, tok_out, save.at[1])
        saved.start()
        saved.wait()
        pltpu.make_async_copy(w4_all, w4_out, save.at[2]).wait()

    block = (rows, width)
    return call(
        kernel, "attention_forward", 1,
        [
            shape(A, B, wrows, 4 * wcols), shape(8, width, dtype=f32), shape(4, *block),
            shape(X, A, X, *block), shape(A, B, wrows, 2 * fcols), shape(B, pad, width),
            shape(3 * wcols, group), shape(4, wcols, group), shape(*block, dtype=f32),
            shape(*block), shape(2, head_dim // 2, group, dtype=f32), shape(width, group),
        ],
        [ANY, VMEM, ANY, ANY, ANY, ANY, ANY, ANY, VMEM, VMEM, VMEM, VMEM],
        [
            pltpu.VMEM((4, wrows, width), bf), pltpu.VMEM((2, wrows, ff), bf),
            pltpu.VMEM(w_down.shape, bf), pltpu.VMEM((wrows, 4 * wcols), bf),
            pltpu.VMEM((A, wrows, 2 * fcols), bf), pltpu.VMEM((pad, width), bf),
            pltpu.VMEM((8, width), f32), pltpu.VMEM((A, B, 8, width), f32),
            pltpu.VMEM((4,) + block, bf), pltpu.VMEM(block, bf),
            pltpu.VMEM((A, B, wrows, 4 * wcols), bf), pltpu.VMEM((group, width), bf),
            pltpu.VMEM((width - span + 128, group), f32), pltpu.VMEM((group, group), f32),
            pltpu.VMEM((4, wcols, group), bf), pltpu.VMEM((4, rows, span), bf),
            pltpu.VMEM((4, rows, span), bf), DMA((7,)),
        ]
        + spread_sems(B, parts) + spread_sems(B) + share_sems() + widen_sems() + columns_sems(B)
        + sides_sems(B)
        + [
            pltpu.VMEM((3 * wcols, group), bf), DMA((3, 2)), DMA((X, 3, 2)), DMA((4, 2)),
            DMA((3,)),
        ],
        [*weights, *gates, w_down, gains, tokens, cotangent, *ids],
        [ANY] * 7 + [VMEM, ANY] + [VMEM] * 3,
    )


def feed_forward(B, normed_two, d_down, gate_up, down, lefts):
    rows, width = normed_two.shape
    fcols = down.shape[0]
    every = X * A * X * rows
    pair = X * rows
    parts = halves(rows)
    wide = 768
    tile = 384

    wrows = gate_up.shape[0] // (A * B)
    pad = fcols // B
    many = 1152

    def kernel(n_in, d_in, gu_in, dn_in, *refs):
        lefts_in, (out, f_out, ggu_out, gd_out), lefts_out, refs = split_refs(refs, 2, 4, 2, 100)
        bufs, (line_recv, line_send, over_x, over_core), sems = split_refs(refs, 11, 4, 100)
        n_all, d_all, gu, dn, part, hid, d_gu, from_core, from_x, landed, g_all = bufs
        (g_down, load, core_sem, x_sem, line_sem, gu_side, gd_side, gu_sem, gd_sem, f_core, f_x,
         free, core_free, f_line, left_sem) = sems
        place = Place(B)
        a, x, c = place.a, place.x, place.c
        loads = [
            pltpu.make_async_copy(n_in, n_all.at[x, a, c], load.at[0]),
            pltpu.make_async_copy(gu_in, gu, load.at[1]),
            pltpu.make_async_copy(dn_in, dn, load.at[2]),
            pltpu.make_async_copy(d_in, d_all, load.at[3]),
        ]
        for copy in loads:
            copy.start()
        greet(place, True, True, True)

        def to_line(block, way):
            src = n_all.at[x, block, c]
            return remote(
                src, src, line_send.at[block, (1 - way) // 2], line_recv.at[block],
                place.line(a + way),
            )

        def to_x(block):
            src = n_all.at[x, block, c]
            return remote(src, src, over_x.at[block, 0], over_x.at[block, 1], place.over_x)

        def to_core(side, block):
            src = n_all.at[side, block, c]
            return remote(
                src, src, over_core.at[side, block, 0], over_core.at[side, block, 1],
                place.over_core,
            )

        def sum_core(side, d, h):
            return remote(
                piece(part, (side, d, 1 - c), h, parts), piece(from_core, (side, d), h, parts),
                core_sem.at[side, d, h, 0], core_sem.at[side, d, h, 1], place.over_core,
            )

        def sum_x(d, h):
            return remote(
                piece(part, (1 - x, d, c), h, parts), piece(from_x, d, h, parts),
                x_sem.at[d, h, 0], x_sem.at[d, h, 1], place.over_x,
            )

        def merge(side, d, h):
            sum_core(side, d, h).wait_recv()
            here = piece(part, (side, d, c), h, parts)
            add_into(here, here, piece(from_core, (side, d), h, parts))

        def send_sum(d):
            for h in range(parts):
                merge(1 - x, d, h)
                sum_x(d, h).start()

        loads[0].wait()

        @pl.when(a < A - 1)
        def _():
            to_line(a, 1).start()

        @pl.when(a > 0)
        def _():
            to_line(a, -1).start()

        to_x(a).start()
        to_core(x, a).start()

        def left_aside(i, d, k):
            to = (place.b + k) % B
            return remote(
                lefts_in[i].at[d, to], lefts_out[i].at[k - 1, d], left_sem.at[i, k, d, 0],
                left_sem.at[i, k, d, 1], place.side(to),
            )

        left_copies = [(i, d, k) for i in range(2) for d in range(A) for k in range(1, B)]
        for at in left_copies:
            left_aside(*at).start()
        for copy in loads[1:]:
            copy.wait()

        def nearest(i):
            left = jnp.where(a == 1, jnp.where(i == 1, 0, i), jnp.where(i == 0, 0, i))
            left = jnp.where((a == 1) & (i == 0), 1, left)
            right = jnp.where(a == 2, jnp.where(i == 0, 2, jnp.where(i == 1, 1, 3)), A - 1 - i)
            right = jnp.where((a == 2) & (i == A - 1), 0, right)
            return jnp.where(a < 2, left, right)

        def item(j):
            near = (j == 0) | ((j % 2 == 1) & (j < 2 * A - 1))
            i = jnp.where(near, (j + 1) // 2, jnp.where(j == 2 * A - 1, A - 1, j // 2 - 1))
            return near, nearest(i)

        def compute(side, block):
            n = n_all[side, block].reshape(pair, width)
            d = d_all[side, block].reshape(pair, width)
            both = product(n, gu[...])
            gate, up = both[:, :fcols], both[:, fcols:]
            d_hidden = against(d, dn[...])
            sig = jax.nn.sigmoid(gate)
            at = pl.ds(pl.multiple_of((side * A + block) * pair, pair), pair)
            hid[at, :] = (gate * sig * up).astype(bf)
            d_gate = (d_hidden * up * sig * (1.0 + gate * (1.0 - sig))).astype(bf)
            d_up = (d_hidden * gate * sig).astype(bf)
            both = jnp.concatenate([d_gate, d_up], axis=1)
            d_gu[at, :] = both
            for k in range(width // wide):
                cols = pl.ds(k * wide, wide)
                value = against(both, gu[cols, :]).astype(bf)
                part[side, block, :, :, cols] = value.reshape(X, rows, wide)

        def arrive(j, carry):
            near, block = item(j)
            side = jnp.where(near, x, 1 - x)

            @pl.when(near & (j > 0))
            def _():
                way = jnp.where(block < a, 1, -1)
                to_line(block, way).wait_recv()

                @pl.when((a + way >= 0) & (a + way < A))
                def _():
                    to_line(block, way).start()

                to_x(block).start()
                to_core(x, block).start()

            @pl.when(jnp.logical_not(near))
            def _():
                to_x(block).wait_recv()
                to_core(1 - x, block).start()

            to_core(side, block).wait_recv()
            compute(side, block)
            for h in range(parts):
                sum_core(side, block, h).start()

            before, last = item(jnp.maximum(j - 1, 0))

            @pl.when((j > 3) & jnp.logical_not(before))
            def _():
                send_sum(last)

            return carry

        lax.fori_loop(0, 2 * A, arrive, 0)
        send_sum(nearest(A - 1))
        send_sum(a)
        for d in range(A):
            for h in range(parts):
                merge(x, d, h)
        pl.semaphore_signal(
            core_free, inc=1, device_id=place.over_core, device_id_type=MESH
        )

        def ready(d, h):
            sum_x(d, h).wait_recv()
            here = piece(part, (x, d, c), h, parts)
            add_into(here, here, piece(from_x, d, h, parts))

        piece_rows = rows // parts

        def final(h):
            at = pl.ds(h * piece_rows, piece_rows)
            out[at, :] = part[x, a, c, at, :]

        chain = line_slots(
            place, lambda d: part.at[x, d, c], lambda d, way: landed.at[d + (way > 0)], line_sem,
            parts, ready, final, near=True,
        )

        def grad_down(k, carry):
            at = pl.ds(pl.multiple_of(k * tile, tile), tile)
            d = d_all[:, :, :, :, at].reshape(every, tile)
            g_down[:, at] = across(hid[...], d).astype(bf)
            return carry

        def grad_gate_up(k, carry):
            at = pl.ds(pl.multiple_of(k * many, many), many)
            n = n_all[:, :, :, :, at].reshape(every, many)
            count = many // wrows
            for i in range(2):
                cols = pl.ds(i * fcols, fcols)
                value = across(n, d_gu[:, cols]).astype(bf)
                g_all[pl.ds(k * count, count), :, cols] = value.reshape(count, wrows, fcols)
            return carry

        def aside(d, k):
            to = (place.b + k) % B
            return remote(
                g_all.at[d * B + to], gu_side.at[k - 1, d], gu_sem.at[k, d, 0],
                gu_sem.at[k, d, 1], place.side(to),
            )

        def aside_down(k):
            to = (place.b + k) % B
            at = pl.ds(pl.multiple_of(to * pad, 16), pad)
            return remote(
                g_down.at[at], gd_side.at[k - 1], gd_sem.at[k, 0], gd_sem.at[k, 1], place.side(to)
            )

        def forward(k, carry):
            side, block = k // A, k % A
            at = pl.ds(pl.multiple_of(k * pair, pair), pair)
            for i in range(width // wide):
                cols = pl.ds(i * wide, wide)
                value = product(hid[at, :], dn[:, cols]).astype(bf)
                d_all[side, block, :, :, cols] = value.reshape(X, rows, wide)
            return carry

        mine = pl.ds(pl.multiple_of(place.b * pad, 16), pad)
        outs = [pltpu.make_async_copy(g_down.at[mine], gd_out, load.at[0])] + [
            pltpu.make_async_copy(g_all.at[d * B + place.b], ggu_out.at[d], load.at[1 + d])
            for d in range(A)
        ]

        def out_core(side, d):
            return remote(
                d_all.at[side, d, 1 - c], from_core.at[side, d], f_core.at[side, d, 0],
                f_core.at[side, d, 1], place.over_core,
            )

        def out_x(d):
            return remote(
                d_all.at[1 - x, d, c], n_all.at[0, d, 1], f_x.at[d, 0], f_x.at[d, 1],
                place.over_x,
            )

        def out_merge(side, d):
            out_core(side, d).wait_recv()
            here = d_all.at[side, d, c]
            add_into(here, here, from_core.at[side, d])

        def out_ready(d, h):
            out_merge(x, d)
            out_x(d).wait_recv()
            here = d_all.at[x, d, c]
            add_into(here, here, n_all.at[0, d, 1])

        def out_final(h):
            pltpu.make_async_copy(d_all.at[x, a, c], f_out, load.at[1 + A]).start()

        def out_landing(d, way):
            return part.at[0, d, 1 - c] if way > 0 else n_all.at[1, d, 1]

        out_chain = line_slots(
            place, lambda d: d_all.at[x, d, c], out_landing, f_line, 1, out_ready, out_final
        )

        lax.fori_loop(0, width // tile, grad_down, 0)
        for k in range(1, B):
            aside_down(k).start()
        next(chain)
        lax.fori_loop(0, X * A, forward, 0)
        pl.semaphore_wait(core_free, 1)
        for side in (1 - x, x):
            for i in range(A):
                out_core(side, far_first(a, i)).start()
        next(chain)
        for k in range(width // many):
            grad_gate_up(k, 0)
            for d in range(k * many // (wrows * B), (k + 1) * many // (wrows * B)):
                for j in range(1, B):
                    aside(d, j).start()
            next(chain)
        for d in range(A):
            to_x(d).wait_send()
            for side in range(X):
                to_core(side, d).wait_send()
                for h in range(parts):
                    sum_core(side, d, h).wait_send()

            @pl.when((a < A - 1) & (d <= a))
            def _():
                to_line(d, 1).wait_send()

            @pl.when((a > 0) & (d >= a))
            def _():
                to_line(d, -1).wait_send()

        for device in [place.over_x] + [place.line((a + k) % A) for k in range(1, A)]:
            pl.semaphore_signal(free, inc=1, device_id=device, device_id_type=MESH)
        for i in range(A):
            out_merge(1 - x, far_first(a, i))
        pl.semaphore_wait(free, A)
        for i in range(A):
            out_x(far_first(a, i)).start()
        next(chain)
        for k in range(1, B):
            aside_down(k).wait_recv()
            add_into(g_down.at[mine], g_down.at[mine], gd_side.at[k - 1])
        outs[0].start()
        for _ in chain:
            pass
        next(out_chain)
        for d in range(A):
            for k in range(1, B):
                aside(d, k).wait_recv()
                here = g_all.at[d * B + place.b]
                add_into(here, here, gu_side.at[k - 1, d])
            outs[1 + d].start()
        for _ in out_chain:
            pass
        pltpu.make_async_copy(d_all.at[x, a, c], f_out, load.at[1 + A]).wait()
        for at in left_copies:
            left_aside(*at).wait()
        for copy in outs:
            copy.wait()
        for k in range(1, B):
            aside_down(k).wait_send()
            for d in range(A):
                aside(d, k).wait_send()
        for d in range(A):
            out_x(d).wait_send()
            for side in range(X):
                out_core(side, d).wait_send()
            for h in range(parts):
                sum_x(d, h).wait_send()

    block = (rows, width)
    return call(
        kernel, "feed_forward", 2,
        [
            shape(*block), shape(*block), shape(A, wrows, 2 * fcols),
            shape(pad, width),
        ]
        + [shape(B - 1, A, *v.shape[2:]) for v in lefts],
        [VMEM] + [ANY] * 5,
        [
            pltpu.VMEM((X, A, X) + block, bf), pltpu.VMEM((X, A, X) + block, bf),
            pltpu.VMEM(gate_up.shape, bf), pltpu.VMEM(down.shape, bf),
            pltpu.VMEM((X, A, X) + block, bf), pltpu.VMEM((every, fcols), bf),
            pltpu.VMEM((every, 2 * fcols), bf), pltpu.VMEM((X, A) + block, bf),
            pltpu.VMEM((A,) + block, bf), pltpu.VMEM((A + 1,) + block, bf),
            pltpu.VMEM((A * B, wrows, 2 * fcols), bf),
            DMA((A,)), DMA((A, 2)), DMA((A, 2)), DMA((X, A, 2)),
            pltpu.VMEM((fcols, width), bf), DMA((2 + A,)), DMA((X, A, parts, 2)),
            DMA((A, parts, 2)), DMA((2, A, parts, 2)),
            pltpu.VMEM((B - 1, A, wrows, 2 * fcols), bf), pltpu.VMEM((B - 1, pad, width), bf),
            DMA((B, A, 2)), DMA((B, 2)), DMA((X, A, 2)), DMA((A, 2)), pltpu.SemaphoreType.REGULAR,
            pltpu.SemaphoreType.REGULAR,
            DMA((2, A, 1, 2)), DMA((2, B, A, 2)),
        ],
        [normed_two, d_down, gate_up, down, *lefts],
        [ANY] * 6,
    )


def fold_scratch(rows, width):
    block = (rows, width)
    return [
        pltpu.VMEM((X * X,) + block, bf), pltpu.VMEM((X,) + block, bf), pltpu.VMEM(block, bf),
        DMA((X, 2)), DMA((2,)),
    ]


def fold_flow(place, scratch):
    part, from_core, from_x, core_sem, x_sem = scratch
    x, c = place.x, place.c

    def to_core(i):
        return remote(
            part.at[i * X + 1 - c], from_core.at[i], core_sem.at[i, 0], core_sem.at[i, 1],
            place.over_core,
        )

    def merge(i):
        to_core(i).wait_recv()
        here = part.at[i * X + c]
        add_into(here, here, from_core.at[i])

    to_x = remote(part.at[place.rx], from_x, x_sem.at[0], x_sem.at[1], place.over_x)
    to_core(1 - x).start()
    to_core(x).start()
    yield
    merge(1 - x)
    to_x.start()
    merge(x)
    yield
    to_x.wait_recv()
    here = part.at[place.r]
    add_into(here, here, from_x)
    yield
    to_x.wait_send()
    for i in range(X):
        to_core(i).wait_send()


def owners_flow(place, own, out, sems):
    line, local = sems
    a = place.a
    keep = pltpu.make_async_copy(own.at[a], out.at[a], local.at[0])
    keep.start()
    copies = []
    for k in (1, 3, 2):
        to = (a + k) % A
        copies.append(
            remote(own.at[to], out.at[a], line.at[k, 0], line.at[k, 1], place.line(to))
        )
        copies[-1].start()
    yield
    keep.wait()
    for copy in copies:
        copy.wait()


def grad_scratch(rows, width):
    block = (rows, width)
    P_ = halves(rows)
    return [
        pltpu.VMEM((A,) + block, bf), pltpu.VMEM((A + 1,) + block, bf), DMA((2, A, P_, 2)),
        DMA((P_, 2)), DMA((X, P_, 2)), DMA((P_,)),
    ]


def grad_flow(place, produce, out, scratch):
    sums, landed, line_sem, x_sem, core_sem, local = scratch
    r, x = place.r, place.x
    parts = halves(out.shape[1])
    for i in range(A):
        d = far_first(place.a, i)
        sums[d] = produce(d)
    yield

    def keep(src, h):
        return pltpu.make_async_copy(src, piece(out, r, h, parts), local.at[h])

    def to_x(src, h):
        return remote(src, piece(out, r, h, parts), x_sem.at[h, 0], x_sem.at[h, 1], place.over_x)

    def near(src, h):
        return remote(
            src, piece(out, r, h, parts), core_sem.at[x, h, 0], core_sem.at[x, h, 1],
            place.over_core,
        )

    def far(h):
        src = piece(out, place.rx, h, parts)
        return remote(
            src, src, core_sem.at[1 - x, h, 0], core_sem.at[1 - x, h, 1], place.over_core
        )

    def final(h):
        src = piece(sums, place.a, h, parts)
        to_x(src, h).start()
        near(src, h).start()
        keep(src, h).start()

    yield from line_slots(
        place, lambda d: sums.at[d], lambda d, way: landed.at[d + (way > 0)], line_sem, parts,
        lambda d, h: None, final,
    )
    for h in range(parts):
        src = piece(out, r, h, parts)
        keep(src, h).wait()
        near(src, h).wait()
    yield
    for h in range(parts):
        src = piece(out, r, h, parts)
        to_x(src, h).wait_recv()
        far(h).start()
    yield
    for h in range(parts):
        to_x(piece(out, r, h, parts), h).wait_send()
        far(h).wait()


def attention_backward(
    B, S, d_n2, after_attn, cotangent, gains, w4, qkv, tokens, lefts, tables, ids, g_gate_up,
    g_down,
):
    rows, width = d_n2.shape
    group = 4 * rows
    wrows, wcols = width // S, width // 4
    head_dim = width // H
    heads = H // 4
    wide = 384
    span = -(-wcols // 128) * 128
    skip = wcols - (span - 128)
    tail = width - span + 128
    trio = 3
    third = 2 * trio * head_dim
    thirds = heads // trio
    score_scale = 1.0 / math.sqrt(head_dim)
    widths = (span - 128, span) + (third,) * thirds
    count = len(widths)
    wrows_wide = -(-wrows // 128) * 128

    def kernel(*refs):
        ins, lefts_in, ids_in, outs, mids, own, refs = split_refs(
            refs, 10, 4, 2, 2, count + 3, 20, 100
        )
        (dn2_in, after_in, cot_in, gain_in, w4_in, qkv_in, tok_in, table_in, gu_in, gd_in) = ins
        seq_row, blk_row = ids_in
        gt_out, gain_out = outs
        shared, (gu_cols, gu_all, gd_all) = mids[:count], mids[count:]
        (w4, qkv_, mix, mix_far, n_t, n_far, tok, bias, factors, d_t, d_nat, d_far, ex_send,
         ex_all, ex_far, d_after, own_gain, gain_all, load, side_sem) = own
        f1, f2, u1, u2, u3, (ex_sem, gain_sem), *grads = split_refs(
            refs, 5, 5, 2, 3, 3, 2, *(6,) * count
        )
        place = Place(B)
        r, x, c = place.r, place.x, place.c
        loads = [
            pltpu.make_async_copy(src, dst, load.at[i])
            for i, (src, dst) in enumerate(
                [
                    (tok_in, tok), (w4_in, w4), (lefts_in[0].at[:, place.b], mix),
                    (lefts_in[1], mix_far), (qkv_in, qkv_), (lefts_in[2].at[:, place.b], n_t),
                    (lefts_in[3], n_far),
                ]
            )
        ]
        for copy in loads:
            copy.start()
        part1, part2 = f1[0], f2[0]
        gain_one, gain_two = gain_in[0:1], gain_in[1:2]
        own_gain[...] = jnp.zeros_like(own_gain)
        step = 32

        def back_two(i, carry):
            at = pl.ds(pl.multiple_of(i * step, step), step)
            after = after_in[at, :]
            d = dn2_in[at, :].astype(f32)
            factor = lax.rsqrt(jnp.mean(after * after, axis=1, keepdims=True) + norm_eps)
            own_gain[1:2, :] += jnp.sum(d * after * factor, axis=0, keepdims=True)
            u = d * gain_two
            mean = jnp.mean(u * after, axis=1, keepdims=True)
            d_after[at, :] = (
                cot_in[at, :].astype(f32) + factor * u - after * (factor * factor * factor) * mean
            )
            return carry

        lax.fori_loop(0, rows // step, back_two, 0)
        d_proj = (branch_scale * d_after[...]).astype(bf)
        for k in range(4):
            at = k * wcols // 128 * 128
            ex_send[k] = product(
                d_proj[:, at : at + span], select(span, span, k * wcols - at, 0, wcols)
            ).astype(bf)
        ex_all[r] = ex_send[r]
        greet(place, True, True, True)
        exchange = []
        for k in (2, 3, 1):
            to = (r + k) % 4
            exchange.append(
                remote(
                    ex_send.at[to], ex_all.at[r], ex_sem.at[k, 0], ex_sem.at[k, 1],
                    (place.s, to),
                )
            )
            exchange[-1].start()

        def at_head(part, n):
            return pl.ds(pl.multiple_of(part * wcols + n * head_dim, 64), head_dim)

        def probs_of(n):
            scores = across(qkv_[at_head(2, n), :], qkv_[at_head(1, n), :]) * score_scale
            scores = scores + bias[...].astype(f32)
            powers = jnp.exp(scores - jnp.max(scores, axis=0, keepdims=True))
            return powers * (1.0 / jnp.sum(powers, axis=0, keepdims=True))

        def aside(src, dst, i):
            return [
                remote(
                    src, dst(k - 1), side_sem.at[i, k, 0], side_sem.at[i, k, 1],
                    place.side((place.b + k) % B),
                )
                for k in range(1, B)
            ]

        def lanes(i):
            return pl.ds(0, span) if i == 1 else pl.ds(span + (i - 2) * third, third)

        def aside_of(i):
            if i == 0:
                return aside(ex_all, lambda k: ex_far.at[k], 0)
            return aside(d_nat.at[:, lanes(i)], lambda k: d_far.at[k, :, lanes(i)], i)

        def compute():
            _, allowed = masks(seq_row, blk_row)
            bias[...] = jnp.where(allowed, 0.0, masked_score).astype(bf)
            for i in range(4):
                loads[0].wait() if i == 0 else None
                value = tok[i].astype(f32)
                factors[i * rows : (i + 1) * rows, :] = lax.rsqrt(
                    jnp.mean(value * value, axis=1, keepdims=True) + norm_eps
                )
            for copy in exchange:
                copy.wait()
            for copy in aside_of(0):
                copy.start()
            for copy in loads[1:]:
                copy.wait()
            d_proj = ex_all[...].reshape(group, span)
            for i in (1 - c, c):
                for side in range(X):
                    k = side * X + i
                    at = pl.ds(pl.multiple_of(k * wcols, 64), wcols)
                    part1[k] = against(w4[at, :span], d_proj).astype(bf)
            yield

            def values_back(n, carry):
                d_m = part1[r, pl.ds(pl.multiple_of(n * head_dim, 64), head_dim), :]
                value = against(d_m, probs_of(n).astype(bf))
                at = pl.ds(pl.multiple_of(skip + n * head_dim, 64), head_dim)
                d_t[at, :] = value.astype(bf)
                return carry

            def flip(n, carry):
                at = pl.ds(pl.multiple_of(n * 128, 128), 128)
                d_nat[:, at] = d_t[at, :].astype(f32).T.astype(bf)
                return carry

            d_t[:skip, :] = jnp.zeros((skip, group), bf)
            for k in range(thirds):
                lax.fori_loop(trio * k, trio * (k + 1), values_back, 0)
                if k + 1 < thirds:
                    yield
            lax.fori_loop(0, span // 128, flip, 0)
            for copy in aside_of(1):
                copy.start()
            yield
            cosine, sine = table_in[0], table_in[1]
            half = head_dim // 2

            def turn_back(value, at):
                former, latter = value[:half], value[half:]
                d_t[pl.ds(at, half), :] = (former * cosine + latter * sine).astype(bf)
                d_t[pl.ds(at + half, half), :] = (latter * cosine - former * sine).astype(bf)

            def scores_back(n, carry):
                d_m = part1[r, pl.ds(pl.multiple_of(n * head_dim, 64), head_dim), :]
                probs = probs_of(n)
                d_probs = across(qkv_[at_head(0, n), :], d_m)
                d_s = probs * (d_probs - jnp.sum(d_probs * probs, axis=0, keepdims=True))
                d_s = d_s.astype(bf)
                at = span + n // trio * third + n % trio * head_dim
                turn_back(
                    product(qkv_[at_head(2, n), :], d_s) * score_scale, pl.multiple_of(at, 64)
                )
                turn_back(
                    against(qkv_[at_head(1, n), :], d_s) * score_scale,
                    pl.multiple_of(at + third // 2, 64),
                )
                return carry

            for k in range(thirds):
                lax.fori_loop(trio * k, trio * (k + 1), scores_back, 0)
                first = (span + third * k) // 128
                lax.fori_loop(first, first + third // 128, flip, 0)
                for copy in aside_of(2 + k):
                    copy.start()
                yield

            def inputs_back(n, carry):
                at = pl.ds(pl.multiple_of(n * wide, 128), wide)
                value = against(d_nat[...], w4[at, pl.ds(span - 128, tail)])
                x_f = tok[:, :, at].reshape(group, wide).astype(f32) * factors[...]
                own_gain[0:1, at] = jnp.sum(value * x_f, axis=0, keepdims=True)
                part2[:, :, at] = value.astype(bf).reshape(4, rows, wide)
                return carry

            lax.fori_loop(0, width // wide, inputs_back, 0)

        def make(i):
            def produce(d):
                if i == 0:
                    own, far, right = mix, mix_far, ex_all[:, :, : span - 128]
                    right = right.reshape(group, span - 128)
                else:
                    own, far, right = n_t, n_far, d_nat[:, lanes(i)]
                total = product(own[d], right)
                for k in range(B - 1):
                    if i == 0:
                        right = ex_far[k, :, :, : span - 128].reshape(group, span - 128)
                    else:
                        right = d_far[k, :, lanes(i)]
                    total += product(far[k, d], right)
                if i == 1:
                    last = product(mix[d], ex_all[:, :, span - 128 :].reshape(group, 128))
                    for k in range(B - 1):
                        right = ex_far[k, :, :, span - 128 :].reshape(group, 128)
                        last += product(mix_far[k, d], right)
                    total = jnp.concatenate([total[:, :128] + last, total[:, 128:]], axis=1)
                return total.astype(bf)

            return produce

        def grad(i):
            for copy in aside_of(i):
                copy.wait_recv()
            yield from grad_flow(place, make(i), shared[i], grads[i])
            for copy in aside_of(i):
                copy.wait_send()

        def gains_flow():
            def send(i, device):
                return remote(
                    own_gain, gain_all.at[i], gain_sem.at[i, 0], gain_sem.at[i, 1], device
                )

            stages = [
                [place.over_core], [place.over_x],
                [place.side((place.b + k) % B) for k in range(1, B)],
                [place.line((place.a + k) % A) for k in range(1, A)],
            ]
            at = 0
            for stage in stages:
                copies = [send(at + i, device) for i, device in enumerate(stage)]
                for copy in copies:
                    copy.start()
                yield
                for copy in copies:
                    copy.wait()
                for i in range(len(stage)):
                    own_gain[...] += gain_all[at + i]
                at += len(stage)
            for n in range(width // wide):
                own = slice(n * wide, (n + 1) * wide)
                total = own_gain[:, own]
                pick = select(wide, wrows_wide, place.s * wrows - n * wide, 0, wrows)
                value = jnp.zeros((8, wrows_wide), f32)
                for _ in range(3):
                    low = total.astype(bf)
                    value += product(low, pick)
                    total = total - low.astype(f32)
                gain_out[...] = value if n == 0 else gain_out[...] + value

        def input_end():
            def back_one(i, carry):
                at = pl.ds(pl.multiple_of(i * step, step), step)
                value = tok[r, at, :].astype(f32)
                d = part2[r, at, :].astype(f32)
                factor = lax.rsqrt(jnp.mean(value * value, axis=1, keepdims=True) + norm_eps)
                u = d * gain_one
                mean = jnp.mean(u * value, axis=1, keepdims=True)
                gt_out[at, :] = (
                    d_after[at, :] + factor * u - value * (factor * factor * factor) * mean
                ).astype(bf)
                return carry

            lax.fori_loop(0, rows // step, back_one, 0)
            yield

        M, F1, F2, GU, SU, SD, G, T, O, V, P, Q, R = range(13)
        flows = [
            compute(),
            fold_flow(place, f1),
            fold_flow(place, f2),
            owners_flow(place, gu_in, gu_cols, u1),
            share_flow(place, gu_cols, gu_all, u2),
            share_flow(place, gd_in, gd_all, u3),
            gains_flow(),
            input_end(),
        ] + [grad(i) for i in range(count)]
        turns = [
            GU, M, F1, F1, F1, F1, SD, O, O, M, M, M, GU, SU, M, O, V, M, O, V, M, O, V, P, M, SD,
            F2, V, P, Q, F2, V, P, Q, R, O, SU, P, Q, R, F2, F2, T, P, Q, R, O, V, Q, R, G, SD, SU,
            V, R, O, P, V, G, R, G, R, G, R, G,
        ]
        run_flows(flows, turns)

    block = (rows, width)
    left = (wrows, group)
    return call(
        kernel, "attention_backward", 3,
        [shape(*block), shape(8, wrows_wide, dtype=f32)]
        + [shape(4, wrows, w) for w in widths]
        + [shape(*g_gate_up.shape), shape(4, *g_gate_up.shape), shape(4, *g_down.shape)],
        [VMEM, VMEM] + [ANY] * (count + 3),
        [
            pltpu.VMEM((width, width), bf), pltpu.VMEM((3 * wcols, group), bf),
            pltpu.VMEM((A,) + left, bf), pltpu.VMEM((B - 1, A) + left, bf),
            pltpu.VMEM((A,) + left, bf), pltpu.VMEM((B - 1, A) + left, bf),
            pltpu.VMEM((4,) + block, bf), pltpu.VMEM((group, group), bf),
            pltpu.VMEM((group, 1), f32), pltpu.VMEM((tail, group), bf),
            pltpu.VMEM((group, tail), bf), pltpu.VMEM((B - 1, group, tail), bf),
            pltpu.VMEM((4, rows, span), bf), pltpu.VMEM((4, rows, span), bf),
            pltpu.VMEM((B - 1, 4, rows, span), bf), pltpu.VMEM(block, f32),
            pltpu.VMEM((8, width), f32), pltpu.VMEM((A + B, 8, width), f32), DMA((7,)),
            DMA((count, B, 2)),
        ]
        + fold_scratch(wcols, group) + fold_scratch(*block)
        + [DMA((A, 2)), DMA((1,))] + share_sems() + share_sems()
        + [DMA((4, 2)), DMA((A + B, 2))]
        + [v for w in widths for v in grad_scratch(wrows, w)],
        [
            d_n2, after_attn, cotangent, gains, w4, qkv, tokens, tables, g_gate_up, g_down,
            *lefts, *ids,
        ],
        [VMEM] * 4 + [ANY] * 3 + [VMEM] + [ANY] * 6 + [VMEM] * 2,
    )


def lay_out(S, ff, width, out, value, groups, gate_up, down, after_attn, ffn_out):
    wrows, span = value.shape[1:]
    tokens = after_attn.shape[0]
    wcols = width // 4
    pair = 2 * wcols
    skip = wcols - (span - 128)
    sub = ff // (S * 4)
    pad = down.shape[1]
    fcols = gate_up.shape[3] // 2
    B = fcols // pad
    drows = ff // S
    steps = 3 if wrows % (3 * 16) == 0 else 1
    rows, cols = wrows // steps, width // steps

    def kernel(o_in, v_in, *refs):
        g_in, ins, outs = split_refs(refs, len(groups), 4, 8)
        gu_in, d_in, after_in, f_in = ins
        o_out, q_out, k_out, v_out, g_out, u_out, d_out, r_out = outs
        r_out[...] = (after_in[...] + branch_scale * f_in[...].astype(f32)).astype(bf)

        def beside(pieces, to):
            for side in range(2):
                parts = [
                    ref[side * 2 + core].astype(f32)[:, at : at + size]
                    for core in range(2) for ref, at, size in pieces
                ]
                to[:, side * pair : (side + 1) * pair] = jnp.concatenate(parts, axis=1)

        half = groups[0].shape[2] // 2
        beside([(o_in, 0, wcols - skip), (v_in, 0, skip)], o_out)
        beside([(v_in, skip, wcols)], v_out)
        beside([(ref, 0, half) for ref in g_in], q_out)
        beside([(ref, half, half) for ref in g_in], k_out)
        for i, to in enumerate((g_out, u_out)):
            parts = []
            for m in range(4 * S):
                s = m // 4
                at = i * fcols + s % B * pad
                parts.append(gu_in[m % 4, s // B].astype(f32)[:, at : at + sub])
            to[...] = jnp.concatenate(parts, axis=1)
        d_out[...] = jnp.concatenate([d_in[k].astype(f32)[:sub] for k in range(4)], axis=0)

    def by_rows(ref):
        lead = len(ref.shape) - 2
        return pl.BlockSpec(
            ref.shape[:lead] + (rows, ref.shape[-1]), lambda i: (0,) * lead + (i, 0)
        )

    outs = [shape(wrows, width, dtype=f32)] * 4 + [shape(wrows, ff, dtype=f32)] * 2
    return pl.pallas_call(
        kernel,
        grid=(steps,),
        out_shape=outs + [shape(drows, width, dtype=f32), shape(tokens, width)],
        in_specs=[by_rows(v) for v in (out, value, *groups, gate_up)]
        + [pl.BlockSpec((4, pad, cols), lambda i: (0, 0, i))]
        + [pl.BlockSpec((tokens, cols), lambda i: (0, i))] * 2,
        out_specs=[by_rows(v) for v in outs]
        + [pl.BlockSpec((n, cols), lambda i: (0, i)) for n in (drows, tokens)],
        name="lay_out",
        compiler_params=pltpu.CompilerParams(vmem_limit_bytes=60 * 2**20),
    )(out, value, *groups, gate_up, down, after_attn, ffn_out)


def product(left_side, right_side):
    return jnp.dot(left_side, right_side, preferred_element_type=f32)


def against(left_side, right_side):
    return lax.dot_general(
        left_side, right_side, (((1,), (1,)), ((), ())), preferred_element_type=f32
    )


def across(left_side, right_side):
    return lax.dot_general(
        left_side, right_side, (((0,), (0,)), ((), ())), preferred_element_type=f32
    )


def body(
    tokens,
    attn_gain,
    w_query,
    w_key,
    w_value,
    w_out,
    ffn_gain,
    w_gate,
    w_up,
    w_down,
    seq_ids,
    block_ids,
    cotangent,
):
    S = lax.axis_size("shard")
    R = lax.axis_size("replica")
    B = S // A
    rows, width = tokens.shape
    ff = w_gate.shape[1]
    wrows = width // S
    ids = (seq_ids[None, :], block_ids[None, :])
    gains = jnp.pad(jnp.stack([attn_gain, ffn_gain]), ((0, 6), (0, 0)))
    (
        w4, gains, tokens_group, d_down, gate_up, down_w, qkv, mixed_all, after_attn, normed_two,
        tables, normed_t,
    ) = attention_forward(
        B, [w_out, w_value, w_query, w_key], [w_gate, w_up], w_down, gains, tokens, cotangent, ids
    )
    lefts = [v.reshape(A, B, wrows, -1) for v in (mixed_all, normed_t)]
    d_n2, ffn_out, g_gate_up, g_down, mixed_far, normed_far = feed_forward(
        B, normed_two, d_down, gate_up.reshape(width, -1), down_w.reshape(-1, width), lefts
    )
    grad_tokens, gain_sums, g_out, g_value, *parts = attention_backward(
        B, S, d_n2, after_attn, cotangent, gains, w4.reshape(width, width), qkv, tokens_group,
        [lefts[0], mixed_far, lefts[1], normed_far], tables, ids, g_gate_up, g_down,
    )
    g_out, g_query, g_key, g_value, g_gate, g_up, g_down, result = lay_out(
        S, ff, width, g_out, g_value, parts[:-3], *parts[-2:], after_attn, ffn_out
    )
    return (
        result, grad_tokens, gain_sums[0, :wrows], g_query, g_key, g_value, g_out,
        gain_sums[1, :wrows], g_gate, g_up, g_down,
    )


def solution(mesh):
    split = P(("shard", "replica"), None)
    vec, mat = P("shard"), P("shard", None)
    in_specs = (split, vec, mat, mat, mat, mat, vec, mat, mat, mat, vec, vec, split)
    out_specs = (split, split, vec, mat, mat, mat, mat, vec, mat, mat, mat)
    return jax.shard_map(body, mesh=mesh, in_specs=in_specs, out_specs=out_specs, check_vma=False)
```

```python
import functools
import math

import jax
import jax.numpy as jnp
from jax import lax
from jax.experimental import pallas as pl
from jax.experimental.pallas import tpu as pltpu
from jax.sharding import PartitionSpec as P

H = 36
A = 4
X = 2

branch_scale = 1.4 / math.sqrt(40.0)
norm_eps = 1e-05
rope_base = 10000.0
masked_score = -1e30
MESH = pl.DeviceIdType.MESH
bf = jnp.bfloat16
f32 = jnp.float32
DMA = pltpu.SemaphoreType.DMA


class Place:
    def __init__(self, B):
        self.B = B
        s, r = lax.axis_index("shard"), lax.axis_index("replica")
        self.s, self.r = s, r
        self.a, self.b = s // B, s % B
        self.x, self.c = r // X, r % X
        self.rx = (1 - self.x) * X + self.c
        self.rc = self.x * X + 1 - self.c

    def line(self, a):
        return (a * self.B + self.b, self.r)

    def side(self, b):
        return (self.a * self.B + b, self.r)

    @property
    def over_x(self):
        return (self.s, self.rx)

    @property
    def over_core(self):
        return (self.s, self.rc)


def greet(place, a_peers=True, b_peers=False, r_peers=True):
    barrier = pltpu.get_barrier_semaphore()
    devices = []
    if a_peers:
        devices += [place.line((place.a + k) % A) for k in range(1, A)]
    if b_peers:
        devices += [place.side((place.b + k) % place.B) for k in range(1, place.B)]
    if r_peers:
        devices += [(place.s, (place.r + k) % 4) for k in range(1, 4)]
    for device in devices:
        pl.semaphore_signal(barrier, inc=1, device_id=device, device_id_type=MESH)
    return lambda: pl.semaphore_wait(barrier, len(devices))


def remote(src, dst, send, recv, device):
    return pltpu.make_async_remote_copy(
        src_ref=src, dst_ref=dst, send_sem=send, recv_sem=recv, device_id=device,
        device_id_type=MESH,
    )


def add_into(dst, first, second, tile=32):
    rows = dst.shape[0]
    tile = math.gcd(rows, tile) if math.gcd(rows, tile) >= 16 else rows

    def step(i, carry):
        at = pl.ds(pl.multiple_of(i * tile, tile), tile)
        dst[at, :] = (first[at, :].astype(f32) + second[at, :].astype(f32)).astype(dst.dtype)
        return carry

    lax.fori_loop(0, rows // tile, step, 0)


def run_flows(flows, turns=()):
    ended = set()

    def step(at):
        if at not in ended:
            try:
                next(flows[at])
            except StopIteration:
                ended.add(at)

    for at in turns:
        step(at)
    while len(ended) < len(flows):
        for at in range(len(flows)):
            step(at)


def halves(rows):
    return 2 if rows % 32 == 0 else 1


def piece(ref, at, h, parts):
    if parts == 1:
        return ref.at[at]
    rows = ref.shape[-2] // parts
    index = at if isinstance(at, tuple) else (at,)
    return ref.at[index + (pl.ds(h * rows, rows),)]


def widen_sems():
    return [DMA((A,)), DMA((X,)), DMA((A, 2)), DMA((A, 2)), DMA((X, A, 2)), DMA((1,))]


def widen_flow(place, own, out, sems):
    line_recv, _, line_send, over_x, over_core, local = sems
    a, x, c = place.a, place.x, place.c
    keep = pltpu.make_async_copy(own, out.at[x, a, c], local.at[0])
    keep.start()

    def to_line(src, block, way):
        at = 0 if way > 0 else 1
        return remote(
            src, out.at[x, block, c], line_send.at[block, at], line_recv.at[block],
            place.line(a + way),
        )

    def to_x(src, block):
        return remote(
            src, out.at[x, block, c], over_x.at[block, 0], over_x.at[block, 1], place.over_x
        )

    def to_core(src, side, block):
        return remote(
            src, out.at[side, block, c], over_core.at[side, block, 0],
            over_core.at[side, block, 1], place.over_core,
        )

    @pl.when(a < A - 1)
    def _():
        to_line(own, a, 1).start()

    @pl.when(a > 0)
    def _():
        to_line(own, a, -1).start()

    to_x(own, a).start()
    to_core(own, x, a).start()

    def pass_x(k):
        for ok, block in ((a - k >= 0, a - k), (a + k < A, a + k)) if k else ((None, a),):
            def go():
                src = out.at[1 - x, block, c]
                to_x(src, block).wait_recv()
                to_core(src, 1 - x, block).start()

            go() if ok is None else pl.when(ok)(go)

    for k in range(1, A):
        yield
        for way in (1, -1):
            block = a - way * k

            @pl.when((block >= 0) & (block < A))
            def _():
                src = out.at[x, block, c]
                to_line(src, block, way).wait_recv()

                @pl.when((a + way >= 0) & (a + way < A))
                def _():
                    to_line(src, block, way).start()

                to_x(src, block).start()
                to_core(src, x, block).start()

        yield
        pass_x(k - 1)
    yield
    pass_x(A - 1)
    yield
    keep.wait()
    for block in range(A):
        src = out.at[x, block, c]

        @pl.when((a < A - 1) & (block <= a))
        def _():
            to_line(src, block, 1).wait_send()

        @pl.when((a > 0) & (block >= a))
        def _():
            to_line(src, block, -1).wait_send()

        to_x(src, block).wait_send()
        for side in range(X):
            to_core(src, side, block).wait()


def shrink_scratch(rows, width):
    block = (rows, width)
    P_ = halves(rows)
    return [
        pltpu.VMEM((X, A) + block, bf),
        pltpu.VMEM((X, A) + block, bf),
        pltpu.VMEM((A,) + block, bf),
        pltpu.VMEM((A + 1,) + block, bf),
        DMA((X, A, P_)), DMA((X, A, P_, 2)), DMA((A, P_, 2)), DMA((2, A, P_, 2)),
    ]


def far_first(a, i):
    inner = (3, 0, 2, 1)[i]
    return jnp.where(a == 0, 3 - i, jnp.where(a == 1, inner, jnp.where(a == 2, 3 - inner, i)))


def line_slots(place, sums, landing, sems, parts, ready, final, near=False):
    a = place.a
    last = 2 * A - 3 if near else A - 1

    def part(ref, h):
        if parts == 1:
            return ref
        rows = ref.shape[0] // parts
        return ref.at[pl.ds(h * rows, rows)]

    def hop(d, h, way):
        at = 0 if way > 0 else 1
        return remote(
            part(sums(d), h), part(landing(d, way), h), sems.at[at, d, h, 0],
            sems.at[at, d, h, 1], place.line(a + way),
        )

    def take(d, h, way):
        @pl.when((a - way >= 0) & (a - way < A))
        def _():
            hop(d, h, way).wait_recv()
            here = part(sums(d), h)
            add_into(here, here, part(landing(d, way), h))

    for t in range(last + 1):
        for way in (1, -1):
            at = a if way > 0 else A - 1 - a
            to = t - at + 1 if near else A - 1 - t + at
            d = to if way > 0 else A - 1 - to

            @pl.when((to > at) & (to < A))
            def _():
                for h in range(parts):
                    ready(d, h)
                    take(d, h, way)
                    hop(d, h, way).start()

        if t == last:
            for h in range(parts):
                ready(a, h)
                take(a, h, 1)
                take(a, h, -1)
                final(h)
        yield
    for d in range(A):
        for h in range(parts):
            for way in (1, -1):
                @pl.when((d - a) * way > 0)
                def _():
                    hop(d, h, way).wait_send()


def share_sems():
    return [DMA((2,)), DMA((X, 2)), DMA((1,))]


def share_flow(place, own, out, sems, ready=None):
    x_sem, core_sem, local = sems
    r, x, c = place.r, place.x, place.c
    if ready is not None:
        yield
        ready()
    keep = pltpu.make_async_copy(own, out.at[r], local.at[0])
    to_x = remote(own, out.at[r], x_sem.at[0], x_sem.at[1], place.over_x)
    near = remote(own, out.at[r], core_sem.at[x, 0], core_sem.at[x, 1], place.over_core)
    far = remote(
        out.at[place.rx], out.at[place.rx], core_sem.at[1 - x, 0], core_sem.at[1 - x, 1],
        place.over_core,
    )
    to_x.start()
    near.start()
    keep.start()
    yield
    to_x.wait_recv()
    far.start()
    yield
    keep.wait()
    to_x.wait_send()
    near.wait()
    far.wait()


def spread_sems(B, parts=1):
    return [DMA((A, parts)), DMA((A, 2, parts)), DMA((B, A, parts, 2)), DMA((1,))]


def spread_flow(place, own, out, sems, parts=1):
    line_recv, line_send, side, local = sems
    a, b, B = place.a, place.b, place.B
    keep = pltpu.make_async_copy(own, out.at[a, b], local.at[0])
    keep.start()

    def half(h):
        return own if parts == 1 else own.at[pl.ds(h * own.shape[0] // parts, own.shape[0] // parts)]

    def to_line(src, block, h, way):
        return remote(
            src, piece(out, (block, b), h, parts), line_send.at[block, 0 if way > 0 else 1, h],
            line_recv.at[block, h], place.line(a + way),
        )

    def to_side(src, block, h, k):
        return remote(
            src, piece(out, (block, b), h, parts), side.at[k, block, h, 0],
            side.at[k, block, h, 1], place.side((b + k) % B),
        )

    for h in range(parts):
        @pl.when(a < A - 1)
        def _():
            to_line(half(h), a, h, 1).start()

        @pl.when(a > 0)
        def _():
            to_line(half(h), a, h, -1).start()

        for k in range(1, B):
            to_side(half(h), a, h, k).start()
    for step in range(1, A):
        for h in range(parts):
            yield
            for way in (1, -1):
                block = a - way * step

                @pl.when((block >= 0) & (block < A))
                def _():
                    src = piece(out, (block, b), h, parts)
                    to_line(src, block, h, way).wait_recv()

                    @pl.when((a + way >= 0) & (a + way < A))
                    def _():
                        to_line(src, block, h, way).start()

                    for k in range(1, B):
                        to_side(src, block, h, k).start()

    yield
    keep.wait()
    for block in range(A):
        for h in range(parts):
            src = piece(out, (block, b), h, parts)

            @pl.when((a < A - 1) & (block <= a))
            def _():
                to_line(src, block, h, 1).wait_send()

            @pl.when((a > 0) & (block >= a))
            def _():
                to_line(src, block, h, -1).wait_send()

            for k in range(1, B):
                to_side(src, block, h, k).wait()


def columns_sems(B):
    return [DMA((A, 2)), DMA((B, A, 2)), DMA((1,))]


def columns_flow(place, own, out, sems):
    line, side, local = sems
    a, b, B = place.a, place.b, place.B
    keep = pltpu.make_async_copy(own.at[a], out.at[a, b], local.at[0])
    keep.start()

    def to_line(k):
        to = (a + k) % A
        return remote(own.at[to], out.at[a, b], line.at[k, 0], line.at[k, 1], place.line(to))

    def to_side(src, block, k):
        return remote(
            src, out.at[block, b], side.at[k, block, 0], side.at[k, block, 1],
            place.side((b + k) % B),
        )

    for k in range(1, A):
        to_line(k).start()
    for k in range(1, B):
        to_side(own.at[a], a, k).start()
    for k in (1, 3, 2):
        yield
        to_line(k).wait_recv()
        block = (a + A - k) % A
        for j in range(1, B):
            to_side(out.at[block, b], block, j).start()
    yield
    keep.wait()
    for k in range(1, A):
        to_line(k).wait_send()
    for block in range(A):
        for k in range(1, B):
            to_side(out.at[block, b], block, k).wait()


def sides_sems(B):
    return [DMA((B, 2)), DMA((1,))]


def sides_flow(place, own, out, sems):
    side, local = sems
    b, B = place.b, place.B
    keep = pltpu.make_async_copy(own, out.at[b], local.at[0])
    keep.start()
    copies = [
        remote(own, out.at[b], side.at[k, 0], side.at[k, 1], place.side((b + k) % B))
        for k in range(1, B)
    ]
    for copy in copies:
        copy.start()
    yield
    keep.wait()
    for copy in copies:
        copy.wait()


ANY = pl.BlockSpec(memory_space=pl.ANY)
VMEM = pl.BlockSpec(memory_space=pltpu.VMEM)


def call(kernel, name, collective_id, outs, out_specs, scratch, args, in_specs):
    return pl.pallas_call(
        kernel,
        out_shape=outs,
        in_specs=in_specs,
        out_specs=out_specs,
        scratch_shapes=scratch,
        name=name,
        compiler_params=pltpu.CompilerParams(
            collective_id=collective_id, has_side_effects=True, vmem_limit_bytes=63 * 2**20
        ),
    )(*args)


def shape(*dims, dtype=bf):
    return jax.ShapeDtypeStruct(dims, dtype)


def split_refs(refs, *sizes):
    found, at = [], 0
    for size in sizes:
        found.append(refs[at : at + size])
        at += size
    return found


def select(rows, cols, shift, at, width):
    j = lax.broadcasted_iota(jnp.int32, (1, cols), 1) - at
    wanted = jnp.where((j >= 0) & (j < width), j + shift, -1)
    row = lax.broadcasted_iota(jnp.int32, (rows, cols), 0)
    return jnp.where(row == wanted, 1.0, 0.0).astype(bf)


def select_mixed(rows, cols, shift, j, part):
    col = lax.broadcasted_iota(jnp.int32, (1, cols), 1)
    wanted = jnp.where(
        col // part % 2 == j, shift + col // (2 * part) * part + col % part, -1
    )
    row = lax.broadcasted_iota(jnp.int32, (rows, cols), 0)
    return jnp.where(row == wanted, 1.0, 0.0).astype(bf)


def masks(seq_row, blk_row):
    def columns(ref):
        row = ref[...].astype(f32)
        return row, jnp.broadcast_to(row, (8, row.shape[1])).T[:, :1]

    seq, seq_t = columns(seq_row)
    blk, blk_t = columns(blk_row)
    return seq_t < seq, (seq_t == seq) & (blk_t <= blk)


def rope(ref, at, cosine, sine, out, to, head_dim):
    half = head_dim // 2
    former, latter = ref[pl.ds(at, half), :], ref[pl.ds(at + half, half), :]
    out[pl.ds(to, half), :] = (former * cosine - latter * sine).astype(out.dtype)
    out[pl.ds(to + half, half), :] = (latter * cosine + former * sine).astype(out.dtype)


def attention_forward(B, weights, gates, w_down, gains, tokens, cotangent, ids):
    wrows, width = weights[0].shape
    rows = tokens.shape[0]
    group = 4 * rows
    ff = gates[0].shape[1]
    wcols = width // 4
    head_dim = width // H
    heads = H // 4
    sub = ff // (A * B * 4)
    pad = -(-sub // 16) * 16
    fcols = B * pad
    wide = 384
    span = -(-wcols // 128) * 128
    pair = 2 * wcols
    parts = halves(wrows)
    trio = 3
    score_scale = 1.0 / math.sqrt(head_dim)

    def kernel(*refs):
        w_in, g_in, ins, outs, scratch, refs = split_refs(refs, 4, 2, 6, 12, 19, 100)
        wd_in, gain_in, tok_in, cot_in, seq_row, blk_row = ins
        (w4_out, gain_out, tok_out, d_out, gu_out, dn_out, qkv_out, mixed_out, after_out,
         n2_out, table_out, nt_out) = outs
        (w_all, g_all, wd_all, own4, gu_own, dn_own, own_gain, gain_all, tok_all, d_own, w4_all,
         normed, normed_t, raw, bias, mixed, proj, proj_all, load) = scratch
        s1, s2, s3, s4, s5, s6, s7 = split_refs(refs, 4, 4, 3, 6, 3, 2, 100)
        qkv, mix_x, mix_core, ex_sem, save = s7
        place = Place(B)
        met = greet(place, True, True, True)
        r, x, c = place.r, place.x, place.c
        loads = [pltpu.make_async_copy(w, w_all.at[i], load.at[i]) for i, w in enumerate(w_in)]
        loads += [
            pltpu.make_async_copy(w, g_all.at[i], load.at[4 + i]) for i, w in enumerate(g_in)
        ]
        loads.append(pltpu.make_async_copy(wd_in, wd_all, load.at[6]))
        for copy in loads:
            copy.start()
        start = pl.multiple_of(r * wcols // 128 * 128, 128)
        shift = r * wcols - start
        for i in range(2):
            total = jnp.zeros((wrows, pair), f32)
            for j in range(2):
                loads[2 * i + j].wait()
                pick = select(span, pair, shift, j * wcols, wcols)
                if i:
                    pick = select_mixed(span, pair, shift, j, trio * head_dim)
                total += product(w_all[2 * i + j, :, pl.ds(start, span)], pick)
            own4[:, i * pair : (i + 1) * pair] = total.astype(bf)
        for k in range(width // wide):
            own_gain[:, k * wide : (k + 1) * wide] = jnp.dot(
                gain_in[...], select(wrows, wide, 0, place.s * wrows - k * wide, wrows),
                preferred_element_type=f32,
            )
        met()

        def prepare():
            for i in range(2):
                loads[4 + i].wait()
            loads[6].wait()

            def one(n, carry):
                i, block = n // A, n % A
                total = jnp.zeros((wrows, fcols), f32)
                for j in range(B):
                    first = ((block * B + j) * 4 + r) * sub
                    at = pl.multiple_of(jnp.minimum(first // 128 * 128, ff - wide), 128)
                    total += jnp.dot(
                        g_all[i, :, pl.ds(at, wide)],
                        select(wide, fcols, first - at, j * pad, sub),
                        preferred_element_type=f32,
                    )
                at = pl.multiple_of(i * fcols, 128)
                gu_own[block, :, pl.ds(at, fcols)] = total.astype(bf)
                return carry

            lax.fori_loop(0, 2 * A, one, 0)
            row = lax.broadcasted_iota(jnp.int32, (pad, ff // (A * B)), 0)
            col = lax.broadcasted_iota(jnp.int32, (pad, ff // (A * B)), 1)
            pick = jnp.where((col - r * sub == row) & (row < sub), 1.0, 0.0).astype(bf)
            tile = 768

            def down(n, carry):
                at = pl.ds(pl.multiple_of(n * tile, tile), tile)
                dn_own[:, at] = jnp.dot(
                    pick, wd_all[:, at], preferred_element_type=f32
                ).astype(bf)
                return carry

            lax.fori_loop(0, width // tile, down, 0)
            d_own[...] = (branch_scale * cot_in[...].astype(f32)).astype(bf)
            less, allowed = masks(seq_row, blk_row)
            earlier = jnp.sum(jnp.where(less, 1.0, 0.0), axis=0, keepdims=True)
            at = lax.broadcasted_iota(jnp.int32, (1, group), 1).astype(f32) - earlier
            half = head_dim // 2
            index = lax.broadcasted_iota(jnp.int32, (half, group), 0).astype(f32)
            angle = at * jnp.exp(index * (-2.0 * math.log(rope_base) / head_dim))
            table_out[0] = jnp.cos(angle)
            table_out[1] = jnp.sin(angle)
            bias[...] = jnp.where(allowed, 0.0, masked_score)
            yield
            total = jnp.zeros((8, width), f32)
            for block in range(A):
                for side in range(B):
                    total += gain_all[block, side]
            gain_out[...] = total
            for i in range(4):
                value = tok_all[i].astype(f32)
                factor = lax.rsqrt(jnp.mean(value * value, axis=1, keepdims=True) + norm_eps)
                value = value * factor * total[0:1]
                at = slice(i * rows, (i + 1) * rows)
                normed[at, :] = value.astype(bf)
                normed_t[:, at] = value.T.astype(bf)
            early = [
                pltpu.make_async_copy(normed_t, nt_out, load.at[1]),
                pltpu.make_async_copy(tok_all, tok_out, load.at[2]),
            ]
            for copy in early:
                copy.start()
            yield
            for copy in early:
                copy.wait()

        def share_piece(k):
            at = pl.ds(k * trio * head_dim, trio * head_dim)
            own = mixed.at[r, at]
            far = mixed.at[place.rx, at]
            return (
                remote(own, own, mix_x.at[k, 0], mix_x.at[k, 1], place.over_x),
                remote(own, own, mix_core.at[x, k, 0], mix_core.at[x, k, 1], place.over_core),
                remote(
                    far, far, mix_core.at[1 - x, k, 0], mix_core.at[1 - x, k, 1],
                    place.over_core,
                ),
            )

        pieces = heads // trio

        def attend():
            step = 256

            def project(n, carry):
                cols = pl.ds(pl.multiple_of(span - 128 + n * step, 128), step)
                w = w4_all[:, :, :, cols].reshape(width, step)
                at = pl.ds(pl.multiple_of(n * step, step), step)
                raw[at, :] = product(normed[...], w).T
                return carry

            lax.fori_loop(0, (width - span + 128) // step, project, 0)
            skip = wcols - (span - 128)
            cosine, sine = table_out[0], table_out[1]

            def turn(n, carry):
                at = pl.multiple_of(wcols + n * head_dim, 32)
                i, h = n // heads, n % heads
                first = skip + wcols + (h // trio * 2 + i) * trio * head_dim + h % trio * head_dim
                rope(raw, pl.multiple_of(first, 32), cosine, sine, qkv, at, head_dim)
                return carry

            lax.fori_loop(0, 2 * heads, turn, 0)
            qkv[:wcols, :] = raw[pl.ds(skip, wcols), :].astype(bf)
            pltpu.make_async_copy(qkv, qkv_out, save.at[0]).start()
            yield

            def head(n, carry):
                at = lambda part: pl.ds(pl.multiple_of(part * wcols + n * head_dim, 64), head_dim)
                scores = across(qkv[at(2), :], qkv[at(1), :]) * score_scale + bias[...]
                top = jnp.max(scores, axis=0, keepdims=True)
                powers = jnp.exp(scores - top)
                probs = powers * (1.0 / jnp.sum(powers, axis=0, keepdims=True))
                mixed[r, at(0), :] = product(qkv[at(0), :], probs.astype(bf)).astype(bf)
                return carry

            for k in range(pieces):
                lax.fori_loop(k * trio, (k + 1) * trio, head, 0)
                to_x, near, far = share_piece(k)
                to_x.start()
                near.start()
                if k:
                    to_x, near, far = share_piece(k - 1)
                    to_x.wait_recv()
                    far.start()
                yield
            to_x, near, far = share_piece(pieces - 1)
            to_x.wait_recv()
            far.start()
            for k in range(pieces):
                to_x, near, far = share_piece(k)
                near.wait_recv()
                far.wait_recv()
            everyone = mixed[...].reshape(width, group)
            value = across(everyone, w4_all[:, :, :, :span].reshape(width, span))
            proj[...] = value.astype(bf).reshape(4, rows, span)
            proj_all[r] = proj[r]
            copies = []
            for k in (2, 3, 1):
                to = (r + k) % 4
                copies.append(
                    remote(
                        proj.at[to], proj_all.at[r], ex_sem.at[k, 0], ex_sem.at[k, 1],
                        (place.s, to),
                    )
                )
                copies[-1].start()
            saved = pltpu.make_async_copy(mixed, mixed_out, save.at[1])
            saved.start()
            yield
            for copy in copies:
                copy.wait()
            own = tok_all[r].astype(f32)
            halves_ = []
            for side in range(2):
                total = jnp.zeros((rows, pair), f32)
                for core in range(2):
                    total += jnp.dot(
                        proj_all[side * 2 + core],
                        select(span, pair, 0, core * wcols, wcols), preferred_element_type=f32,
                    )
                at = slice(side * pair, (side + 1) * pair)
                halves_.append(own[:, at] + branch_scale * total)
                after_out[:, at] = halves_[-1]
            mean = sum(jnp.sum(v * v, axis=1, keepdims=True) for v in halves_) / width
            factor = lax.rsqrt(mean + norm_eps)
            for side in range(2):
                at = slice(side * pair, (side + 1) * pair)
                n2_out[:, at] = (halves_[side] * factor * gain_out[1:2, at]).astype(bf)
            yield
            saved.wait()
            pltpu.make_async_copy(qkv, qkv_out, save.at[0]).wait()
            for k in range(pieces):
                to_x, near, far = share_piece(k)
                to_x.wait_send()
                near.wait_send()
                far.wait_send()

        def weights_flow():
            yield from spread_flow(place, own4, w4_all, s1, parts)
            pltpu.make_async_copy(w4_all, w4_out, save.at[2]).start()

        run_flows(
            [
                weights_flow(),
                share_flow(place, tok_in, tok_all, s3),
                spread_flow(place, own_gain, gain_all, s2),
                prepare(),
                widen_flow(place, d_own, d_out, s4),
                columns_flow(place, gu_own, gu_out, s5),
                sides_flow(place, dn_own, dn_out, s6),
                attend(),
            ],
            (0, 1, 2, 3, 1, 1, 1, 2, 2, 2, 2, 2, 3, 3) + (0,) * (2 * parts) + (4,)
            + (0,) * parts + (4, 4, 0, 6, 5, 7, 4, 7, 7, 7, 5, 4, 7, 4, 5, 7, 5, 4, 4, 7, 6, 5, 4),
        )
        pltpu.make_async_copy(w4_all, w4_out, save.at[2]).wait()

    block = (rows, width)
    return call(
        kernel, "attention_forward", 1,
        [
            shape(A, B, wrows, 4 * wcols), shape(8, width, dtype=f32), shape(4, *block),
            shape(X, A, X, *block), shape(A, B, wrows, 2 * fcols), shape(B, pad, width),
            shape(3 * wcols, group), shape(4, wcols, group), shape(*block, dtype=f32),
            shape(*block), shape(2, head_dim // 2, group, dtype=f32), shape(width, group),
        ],
        [ANY, VMEM, ANY, ANY, ANY, ANY, ANY, ANY, VMEM, VMEM, VMEM, ANY],
        [
            pltpu.VMEM((4, wrows, width), bf), pltpu.VMEM((2, wrows, ff), bf),
            pltpu.VMEM(w_down.shape, bf), pltpu.VMEM((wrows, 4 * wcols), bf),
            pltpu.VMEM((A, wrows, 2 * fcols), bf), pltpu.VMEM((pad, width), bf),
            pltpu.VMEM((8, width), f32), pltpu.VMEM((A, B, 8, width), f32),
            pltpu.VMEM((4,) + block, bf), pltpu.VMEM(block, bf),
            pltpu.VMEM((A, B, wrows, 4 * wcols), bf), pltpu.VMEM((group, width), bf),
            pltpu.VMEM((width, group), bf),
            pltpu.VMEM((width - span + 128, group), f32), pltpu.VMEM((group, group), f32),
            pltpu.VMEM((4, wcols, group), bf), pltpu.VMEM((4, rows, span), bf),
            pltpu.VMEM((4, rows, span), bf), DMA((7,)),
        ]
        + spread_sems(B, parts) + spread_sems(B) + share_sems() + widen_sems() + columns_sems(B)
        + sides_sems(B)
        + [
            pltpu.VMEM((3 * wcols, group), bf), DMA((3, 2)), DMA((X, 3, 2)), DMA((4, 2)),
            DMA((3,)),
        ],
        [*weights, *gates, w_down, gains, tokens, cotangent, *ids],
        [ANY] * 7 + [VMEM, ANY] + [VMEM] * 3,
    )


def feed_forward(B, normed_two, d_down, gate_up, down, lefts):
    rows, width = normed_two.shape
    fcols = down.shape[0]
    every = X * A * X * rows
    pair = X * rows
    parts = halves(rows)
    wide = 768
    tile = 384

    wrows = gate_up.shape[0] // (A * B)
    pad = fcols // B
    many = 1152
    most = rows * 3 // 4

    def kernel(n_in, d_in, gu_in, dn_in, *refs):
        lefts_in, (out, f_out, ggu_out, gd_out), lefts_out, refs = split_refs(refs, 2, 4, 2, 100)
        bufs, (line_recv, line_send, over_x, over_core), sems = split_refs(refs, 11, 4, 100)
        n_all, d_all, gu, dn, part, hid, d_gu, from_core, from_x, landed, g_all = bufs
        (g_down, load, core_sem, x_sem, line_sem, gu_side, gd_side, gu_sem, gd_sem, f_core, f_x,
         free, core_free, f_line, left_sem, rest_send, rest_recv) = sems
        place = Place(B)
        a, x, c = place.a, place.x, place.c
        loads = [
            pltpu.make_async_copy(n_in, n_all.at[x, a, c], load.at[0]),
            pltpu.make_async_copy(gu_in, gu, load.at[1]),
            pltpu.make_async_copy(dn_in, dn, load.at[2]),
            pltpu.make_async_copy(d_in, d_all, load.at[3]),
        ]
        for copy in loads:
            copy.start()
        greet(place, True, True, True)()

        def to_line(block, way):
            src = n_all.at[x, block, c]
            return remote(
                src, src, line_send.at[block, (1 - way) // 2], line_recv.at[block],
                place.line(a + way),
            )

        def to_x(block, some=True):
            src = n_all.at[x, block, c]
            if some:
                src = src.at[pl.ds(0, most)]
            return remote(src, src, over_x.at[block, 0], over_x.at[block, 1], place.over_x)

        def rest_to_line(block, way):
            src = n_all.at[1 - x, block, c, pl.ds(most, rows - most)]
            return remote(
                src, src, rest_send.at[block, (1 - way) // 2], rest_recv.at[block],
                place.line(a + way),
            )

        def to_core(side, block):
            src = n_all.at[side, block, c]
            return remote(
                src, src, over_core.at[side, block, 0], over_core.at[side, block, 1],
                place.over_core,
            )

        def sum_core(side, d, h):
            return remote(
                piece(part, (side, d, 1 - c), h, parts), piece(from_core, (side, d), h, parts),
                core_sem.at[side, d, h, 0], core_sem.at[side, d, h, 1], place.over_core,
            )

        def sum_x(d, h):
            return remote(
                piece(part, (1 - x, d, c), h, parts), piece(from_x, d, h, parts),
                x_sem.at[d, h, 0], x_sem.at[d, h, 1], place.over_x,
            )

        def merge(side, d, h):
            sum_core(side, d, h).wait_recv()
            here = piece(part, (side, d, c), h, parts)
            add_into(here, here, piece(from_core, (side, d), h, parts))

        def send_sum(d):
            for h in range(parts):
                merge(1 - x, d, h)
                sum_x(d, h).start()

        loads[0].wait()

        @pl.when(a < A - 1)
        def _():
            to_line(a, 1).start()

        @pl.when(a > 0)
        def _():
            to_line(a, -1).start()

        to_x(a, False).start()
        to_core(x, a).start()

        def left_aside(i, d, k):
            to = (place.b + k) % B
            return remote(
                lefts_in[i].at[d, to], lefts_out[i].at[k - 1, d], left_sem.at[i, k, d, 0],
                left_sem.at[i, k, d, 1], place.side(to),
            )

        left_copies = [(i, d, k) for i in range(2) for d in range(A) for k in range(1, B)]
        for at in left_copies:
            left_aside(*at).start()
        for copy in loads[1:]:
            copy.wait()

        def nearest(i):
            left = jnp.where(a == 1, jnp.where(i == 1, 0, i), jnp.where(i == 0, 0, i))
            left = jnp.where((a == 1) & (i == 0), 1, left)
            right = jnp.where(a == 2, jnp.where(i == 0, 2, jnp.where(i == 1, 1, 3)), A - 1 - i)
            right = jnp.where((a == 2) & (i == A - 1), 0, right)
            return jnp.where(a < 2, left, right)

        def item(j):
            near = (j == 0) | ((j % 2 == 1) & (j < 2 * A - 1))
            i = jnp.where(near, (j + 1) // 2, jnp.where(j == 2 * A - 1, A - 1, j // 2 - 1))
            return near, nearest(i)

        def compute(side, block):
            n = n_all[side, block].reshape(pair, width)
            d = d_all[side, block].reshape(pair, width)
            both = product(n, gu[...])
            gate, up = both[:, :fcols], both[:, fcols:]
            d_hidden = against(d, dn[...])
            sig = jax.nn.sigmoid(gate)
            at = pl.ds(pl.multiple_of((side * A + block) * pair, pair), pair)
            hid[at, :] = (gate * sig * up).astype(bf)
            d_gate = (d_hidden * up * sig * (1.0 + gate * (1.0 - sig))).astype(bf)
            d_up = (d_hidden * gate * sig).astype(bf)
            both = jnp.concatenate([d_gate, d_up], axis=1)
            d_gu[at, :] = both
            for k in range(width // wide):
                cols = pl.ds(k * wide, wide)
                value = against(both, gu[cols, :]).astype(bf)
                part[side, block, :, :, cols] = value.reshape(X, rows, wide)

        def arrive(j, carry):
            near, block = item(j)
            side = jnp.where(near, x, 1 - x)

            @pl.when(near & (j > 0))
            def _():
                way = jnp.where(block < a, 1, -1)
                to_line(block, way).wait_recv()

                @pl.when((a + way >= 0) & (a + way < A))
                def _():
                    to_line(block, way).start()

                to_x(block).start()
                to_core(x, block).start()

            @pl.when(jnp.logical_not(near))
            def _():
                @pl.when(block == a)
                def _():
                    to_x(block, False).wait_recv()
                    for way in (1, -1):
                        @pl.when((a + way >= 0) & (a + way < A))
                        def _():
                            rest_to_line(block, way).start()

                @pl.when(block != a)
                def _():
                    way = jnp.where(block < a, 1, -1)
                    rest_to_line(block, way).wait_recv()

                    @pl.when((a + way >= 0) & (a + way < A))
                    def _():
                        rest_to_line(block, way).start()

                    to_x(block).wait_recv()

                to_core(1 - x, block).start()

            to_core(side, block).wait_recv()
            compute(side, block)
            for h in range(parts):
                sum_core(side, block, h).start()

            before, last = item(jnp.maximum(j - 1, 0))

            @pl.when((j > 3) & jnp.logical_not(before))
            def _():
                send_sum(last)

            return carry

        lax.fori_loop(0, 2 * A, arrive, 0)
        send_sum(nearest(A - 1))
        send_sum(a)
        for d in range(A):
            for h in range(parts):
                merge(x, d, h)
        pl.semaphore_signal(
            core_free, inc=1, device_id=place.over_core, device_id_type=MESH
        )

        def ready(d, h):
            sum_x(d, h).wait_recv()
            here = piece(part, (x, d, c), h, parts)
            add_into(here, here, piece(from_x, d, h, parts))

        piece_rows = rows // parts

        def final(h):
            at = pl.ds(h * piece_rows, piece_rows)
            out[at, :] = part[x, a, c, at, :]

        chain = line_slots(
            place, lambda d: part.at[x, d, c], lambda d, way: landed.at[d + (way > 0)], line_sem,
            parts, ready, final, near=True,
        )

        def grad_down(k, carry):
            at = pl.ds(pl.multiple_of(k * tile, tile), tile)
            d = d_all[:, :, :, :, at].reshape(every, tile)
            g_down[:, at] = across(hid[...], d).astype(bf)
            return carry

        def grad_gate_up(k, carry):
            at = pl.ds(pl.multiple_of(k * many, many), many)
            n = n_all[:, :, :, :, at].reshape(every, many)
            count = many // wrows
            for i in range(2):
                cols = pl.ds(i * fcols, fcols)
                value = across(n, d_gu[:, cols]).astype(bf)
                g_all[pl.ds(k * count, count), :, cols] = value.reshape(count, wrows, fcols)
            return carry

        def aside(d, k):
            to = (place.b + k) % B
            return remote(
                g_all.at[d * B + to], gu_side.at[k - 1, d], gu_sem.at[k, d, 0],
                gu_sem.at[k, d, 1], place.side(to),
            )

        def aside_down(k):
            to = (place.b + k) % B
            at = pl.ds(pl.multiple_of(to * pad, 16), pad)
            return remote(
                g_down.at[at], gd_side.at[k - 1], gd_sem.at[k, 0], gd_sem.at[k, 1], place.side(to)
            )

        def forward(k, carry):
            side, block = k // A, k % A
            at = pl.ds(pl.multiple_of(k * pair, pair), pair)
            for i in range(width // wide):
                cols = pl.ds(i * wide, wide)
                value = product(hid[at, :], dn[:, cols]).astype(bf)
                d_all[side, block, :, :, cols] = value.reshape(X, rows, wide)
            return carry

        mine = pl.ds(pl.multiple_of(place.b * pad, 16), pad)
        outs = [pltpu.make_async_copy(g_down.at[mine], gd_out, load.at[0])] + [
            pltpu.make_async_copy(g_all.at[d * B + place.b], ggu_out.at[d], load.at[1 + d])
            for d in range(A)
        ]

        def out_core(side, d):
            return remote(
                d_all.at[side, d, 1 - c], from_core.at[side, d], f_core.at[side, d, 0],
                f_core.at[side, d, 1], place.over_core,
            )

        def out_x(d):
            return remote(
                d_all.at[1 - x, d, c], n_all.at[0, d, 1], f_x.at[d, 0], f_x.at[d, 1],
                place.over_x,
            )

        def out_merge(side, d):
            out_core(side, d).wait_recv()
            here = d_all.at[side, d, c]
            add_into(here, here, from_core.at[side, d])

        def out_ready(d, h):
            out_merge(x, d)
            out_x(d).wait_recv()
            here = d_all.at[x, d, c]
            add_into(here, here, n_all.at[0, d, 1])

        def out_final(h):
            pltpu.make_async_copy(d_all.at[x, a, c], f_out, load.at[1 + A]).start()

        def out_landing(d, way):
            return part.at[0, d, 1 - c] if way > 0 else n_all.at[1, d, 1]

        out_chain = line_slots(
            place, lambda d: d_all.at[x, d, c], out_landing, f_line, 1, out_ready, out_final
        )

        lax.fori_loop(0, width // tile, grad_down, 0)
        for k in range(1, B):
            aside_down(k).start()
        next(chain)
        lax.fori_loop(0, X * A, forward, 0)
        pl.semaphore_wait(core_free, 1)
        for side in (1 - x, x):
            for i in range(A):
                out_core(side, far_first(a, i)).start()
        next(chain)
        for k in range(width // many):
            grad_gate_up(k, 0)
            for d in range(k * many // (wrows * B), (k + 1) * many // (wrows * B)):
                for j in range(1, B):
                    aside(d, j).start()
            next(chain)
        for d in range(A):
            @pl.when(d == a)
            def _():
                to_x(d, False).wait_send()

            @pl.when(d != a)
            def _():
                to_x(d).wait_send()

            for side in range(X):
                to_core(side, d).wait_send()
                for h in range(parts):
                    sum_core(side, d, h).wait_send()

            @pl.when((a < A - 1) & (d <= a))
            def _():
                to_line(d, 1).wait_send()
                rest_to_line(d, 1).wait_send()

            @pl.when((a > 0) & (d >= a))
            def _():
                to_line(d, -1).wait_send()
                rest_to_line(d, -1).wait_send()

        for device in [place.over_x] + [place.line((a + k) % A) for k in range(1, A)]:
            pl.semaphore_signal(free, inc=1, device_id=device, device_id_type=MESH)
        for i in range(A):
            out_merge(1 - x, far_first(a, i))
        pl.semaphore_wait(free, A)
        for i in range(A):
            out_x(far_first(a, i)).start()
        next(chain)
        for k in range(1, B):
            aside_down(k).wait_recv()
            add_into(g_down.at[mine], g_down.at[mine], gd_side.at[k - 1])
        outs[0].start()
        for _ in chain:
            pass
        next(out_chain)
        for d in range(A):
            for k in range(1, B):
                aside(d, k).wait_recv()
                here = g_all.at[d * B + place.b]
                add_into(here, here, gu_side.at[k - 1, d])
            outs[1 + d].start()
        for _ in out_chain:
            pass
        pltpu.make_async_copy(d_all.at[x, a, c], f_out, load.at[1 + A]).wait()
        for at in left_copies:
            left_aside(*at).wait()
        for copy in outs:
            copy.wait()
        for k in range(1, B):
            aside_down(k).wait_send()
            for d in range(A):
                aside(d, k).wait_send()
        for d in range(A):
            out_x(d).wait_send()
            for side in range(X):
                out_core(side, d).wait_send()
            for h in range(parts):
                sum_x(d, h).wait_send()

    block = (rows, width)
    return call(
        kernel, "feed_forward", 2,
        [
            shape(*block), shape(*block), shape(A, wrows, 2 * fcols),
            shape(pad, width),
        ]
        + [shape(B - 1, A, *v.shape[2:]) for v in lefts],
        [VMEM] + [ANY] * 5,
        [
            pltpu.VMEM((X, A, X) + block, bf), pltpu.VMEM((X, A, X) + block, bf),
            pltpu.VMEM(gate_up.shape, bf), pltpu.VMEM(down.shape, bf),
            pltpu.VMEM((X, A, X) + block, bf), pltpu.VMEM((every, fcols), bf),
            pltpu.VMEM((every, 2 * fcols), bf), pltpu.VMEM((X, A) + block, bf),
            pltpu.VMEM((A,) + block, bf), pltpu.VMEM((A + 1,) + block, bf),
            pltpu.VMEM((A * B, wrows, 2 * fcols), bf),
            DMA((A,)), DMA((A, 2)), DMA((A, 2)), DMA((X, A, 2)),
            pltpu.VMEM((fcols, width), bf), DMA((2 + A,)), DMA((X, A, parts, 2)),
            DMA((A, parts, 2)), DMA((2, A, parts, 2)),
            pltpu.VMEM((B - 1, A, wrows, 2 * fcols), bf), pltpu.VMEM((B - 1, pad, width), bf),
            DMA((B, A, 2)), DMA((B, 2)), DMA((X, A, 2)), DMA((A, 2)), pltpu.SemaphoreType.REGULAR,
            pltpu.SemaphoreType.REGULAR,
            DMA((2, A, 1, 2)), DMA((2, B, A, 2)), DMA((A, 2)), DMA((A,)),
        ],
        [normed_two, d_down, gate_up, down, *lefts],
        [ANY] * 6,
    )


def fold_scratch(rows, width):
    block = (rows, width)
    return [
        pltpu.VMEM((X * X,) + block, bf), pltpu.VMEM((X,) + block, bf), pltpu.VMEM(block, bf),
        DMA((X, 2)), DMA((2,)),
    ]


def fold_flow(place, scratch):
    part, from_core, from_x, core_sem, x_sem = scratch
    x, c = place.x, place.c

    def to_core(i):
        return remote(
            part.at[i * X + 1 - c], from_core.at[i], core_sem.at[i, 0], core_sem.at[i, 1],
            place.over_core,
        )

    def merge(i):
        to_core(i).wait_recv()
        here = part.at[i * X + c]
        add_into(here, here, from_core.at[i])

    to_x = remote(part.at[place.rx], from_x, x_sem.at[0], x_sem.at[1], place.over_x)
    to_core(1 - x).start()
    to_core(x).start()
    yield
    merge(1 - x)
    to_x.start()
    merge(x)
    yield
    to_x.wait_recv()
    here = part.at[place.r]
    add_into(here, here, from_x)
    yield
    to_x.wait_send()
    for i in range(X):
        to_core(i).wait_send()


def owners_flow(place, own, out, sems):
    line, local = sems
    a = place.a
    keep = pltpu.make_async_copy(own.at[a], out.at[a], local.at[0])
    keep.start()
    copies = []
    for k in (1, 3, 2):
        to = (a + k) % A
        copies.append(
            remote(own.at[to], out.at[a], line.at[k, 0], line.at[k, 1], place.line(to))
        )
        copies[-1].start()
    yield
    keep.wait()
    for copy in copies:
        copy.wait()


def grad_scratch(rows, width):
    block = (rows, width)
    P_ = halves(rows)
    return [
        pltpu.VMEM((A,) + block, bf), pltpu.VMEM((A + 1,) + block, bf), DMA((2, A, P_, 2)),
        DMA((P_, 2)), DMA((X, P_, 2)), DMA((P_,)),
    ]


def grad_flow(place, produce, out, scratch):
    sums, landed, line_sem, x_sem, core_sem, local = scratch
    r, x = place.r, place.x
    parts = halves(out.shape[1])
    for i in range(A):
        d = far_first(place.a, i)
        sums[d] = produce(d)
    yield

    def keep(src, h):
        return pltpu.make_async_copy(src, piece(out, r, h, parts), local.at[h])

    def to_x(src, h):
        return remote(src, piece(out, r, h, parts), x_sem.at[h, 0], x_sem.at[h, 1], place.over_x)

    def near(src, h):
        return remote(
            src, piece(out, r, h, parts), core_sem.at[x, h, 0], core_sem.at[x, h, 1],
            place.over_core,
        )

    def far(h):
        src = piece(out, place.rx, h, parts)
        return remote(
            src, src, core_sem.at[1 - x, h, 0], core_sem.at[1 - x, h, 1], place.over_core
        )

    def final(h):
        src = piece(sums, place.a, h, parts)
        to_x(src, h).start()
        near(src, h).start()
        keep(src, h).start()

    yield from line_slots(
        place, lambda d: sums.at[d], lambda d, way: landed.at[d + (way > 0)], line_sem, parts,
        lambda d, h: None, final,
    )
    for h in range(parts):
        src = piece(out, r, h, parts)
        keep(src, h).wait()
        near(src, h).wait()
    yield
    for h in range(parts):
        src = piece(out, r, h, parts)
        to_x(src, h).wait_recv()
        far(h).start()
    yield
    for h in range(parts):
        to_x(piece(out, r, h, parts), h).wait_send()
        far(h).wait()


def attention_backward(
    B, S, d_n2, after_attn, cotangent, gains, w4, qkv, tokens, lefts, tables, ids, g_gate_up,
    g_down,
):
    rows, width = d_n2.shape
    group = 4 * rows
    wrows, wcols = width // S, width // 4
    head_dim = width // H
    heads = H // 4
    wide = 384
    span = -(-wcols // 128) * 128
    skip = wcols - (span - 128)
    tail = width - span + 128
    trio = 3
    third = 2 * trio * head_dim
    thirds = heads // trio
    score_scale = 1.0 / math.sqrt(head_dim)
    widths = (span - 128, span) + (third,) * thirds
    count = len(widths)
    wrows_wide = -(-wrows // 128) * 128

    def kernel(*refs):
        ins, lefts_in, ids_in, outs, mids, own, refs = split_refs(
            refs, 10, 4, 2, 2, count + 3, 20, 100
        )
        (dn2_in, after_in, cot_in, gain_in, w4_in, qkv_in, tok_in, table_in, gu_in, gd_in) = ins
        seq_row, blk_row = ids_in
        gt_out, gain_out = outs
        shared, (gu_cols, gu_all, gd_all) = mids[:count], mids[count:]
        (w4, qkv_, mix, mix_far, n_t, n_far, tok, bias, factors, d_t, d_nat, d_far, ex_send,
         ex_all, ex_far, d_after, own_gain, gain_all, load, side_sem) = own
        f1, f2, u1, u2, u3, (ex_sem, gain_sem), *grads = split_refs(
            refs, 5, 5, 2, 3, 3, 2, *(6,) * count
        )
        place = Place(B)
        met = greet(place, True, True, True)
        r, x, c = place.r, place.x, place.c
        loads = [
            pltpu.make_async_copy(src, dst, load.at[i])
            for i, (src, dst) in enumerate(
                [
                    (tok_in, tok), (w4_in, w4), (lefts_in[0].at[:, place.b], mix),
                    (lefts_in[1], mix_far), (qkv_in, qkv_), (lefts_in[2].at[:, place.b], n_t),
                    (lefts_in[3], n_far),
                ]
            )
        ]
        for copy in loads:
            copy.start()
        part1, part2 = f1[0], f2[0]
        gain_one, gain_two = gain_in[0:1], gain_in[1:2]
        own_gain[...] = jnp.zeros_like(own_gain)
        step = 32

        def back_two(i, carry):
            at = pl.ds(pl.multiple_of(i * step, step), step)
            after = after_in[at, :]
            d = dn2_in[at, :].astype(f32)
            factor = lax.rsqrt(jnp.mean(after * after, axis=1, keepdims=True) + norm_eps)
            own_gain[1:2, :] += jnp.sum(d * after * factor, axis=0, keepdims=True)
            u = d * gain_two
            mean = jnp.mean(u * after, axis=1, keepdims=True)
            d_after[at, :] = (
                cot_in[at, :].astype(f32) + factor * u - after * (factor * factor * factor) * mean
            )
            return carry

        lax.fori_loop(0, rows // step, back_two, 0)
        d_proj = (branch_scale * d_after[...]).astype(bf)
        for k in range(4):
            at = k * wcols // 128 * 128
            ex_send[k] = product(
                d_proj[:, at : at + span], select(span, span, k * wcols - at, 0, wcols)
            ).astype(bf)
        ex_all[r] = ex_send[r]
        met()
        exchange = []
        for k in (2, 3, 1):
            to = (r + k) % 4
            exchange.append(
                remote(
                    ex_send.at[to], ex_all.at[r], ex_sem.at[k, 0], ex_sem.at[k, 1],
                    (place.s, to),
                )
            )
            exchange[-1].start()

        def at_head(part, n):
            return pl.ds(pl.multiple_of(part * wcols + n * head_dim, 64), head_dim)

        def probs_of(n):
            scores = across(qkv_[at_head(2, n), :], qkv_[at_head(1, n), :]) * score_scale
            scores = scores + bias[...].astype(f32)
            powers = jnp.exp(scores - jnp.max(scores, axis=0, keepdims=True))
            return powers * (1.0 / jnp.sum(powers, axis=0, keepdims=True))

        def aside(src, dst, i):
            return [
                remote(
                    src, dst(k - 1), side_sem.at[i, k, 0], side_sem.at[i, k, 1],
                    place.side((place.b + k) % B),
                )
                for k in range(1, B)
            ]

        def lanes(i):
            return pl.ds(0, span) if i == 1 else pl.ds(span + (i - 2) * third, third)

        def aside_of(i):
            if i == 0:
                return aside(ex_all, lambda k: ex_far.at[k], 0)
            return aside(d_nat.at[:, lanes(i)], lambda k: d_far.at[k, :, lanes(i)], i)

        def compute():
            _, allowed = masks(seq_row, blk_row)
            bias[...] = jnp.where(allowed, 0.0, masked_score).astype(bf)
            for i in range(4):
                loads[0].wait() if i == 0 else None
                value = tok[i].astype(f32)
                factors[i * rows : (i + 1) * rows, :] = lax.rsqrt(
                    jnp.mean(value * value, axis=1, keepdims=True) + norm_eps
                )
            for copy in exchange:
                copy.wait()
            for copy in aside_of(0):
                copy.start()
            for copy in loads[1:]:
                copy.wait()
            d_proj = ex_all[...].reshape(group, span)
            for i in (1 - c, c):
                for side in range(X):
                    k = side * X + i
                    at = pl.ds(pl.multiple_of(k * wcols, 64), wcols)
                    part1[k] = against(w4[at, :span], d_proj).astype(bf)
            yield

            def values_back(n, carry):
                d_m = part1[r, pl.ds(pl.multiple_of(n * head_dim, 64), head_dim), :]
                value = against(d_m, probs_of(n).astype(bf))
                at = pl.ds(pl.multiple_of(skip + n * head_dim, 64), head_dim)
                d_t[at, :] = value.astype(bf)
                return carry

            def flip(n, carry):
                at = pl.ds(pl.multiple_of(n * 128, 128), 128)
                d_nat[:, at] = d_t[at, :].astype(f32).T.astype(bf)
                return carry

            d_t[:skip, :] = jnp.zeros((skip, group), bf)
            for k in range(thirds):
                lax.fori_loop(trio * k, trio * (k + 1), values_back, 0)
                if k + 1 < thirds:
                    yield
            lax.fori_loop(0, span // 128, flip, 0)
            for copy in aside_of(1):
                copy.start()
            yield
            cosine, sine = table_in[0], table_in[1]
            half = head_dim // 2

            def turn_back(value, at):
                former, latter = value[:half], value[half:]
                d_t[pl.ds(at, half), :] = (former * cosine + latter * sine).astype(bf)
                d_t[pl.ds(at + half, half), :] = (latter * cosine - former * sine).astype(bf)

            def scores_back(n, carry):
                d_m = part1[r, pl.ds(pl.multiple_of(n * head_dim, 64), head_dim), :]
                probs = probs_of(n)
                d_probs = across(qkv_[at_head(0, n), :], d_m)
                d_s = probs * (d_probs - jnp.sum(d_probs * probs, axis=0, keepdims=True))
                d_s = d_s.astype(bf)
                at = span + n // trio * third + n % trio * head_dim
                turn_back(
                    product(qkv_[at_head(2, n), :], d_s) * score_scale, pl.multiple_of(at, 64)
                )
                turn_back(
                    against(qkv_[at_head(1, n), :], d_s) * score_scale,
                    pl.multiple_of(at + third // 2, 64),
                )
                return carry

            for k in range(thirds):
                lax.fori_loop(trio * k, trio * (k + 1), scores_back, 0)
                first = (span + third * k) // 128
                lax.fori_loop(first, first + third // 128, flip, 0)
                for copy in aside_of(2 + k):
                    copy.start()
                yield

            def inputs_back(n, carry):
                at = pl.ds(pl.multiple_of(n * wide, 128), wide)
                value = against(d_nat[...], w4[at, pl.ds(span - 128, tail)])
                x_f = tok[:, :, at].reshape(group, wide).astype(f32) * factors[...]
                own_gain[0:1, at] = jnp.sum(value * x_f, axis=0, keepdims=True)
                part2[:, :, at] = value.astype(bf).reshape(4, rows, wide)
                return carry

            lax.fori_loop(0, width // wide, inputs_back, 0)

        def make(i):
            def produce(d):
                if i == 0:
                    own, far, right = mix, mix_far, ex_all[:, :, : span - 128]
                    right = right.reshape(group, span - 128)
                else:
                    own, far, right = n_t, n_far, d_nat[:, lanes(i)]
                total = product(own[d], right)
                for k in range(B - 1):
                    if i == 0:
                        right = ex_far[k, :, :, : span - 128].reshape(group, span - 128)
                    else:
                        right = d_far[k, :, lanes(i)]
                    total += product(far[k, d], right)
                if i == 1:
                    last = product(mix[d], ex_all[:, :, span - 128 :].reshape(group, 128))
                    for k in range(B - 1):
                        right = ex_far[k, :, :, span - 128 :].reshape(group, 128)
                        last += product(mix_far[k, d], right)
                    total = jnp.concatenate([total[:, :128] + last, total[:, 128:]], axis=1)
                return total.astype(bf)

            return produce

        def grad(i):
            for copy in aside_of(i):
                copy.wait_recv()
            yield from grad_flow(place, make(i), shared[i], grads[i])
            for copy in aside_of(i):
                copy.wait_send()

        def gains_flow():
            def send(i, device):
                return remote(
                    own_gain, gain_all.at[i], gain_sem.at[i, 0], gain_sem.at[i, 1], device
                )

            stages = [
                [place.over_core], [place.over_x],
                [place.side((place.b + k) % B) for k in range(1, B)],
                [place.line((place.a + k) % A) for k in range(1, A)],
            ]
            at = 0
            for stage in stages:
                copies = [send(at + i, device) for i, device in enumerate(stage)]
                for copy in copies:
                    copy.start()
                yield
                for copy in copies:
                    copy.wait()
                for i in range(len(stage)):
                    own_gain[...] += gain_all[at + i]
                at += len(stage)
            for n in range(width // wide):
                own = slice(n * wide, (n + 1) * wide)
                total = own_gain[:, own]
                pick = select(wide, wrows_wide, place.s * wrows - n * wide, 0, wrows)
                value = jnp.zeros((8, wrows_wide), f32)
                for _ in range(3):
                    low = total.astype(bf)
                    value += product(low, pick)
                    total = total - low.astype(f32)
                gain_out[...] = value if n == 0 else gain_out[...] + value

        def input_end():
            def back_one(i, carry):
                at = pl.ds(pl.multiple_of(i * step, step), step)
                value = tok[r, at, :].astype(f32)
                d = part2[r, at, :].astype(f32)
                factor = lax.rsqrt(jnp.mean(value * value, axis=1, keepdims=True) + norm_eps)
                u = d * gain_one
                mean = jnp.mean(u * value, axis=1, keepdims=True)
                gt_out[at, :] = (
                    d_after[at, :] + factor * u - value * (factor * factor * factor) * mean
                ).astype(bf)
                return carry

            lax.fori_loop(0, rows // step, back_one, 0)
            yield

        M, F1, F2, GU, SU, SD, G, T, O, V, P, Q, R = range(13)
        flows = [
            compute(),
            fold_flow(place, f1),
            fold_flow(place, f2),
            owners_flow(place, gu_in, gu_cols, u1),
            share_flow(place, gu_cols, gu_all, u2),
            share_flow(place, gd_in, gd_all, u3),
            gains_flow(),
            input_end(),
        ] + [grad(i) for i in range(count)]
        turns = [
            GU, M, F1, F1, F1, F1, SD, O, O, M, M, M, GU, SU, M, O, V, M, O, V, M, O, V, P, M, SD,
            F2, V, P, Q, F2, V, P, Q, R, O, SU, P, Q, R, F2, F2, T, P, Q, R, O, V, Q, R, G, SD, SU,
            V, R, O, P, V, G, R, G, R, G, R, G,
        ]
        run_flows(flows, turns)

    block = (rows, width)
    left = (wrows, group)
    return call(
        kernel, "attention_backward", 3,
        [shape(*block), shape(8, wrows_wide, dtype=f32)]
        + [shape(4, wrows, w) for w in widths]
        + [shape(*g_gate_up.shape), shape(4, *g_gate_up.shape), shape(4, *g_down.shape)],
        [VMEM, VMEM] + [ANY] * (count + 3),
        [
            pltpu.VMEM((width, width), bf), pltpu.VMEM((3 * wcols, group), bf),
            pltpu.VMEM((A,) + left, bf), pltpu.VMEM((B - 1, A) + left, bf),
            pltpu.VMEM((A,) + left, bf), pltpu.VMEM((B - 1, A) + left, bf),
            pltpu.VMEM((4,) + block, bf), pltpu.VMEM((group, group), bf),
            pltpu.VMEM((group, 1), f32), pltpu.VMEM((tail, group), bf),
            pltpu.VMEM((group, tail), bf), pltpu.VMEM((B - 1, group, tail), bf),
            pltpu.VMEM((4, rows, span), bf), pltpu.VMEM((4, rows, span), bf),
            pltpu.VMEM((B - 1, 4, rows, span), bf), pltpu.VMEM(block, f32),
            pltpu.VMEM((8, width), f32), pltpu.VMEM((A + B, 8, width), f32), DMA((7,)),
            DMA((count, B, 2)),
        ]
        + fold_scratch(wcols, group) + fold_scratch(*block)
        + [DMA((A, 2)), DMA((1,))] + share_sems() + share_sems()
        + [DMA((4, 2)), DMA((A + B, 2))]
        + [v for w in widths for v in grad_scratch(wrows, w)],
        [
            d_n2, after_attn, cotangent, gains, w4, qkv, tokens, tables, g_gate_up, g_down,
            *lefts, *ids,
        ],
        [VMEM] * 4 + [ANY] * 3 + [VMEM] + [ANY] * 6 + [VMEM] * 2,
    )


def lay_out(S, ff, width, out, value, groups, gate_up, down, after_attn, ffn_out):
    wrows, span = value.shape[1:]
    tokens = after_attn.shape[0]
    wcols = width // 4
    pair = 2 * wcols
    skip = wcols - (span - 128)
    sub = ff // (S * 4)
    pad = down.shape[1]
    fcols = gate_up.shape[3] // 2
    B = fcols // pad
    drows = ff // S
    steps = 3 if wrows % (3 * 16) == 0 else 1
    rows, cols = wrows // steps, width // steps

    def kernel(o_in, v_in, *refs):
        g_in, ins, outs = split_refs(refs, len(groups), 4, 8)
        gu_in, d_in, after_in, f_in = ins
        o_out, q_out, k_out, v_out, g_out, u_out, d_out, r_out = outs
        r_out[...] = (after_in[...] + branch_scale * f_in[...].astype(f32)).astype(bf)

        def beside(pieces, to):
            for side in range(2):
                parts = [
                    ref[side * 2 + core].astype(f32)[:, at : at + size]
                    for core in range(2) for ref, at, size in pieces
                ]
                to[:, side * pair : (side + 1) * pair] = jnp.concatenate(parts, axis=1)

        half = groups[0].shape[2] // 2
        beside([(o_in, 0, wcols - skip), (v_in, 0, skip)], o_out)
        beside([(v_in, skip, wcols)], v_out)
        beside([(ref, 0, half) for ref in g_in], q_out)
        beside([(ref, half, half) for ref in g_in], k_out)
        for i, to in enumerate((g_out, u_out)):
            parts = []
            for m in range(4 * S):
                s = m // 4
                at = i * fcols + s % B * pad
                parts.append(gu_in[m % 4, s // B].astype(f32)[:, at : at + sub])
            to[...] = jnp.concatenate(parts, axis=1)
        d_out[...] = jnp.concatenate([d_in[k].astype(f32)[:sub] for k in range(4)], axis=0)

    def by_rows(ref):
        lead = len(ref.shape) - 2
        return pl.BlockSpec(
            ref.shape[:lead] + (rows, ref.shape[-1]), lambda i: (0,) * lead + (i, 0)
        )

    outs = [shape(wrows, width, dtype=f32)] * 4 + [shape(wrows, ff, dtype=f32)] * 2
    return pl.pallas_call(
        kernel,
        grid=(steps,),
        out_shape=outs + [shape(drows, width, dtype=f32), shape(tokens, width)],
        in_specs=[by_rows(v) for v in (out, value, *groups, gate_up)]
        + [pl.BlockSpec((4, pad, cols), lambda i: (0, 0, i))]
        + [pl.BlockSpec((tokens, cols), lambda i: (0, i))] * 2,
        out_specs=[by_rows(v) for v in outs]
        + [pl.BlockSpec((n, cols), lambda i: (0, i)) for n in (drows, tokens)],
        name="lay_out",
        compiler_params=pltpu.CompilerParams(vmem_limit_bytes=60 * 2**20),
    )(out, value, *groups, gate_up, down, after_attn, ffn_out)


def product(left_side, right_side):
    return jnp.dot(left_side, right_side, preferred_element_type=f32)


def against(left_side, right_side):
    return lax.dot_general(
        left_side, right_side, (((1,), (1,)), ((), ())), preferred_element_type=f32
    )


def across(left_side, right_side):
    return lax.dot_general(
        left_side, right_side, (((0,), (0,)), ((), ())), preferred_element_type=f32
    )


def body(
    tokens,
    attn_gain,
    w_query,
    w_key,
    w_value,
    w_out,
    ffn_gain,
    w_gate,
    w_up,
    w_down,
    seq_ids,
    block_ids,
    cotangent,
):
    S = lax.axis_size("shard")
    R = lax.axis_size("replica")
    B = S // A
    rows, width = tokens.shape
    ff = w_gate.shape[1]
    wrows = width // S
    ids = (seq_ids[None, :], block_ids[None, :])
    gains = jnp.pad(jnp.stack([attn_gain, ffn_gain]), ((0, 6), (0, 0)))
    (
        w4, gains, tokens_group, d_down, gate_up, down_w, qkv, mixed_all, after_attn, normed_two,
        tables, normed_t,
    ) = attention_forward(
        B, [w_out, w_value, w_query, w_key], [w_gate, w_up], w_down, gains, tokens, cotangent, ids
    )
    lefts = [v.reshape(A, B, wrows, -1) for v in (mixed_all, normed_t)]
    d_n2, ffn_out, g_gate_up, g_down, mixed_far, normed_far = feed_forward(
        B, normed_two, d_down, gate_up.reshape(width, -1), down_w.reshape(-1, width), lefts
    )
    grad_tokens, gain_sums, g_out, g_value, *parts = attention_backward(
        B, S, d_n2, after_attn, cotangent, gains, w4.reshape(width, width), qkv, tokens_group,
        [lefts[0], mixed_far, lefts[1], normed_far], tables, ids, g_gate_up, g_down,
    )
    g_out, g_query, g_key, g_value, g_gate, g_up, g_down, result = lay_out(
        S, ff, width, g_out, g_value, parts[:-3], *parts[-2:], after_attn, ffn_out
    )
    return (
        result, grad_tokens, gain_sums[0, :wrows], g_query, g_key, g_value, g_out,
        gain_sums[1, :wrows], g_gate, g_up, g_down,
    )


def solution(mesh):
    split = P(("shard", "replica"), None)
    vec, mat = P("shard"), P("shard", None)
    in_specs = (split, vec, mat, mat, mat, mat, vec, mat, mat, mat, vec, vec, split)
    out_specs = (split, split, vec, mat, mat, mat, mat, vec, mat, mat, mat)
    return jax.shard_map(body, mesh=mesh, in_specs=in_specs, out_specs=out_specs, check_vma=False)
```

```python
import functools
import math

import jax
import jax.numpy as jnp
from jax import lax
from jax.experimental import pallas as pl
from jax.experimental.pallas import tpu as pltpu
from jax.sharding import PartitionSpec as P

H = 36
A = 4
X = 2

branch_scale = 1.4 / math.sqrt(40.0)
norm_eps = 1e-05
rope_base = 10000.0
masked_score = -1e30
MESH = pl.DeviceIdType.MESH
bf = jnp.bfloat16
f32 = jnp.float32
DMA = pltpu.SemaphoreType.DMA


class Place:
    def __init__(self, B):
        self.B = B
        s, r = lax.axis_index("shard"), lax.axis_index("replica")
        self.s, self.r = s, r
        self.a, self.b = s // B, s % B
        self.x, self.c = r // X, r % X
        self.rx = (1 - self.x) * X + self.c
        self.rc = self.x * X + 1 - self.c

    def line(self, a):
        return (a * self.B + self.b, self.r)

    def side(self, b):
        return (self.a * self.B + b, self.r)

    @property
    def over_x(self):
        return (self.s, self.rx)

    @property
    def over_core(self):
        return (self.s, self.rc)


def greet(place, a_peers=True, b_peers=False, r_peers=True):
    barrier = pltpu.get_barrier_semaphore()
    devices = []
    if a_peers:
        devices += [place.line((place.a + k) % A) for k in range(1, A)]
    if b_peers:
        devices += [place.side((place.b + k) % place.B) for k in range(1, place.B)]
    if r_peers:
        devices += [(place.s, (place.r + k) % 4) for k in range(1, 4)]
    for device in devices:
        pl.semaphore_signal(barrier, inc=1, device_id=device, device_id_type=MESH)
    return lambda: pl.semaphore_wait(barrier, len(devices))


def remote(src, dst, send, recv, device):
    return pltpu.make_async_remote_copy(
        src_ref=src, dst_ref=dst, send_sem=send, recv_sem=recv, device_id=device,
        device_id_type=MESH,
    )


def add_into(dst, first, second, tile=32):
    rows = dst.shape[0]
    tile = math.gcd(rows, tile) if math.gcd(rows, tile) >= 16 else rows

    def step(i, carry):
        at = pl.ds(pl.multiple_of(i * tile, tile), tile)
        dst[at, :] = (first[at, :].astype(f32) + second[at, :].astype(f32)).astype(dst.dtype)
        return carry

    lax.fori_loop(0, rows // tile, step, 0)


def run_flows(flows, turns=()):
    ended = set()

    def step(at):
        if at not in ended:
            try:
                next(flows[at])
            except StopIteration:
                ended.add(at)

    for at in turns:
        step(at)
    while len(ended) < len(flows):
        for at in range(len(flows)):
            step(at)


def halves(rows):
    return 2 if rows % 32 == 0 else 1


def piece(ref, at, h, parts):
    if parts == 1:
        return ref.at[at]
    rows = ref.shape[-2] // parts
    index = at if isinstance(at, tuple) else (at,)
    return ref.at[index + (pl.ds(h * rows, rows),)]


def widen_sems():
    return [DMA((A,)), DMA((X,)), DMA((A, 2)), DMA((A, 2)), DMA((X, A, 2)), DMA((1,))]


def widen_flow(place, own, out, sems):
    line_recv, _, line_send, over_x, over_core, local = sems
    a, x, c = place.a, place.x, place.c
    keep = pltpu.make_async_copy(own, out.at[x, a, c], local.at[0])
    keep.start()

    def to_line(src, block, way):
        at = 0 if way > 0 else 1
        return remote(
            src, out.at[x, block, c], line_send.at[block, at], line_recv.at[block],
            place.line(a + way),
        )

    def to_x(src, block):
        return remote(
            src, out.at[x, block, c], over_x.at[block, 0], over_x.at[block, 1], place.over_x
        )

    def to_core(src, side, block):
        return remote(
            src, out.at[side, block, c], over_core.at[side, block, 0],
            over_core.at[side, block, 1], place.over_core,
        )

    @pl.when(a < A - 1)
    def _():
        to_line(own, a, 1).start()

    @pl.when(a > 0)
    def _():
        to_line(own, a, -1).start()

    to_x(own, a).start()
    to_core(own, x, a).start()

    def pass_x(k):
        for ok, block in ((a - k >= 0, a - k), (a + k < A, a + k)) if k else ((None, a),):
            def go():
                src = out.at[1 - x, block, c]
                to_x(src, block).wait_recv()
                to_core(src, 1 - x, block).start()

            go() if ok is None else pl.when(ok)(go)

    for k in range(1, A):
        yield
        for way in (1, -1):
            block = a - way * k

            @pl.when((block >= 0) & (block < A))
            def _():
                src = out.at[x, block, c]
                to_line(src, block, way).wait_recv()

                @pl.when((a + way >= 0) & (a + way < A))
                def _():
                    to_line(src, block, way).start()

                to_x(src, block).start()
                to_core(src, x, block).start()

        yield
        pass_x(k - 1)
    yield
    pass_x(A - 1)
    yield
    keep.wait()
    for block in range(A):
        src = out.at[x, block, c]

        @pl.when((a < A - 1) & (block <= a))
        def _():
            to_line(src, block, 1).wait_send()

        @pl.when((a > 0) & (block >= a))
        def _():
            to_line(src, block, -1).wait_send()

        to_x(src, block).wait_send()
        for side in range(X):
            to_core(src, side, block).wait()


def shrink_scratch(rows, width):
    block = (rows, width)
    P_ = halves(rows)
    return [
        pltpu.VMEM((X, A) + block, bf),
        pltpu.VMEM((X, A) + block, bf),
        pltpu.VMEM((A,) + block, bf),
        pltpu.VMEM((A + 1,) + block, bf),
        DMA((X, A, P_)), DMA((X, A, P_, 2)), DMA((A, P_, 2)), DMA((2, A, P_, 2)),
    ]


def far_first(a, i):
    inner = (3, 0, 2, 1)[i]
    return jnp.where(a == 0, 3 - i, jnp.where(a == 1, inner, jnp.where(a == 2, 3 - inner, i)))


def line_slots(place, sums, landing, sems, parts, ready, final, near=False):
    a = place.a
    last = 2 * A - 3 if near else A - 1

    def part(ref, h):
        if parts == 1:
            return ref
        rows = ref.shape[0] // parts
        return ref.at[pl.ds(h * rows, rows)]

    def hop(d, h, way):
        at = 0 if way > 0 else 1
        return remote(
            part(sums(d), h), part(landing(d, way), h), sems.at[at, d, h, 0],
            sems.at[at, d, h, 1], place.line(a + way),
        )

    def take(d, h, way):
        @pl.when((a - way >= 0) & (a - way < A))
        def _():
            hop(d, h, way).wait_recv()
            here = part(sums(d), h)
            add_into(here, here, part(landing(d, way), h))

    for t in range(last + 1):
        for way in (1, -1):
            at = a if way > 0 else A - 1 - a
            to = t - at + 1 if near else A - 1 - t + at
            d = to if way > 0 else A - 1 - to

            @pl.when((to > at) & (to < A))
            def _():
                for h in range(parts):
                    ready(d, h)
                    take(d, h, way)
                    hop(d, h, way).start()

        if t == last:
            for h in range(parts):
                ready(a, h)
                take(a, h, 1)
                take(a, h, -1)
                final(h)
        yield
    for d in range(A):
        for h in range(parts):
            for way in (1, -1):
                @pl.when((d - a) * way > 0)
                def _():
                    hop(d, h, way).wait_send()


def share_sems():
    return [DMA((2,)), DMA((X, 2)), DMA((1,))]


def share_flow(place, own, out, sems, ready=None):
    x_sem, core_sem, local = sems
    r, x, c = place.r, place.x, place.c
    if ready is not None:
        yield
        ready()
    keep = pltpu.make_async_copy(own, out.at[r], local.at[0])
    to_x = remote(own, out.at[r], x_sem.at[0], x_sem.at[1], place.over_x)
    near = remote(own, out.at[r], core_sem.at[x, 0], core_sem.at[x, 1], place.over_core)
    far = remote(
        out.at[place.rx], out.at[place.rx], core_sem.at[1 - x, 0], core_sem.at[1 - x, 1],
        place.over_core,
    )
    to_x.start()
    near.start()
    keep.start()
    yield
    to_x.wait_recv()
    far.start()
    yield
    keep.wait()
    to_x.wait_send()
    near.wait()
    far.wait()


def spread_sems(B, parts=1):
    return [DMA((A, parts)), DMA((A, 2, parts)), DMA((B, A, parts, 2)), DMA((1,))]


def spread_flow(place, own, out, sems, parts=1):
    line_recv, line_send, side, local = sems
    a, b, B = place.a, place.b, place.B
    keep = pltpu.make_async_copy(own, out.at[a, b], local.at[0])
    keep.start()

    def half(h):
        return own if parts == 1 else own.at[pl.ds(h * own.shape[0] // parts, own.shape[0] // parts)]

    def to_line(src, block, h, way):
        return remote(
            src, piece(out, (block, b), h, parts), line_send.at[block, 0 if way > 0 else 1, h],
            line_recv.at[block, h], place.line(a + way),
        )

    def to_side(src, block, h, k):
        return remote(
            src, piece(out, (block, b), h, parts), side.at[k, block, h, 0],
            side.at[k, block, h, 1], place.side((b + k) % B),
        )

    for h in range(parts):
        @pl.when(a < A - 1)
        def _():
            to_line(half(h), a, h, 1).start()

        @pl.when(a > 0)
        def _():
            to_line(half(h), a, h, -1).start()

        for k in range(1, B):
            to_side(half(h), a, h, k).start()
    for step in range(1, A):
        for h in range(parts):
            yield
            for way in (1, -1):
                block = a - way * step

                @pl.when((block >= 0) & (block < A))
                def _():
                    src = piece(out, (block, b), h, parts)
                    to_line(src, block, h, way).wait_recv()

                    @pl.when((a + way >= 0) & (a + way < A))
                    def _():
                        to_line(src, block, h, way).start()

                    for k in range(1, B):
                        to_side(src, block, h, k).start()

    yield
    keep.wait()
    for block in range(A):
        for h in range(parts):
            src = piece(out, (block, b), h, parts)

            @pl.when((a < A - 1) & (block <= a))
            def _():
                to_line(src, block, h, 1).wait_send()

            @pl.when((a > 0) & (block >= a))
            def _():
                to_line(src, block, h, -1).wait_send()

            for k in range(1, B):
                to_side(src, block, h, k).wait()


def columns_sems(B):
    return [DMA((A, 2)), DMA((B, A, 2)), DMA((1,))]


def columns_flow(place, own, out, sems):
    line, side, local = sems
    a, b, B = place.a, place.b, place.B
    keep = pltpu.make_async_copy(own.at[a], out.at[a, b], local.at[0])
    keep.start()

    def to_line(k):
        to = (a + k) % A
        return remote(own.at[to], out.at[a, b], line.at[k, 0], line.at[k, 1], place.line(to))

    def to_side(src, block, k):
        return remote(
            src, out.at[block, b], side.at[k, block, 0], side.at[k, block, 1],
            place.side((b + k) % B),
        )

    for k in range(1, A):
        to_line(k).start()
    for k in range(1, B):
        to_side(own.at[a], a, k).start()
    for k in (1, 3, 2):
        yield
        to_line(k).wait_recv()
        block = (a + A - k) % A
        for j in range(1, B):
            to_side(out.at[block, b], block, j).start()
    yield
    keep.wait()
    for k in range(1, A):
        to_line(k).wait_send()
    for block in range(A):
        for k in range(1, B):
            to_side(out.at[block, b], block, k).wait()


def sides_sems(B):
    return [DMA((B, 2)), DMA((1,))]


def sides_flow(place, own, out, sems):
    side, local = sems
    b, B = place.b, place.B
    keep = pltpu.make_async_copy(own, out.at[b], local.at[0])
    keep.start()
    copies = [
        remote(own, out.at[b], side.at[k, 0], side.at[k, 1], place.side((b + k) % B))
        for k in range(1, B)
    ]
    for copy in copies:
        copy.start()
    yield
    keep.wait()
    for copy in copies:
        copy.wait()


ANY = pl.BlockSpec(memory_space=pl.ANY)
VMEM = pl.BlockSpec(memory_space=pltpu.VMEM)


def call(kernel, name, collective_id, outs, out_specs, scratch, args, in_specs):
    return pl.pallas_call(
        kernel,
        out_shape=outs,
        in_specs=in_specs,
        out_specs=out_specs,
        scratch_shapes=scratch,
        name=name,
        compiler_params=pltpu.CompilerParams(
            collective_id=collective_id, has_side_effects=True, vmem_limit_bytes=63 * 2**20
        ),
    )(*args)


def shape(*dims, dtype=bf):
    return jax.ShapeDtypeStruct(dims, dtype)


def split_refs(refs, *sizes):
    found, at = [], 0
    for size in sizes:
        found.append(refs[at : at + size])
        at += size
    return found


def select(rows, cols, shift, at, width):
    j = lax.broadcasted_iota(jnp.int32, (1, cols), 1) - at
    wanted = jnp.where((j >= 0) & (j < width), j + shift, -1)
    row = lax.broadcasted_iota(jnp.int32, (rows, cols), 0)
    return jnp.where(row == wanted, 1.0, 0.0).astype(bf)


def select_mixed(rows, cols, shift, j, part):
    col = lax.broadcasted_iota(jnp.int32, (1, cols), 1)
    wanted = jnp.where(
        col // part % 2 == j, shift + col // (2 * part) * part + col % part, -1
    )
    row = lax.broadcasted_iota(jnp.int32, (rows, cols), 0)
    return jnp.where(row == wanted, 1.0, 0.0).astype(bf)


def masks(seq_row, blk_row):
    def columns(ref):
        row = ref[...].astype(f32)
        return row, jnp.broadcast_to(row, (8, row.shape[1])).T[:, :1]

    seq, seq_t = columns(seq_row)
    blk, blk_t = columns(blk_row)
    return seq_t < seq, (seq_t == seq) & (blk_t <= blk)


def rope(ref, at, cosine, sine, out, to, head_dim):
    half = head_dim // 2
    former, latter = ref[pl.ds(at, half), :], ref[pl.ds(at + half, half), :]
    out[pl.ds(to, half), :] = (former * cosine - latter * sine).astype(out.dtype)
    out[pl.ds(to + half, half), :] = (latter * cosine + former * sine).astype(out.dtype)


def attention_forward(B, weights, gates, w_down, gains, tokens, cotangent, ids):
    wrows, width = weights[0].shape
    rows = tokens.shape[0]
    group = 4 * rows
    ff = gates[0].shape[1]
    wcols = width // 4
    head_dim = width // H
    heads = H // 4
    sub = ff // (A * B * 4)
    pad = -(-sub // 16) * 16
    fcols = B * pad
    wide = 384
    span = -(-wcols // 128) * 128
    pair = 2 * wcols
    parts = halves(wrows)
    trio = 3
    score_scale = 1.0 / math.sqrt(head_dim)

    def kernel(*refs):
        w_in, g_in, ins, outs, scratch, refs = split_refs(refs, 4, 2, 6, 12, 19, 100)
        wd_in, gain_in, tok_in, cot_in, seq_row, blk_row = ins
        (w4_out, gain_out, tok_out, d_out, gu_out, dn_out, qkv_out, mixed_out, after_out,
         n2_out, table_out, nt_out) = outs
        (w_all, g_all, wd_all, own4, gu_own, dn_own, own_gain, gain_all, tok_all, d_own, w4_all,
         normed, normed_t, raw, bias, mixed, proj, proj_all, load) = scratch
        s1, s2, s3, s4, s5, s6, s7 = split_refs(refs, 4, 4, 3, 6, 3, 2, 100)
        qkv, mix_x, mix_core, ex_sem, save = s7
        place = Place(B)
        met = greet(place, True, True, True)
        r, x, c = place.r, place.x, place.c
        loads = [pltpu.make_async_copy(w, w_all.at[i], load.at[i]) for i, w in enumerate(w_in)]
        loads += [
            pltpu.make_async_copy(w, g_all.at[i], load.at[4 + i]) for i, w in enumerate(g_in)
        ]
        loads.append(pltpu.make_async_copy(wd_in, wd_all, load.at[6]))
        for copy in loads:
            copy.start()
        start = pl.multiple_of(r * wcols // 128 * 128, 128)
        shift = r * wcols - start
        for i in range(2):
            total = jnp.zeros((wrows, pair), f32)
            for j in range(2):
                loads[2 * i + j].wait()
                pick = select(span, pair, shift, j * wcols, wcols)
                if i:
                    pick = select_mixed(span, pair, shift, j, trio * head_dim)
                total += product(w_all[2 * i + j, :, pl.ds(start, span)], pick)
            own4[:, i * pair : (i + 1) * pair] = total.astype(bf)
        for k in range(width // wide):
            own_gain[:, k * wide : (k + 1) * wide] = jnp.dot(
                gain_in[...], select(wrows, wide, 0, place.s * wrows - k * wide, wrows),
                preferred_element_type=f32,
            )
        met()

        def prepare():
            for i in range(2):
                loads[4 + i].wait()
            loads[6].wait()

            def one(n, carry):
                i, block = n // A, n % A
                total = jnp.zeros((wrows, fcols), f32)
                for j in range(B):
                    first = ((block * B + j) * 4 + r) * sub
                    at = pl.multiple_of(jnp.minimum(first // 128 * 128, ff - wide), 128)
                    total += jnp.dot(
                        g_all[i, :, pl.ds(at, wide)],
                        select(wide, fcols, first - at, j * pad, sub),
                        preferred_element_type=f32,
                    )
                at = pl.multiple_of(i * fcols, 128)
                gu_own[block, :, pl.ds(at, fcols)] = total.astype(bf)
                return carry

            lax.fori_loop(0, 2 * A, one, 0)
            row = lax.broadcasted_iota(jnp.int32, (pad, ff // (A * B)), 0)
            col = lax.broadcasted_iota(jnp.int32, (pad, ff // (A * B)), 1)
            pick = jnp.where((col - r * sub == row) & (row < sub), 1.0, 0.0).astype(bf)
            tile = 768

            def down(n, carry):
                at = pl.ds(pl.multiple_of(n * tile, tile), tile)
                dn_own[:, at] = jnp.dot(
                    pick, wd_all[:, at], preferred_element_type=f32
                ).astype(bf)
                return carry

            lax.fori_loop(0, width // tile, down, 0)
            d_own[...] = (branch_scale * cot_in[...].astype(f32)).astype(bf)
            less, allowed = masks(seq_row, blk_row)
            earlier = jnp.sum(jnp.where(less, 1.0, 0.0), axis=0, keepdims=True)
            at = lax.broadcasted_iota(jnp.int32, (1, group), 1).astype(f32) - earlier
            half = head_dim // 2
            index = lax.broadcasted_iota(jnp.int32, (half, group), 0).astype(f32)
            angle = at * jnp.exp(index * (-2.0 * math.log(rope_base) / head_dim))
            table_out[0] = jnp.cos(angle)
            table_out[1] = jnp.sin(angle)
            bias[...] = jnp.where(allowed, 0.0, masked_score)
            yield
            total = jnp.zeros((8, width), f32)
            for block in range(A):
                for side in range(B):
                    total += gain_all[block, side]
            gain_out[...] = total
            for i in range(4):
                value = tok_all[i].astype(f32)
                factor = lax.rsqrt(jnp.mean(value * value, axis=1, keepdims=True) + norm_eps)
                value = value * factor * total[0:1]
                at = slice(i * rows, (i + 1) * rows)
                normed[at, :] = value.astype(bf)
                normed_t[:, at] = value.T.astype(bf)
            early = [
                pltpu.make_async_copy(normed_t, nt_out, load.at[1]),
                pltpu.make_async_copy(tok_all, tok_out, load.at[2]),
            ]
            for copy in early:
                copy.start()
            yield
            for copy in early:
                copy.wait()

        def share_piece(k):
            at = pl.ds(k * trio * head_dim, trio * head_dim)
            own = mixed.at[r, at]
            far = mixed.at[place.rx, at]
            return (
                remote(own, own, mix_x.at[k, 0], mix_x.at[k, 1], place.over_x),
                remote(own, own, mix_core.at[x, k, 0], mix_core.at[x, k, 1], place.over_core),
                remote(
                    far, far, mix_core.at[1 - x, k, 0], mix_core.at[1 - x, k, 1],
                    place.over_core,
                ),
            )

        pieces = heads // trio

        def attend():
            step = 256

            def project(n, carry):
                cols = pl.ds(pl.multiple_of(span - 128 + n * step, 128), step)
                w = w4_all[:, :, :, cols].reshape(width, step)
                at = pl.ds(pl.multiple_of(n * step, step), step)
                raw[at, :] = product(normed[...], w).T
                return carry

            lax.fori_loop(0, (width - span + 128) // step, project, 0)
            skip = wcols - (span - 128)
            cosine, sine = table_out[0], table_out[1]

            def turn(n, carry):
                at = pl.multiple_of(wcols + n * head_dim, 32)
                i, h = n // heads, n % heads
                first = skip + wcols + (h // trio * 2 + i) * trio * head_dim + h % trio * head_dim
                rope(raw, pl.multiple_of(first, 32), cosine, sine, qkv, at, head_dim)
                return carry

            lax.fori_loop(0, 2 * heads, turn, 0)
            qkv[:wcols, :] = raw[pl.ds(skip, wcols), :].astype(bf)
            pltpu.make_async_copy(qkv, qkv_out, save.at[0]).start()
            yield

            def head(n, carry):
                at = lambda part: pl.ds(pl.multiple_of(part * wcols + n * head_dim, 64), head_dim)
                scores = across(qkv[at(2), :], qkv[at(1), :]) * score_scale + bias[...]
                top = jnp.max(scores, axis=0, keepdims=True)
                powers = jnp.exp(scores - top)
                probs = powers * (1.0 / jnp.sum(powers, axis=0, keepdims=True))
                mixed[r, at(0), :] = product(qkv[at(0), :], probs.astype(bf)).astype(bf)
                return carry

            for k in range(pieces):
                lax.fori_loop(k * trio, (k + 1) * trio, head, 0)
                to_x, near, far = share_piece(k)
                to_x.start()
                near.start()
                if k:
                    to_x, near, far = share_piece(k - 1)
                    to_x.wait_recv()
                    far.start()
                yield
            to_x, near, far = share_piece(pieces - 1)
            to_x.wait_recv()
            far.start()
            for k in range(pieces):
                to_x, near, far = share_piece(k)
                near.wait_recv()
                far.wait_recv()
            everyone = mixed[...].reshape(width, group)
            value = across(everyone, w4_all[:, :, :, :span].reshape(width, span))
            proj[...] = value.astype(bf).reshape(4, rows, span)
            proj_all[r] = proj[r]
            copies = []
            for k in (2, 3, 1):
                to = (r + k) % 4
                copies.append(
                    remote(
                        proj.at[to], proj_all.at[r], ex_sem.at[k, 0], ex_sem.at[k, 1],
                        (place.s, to),
                    )
                )
                copies[-1].start()
            saved = pltpu.make_async_copy(mixed, mixed_out, save.at[1])
            saved.start()
            yield
            for copy in copies:
                copy.wait()
            own = tok_all[r].astype(f32)
            halves_ = []
            for side in range(2):
                total = jnp.zeros((rows, pair), f32)
                for core in range(2):
                    total += jnp.dot(
                        proj_all[side * 2 + core],
                        select(span, pair, 0, core * wcols, wcols), preferred_element_type=f32,
                    )
                at = slice(side * pair, (side + 1) * pair)
                halves_.append(own[:, at] + branch_scale * total)
                after_out[:, at] = halves_[-1]
            mean = sum(jnp.sum(v * v, axis=1, keepdims=True) for v in halves_) / width
            factor = lax.rsqrt(mean + norm_eps)
            for side in range(2):
                at = slice(side * pair, (side + 1) * pair)
                n2_out[:, at] = (halves_[side] * factor * gain_out[1:2, at]).astype(bf)
            yield
            saved.wait()
            pltpu.make_async_copy(qkv, qkv_out, save.at[0]).wait()
            for k in range(pieces):
                to_x, near, far = share_piece(k)
                to_x.wait_send()
                near.wait_send()
                far.wait_send()

        def weights_flow():
            yield from spread_flow(place, own4, w4_all, s1, parts)
            pltpu.make_async_copy(w4_all, w4_out, save.at[2]).start()

        run_flows(
            [
                weights_flow(),
                share_flow(place, tok_in, tok_all, s3),
                spread_flow(place, own_gain, gain_all, s2),
                prepare(),
                widen_flow(place, d_own, d_out, s4),
                columns_flow(place, gu_own, gu_out, s5),
                sides_flow(place, dn_own, dn_out, s6),
                attend(),
            ],
            (0, 1, 2, 3, 1, 1, 1, 2, 2, 2, 2, 2, 3, 3) + (0,) * (2 * parts) + (4,)
            + (0,) * parts + (4, 4, 0, 6, 5, 7, 4, 7, 7, 7, 5, 4, 7, 4, 5, 7, 5, 4, 4, 7, 6, 5, 4),
        )
        pltpu.make_async_copy(w4_all, w4_out, save.at[2]).wait()

    block = (rows, width)
    return call(
        kernel, "attention_forward", 1,
        [
            shape(A, B, wrows, 4 * wcols), shape(8, width, dtype=f32), shape(4, *block),
            shape(X, A, X, *block), shape(A, B, wrows, 2 * fcols), shape(B, pad, width),
            shape(3 * wcols, group), shape(4, wcols, group), shape(*block, dtype=f32),
            shape(*block), shape(2, head_dim // 2, group, dtype=f32), shape(width, group),
        ],
        [ANY, VMEM, ANY, ANY, ANY, ANY, ANY, ANY, VMEM, VMEM, VMEM, ANY],
        [
            pltpu.VMEM((4, wrows, width), bf), pltpu.VMEM((2, wrows, ff), bf),
            pltpu.VMEM(w_down.shape, bf), pltpu.VMEM((wrows, 4 * wcols), bf),
            pltpu.VMEM((A, wrows, 2 * fcols), bf), pltpu.VMEM((pad, width), bf),
            pltpu.VMEM((8, width), f32), pltpu.VMEM((A, B, 8, width), f32),
            pltpu.VMEM((4,) + block, bf), pltpu.VMEM(block, bf),
            pltpu.VMEM((A, B, wrows, 4 * wcols), bf), pltpu.VMEM((group, width), bf),
            pltpu.VMEM((width, group), bf),
            pltpu.VMEM((width - span + 128, group), f32), pltpu.VMEM((group, group), f32),
            pltpu.VMEM((4, wcols, group), bf), pltpu.VMEM((4, rows, span), bf),
            pltpu.VMEM((4, rows, span), bf), DMA((7,)),
        ]
        + spread_sems(B, parts) + spread_sems(B) + share_sems() + widen_sems() + columns_sems(B)
        + sides_sems(B)
        + [
            pltpu.VMEM((3 * wcols, group), bf), DMA((3, 2)), DMA((X, 3, 2)), DMA((4, 2)),
            DMA((3,)),
        ],
        [*weights, *gates, w_down, gains, tokens, cotangent, *ids],
        [ANY] * 7 + [VMEM, ANY] + [VMEM] * 3,
    )


def feed_forward(B, normed_two, d_down, gate_up, down, lefts):
    rows, width = normed_two.shape
    fcols = down.shape[0]
    every = X * A * X * rows
    pair = X * rows
    parts = halves(rows)
    wide = 768
    tile = 384

    wrows = gate_up.shape[0] // (A * B)
    pad = fcols // B
    many = 1152
    most = rows * 3 // 4

    def kernel(n_in, d_in, gu_in, dn_in, *refs):
        lefts_in, (out, f_out, ggu_out, gd_out), lefts_out, refs = split_refs(refs, 2, 4, 2, 100)
        bufs, (line_recv, line_send, over_x, over_core), sems = split_refs(refs, 11, 4, 100)
        n_all, d_all, gu, dn, part, hid, d_gu, from_core, from_x, landed, g_all = bufs
        (g_down, load, core_sem, x_sem, line_sem, gu_side, gd_side, gu_sem, gd_sem, f_core, f_x,
         free, core_free, f_line, left_sem, rest_send, rest_recv) = sems
        place = Place(B)
        a, x, c = place.a, place.x, place.c
        loads = [
            pltpu.make_async_copy(n_in, n_all.at[x, a, c], load.at[0]),
            pltpu.make_async_copy(gu_in, gu, load.at[1]),
            pltpu.make_async_copy(dn_in, dn, load.at[2]),
            pltpu.make_async_copy(d_in, d_all, load.at[3]),
        ]
        for copy in loads:
            copy.start()
        greet(place, True, True, True)()

        def to_line(block, way):
            src = n_all.at[x, block, c]
            return remote(
                src, src, line_send.at[block, (1 - way) // 2], line_recv.at[block],
                place.line(a + way),
            )

        def to_x(block, some=True):
            src = n_all.at[x, block, c]
            if some:
                src = src.at[pl.ds(0, most)]
            return remote(src, src, over_x.at[block, 0], over_x.at[block, 1], place.over_x)

        def rest_to_line(block, way):
            src = n_all.at[1 - x, block, c, pl.ds(most, rows - most)]
            return remote(
                src, src, rest_send.at[block, (1 - way) // 2], rest_recv.at[block],
                place.line(a + way),
            )

        def to_core(side, block):
            src = n_all.at[side, block, c]
            return remote(
                src, src, over_core.at[side, block, 0], over_core.at[side, block, 1],
                place.over_core,
            )

        def sum_core(side, d, h):
            return remote(
                piece(part, (side, d, 1 - c), h, parts), piece(from_core, (side, d), h, parts),
                core_sem.at[side, d, h, 0], core_sem.at[side, d, h, 1], place.over_core,
            )

        def sum_x(d, h):
            return remote(
                piece(part, (1 - x, d, c), h, parts), piece(from_x, d, h, parts),
                x_sem.at[d, h, 0], x_sem.at[d, h, 1], place.over_x,
            )

        def merge(side, d, h):
            sum_core(side, d, h).wait_recv()
            here = piece(part, (side, d, c), h, parts)
            add_into(here, here, piece(from_core, (side, d), h, parts))

        def send_sum(d):
            for h in range(parts):
                merge(1 - x, d, h)
                sum_x(d, h).start()

        loads[0].wait()

        @pl.when(a < A - 1)
        def _():
            to_line(a, 1).start()

        @pl.when(a > 0)
        def _():
            to_line(a, -1).start()

        to_x(a, False).start()
        to_core(x, a).start()

        def left_aside(i, d, k):
            to = (place.b + k) % B
            return remote(
                lefts_in[i].at[d, to], lefts_out[i].at[k - 1, d], left_sem.at[i, k, d, 0],
                left_sem.at[i, k, d, 1], place.side(to),
            )

        left_copies = [(i, d, k) for i in range(2) for d in range(A) for k in range(1, B)]
        for at in left_copies:
            left_aside(*at).start()
        for copy in loads[1:]:
            copy.wait()

        def nearest(i):
            left = jnp.where(a == 1, jnp.where(i == 1, 0, i), jnp.where(i == 0, 0, i))
            left = jnp.where((a == 1) & (i == 0), 1, left)
            right = jnp.where(a == 2, jnp.where(i == 0, 2, jnp.where(i == 1, 1, 3)), A - 1 - i)
            right = jnp.where((a == 2) & (i == A - 1), 0, right)
            return jnp.where(a < 2, left, right)

        def item(j):
            near = (j == 0) | ((j % 2 == 1) & (j < 2 * A - 1))
            i = jnp.where(near, (j + 1) // 2, jnp.where(j == 2 * A - 1, A - 1, j // 2 - 1))
            return near, nearest(i)

        def compute(side, block):
            n = n_all[side, block].reshape(pair, width)
            d = d_all[side, block].reshape(pair, width)
            both = product(n, gu[...])
            gate, up = both[:, :fcols], both[:, fcols:]
            d_hidden = against(d, dn[...])
            sig = jax.nn.sigmoid(gate)
            at = pl.ds(pl.multiple_of((side * A + block) * pair, pair), pair)
            hid[at, :] = (gate * sig * up).astype(bf)
            d_gate = (d_hidden * up * sig * (1.0 + gate * (1.0 - sig))).astype(bf)
            d_up = (d_hidden * gate * sig).astype(bf)
            both = jnp.concatenate([d_gate, d_up], axis=1)
            d_gu[at, :] = both
            for k in range(width // wide):
                cols = pl.ds(k * wide, wide)
                value = against(both, gu[cols, :]).astype(bf)
                part[side, block, :, :, cols] = value.reshape(X, rows, wide)

        def arrive(j, carry):
            near, block = item(j)
            side = jnp.where(near, x, 1 - x)

            @pl.when(near & (j > 0))
            def _():
                way = jnp.where(block < a, 1, -1)
                to_line(block, way).wait_recv()

                @pl.when((a + way >= 0) & (a + way < A))
                def _():
                    to_line(block, way).start()

                to_x(block).start()
                to_core(x, block).start()

            @pl.when(jnp.logical_not(near))
            def _():
                @pl.when(block == a)
                def _():
                    to_x(block, False).wait_recv()
                    for way in (1, -1):
                        @pl.when((a + way >= 0) & (a + way < A))
                        def _():
                            rest_to_line(block, way).start()

                @pl.when(block != a)
                def _():
                    way = jnp.where(block < a, 1, -1)
                    rest_to_line(block, way).wait_recv()

                    @pl.when((a + way >= 0) & (a + way < A))
                    def _():
                        rest_to_line(block, way).start()

                    to_x(block).wait_recv()

                to_core(1 - x, block).start()

            to_core(side, block).wait_recv()
            compute(side, block)
            for h in range(parts):
                sum_core(side, block, h).start()

            before, last = item(jnp.maximum(j - 1, 0))

            @pl.when((j > 3) & jnp.logical_not(before))
            def _():
                send_sum(last)

            return carry

        lax.fori_loop(0, 2 * A, arrive, 0)
        send_sum(nearest(A - 1))
        send_sum(a)
        for d in range(A):
            for h in range(parts):
                merge(x, d, h)
        pl.semaphore_signal(
            core_free, inc=1, device_id=place.over_core, device_id_type=MESH
        )

        def ready(d, h):
            sum_x(d, h).wait_recv()
            here = piece(part, (x, d, c), h, parts)
            add_into(here, here, piece(from_x, d, h, parts))

        piece_rows = rows // parts

        def final(h):
            at = pl.ds(h * piece_rows, piece_rows)
            out[at, :] = part[x, a, c, at, :]

        chain = line_slots(
            place, lambda d: part.at[x, d, c], lambda d, way: landed.at[d + (way > 0)], line_sem,
            parts, ready, final, near=True,
        )

        def grad_down(k, carry):
            at = pl.ds(pl.multiple_of(k * tile, tile), tile)
            d = d_all[:, :, :, :, at].reshape(every, tile)
            g_down[:, at] = across(hid[...], d).astype(bf)
            return carry

        def grad_gate_up(k, carry):
            at = pl.ds(pl.multiple_of(k * many, many), many)
            n = n_all[:, :, :, :, at].reshape(every, many)
            count = many // wrows
            for i in range(2):
                cols = pl.ds(i * fcols, fcols)
                value = across(n, d_gu[:, cols]).astype(bf)
                g_all[pl.ds(k * count, count), :, cols] = value.reshape(count, wrows, fcols)
            return carry

        def aside(d, k):
            to = (place.b + k) % B
            return remote(
                g_all.at[d * B + to], gu_side.at[k - 1, d], gu_sem.at[k, d, 0],
                gu_sem.at[k, d, 1], place.side(to),
            )

        def aside_down(k):
            to = (place.b + k) % B
            at = pl.ds(pl.multiple_of(to * pad, 16), pad)
            return remote(
                g_down.at[at], gd_side.at[k - 1], gd_sem.at[k, 0], gd_sem.at[k, 1], place.side(to)
            )

        def forward(k, carry):
            side, block = k // A, k % A
            at = pl.ds(pl.multiple_of(k * pair, pair), pair)
            for i in range(width // wide):
                cols = pl.ds(i * wide, wide)
                value = product(hid[at, :], dn[:, cols]).astype(bf)
                d_all[side, block, :, :, cols] = value.reshape(X, rows, wide)
            return carry

        mine = pl.ds(pl.multiple_of(place.b * pad, 16), pad)
        outs = [pltpu.make_async_copy(g_down.at[mine], gd_out, load.at[0])] + [
            pltpu.make_async_copy(g_all.at[d * B + place.b], ggu_out.at[d], load.at[1 + d])
            for d in range(A)
        ]

        def out_core(side, d):
            return remote(
                d_all.at[side, d, 1 - c], from_core.at[side, d], f_core.at[side, d, 0],
                f_core.at[side, d, 1], place.over_core,
            )

        def out_x(d):
            return remote(
                d_all.at[1 - x, d, c], n_all.at[0, d, 1], f_x.at[d, 0], f_x.at[d, 1],
                place.over_x,
            )

        def out_merge(side, d):
            out_core(side, d).wait_recv()
            here = d_all.at[side, d, c]
            add_into(here, here, from_core.at[side, d])

        def out_ready(d, h):
            out_merge(x, d)
            out_x(d).wait_recv()
            here = d_all.at[x, d, c]
            add_into(here, here, n_all.at[0, d, 1])

        def out_final(h):
            pltpu.make_async_copy(d_all.at[x, a, c], f_out, load.at[1 + A]).start()

        def out_landing(d, way):
            return part.at[0, d, 1 - c] if way > 0 else n_all.at[1, d, 1]

        out_chain = line_slots(
            place, lambda d: d_all.at[x, d, c], out_landing, f_line, 1, out_ready, out_final
        )

        lax.fori_loop(0, width // tile, grad_down, 0)
        for k in range(1, B):
            aside_down(k).start()
        next(chain)
        lax.fori_loop(0, X * A, forward, 0)
        pl.semaphore_wait(core_free, 1)
        for side in (1 - x, x):
            for i in range(A):
                out_core(side, far_first(a, i)).start()
        next(chain)
        for k in range(width // many):
            grad_gate_up(k, 0)
            for d in range(k * many // (wrows * B), (k + 1) * many // (wrows * B)):
                for j in range(1, B):
                    aside(d, j).start()
            next(chain)
        for d in range(A):
            @pl.when(d == a)
            def _():
                to_x(d, False).wait_send()

            @pl.when(d != a)
            def _():
                to_x(d).wait_send()

            for side in range(X):
                to_core(side, d).wait_send()
                for h in range(parts):
                    sum_core(side, d, h).wait_send()

            @pl.when((a < A - 1) & (d <= a))
            def _():
                to_line(d, 1).wait_send()
                rest_to_line(d, 1).wait_send()

            @pl.when((a > 0) & (d >= a))
            def _():
                to_line(d, -1).wait_send()
                rest_to_line(d, -1).wait_send()

        for device in [place.over_x] + [place.line((a + k) % A) for k in range(1, A)]:
            pl.semaphore_signal(free, inc=1, device_id=device, device_id_type=MESH)
        for i in range(A):
            out_merge(1 - x, far_first(a, i))
        pl.semaphore_wait(free, A)
        for i in range(A):
            out_x(far_first(a, i)).start()
        next(chain)
        for k in range(1, B):
            aside_down(k).wait_recv()
            add_into(g_down.at[mine], g_down.at[mine], gd_side.at[k - 1])
        outs[0].start()
        for _ in chain:
            pass
        next(out_chain)
        for d in range(A):
            for k in range(1, B):
                aside(d, k).wait_recv()
                here = g_all.at[d * B + place.b]
                add_into(here, here, gu_side.at[k - 1, d])
            outs[1 + d].start()
        for _ in out_chain:
            pass
        pltpu.make_async_copy(d_all.at[x, a, c], f_out, load.at[1 + A]).wait()
        for at in left_copies:
            left_aside(*at).wait()
        for copy in outs:
            copy.wait()
        for k in range(1, B):
            aside_down(k).wait_send()
            for d in range(A):
                aside(d, k).wait_send()
        for d in range(A):
            out_x(d).wait_send()
            for side in range(X):
                out_core(side, d).wait_send()
            for h in range(parts):
                sum_x(d, h).wait_send()

    block = (rows, width)
    return call(
        kernel, "feed_forward", 2,
        [
            shape(*block), shape(*block), shape(A, wrows, 2 * fcols),
            shape(pad, width),
        ]
        + [shape(B - 1, A, *v.shape[2:]) for v in lefts],
        [VMEM] + [ANY] * 5,
        [
            pltpu.VMEM((X, A, X) + block, bf), pltpu.VMEM((X, A, X) + block, bf),
            pltpu.VMEM(gate_up.shape, bf), pltpu.VMEM(down.shape, bf),
            pltpu.VMEM((X, A, X) + block, bf), pltpu.VMEM((every, fcols), bf),
            pltpu.VMEM((every, 2 * fcols), bf), pltpu.VMEM((X, A) + block, bf),
            pltpu.VMEM((A,) + block, bf), pltpu.VMEM((A + 1,) + block, bf),
            pltpu.VMEM((A * B, wrows, 2 * fcols), bf),
            DMA((A,)), DMA((A, 2)), DMA((A, 2)), DMA((X, A, 2)),
            pltpu.VMEM((fcols, width), bf), DMA((2 + A,)), DMA((X, A, parts, 2)),
            DMA((A, parts, 2)), DMA((2, A, parts, 2)),
            pltpu.VMEM((B - 1, A, wrows, 2 * fcols), bf), pltpu.VMEM((B - 1, pad, width), bf),
            DMA((B, A, 2)), DMA((B, 2)), DMA((X, A, 2)), DMA((A, 2)), pltpu.SemaphoreType.REGULAR,
            pltpu.SemaphoreType.REGULAR,
            DMA((2, A, 1, 2)), DMA((2, B, A, 2)), DMA((A, 2)), DMA((A,)),
        ],
        [normed_two, d_down, gate_up, down, *lefts],
        [ANY] * 6,
    )


def fold_scratch(rows, width):
    block = (rows, width)
    return [
        pltpu.VMEM((X * X,) + block, bf), pltpu.VMEM((X,) + block, bf), pltpu.VMEM(block, bf),
        DMA((X, 2)), DMA((2,)),
    ]


def fold_flow(place, scratch):
    part, from_core, from_x, core_sem, x_sem = scratch
    x, c = place.x, place.c

    def to_core(i):
        return remote(
            part.at[i * X + 1 - c], from_core.at[i], core_sem.at[i, 0], core_sem.at[i, 1],
            place.over_core,
        )

    def merge(i):
        to_core(i).wait_recv()
        here = part.at[i * X + c]
        add_into(here, here, from_core.at[i])

    to_x = remote(part.at[place.rx], from_x, x_sem.at[0], x_sem.at[1], place.over_x)
    to_core(1 - x).start()
    to_core(x).start()
    yield
    merge(1 - x)
    to_x.start()
    merge(x)
    yield
    to_x.wait_recv()
    here = part.at[place.r]
    add_into(here, here, from_x)
    yield
    to_x.wait_send()
    for i in range(X):
        to_core(i).wait_send()


def owners_flow(place, own, out, sems):
    line, local = sems
    a = place.a
    keep = pltpu.make_async_copy(own.at[a], out.at[a], local.at[0])
    keep.start()
    copies = []
    for k in (1, 3, 2):
        to = (a + k) % A
        copies.append(
            remote(own.at[to], out.at[a], line.at[k, 0], line.at[k, 1], place.line(to))
        )
        copies[-1].start()
    yield
    keep.wait()
    for copy in copies:
        copy.wait()


def grad_scratch(rows, width):
    block = (rows, width)
    P_ = halves(rows)
    return [
        pltpu.VMEM((A,) + block, bf), pltpu.VMEM((A + 1,) + block, bf), DMA((2, A, P_, 2)),
        DMA((P_, 2)), DMA((X, P_, 2)), DMA((P_,)),
    ]


def grad_flow(place, produce, out, scratch):
    sums, landed, line_sem, x_sem, core_sem, local = scratch
    r, x = place.r, place.x
    parts = halves(out.shape[1])
    for i in range(A):
        d = far_first(place.a, i)
        sums[d] = produce(d)
    yield

    def keep(src, h):
        return pltpu.make_async_copy(src, piece(out, r, h, parts), local.at[h])

    def to_x(src, h):
        return remote(src, piece(out, r, h, parts), x_sem.at[h, 0], x_sem.at[h, 1], place.over_x)

    def near(src, h):
        return remote(
            src, piece(out, r, h, parts), core_sem.at[x, h, 0], core_sem.at[x, h, 1],
            place.over_core,
        )

    def far(h):
        src = piece(out, place.rx, h, parts)
        return remote(
            src, src, core_sem.at[1 - x, h, 0], core_sem.at[1 - x, h, 1], place.over_core
        )

    def final(h):
        src = piece(sums, place.a, h, parts)
        to_x(src, h).start()
        near(src, h).start()
        keep(src, h).start()

    yield from line_slots(
        place, lambda d: sums.at[d], lambda d, way: landed.at[d + (way > 0)], line_sem, parts,
        lambda d, h: None, final,
    )
    for h in range(parts):
        src = piece(out, r, h, parts)
        keep(src, h).wait()
        near(src, h).wait()
    yield
    for h in range(parts):
        src = piece(out, r, h, parts)
        to_x(src, h).wait_recv()
        far(h).start()
    yield
    for h in range(parts):
        to_x(piece(out, r, h, parts), h).wait_send()
        far(h).wait()


def attention_backward(
    B, S, d_n2, after_attn, cotangent, gains, w4, qkv, tokens, lefts, tables, ids, g_gate_up,
    g_down,
):
    rows, width = d_n2.shape
    group = 4 * rows
    wrows, wcols = width // S, width // 4
    head_dim = width // H
    heads = H // 4
    wide = 384
    span = -(-wcols // 128) * 128
    skip = wcols - (span - 128)
    tail = width - span + 128
    trio = 3
    third = 2 * trio * head_dim
    thirds = heads // trio
    score_scale = 1.0 / math.sqrt(head_dim)
    widths = (span - 128, span) + (third,) * thirds
    count = len(widths)
    wrows_wide = -(-wrows // 128) * 128

    def kernel(*refs):
        ins, lefts_in, ids_in, outs, mids, own, refs = split_refs(
            refs, 10, 4, 2, 2, count + 3, 20, 100
        )
        (dn2_in, after_in, cot_in, gain_in, w4_in, qkv_in, tok_in, table_in, gu_in, gd_in) = ins
        seq_row, blk_row = ids_in
        gt_out, gain_out = outs
        shared, (gu_cols, gu_all, gd_all) = mids[:count], mids[count:]
        (w4, qkv_, mix, mix_far, n_t, n_far, tok, bias, factors, d_t, d_nat, d_far, ex_send,
         ex_all, ex_far, d_after, own_gain, gain_all, load, side_sem) = own
        f1, f2, u1, u2, u3, (ex_sem, gain_sem), *grads = split_refs(
            refs, 5, 5, 2, 3, 3, 2, *(6,) * count
        )
        place = Place(B)
        met = greet(place, True, True, True)
        r, x, c = place.r, place.x, place.c
        loads = [
            pltpu.make_async_copy(src, dst, load.at[i])
            for i, (src, dst) in enumerate(
                [
                    (tok_in, tok), (w4_in, w4), (lefts_in[0].at[:, place.b], mix),
                    (lefts_in[1], mix_far), (qkv_in, qkv_), (lefts_in[2].at[:, place.b], n_t),
                    (lefts_in[3], n_far),
                ]
            )
        ]
        for copy in loads:
            copy.start()
        part1, part2 = f1[0], f2[0]
        gain_one, gain_two = gain_in[0:1], gain_in[1:2]
        own_gain[...] = jnp.zeros_like(own_gain)
        step = 32

        def back_two(i, carry):
            at = pl.ds(pl.multiple_of(i * step, step), step)
            after = after_in[at, :]
            d = dn2_in[at, :].astype(f32)
            factor = lax.rsqrt(jnp.mean(after * after, axis=1, keepdims=True) + norm_eps)
            own_gain[1:2, :] += jnp.sum(d * after * factor, axis=0, keepdims=True)
            u = d * gain_two
            mean = jnp.mean(u * after, axis=1, keepdims=True)
            d_after[at, :] = (
                cot_in[at, :].astype(f32) + factor * u - after * (factor * factor * factor) * mean
            )
            return carry

        lax.fori_loop(0, rows // step, back_two, 0)
        d_proj = (branch_scale * d_after[...]).astype(bf)
        for k in range(4):
            at = k * wcols // 128 * 128
            ex_send[k] = product(
                d_proj[:, at : at + span], select(span, span, k * wcols - at, 0, wcols)
            ).astype(bf)
        ex_all[r] = ex_send[r]
        met()
        exchange = []
        for k in (2, 3, 1):
            to = (r + k) % 4
            exchange.append(
                remote(
                    ex_send.at[to], ex_all.at[r], ex_sem.at[k, 0], ex_sem.at[k, 1],
                    (place.s, to),
                )
            )
            exchange[-1].start()

        def at_head(part, n):
            return pl.ds(pl.multiple_of(part * wcols + n * head_dim, 64), head_dim)

        def probs_of(n):
            scores = across(qkv_[at_head(2, n), :], qkv_[at_head(1, n), :]) * score_scale
            scores = scores + bias[...].astype(f32)
            powers = jnp.exp(scores - jnp.max(scores, axis=0, keepdims=True))
            return powers * (1.0 / jnp.sum(powers, axis=0, keepdims=True))

        def aside(src, dst, i):
            return [
                remote(
                    src, dst(k - 1), side_sem.at[i, k, 0], side_sem.at[i, k, 1],
                    place.side((place.b + k) % B),
                )
                for k in range(1, B)
            ]

        def lanes(i):
            return pl.ds(0, span) if i == 1 else pl.ds(span + (i - 2) * third, third)

        def aside_of(i):
            if i == 0:
                return aside(ex_all, lambda k: ex_far.at[k], 0)
            return aside(d_nat.at[:, lanes(i)], lambda k: d_far.at[k, :, lanes(i)], i)

        def compute():
            _, allowed = masks(seq_row, blk_row)
            bias[...] = jnp.where(allowed, 0.0, masked_score).astype(bf)
            for i in range(4):
                loads[0].wait() if i == 0 else None
                value = tok[i].astype(f32)
                factors[i * rows : (i + 1) * rows, :] = lax.rsqrt(
                    jnp.mean(value * value, axis=1, keepdims=True) + norm_eps
                )
            for copy in exchange:
                copy.wait()
            for copy in aside_of(0):
                copy.start()
            for copy in loads[1:]:
                copy.wait()
            d_proj = ex_all[...].reshape(group, span)
            for i in (1 - c, c):
                for side in range(X):
                    k = side * X + i
                    at = pl.ds(pl.multiple_of(k * wcols, 64), wcols)
                    part1[k] = against(w4[at, :span], d_proj).astype(bf)
            yield

            def values_back(n, carry):
                d_m = part1[r, pl.ds(pl.multiple_of(n * head_dim, 64), head_dim), :]
                value = against(d_m, probs_of(n).astype(bf))
                at = pl.ds(pl.multiple_of(skip + n * head_dim, 64), head_dim)
                d_t[at, :] = value.astype(bf)
                return carry

            def flip(n, carry):
                at = pl.ds(pl.multiple_of(n * 128, 128), 128)
                d_nat[:, at] = d_t[at, :].astype(f32).T.astype(bf)
                return carry

            d_t[:skip, :] = jnp.zeros((skip, group), bf)
            for k in range(thirds):
                lax.fori_loop(trio * k, trio * (k + 1), values_back, 0)
                if k + 1 < thirds:
                    yield
            lax.fori_loop(0, span // 128, flip, 0)
            for copy in aside_of(1):
                copy.start()
            yield
            cosine, sine = table_in[0], table_in[1]
            half = head_dim // 2

            def turn_back(value, at):
                former, latter = value[:half], value[half:]
                d_t[pl.ds(at, half), :] = (former * cosine + latter * sine).astype(bf)
                d_t[pl.ds(at + half, half), :] = (latter * cosine - former * sine).astype(bf)

            def scores_back(n, carry):
                d_m = part1[r, pl.ds(pl.multiple_of(n * head_dim, 64), head_dim), :]
                probs = probs_of(n)
                d_probs = across(qkv_[at_head(0, n), :], d_m)
                d_s = probs * (d_probs - jnp.sum(d_probs * probs, axis=0, keepdims=True))
                d_s = d_s.astype(bf)
                at = span + n // trio * third + n % trio * head_dim
                turn_back(
                    product(qkv_[at_head(2, n), :], d_s) * score_scale, pl.multiple_of(at, 64)
                )
                turn_back(
                    against(qkv_[at_head(1, n), :], d_s) * score_scale,
                    pl.multiple_of(at + third // 2, 64),
                )
                return carry

            for k in range(thirds):
                lax.fori_loop(trio * k, trio * (k + 1), scores_back, 0)
                first = (span + third * k) // 128
                lax.fori_loop(first, first + third // 128, flip, 0)
                for copy in aside_of(2 + k):
                    copy.start()
                yield

            def inputs_back(n, carry):
                at = pl.ds(pl.multiple_of(n * wide, 128), wide)
                value = against(d_nat[...], w4[at, pl.ds(span - 128, tail)])
                x_f = tok[:, :, at].reshape(group, wide).astype(f32) * factors[...]
                own_gain[0:1, at] = jnp.sum(value * x_f, axis=0, keepdims=True)
                part2[:, :, at] = value.astype(bf).reshape(4, rows, wide)
                return carry

            lax.fori_loop(0, width // wide, inputs_back, 0)

        def make(i):
            def produce(d):
                if i == 0:
                    own, far, right = mix, mix_far, ex_all[:, :, : span - 128]
                    right = right.reshape(group, span - 128)
                else:
                    own, far, right = n_t, n_far, d_nat[:, lanes(i)]
                total = product(own[d], right)
                for k in range(B - 1):
                    if i == 0:
                        right = ex_far[k, :, :, : span - 128].reshape(group, span - 128)
                    else:
                        right = d_far[k, :, lanes(i)]
                    total += product(far[k, d], right)
                if i == 1:
                    last = product(mix[d], ex_all[:, :, span - 128 :].reshape(group, 128))
                    for k in range(B - 1):
                        right = ex_far[k, :, :, span - 128 :].reshape(group, 128)
                        last += product(mix_far[k, d], right)
                    total = jnp.concatenate([total[:, :128] + last, total[:, 128:]], axis=1)
                return total.astype(bf)

            return produce

        def grad(i):
            for copy in aside_of(i):
                copy.wait_recv()
            yield from grad_flow(place, make(i), shared[i], grads[i])
            for copy in aside_of(i):
                copy.wait_send()

        def gains_flow():
            def send(i, device):
                return remote(
                    own_gain, gain_all.at[i], gain_sem.at[i, 0], gain_sem.at[i, 1], device
                )

            stages = [
                [place.over_core], [place.over_x],
                [place.side((place.b + k) % B) for k in range(1, B)],
                [place.line((place.a + k) % A) for k in range(1, A)],
            ]
            at = 0
            for stage in stages:
                copies = [send(at + i, device) for i, device in enumerate(stage)]
                for copy in copies:
                    copy.start()
                yield
                for copy in copies:
                    copy.wait()
                for i in range(len(stage)):
                    own_gain[...] += gain_all[at + i]
                at += len(stage)
            for n in range(width // wide):
                own = slice(n * wide, (n + 1) * wide)
                total = own_gain[:, own]
                pick = select(wide, wrows_wide, place.s * wrows - n * wide, 0, wrows)
                value = jnp.zeros((8, wrows_wide), f32)
                for _ in range(3):
                    low = total.astype(bf)
                    value += product(low, pick)
                    total = total - low.astype(f32)
                gain_out[...] = value if n == 0 else gain_out[...] + value

        def input_end():
            def back_one(i, carry):
                at = pl.ds(pl.multiple_of(i * step, step), step)
                value = tok[r, at, :].astype(f32)
                d = part2[r, at, :].astype(f32)
                factor = lax.rsqrt(jnp.mean(value * value, axis=1, keepdims=True) + norm_eps)
                u = d * gain_one
                mean = jnp.mean(u * value, axis=1, keepdims=True)
                gt_out[at, :] = (
                    d_after[at, :] + factor * u - value * (factor * factor * factor) * mean
                ).astype(bf)
                return carry

            lax.fori_loop(0, rows // step, back_one, 0)
            yield

        M, F1, F2, GU, SU, SD, G, T, O, V, P, Q, R = range(13)
        flows = [
            compute(),
            fold_flow(place, f1),
            fold_flow(place, f2),
            owners_flow(place, gu_in, gu_cols, u1),
            share_flow(place, gu_cols, gu_all, u2),
            share_flow(place, gd_in, gd_all, u3),
            gains_flow(),
            input_end(),
        ] + [grad(i) for i in range(count)]
        turns = [
            GU, M, F1, F1, F1, F1, SD, O, O, M, M, M, GU, SU, M, O, V, M, O, V, M, O, V, P, M, SD,
            F2, V, P, Q, F2, V, P, Q, R, O, SU, P, Q, R, F2, F2, T, P, Q, R, O, V, Q, R, G, SD, SU,
            V, R, O, P, V, G, R, G, R, G, R, G,
        ]
        run_flows(flows, turns)

    block = (rows, width)
    left = (wrows, group)
    return call(
        kernel, "attention_backward", 3,
        [shape(*block), shape(8, wrows_wide, dtype=f32)]
        + [shape(4, wrows, w) for w in widths]
        + [shape(*g_gate_up.shape), shape(4, *g_gate_up.shape), shape(4, *g_down.shape)],
        [VMEM, VMEM] + [ANY] * (count + 3),
        [
            pltpu.VMEM((width, width), bf), pltpu.VMEM((3 * wcols, group), bf),
            pltpu.VMEM((A,) + left, bf), pltpu.VMEM((B - 1, A) + left, bf),
            pltpu.VMEM((A,) + left, bf), pltpu.VMEM((B - 1, A) + left, bf),
            pltpu.VMEM((4,) + block, bf), pltpu.VMEM((group, group), bf),
            pltpu.VMEM((group, 1), f32), pltpu.VMEM((tail, group), bf),
            pltpu.VMEM((group, tail), bf), pltpu.VMEM((B - 1, group, tail), bf),
            pltpu.VMEM((4, rows, span), bf), pltpu.VMEM((4, rows, span), bf),
            pltpu.VMEM((B - 1, 4, rows, span), bf), pltpu.VMEM(block, f32),
            pltpu.VMEM((8, width), f32), pltpu.VMEM((A + B, 8, width), f32), DMA((7,)),
            DMA((count, B, 2)),
        ]
        + fold_scratch(wcols, group) + fold_scratch(*block)
        + [DMA((A, 2)), DMA((1,))] + share_sems() + share_sems()
        + [DMA((4, 2)), DMA((A + B, 2))]
        + [v for w in widths for v in grad_scratch(wrows, w)],
        [
            d_n2, after_attn, cotangent, gains, w4, qkv, tokens, tables, g_gate_up, g_down,
            *lefts, *ids,
        ],
        [VMEM] * 4 + [ANY] * 3 + [VMEM] + [ANY] * 6 + [VMEM] * 2,
    )


def lay_out(S, ff, width, out, value, groups, gate_up, down, after_attn, ffn_out):
    wrows, span = value.shape[1:]
    tokens = after_attn.shape[0]
    wcols = width // 4
    pair = 2 * wcols
    skip = wcols - (span - 128)
    sub = ff // (S * 4)
    pad = down.shape[1]
    fcols = gate_up.shape[3] // 2
    B = fcols // pad
    drows = ff // S
    steps = 2 if wrows % (2 * 16) == 0 else 1
    rows, cols = wrows // steps, width // steps

    def kernel(o_in, v_in, *refs):
        g_in, ins, outs = split_refs(refs, len(groups), 4, 8)
        gu_in, d_in, after_in, f_in = ins
        o_out, q_out, k_out, v_out, g_out, u_out, d_out, r_out = outs
        r_out[...] = (after_in[...] + branch_scale * f_in[...].astype(f32)).astype(bf)

        def beside(pieces, to):
            for side in range(2):
                parts = [
                    ref[side * 2 + core].astype(f32)[:, at : at + size]
                    for core in range(2) for ref, at, size in pieces
                ]
                to[:, side * pair : (side + 1) * pair] = jnp.concatenate(parts, axis=1)

        half = groups[0].shape[2] // 2
        beside([(o_in, 0, wcols - skip), (v_in, 0, skip)], o_out)
        beside([(v_in, skip, wcols)], v_out)
        beside([(ref, 0, half) for ref in g_in], q_out)
        beside([(ref, half, half) for ref in g_in], k_out)
        for i, to in enumerate((g_out, u_out)):
            parts = []
            for m in range(4 * S):
                s = m // 4
                at = i * fcols + s % B * pad
                parts.append(gu_in[m % 4, s // B].astype(f32)[:, at : at + sub])
            to[...] = jnp.concatenate(parts, axis=1)
        d_out[...] = jnp.concatenate([d_in[k].astype(f32)[:sub] for k in range(4)], axis=0)

    def by_rows(ref):
        lead = len(ref.shape) - 2
        return pl.BlockSpec(
            ref.shape[:lead] + (rows, ref.shape[-1]), lambda i: (0,) * lead + (i, 0)
        )

    outs = [shape(wrows, width, dtype=f32)] * 4 + [shape(wrows, ff, dtype=f32)] * 2
    return pl.pallas_call(
        kernel,
        grid=(steps,),
        out_shape=outs + [shape(drows, width, dtype=f32), shape(tokens, width)],
        in_specs=[by_rows(v) for v in (out, value, *groups, gate_up)]
        + [pl.BlockSpec((4, pad, cols), lambda i: (0, 0, i))]
        + [pl.BlockSpec((tokens, cols), lambda i: (0, i))] * 2,
        out_specs=[by_rows(v) for v in outs]
        + [pl.BlockSpec((n, cols), lambda i: (0, i)) for n in (drows, tokens)],
        name="lay_out",
        compiler_params=pltpu.CompilerParams(vmem_limit_bytes=60 * 2**20),
    )(out, value, *groups, gate_up, down, after_attn, ffn_out)


def product(left_side, right_side):
    return jnp.dot(left_side, right_side, preferred_element_type=f32)


def against(left_side, right_side):
    return lax.dot_general(
        left_side, right_side, (((1,), (1,)), ((), ())), preferred_element_type=f32
    )


def across(left_side, right_side):
    return lax.dot_general(
        left_side, right_side, (((0,), (0,)), ((), ())), preferred_element_type=f32
    )


def body(
    tokens,
    attn_gain,
    w_query,
    w_key,
    w_value,
    w_out,
    ffn_gain,
    w_gate,
    w_up,
    w_down,
    seq_ids,
    block_ids,
    cotangent,
):
    S = lax.axis_size("shard")
    R = lax.axis_size("replica")
    B = S // A
    rows, width = tokens.shape
    ff = w_gate.shape[1]
    wrows = width // S
    ids = (seq_ids[None, :], block_ids[None, :])
    gains = jnp.pad(jnp.stack([attn_gain, ffn_gain]), ((0, 6), (0, 0)))
    (
        w4, gains, tokens_group, d_down, gate_up, down_w, qkv, mixed_all, after_attn, normed_two,
        tables, normed_t,
    ) = attention_forward(
        B, [w_out, w_value, w_query, w_key], [w_gate, w_up], w_down, gains, tokens, cotangent, ids
    )
    lefts = [v.reshape(A, B, wrows, -1) for v in (mixed_all, normed_t)]
    d_n2, ffn_out, g_gate_up, g_down, mixed_far, normed_far = feed_forward(
        B, normed_two, d_down, gate_up.reshape(width, -1), down_w.reshape(-1, width), lefts
    )
    grad_tokens, gain_sums, g_out, g_value, *parts = attention_backward(
        B, S, d_n2, after_attn, cotangent, gains, w4.reshape(width, width), qkv, tokens_group,
        [lefts[0], mixed_far, lefts[1], normed_far], tables, ids, g_gate_up, g_down,
    )
    g_out, g_query, g_key, g_value, g_gate, g_up, g_down, result = lay_out(
        S, ff, width, g_out, g_value, parts[:-3], *parts[-2:], after_attn, ffn_out
    )
    return (
        result, grad_tokens, gain_sums[0, :wrows], g_query, g_key, g_value, g_out,
        gain_sums[1, :wrows], g_gate, g_up, g_down,
    )


def solution(mesh):
    split = P(("shard", "replica"), None)
    vec, mat = P("shard"), P("shard", None)
    in_specs = (split, vec, mat, mat, mat, mat, vec, mat, mat, mat, vec, vec, split)
    out_specs = (split, split, vec, mat, mat, mat, mat, vec, mat, mat, mat)
    return jax.shard_map(body, mesh=mesh, in_specs=in_specs, out_specs=out_specs, check_vma=False)
```
